32 devices in a mesh: groups: 2 (over x), mp: 8 (over z, y), pool: 2 (over core).
Axes of the slice: x: 2, y: 2, z: 4, core: 2. Of those that a mesh axis runs over, the one named last changes fastest.
Arguments:
- states: bfloat16 [4, 512, 8192], P(('groups', 'pool'), 'mp'), parts along dimension 0, may hold values from -6 to 6
- norm_gain: bfloat16 [8192], replicated, may hold values from 0.099609375 to 1.8984375
- w_query: bfloat16 [8192, 8192], P(None, 'mp'), may hold values from -0.0625 to 0.0625
- q_bias: bfloat16 [8192], P('mp'), may hold values from -36 to 36
- w_key: bfloat16 [8192, 1024], P(None, 'mp'), may hold values from -0.0625 to 0.0625
- w_value: bfloat16 [8192, 1024], P(None, 'mp'), may hold values from -0.0625 to 0.0625
- k_bias: bfloat16 [1024], P('mp'), may hold values from -3 to 3
- v_bias: bfloat16 [1024], P('mp'), may hold values from -3 to 3
- w_out: bfloat16 [8192, 8192], P('mp'), may hold values from -0.0625 to 0.0625
- kv_pool: bfloat16 [32, 64, 16, 2048], P(('groups', 'mp', 'pool')), parts along dimension 0, may hold values from -12 to 12
- hit_holder: int32 [4, 256], P('groups'), parts along dimension 0, may hold values from 0 to 15, as said below
- hit_slot: int32 [4, 256], P('groups'), parts along dimension 0, may hold values from 0 to 63
- prefix_len: int32 [4], P('groups'), parts along dimension 0, may hold values from 2048 to 4096, as said below
Outputs:
- attn_out: bfloat16 [4, 512, 8192], P(('groups', 'pool'), 'mp'), parts along dimension 0
- kv_new: bfloat16 [4, 512, 2048], P(('groups', 'pool'), 'mp'), parts along dimension 0
The draws below stay inside these ranges and needn't reach their ends.
There are 2 independent parts, one for each index of `groups`. The reference program is written for one: setup_inputs(seed, part) draws one part's arguments, and reference() takes and returns one part's arrays. A program takes and returns all parts, laid end to end along the dimension named above; an argument that names none is the same for every part. Nothing has to cross between parts.
Inputs may be any that keep to these rules, and one draw needn't show every extreme that they name: `hit_holder`: for each request, at most 32 of its blocks name one holder, and exactly 32 name some holder. `prefix_len`: one request's prefix has exactly 4096 tokens.
All inputs are finite; a program needn't handle non-finite values.
Results may differ from the reference program's by a relative error of at most 0.014.
Values may be sent and summed in bfloat16 or wider, within the bound.
No kernel may reach another device: no remote copies, remote signals or barrier semaphores. Data moves between devices by JAX's collectives and lax.ppermute only.
A program may use at most 192 MiB of HBM per device.

```python
import jax
import jax.numpy as jnp
from jax import lax

D = 8192
QH = 64
KVH = 8
HD = 128
SUF = 512
PRE = 4096
BT = 16
REQS = 2
NBLK = 256
HOLDERS = 16
CAP = 32
SLOTS = 64
N_MP = 8


def draw_hit_holder(key, part):
    key = jax.random.fold_in(key, 11)
    tables = []
    for request in range(REQS):
        request_key = jax.random.fold_in(key, request)
        first_key, second_key, third_key = jax.random.split(request_key, 3)
        special = jax.random.randint(first_key, (), 0, HOLDERS)
        others = (special + 1 + jnp.arange((HOLDERS - 1) * CAP) // CAP) % HOLDERS
        shuffled = jax.random.permutation(second_key, (HOLDERS - 1) * CAP)
        picked = others[shuffled[:NBLK - CAP]]
        listed = jnp.concatenate([jnp.full((CAP,), special), picked])
        reorder = jax.random.permutation(third_key, NBLK)
        tables.append(listed[reorder])
    return jnp.stack(tables).astype(jnp.int32)


def draw_prefix_len(key, part):
    key = jax.random.fold_in(key, 23)
    first_key, second_key = jax.random.split(key)
    drawn_lengths = jax.random.randint(first_key, (REQS,), PRE // 2, PRE + 1)
    chosen_row = jax.random.randint(second_key, (), 0, REQS)
    return jnp.where(jnp.arange(REQS) == chosen_row, PRE, drawn_lengths).astype(jnp.int32)


def draw_q_bias(key, part):
    key = jax.random.fold_in(key, 37)
    first_key = jax.random.fold_in(key, 0)
    base_values = 0.5 * jnp.clip(jax.random.normal(first_key, (QH, HD), jnp.float32), -6.0, 6.0)
    return base_values.reshape(QH * HD).astype(jnp.bfloat16)


def draw_kv_pool(key, part):
    key = jax.random.fold_in(key, 41)
    first_key = jax.random.fold_in(key, 0)
    full_shape = (HOLDERS, SLOTS, BT, KVH, 2, HD)
    part_scale = jnp.array([2.5, 1.0], jnp.float32)[:, None]
    base_values = jnp.clip(jax.random.normal(first_key, full_shape, jnp.float32), -4.0, 4.0) * part_scale
    return base_values.reshape(HOLDERS, SLOTS, BT, KVH * 2 * HD).astype(jnp.bfloat16)


def set_ends(values, rng, smallest, top_value):
    index_at = [jax.random.randint(jax.random.fold_in(rng, axis), (), 0, length) for axis, length in enumerate(values.shape)]
    widest = values.shape.index(max(values.shape))
    beside = index_at[:widest] + [(index_at[widest] + 1) % values.shape[widest]] + index_at[widest + 1:]
    return values.at[tuple(index_at)].set(smallest).at[tuple(beside)].set(top_value)


def block_scale(own_key, extent, cuts, least, top_value):
    loudness = 1.0
    for axis_at, shards_of in cuts:
        steps = jax.random.uniform(jax.random.fold_in(jax.random.fold_in(own_key, 6), axis_at), (shards_of,), jnp.float32, least / len(cuts), top_value / len(cuts))
        loudness = loudness * jnp.repeat(jnp.exp(steps), extent[axis_at] // shards_of).reshape((-1,) + (1,) * (len(extent) - 1 - axis_at))
    return loudness


def normal_values(key, shape, scale, limit, pieces=(), kind=jnp.bfloat16):
    level = block_scale(key, shape, pieces, -0.22, 0.18) if pieces else 1.0
    entries = jax.random.normal(key, shape, jnp.float32) * scale * level
    return jnp.minimum(jnp.maximum(entries, -limit), limit).astype(kind)


def setup_inputs(seed: int = 0, part: int = 0) -> dict:
    key_list = jax.random.split(jax.random.key(seed), 14)
    own_keys = jax.random.split(jax.random.fold_in(key_list[13], part), 14)
    return {
        "states": normal_values(own_keys[0], (REQS, SUF, D), 1.0, 6.0, ((0, 2), (1, 8))),
        "norm_gain": jnp.clip(1.0 + 0.18 * jax.random.normal(key_list[1], (D,), jnp.float32), 0.099609375, 1.8984375).astype(jnp.bfloat16),
        "w_query": normal_values(key_list[2], (D, QH * HD), D ** -0.5, 0.0625, ((1, 8),)),
        "q_bias": draw_q_bias(jax.random.fold_in(key_list[13], 71), part),
        "w_key": normal_values(key_list[4], (D, KVH * HD), D ** -0.5, 0.0625, ((1, 8),)),
        "w_value": normal_values(key_list[5], (D, KVH * HD), D ** -0.5, 0.0625, ((1, 8),)),
        "k_bias": normal_values(key_list[6], (KVH * HD,), 0.5, 3.0, ((0, 8),)),
        "v_bias": normal_values(key_list[7], (KVH * HD,), 0.5, 3.0, ((0, 8),)),
        "w_out": normal_values(key_list[8], (QH * HD, D), (QH * HD) ** -0.5, 0.0625, ((0, 8),)),
        "kv_pool": draw_kv_pool(jax.random.fold_in(jax.random.fold_in(key_list[13], part), 71), part),
        "hit_holder": draw_hit_holder(jax.random.fold_in(jax.random.fold_in(key_list[13], part), 71), part),
        "hit_slot": set_ends(jax.random.randint(own_keys[11], (REQS, NBLK), 0, SLOTS), jax.random.fold_in(own_keys[11], 1), 0, SLOTS - 1).astype(jnp.int32),
        "prefix_len": draw_prefix_len(jax.random.fold_in(jax.random.fold_in(key_list[13], part), 71), part),
    }


ROPE_BASE = 1000000.0
EPSILON = 1e-06

def rotate(vectors, positions):
    half_dim = vectors.shape[-1] // 2
    frequency = jnp.power(jnp.float32(ROPE_BASE), -2.0 * jnp.arange(half_dim, dtype=jnp.float32) / vectors.shape[-1])
    angles = positions.astype(jnp.float32)[:, None] * frequency[None, :]
    cosine = jnp.cos(angles)[:, None, :]
    sine_part = jnp.sin(angles)[:, None, :]
    first_half = vectors[..., :half_dim]
    second = vectors[..., half_dim:]
    return jnp.concatenate([first_half * cosine - second * sine_part, second * cosine + first_half * sine_part], -1)

def normalize(states, gain_vec):
    values = states.astype(jnp.float32)
    inv_rms = lax.rsqrt(lax.optimization_barrier(jnp.mean(values * values, axis=-1, keepdims=True)) + EPSILON)
    return (values * inv_rms * gain_vec.astype(jnp.float32)).astype(jnp.bfloat16)

def reference(states, norm_gain, w_query, q_bias, w_key, w_value, k_bias, v_bias, w_out, kv_pool, hit_holder, hit_slot, prefix_len):
    group_size = QH // KVH
    share_cols = QH * HD // N_MP
    outputs = []
    caches = []
    for request in range(REQS):
        normed = normalize(states[request], norm_gain)
        positions = prefix_len[request] + jnp.arange(SUF, dtype=jnp.int32)
        query_lin = jnp.dot(normed, w_query, preferred_element_type=jnp.float32) + q_bias.astype(jnp.float32)
        queries = rotate(query_lin.reshape(SUF, QH, HD), positions).astype(jnp.bfloat16)
        key_raw = (jnp.dot(normed, w_key, preferred_element_type=jnp.float32) + k_bias.astype(jnp.float32)).astype(jnp.bfloat16)
        value_new = (jnp.dot(normed, w_value, preferred_element_type=jnp.float32) + v_bias.astype(jnp.float32)).astype(jnp.bfloat16)
        key_new = rotate(key_raw.astype(jnp.float32).reshape(SUF, KVH, HD), positions).astype(jnp.bfloat16)
        value_heads = value_new.reshape(SUF, KVH, HD)
        caches.append(jnp.stack([key_new, value_heads], 2).reshape(SUF, KVH * 2 * HD))
        blocks = kv_pool[hit_holder[request], hit_slot[request]].reshape(PRE, KVH, 2, HD)
        key_rows = jnp.concatenate([blocks[:, :, 0], key_new], 0).transpose(1, 0, 2)
        value_rows = jnp.concatenate([blocks[:, :, 1], value_heads], 0).transpose(1, 0, 2)
        prefix_seen = jnp.broadcast_to(jnp.arange(PRE, dtype=jnp.int32)[None, :] < prefix_len[request], (SUF, PRE))
        causal = jnp.arange(SUF)[None, :] <= jnp.arange(SUF)[:, None]
        seen_mask = jnp.concatenate([prefix_seen, causal], 1)
        head_queries = queries.transpose(1, 0, 2)

        def attend(pair_item):
            q_head, head_index = pair_item
            k_head = key_rows[head_index // group_size]
            v_head = value_rows[head_index // group_size]
            scores = jnp.dot(q_head, k_head.T, preferred_element_type=jnp.float32) * HD ** (-0.5)
            scores = jnp.where(seen_mask, scores, -jnp.inf)
            weights = jnp.exp(scores - lax.optimization_barrier(jnp.max(scores, axis=1, keepdims=True)))
            numerator = jnp.dot(weights.astype(jnp.bfloat16), v_head, preferred_element_type=jnp.float32)
            return (numerator / lax.optimization_barrier(jnp.sum(weights, axis=1, keepdims=True))).astype(jnp.bfloat16)
        head_outs = lax.map(attend, (head_queries, jnp.arange(QH, dtype=jnp.int32)))
        mixed_heads = head_outs.transpose(1, 0, 2).reshape(SUF, QH * HD)

        def add_share(running, head_index):
            part_rows = lax.dynamic_slice_in_dim(mixed_heads, head_index * share_cols, share_cols, 1)
            part_weights = lax.dynamic_slice_in_dim(w_out, head_index * share_cols, share_cols, 0)
            term_part = jnp.dot(part_rows, part_weights, preferred_element_type=jnp.float32).astype(jnp.bfloat16)
            term_part = lax.optimization_barrier(term_part)
            return (running + term_part.astype(jnp.float32), None)
        running, _ = lax.scan(add_share, jnp.zeros((SUF, D), jnp.float32), jnp.arange(N_MP, dtype=jnp.int32))
        outputs.append(running.astype(jnp.bfloat16))
    return (jnp.stack(outputs), jnp.stack(caches))
```

```python
import functools
import math

import jax
import jax.numpy as jnp
from jax import lax
from jax.experimental import pallas as pl
from jax.experimental.pallas import tpu as pltpu
from jax.sharding import PartitionSpec as P

QH = 64
HD = 128
ROPE_BASE = 1000000.0
EPSILON = 1e-06
SCORE_SCALE = HD ** (-0.5) * math.log2(math.e)
VMEM_LIMIT = 56 * 1024 * 1024
GATHER_PIECES = 4
ROW_CHUNKS = 4


def angle_tables(positions):
    frequency = jnp.power(
        jnp.float32(ROPE_BASE), -2.0 * jnp.arange(HD // 2, dtype=jnp.float32) / HD
    )
    angles = positions.astype(jnp.float32)[:, None] * frequency[None, :]
    return jnp.cos(angles), jnp.sin(angles)


def rotate(vectors, cosine, sine):
    first_half = vectors[..., : HD // 2]
    second = vectors[..., HD // 2 :]
    cosine = cosine[:, None, :]
    sine = sine[:, None, :]
    return jnp.concatenate(
        [first_half * cosine - second * sine, second * cosine + first_half * sine], -1
    )


def normalize(states, gain_vec):
    values = states.astype(jnp.float32)
    inv_rms = lax.rsqrt(jnp.mean(values * values, axis=-1, keepdims=True) + EPSILON)
    return (values * inv_rms * gain_vec.astype(jnp.float32)).astype(jnp.bfloat16)


def listing(owned_mask, capacity):
    rank_order = jnp.cumsum(owned_mask.astype(jnp.int32), -1) - 1
    slot_index = jnp.arange(capacity, dtype=jnp.int32)
    return owned_mask[..., None, :] & (rank_order[..., None, :] == slot_index[:, None])


def pack_kernel(dest_heads, slots_ref, pool_ref, out_ref):
    requests, capacity = slots_ref.shape

    def place(step, _):
        request = step // capacity
        rank = step % capacity
        block = pool_ref[slots_ref[request, rank]]
        for dest, head in enumerate(dest_heads):
            out_ref[dest, request, rank] = block[:, head * 2 * HD : (head + 1) * 2 * HD]
        return 0

    lax.fori_loop(0, requests * capacity, place, 0)


def pack_blocks(pool, slots, dest_heads):
    block_len = pool.shape[1]
    shape = (len(dest_heads), slots.shape[0], slots.shape[1], block_len, 2 * HD)
    return pl.pallas_call(
        functools.partial(pack_kernel, dest_heads),
        out_shape=jax.ShapeDtypeStruct(shape, jnp.bfloat16),
        in_specs=[
            pl.BlockSpec(memory_space=pltpu.SMEM),
            pl.BlockSpec(memory_space=pltpu.VMEM),
        ],
        out_specs=pl.BlockSpec(memory_space=pltpu.VMEM),
        compiler_params=pltpu.CompilerParams(vmem_limit_bytes=VMEM_LIMIT),
        name="pack_blocks",
    )(slots, pool)


def order_kernel(length_ref, where_ref, arrived_ref, key_ref, value_ref):
    block_len = arrived_ref.shape[1]
    length = length_ref[0]
    first = arrived_ref[where_ref[0]][:1, :HD].astype(jnp.float32)
    row = lax.broadcasted_iota(jnp.int32, (block_len, HD), 0)

    def place(block_id, _):
        block = arrived_ref[where_ref[block_id]].astype(jnp.float32)
        start = pl.multiple_of(block_id * block_len, block_len)
        seen = row + start < length
        rows = pl.ds(start, block_len)
        key_ref[rows, :] = jnp.where(seen, block[:, :HD], first).astype(jnp.bfloat16)
        value_ref[rows, :HD] = jnp.where(seen, block[:, HD:], 0.0).astype(jnp.bfloat16)
        value_ref[rows, HD:] = jnp.where(seen, 1.0, 0.0).astype(jnp.bfloat16)
        return 0

    lax.fori_loop(0, where_ref.shape[0], place, 0)


def order_blocks(arrived, where, length):
    tokens = where.shape[0] * arrived.shape[1]
    return pl.pallas_call(
        order_kernel,
        out_shape=(
            jax.ShapeDtypeStruct((tokens, HD), jnp.bfloat16),
            jax.ShapeDtypeStruct((tokens, 2 * HD), jnp.bfloat16),
        ),
        in_specs=[
            pl.BlockSpec(memory_space=pltpu.SMEM),
            pl.BlockSpec(memory_space=pltpu.SMEM),
            pl.BlockSpec(memory_space=pltpu.VMEM),
        ],
        out_specs=(
            pl.BlockSpec(memory_space=pltpu.VMEM),
            pl.BlockSpec(memory_space=pltpu.VMEM),
        ),
        compiler_params=pltpu.CompilerParams(vmem_limit_bytes=VMEM_LIMIT),
        name="order_blocks",
    )(length, where, arrived)


def dot_keys(queries, keys):
    return lax.dot_general(
        queries, keys, (((1,), (1,)), ((), ())), preferred_element_type=jnp.float32
    )


def attend_kernel(
    span, row_step, chunk, query_ref, key_ref, value_ref, new_key_ref, new_value_ref, out_ref
):
    queries = query_ref[0]
    rows = queries.shape[0]
    spans = key_ref.shape[0] // span
    suffix = new_key_ref.shape[0]
    stride = suffix * row_step // rows
    local = lax.broadcasted_iota(jnp.int32, (rows, suffix), 0)
    token = (local // row_step) * stride + chunk * row_step + local % row_step
    causal = lax.broadcasted_iota(jnp.int32, (rows, suffix), 1) <= token
    scores = jnp.where(causal, dot_keys(queries, new_key_ref[...]), -jnp.inf)
    peak = jnp.max(scores, axis=1, keepdims=True)
    total = None
    values = new_value_ref[...]
    for step in range(spans + 1):
        if step < spans:
            next_scores = dot_keys(queries, key_ref[step * span : (step + 1) * span, :])
            next_peak = jnp.maximum(peak, jnp.max(next_scores, axis=1, keepdims=True))
        weights = jnp.exp2((scores - peak) * SCORE_SCALE).astype(jnp.bfloat16)
        product = jnp.dot(weights, values, preferred_element_type=jnp.float32)
        total = product if total is None else total + product
        if step < spans:
            total = total * jnp.exp2((peak - next_peak) * SCORE_SCALE)
            scores, peak = next_scores, next_peak
            values = value_ref[step * span : (step + 1) * span, :]
    out_ref[...] = (total[:, :HD] / total[:, HD:]).astype(jnp.bfloat16)


def attend(queries, keys, values, new_keys, new_values, row_step, chunk):
    heads, rows, _ = queries.shape
    span = math.gcd(keys.shape[0], 1024)
    whole = lambda array: pl.BlockSpec(array.shape, lambda head: (0, 0))
    count = keys.shape[0] + new_keys.shape[0]
    return pl.pallas_call(
        functools.partial(attend_kernel, span, row_step, chunk),
        grid=(heads,),
        out_shape=jax.ShapeDtypeStruct((rows, heads * HD), jnp.bfloat16),
        in_specs=[
            pl.BlockSpec((1, rows, HD), lambda head: (head, 0, 0)),
            whole(keys),
            whole(values),
            whole(new_keys),
            whole(new_values),
        ],
        out_specs=pl.BlockSpec((rows, HD), lambda head: (0, head)),
        compiler_params=pltpu.CompilerParams(vmem_limit_bytes=VMEM_LIMIT),
        cost_estimate=pl.CostEstimate(
            flops=heads * rows * count * HD * 8,
            bytes_accessed=2 * (count * 3 * HD + 2 * heads * rows * HD),
            transcendentals=heads * rows * count,
        ),
        name="attend",
    )(queries, keys, values, new_keys, new_values)


def on_device(
    n_model,
    n_pool,
    states,
    norm_gain,
    w_query,
    q_bias,
    w_key,
    w_value,
    k_bias,
    v_bias,
    w_out,
    kv_pool,
    hit_holder,
    hit_slot,
    prefix_len,
):
    my_model = lax.axis_index("mp")
    my_pool = lax.axis_index("pool")
    row_count, width = states.shape[1:]
    suffix = row_count * n_model
    q_width = w_query.shape[1]
    q_local = q_width // HD
    kv_local = w_key.shape[1]
    kv_heads = kv_local * n_model // HD
    group_size = QH // kv_heads
    blocks_total = hit_holder.shape[1]
    block_len = kv_pool.shape[2]
    holders = n_model * n_pool
    capacity = 2 * blocks_total // holders
    sharers = HD // kv_local
    dest_heads = tuple(dest * q_local // group_size for dest in range(n_model))

    self_holder = my_model * n_pool + my_pool
    chosen = listing(hit_holder == self_holder, capacity)
    slot_ids = jnp.sum(jnp.where(chosen, hit_slot[:, None, :], 0), -1)
    outgoing = pack_blocks(kv_pool[0], slot_ids, dest_heads)
    arrived = lax.all_to_all(
        outgoing.reshape(holders, capacity * block_len, 2 * HD),
        ("mp", "pool"),
        split_axis=0,
        concat_axis=0,
        tiled=True,
    ).reshape(holders * capacity, block_len, 2 * HD)
    my_holder = hit_holder[my_pool]
    block_ids = jnp.arange(blocks_total, dtype=jnp.int32)
    earlier = (my_holder[:, None] == my_holder[None, :]) & (block_ids[None, :] < block_ids[:, None])
    where = my_holder * capacity + jnp.sum(earlier.astype(jnp.int32), -1)
    prefix_count = prefix_len[my_pool]

    normed = normalize(states[0], norm_gain)
    piece = width // GATHER_PIECES
    query_sum = key_sum = value_sum = None
    for index in range(GATHER_PIECES):
        cols = slice(index * piece, (index + 1) * piece)
        tokens = lax.all_gather(normed[:, cols], "mp", axis=0, tiled=True)
        parts = [
            jnp.dot(tokens, weight[cols], preferred_element_type=jnp.float32)
            for weight in (w_query, w_key, w_value)
        ]
        if index == 0:
            query_sum, key_sum, value_sum = parts
        else:
            query_sum, key_sum, value_sum = (
                query_sum + parts[0],
                key_sum + parts[1],
                value_sum + parts[2],
            )
    positions = prefix_count + jnp.arange(suffix, dtype=jnp.int32)
    cosine, sine = angle_tables(positions)
    queries = rotate(
        (query_sum + q_bias.astype(jnp.float32)).reshape(suffix, q_local, HD), cosine, sine
    ).astype(jnp.bfloat16)
    key_raw = (key_sum + k_bias.astype(jnp.float32)).astype(jnp.bfloat16)
    value_raw = (value_sum + v_bias.astype(jnp.float32)).astype(jnp.bfloat16)
    if sharers > 1:
        together = [
            [first + other for other in range(sharers)] for first in range(0, n_model, sharers)
        ]
        key_raw, value_head = (
            lax.all_gather(part, "mp", axis=1, tiled=True, axis_index_groups=together)
            for part in (key_raw, value_raw)
        )
    else:
        value_head = value_raw
    key_head = rotate(key_raw.astype(jnp.float32)[:, None, :], cosine, sine).astype(jnp.bfloat16)[
        :, 0
    ]

    if sharers > 1:
        first_col = (my_model % sharers) * kv_local
        key_cols = lax.dynamic_slice_in_dim(key_head, first_col, kv_local, 1)
        value_cols = value_raw
    else:
        key_cols, value_cols = key_head, value_head
    pairs = jnp.stack([key_cols, value_cols], 1).reshape(n_model, row_count, 2, kv_local)
    pairs = lax.all_to_all(pairs, "mp", split_axis=0, concat_axis=0, tiled=True)
    cache_rows = (
        pairs.reshape(kv_heads, sharers, row_count, 2, kv_local)
        .transpose(2, 0, 3, 1, 4)
        .reshape(1, row_count, kv_heads * 2 * HD)
    )

    prefix_keys, prefix_values = order_blocks(arrived, where, prefix_count.reshape(1))
    new_values = jnp.concatenate([value_head, jnp.ones_like(value_head)], 1)

    row_step = row_count // ROW_CHUNKS
    by_chunk = queries.reshape(n_model, ROW_CHUNKS, row_step, q_local, HD).transpose(1, 3, 0, 2, 4)
    summed = []
    for chunk in range(ROW_CHUNKS):
        mixed = attend(
            by_chunk[chunk].reshape(q_local, n_model * row_step, HD),
            prefix_keys,
            prefix_values,
            key_head,
            new_values,
            row_step,
            chunk,
        )
        share = jnp.dot(mixed, w_out, preferred_element_type=jnp.float32).astype(jnp.bfloat16)
        summed.append(lax.psum_scatter(share, "mp", scatter_dimension=0, tiled=True))
    return (jnp.concatenate(summed, 0)[None], cache_rows)


def solution(mesh):
    placed = (
        P(("groups", "pool"), "mp", None),
        P(),
        P(None, "mp"),
        P("mp"),
        P(None, "mp"),
        P(None, "mp"),
        P("mp"),
        P("mp"),
        P("mp", None),
        P(("groups", "mp", "pool"), None, None, None),
        P("groups", None),
        P("groups", None),
        P("groups"),
    )
    return jax.shard_map(
        functools.partial(on_device, mesh.shape["mp"], mesh.shape["pool"]),
        mesh=mesh,
        in_specs=placed,
        out_specs=(P(("groups", "pool"), "mp", None), P(("groups", "pool"), "mp", None)),
        check_vma=False,
    )
```

```python
import functools
import math

import jax
import jax.numpy as jnp
from jax import lax
from jax.experimental import pallas as pl
from jax.experimental.pallas import tpu as pltpu
from jax.sharding import PartitionSpec as P

QH = 64
HD = 128
ROPE_BASE = 1000000.0
EPSILON = 1e-06
SCORE_SCALE = HD ** (-0.5) * math.log2(math.e)
VMEM_LIMIT = 56 * 1024 * 1024
GATHER_PIECES = 2
ROW_CHUNKS = 4
LINE_MODELS = 8


def angle_tables(positions):
    frequency = jnp.power(
        jnp.float32(ROPE_BASE), -2.0 * jnp.arange(HD // 2, dtype=jnp.float32) / HD
    )
    angles = positions.astype(jnp.float32)[:, None] * frequency[None, :]
    return jnp.cos(angles), jnp.sin(angles)


def rotate(vectors, cosine, sine):
    first_half = vectors[..., : HD // 2]
    second = vectors[..., HD // 2 :]
    cosine = cosine[:, None, :]
    sine = sine[:, None, :]
    return jnp.concatenate(
        [first_half * cosine - second * sine, second * cosine + first_half * sine], -1
    )


def normalize(states, gain_vec):
    values = states.astype(jnp.float32)
    inv_rms = lax.rsqrt(jnp.mean(values * values, axis=-1, keepdims=True) + EPSILON)
    return (values * inv_rms * gain_vec.astype(jnp.float32)).astype(jnp.bfloat16)


def listing(owned_mask, capacity):
    rank_order = jnp.cumsum(owned_mask.astype(jnp.int32), -1) - 1
    slot_index = jnp.arange(capacity, dtype=jnp.int32)
    return owned_mask[..., None, :] & (rank_order[..., None, :] == slot_index[:, None])


def line_gather(own, n_model):
    length = n_model // 2

    def across(block, low, high):
        pairs = [(2 * z + y, 2 * z + 1 - y) for z in range(low, high) for y in range(2)]
        return lax.ppermute(block, "mp", pairs)

    lower, upper = [], []
    here, there = [own], []
    rising = falling = own
    there.append(across(own, 0, length))
    for step in range(1, length):
        rising = lax.ppermute(
            rising,
            "mp",
            [(2 * z + y, 2 * z + 2 + y) for z in range(step - 1, length - 1) for y in range(2)],
        )
        falling = lax.ppermute(
            falling,
            "mp",
            [(2 * z + y, 2 * z - 2 + y) for z in range(1, length - step + 1) for y in range(2)],
        )
        lower.append((rising, across(rising, step, length)))
        upper.append((falling, across(falling, 0, length - step)))
    here += [pair[0] for pair in lower] + [pair[0] for pair in upper]
    there += [pair[1] for pair in lower] + [pair[1] for pair in upper]
    return here + there


def project_kernel(length, first, last, *refs):
    place_ref = refs[0]
    n_blocks = 2 * (2 * length - 1) if length else 1
    blocks = refs[1 : 1 + n_blocks]
    rest = list(refs[1 + n_blocks :])
    weights = [rest.pop(0) for _ in range(3)]
    if not first:
        partial_ref = rest.pop(0)
    if last:
        q_bias_ref, k_bias_ref, v_bias_ref, cos_ref, sin_ref = rest[:5]
        query_ref, key_ref, value_ref, pair_ref = rest[5:9]
        rest = rest[9:]
    else:
        sum_ref = rest.pop(0)
    tokens_ref, total_ref, sems = rest
    step = pl.program_id(0)
    depth = weights[0].shape[0]
    q_width = weights[0].shape[1]

    def each_copy(act):
        if not length:
            act(pltpu.make_async_copy(blocks[0], tokens_ref, sems.at[0]))
            return
        rows = tokens_ref.shape[0] // (2 * length)
        my_y = place_ref[1]
        for my_z in range(length):

            @pl.when(place_ref[0] == my_z)
            def _():
                for z in range(length):
                    source = abs(z - my_z) + (length - 1 if z > my_z else 0)
                    for side in range(2):
                        y = my_y if side == 0 else 1 - my_y
                        start = pl.multiple_of((2 * z + y) * rows, rows)
                        act(
                            pltpu.make_async_copy(
                                blocks[side * (2 * length - 1) + source],
                                tokens_ref.at[pl.ds(start, rows), :],
                                sems.at[2 * z + side],
                            )
                        )

    @pl.when(step == 0)
    def _():
        each_copy(lambda copy: copy.start())
        total_ref[...] = jnp.zeros_like(total_ref) if first else partial_ref[...]
        each_copy(lambda copy: copy.wait())

    tokens = tokens_ref[:, pl.ds(pl.multiple_of(step * depth, depth), depth)]
    total_ref[:, :q_width] += jnp.dot(
        tokens, weights[0][...], preferred_element_type=jnp.float32
    )
    both = jnp.concatenate([weights[1][...], weights[2][...]], axis=1)
    total_ref[:, q_width:] += jnp.dot(tokens, both, preferred_element_type=jnp.float32)

    @pl.when(step == pl.num_programs(0) - 1)
    def _():
        if not last:
            sum_ref[...] = total_ref[...]
            return
        cosine, sine = cos_ref[...], sin_ref[...]

        def turned(vectors):
            return vectors * cosine + pltpu.roll(vectors, HD // 2, 1) * sine

        for head in range(q_width // HD):
            cols = slice(head * HD, (head + 1) * HD)
            query = total_ref[:, cols] + q_bias_ref[:, cols].astype(jnp.float32)
            query_ref[head] = turned(query).astype(jnp.bfloat16)
        key = total_ref[:, q_width : q_width + HD] + k_bias_ref[...].astype(jnp.float32)
        key = turned(key.astype(jnp.bfloat16).astype(jnp.float32)).astype(jnp.bfloat16)
        value = total_ref[:, q_width + HD :] + v_bias_ref[...].astype(jnp.float32)
        value = value.astype(jnp.bfloat16)
        key_ref[...] = key
        value_ref[:, :HD] = value
        value_ref[:, HD:] = jnp.ones_like(value)
        pair_ref[:, :HD] = key
        pair_ref[:, HD:] = value


def project(place, blocks, weights, piece, pieces, partial, biases, tables):
    length = place_length(blocks)
    width = blocks[0].shape[1]
    rows = blocks[0].shape[0] * (2 * length if length else 1)
    depth = math.gcd(width, 1024)
    steps = width // depth
    out_width = sum(weight.shape[1] for weight in weights)
    q_width = weights[0].shape[1]
    first, last = piece == 0, piece == pieces - 1
    fixed = lambda array: pl.BlockSpec(array.shape, lambda step: (0,) * len(array.shape))
    in_specs = [pl.BlockSpec(memory_space=pltpu.SMEM)]
    in_specs += [pl.BlockSpec(memory_space=pl.ANY)] * len(blocks)
    in_specs += [
        pl.BlockSpec((depth, weight.shape[1]), lambda step: (piece * steps + step, 0))
        for weight in weights
    ]
    operands = [place, *blocks, *weights]
    if not first:
        operands.append(partial)
    if last:
        operands += [*biases, *tables]
        out_shape = (
            jax.ShapeDtypeStruct((q_width // HD, rows, HD), jnp.bfloat16),
            jax.ShapeDtypeStruct((rows, HD), jnp.bfloat16),
            jax.ShapeDtypeStruct((rows, 2 * HD), jnp.bfloat16),
            jax.ShapeDtypeStruct((rows, 2 * HD), jnp.bfloat16),
        )
        out_specs = tuple(fixed(shape) for shape in out_shape)
    else:
        out_shape = jax.ShapeDtypeStruct((rows, out_width), jnp.float32)
        out_specs = fixed(out_shape)
    in_specs += [fixed(array) for array in operands[len(in_specs) :]]
    return pl.pallas_call(
        functools.partial(project_kernel, length, first, last),
        grid=(steps,),
        out_shape=out_shape,
        in_specs=in_specs,
        out_specs=out_specs,
        scratch_shapes=[
            pltpu.VMEM((rows, width), jnp.bfloat16),
            pltpu.VMEM((rows, out_width), jnp.float32),
            pltpu.SemaphoreType.DMA((max(2 * length, 1),)),
        ],
        compiler_params=pltpu.CompilerParams(vmem_limit_bytes=VMEM_LIMIT),
        cost_estimate=pl.CostEstimate(
            flops=2 * rows * width * out_width,
            bytes_accessed=2 * width * (rows + out_width) + 4 * rows * out_width,
            transcendentals=0,
        ),
        name="project",
    )(*operands)


def place_length(blocks):
    return 0 if len(blocks) == 1 else (len(blocks) // 2 + 1) // 2


def ring_scatter(shares, n_model, my_model):
    order = [m for m in range(0, n_model, 2)] + [m for m in range(n_model - 1, 0, -2)]
    inverse = [order.index(m) for m in range(n_model)]
    spot = jnp.array(inverse, jnp.int32)[my_model]
    half = n_model // 2
    width = shares.shape[-1]

    def share_of(offset):
        owner = jnp.array(order, jnp.int32)[(spot + offset + n_model) % n_model]
        return lax.dynamic_index_in_dim(shares, owner, 0, keepdims=False)

    def added(left, right):
        return (left.astype(jnp.float32) + right.astype(jnp.float32)).astype(jnp.bfloat16)

    def pairs(way):
        return [(order[i], order[(i + way) % n_model]) for i in range(n_model)]

    far = share_of(half)
    onward = lax.ppermute(far[:, : width // 2], "mp", pairs(1))
    back = lax.ppermute(far[:, width // 2 :], "mp", pairs(-1))
    for distance in range(half - 1, 0, -1):
        ahead, behind = share_of(distance), share_of(-distance)
        if distance == half - 1:
            onward = jnp.concatenate(
                [added(ahead[:, : width // 2], onward), ahead[:, width // 2 :]], 1
            )
            back = jnp.concatenate(
                [behind[:, : width // 2], added(behind[:, width // 2 :], back)], 1
            )
        else:
            onward, back = added(ahead, onward), added(behind, back)
        onward = lax.ppermute(onward, "mp", pairs(1))
        back = lax.ppermute(back, "mp", pairs(-1))
    own = share_of(0).astype(jnp.float32)
    return (own + onward.astype(jnp.float32) + back.astype(jnp.float32)).astype(jnp.bfloat16)


def pack_kernel(dest_heads, slots_ref, pool_ref, out_ref):
    requests, capacity = slots_ref.shape

    def place(step, _):
        request = step // capacity
        rank = step % capacity
        block = pool_ref[slots_ref[request, rank]]
        for dest, head in enumerate(dest_heads):
            out_ref[dest, request, rank] = block[:, head * 2 * HD : (head + 1) * 2 * HD]
        return 0

    lax.fori_loop(0, requests * capacity, place, 0)


def pack_blocks(pool, slots, dest_heads):
    block_len = pool.shape[1]
    shape = (len(dest_heads), slots.shape[0], slots.shape[1], block_len, 2 * HD)
    return pl.pallas_call(
        functools.partial(pack_kernel, dest_heads),
        out_shape=jax.ShapeDtypeStruct(shape, jnp.bfloat16),
        in_specs=[
            pl.BlockSpec(memory_space=pltpu.SMEM),
            pl.BlockSpec(memory_space=pltpu.VMEM),
        ],
        out_specs=pl.BlockSpec(memory_space=pltpu.VMEM),
        compiler_params=pltpu.CompilerParams(vmem_limit_bytes=VMEM_LIMIT),
        name="pack_blocks",
    )(slots, pool)


def order_kernel(length_ref, where_ref, arrived_ref, key_ref, value_ref):
    block_len = arrived_ref.shape[1]
    length = length_ref[0]
    first = arrived_ref[where_ref[0]][:1, :HD].astype(jnp.float32)
    row = lax.broadcasted_iota(jnp.int32, (block_len, HD), 0)

    def place(block_id, _):
        block = arrived_ref[where_ref[block_id]].astype(jnp.float32)
        start = pl.multiple_of(block_id * block_len, block_len)
        seen = row + start < length
        rows = pl.ds(start, block_len)
        key_ref[rows, :] = jnp.where(seen, block[:, :HD], first).astype(jnp.bfloat16)
        value_ref[rows, :HD] = jnp.where(seen, block[:, HD:], 0.0).astype(jnp.bfloat16)
        value_ref[rows, HD:] = jnp.where(seen, 1.0, 0.0).astype(jnp.bfloat16)
        return 0

    lax.fori_loop(0, where_ref.shape[0], place, 0)


def order_blocks(arrived, where, length):
    tokens = where.shape[0] * arrived.shape[1]
    return pl.pallas_call(
        order_kernel,
        out_shape=(
            jax.ShapeDtypeStruct((tokens, HD), jnp.bfloat16),
            jax.ShapeDtypeStruct((tokens, 2 * HD), jnp.bfloat16),
        ),
        in_specs=[
            pl.BlockSpec(memory_space=pltpu.SMEM),
            pl.BlockSpec(memory_space=pltpu.SMEM),
            pl.BlockSpec(memory_space=pltpu.VMEM),
        ],
        out_specs=(
            pl.BlockSpec(memory_space=pltpu.VMEM),
            pl.BlockSpec(memory_space=pltpu.VMEM),
        ),
        compiler_params=pltpu.CompilerParams(vmem_limit_bytes=VMEM_LIMIT),
        name="order_blocks",
    )(length, where, arrived)


def dot_keys(queries, keys):
    return lax.dot_general(
        queries, keys, (((1,), (1,)), ((), ())), preferred_element_type=jnp.float32
    )


def attend_kernel(
    span, row_step, chunk, query_ref, key_ref, value_ref, new_key_ref, new_value_ref, out_ref
):
    rows = out_ref.shape[0]
    queries = query_ref[0].reshape(rows, HD)
    spans = key_ref.shape[0] // span
    suffix = new_key_ref.shape[0]
    stride = suffix * row_step // rows
    local = lax.broadcasted_iota(jnp.int32, (rows, suffix), 0)
    token = (local // row_step) * stride + chunk * row_step + local % row_step
    causal = lax.broadcasted_iota(jnp.int32, (rows, suffix), 1) <= token
    scores = jnp.where(causal, dot_keys(queries, new_key_ref[...]), -jnp.inf)
    peak = jnp.max(scores, axis=1, keepdims=True)
    total = None
    values = new_value_ref[...]
    for step in range(spans + 1):
        if step < spans:
            next_scores = dot_keys(queries, key_ref[step * span : (step + 1) * span, :])
            next_peak = jnp.maximum(peak, jnp.max(next_scores, axis=1, keepdims=True))
        weights = jnp.exp2((scores - peak) * SCORE_SCALE).astype(jnp.bfloat16)
        product = jnp.dot(weights, values, preferred_element_type=jnp.float32)
        total = product if total is None else total + product
        if step < spans:
            total = total * jnp.exp2((peak - next_peak) * SCORE_SCALE)
            scores, peak = next_scores, next_peak
            values = value_ref[step * span : (step + 1) * span, :]
    out_ref[...] = (total[:, :HD] / total[:, HD:]).astype(jnp.bfloat16)


def attend(queries, keys, values, new_keys, new_values, row_step, chunk):
    heads, owners = queries.shape[:2]
    rows = owners * row_step
    span = math.gcd(keys.shape[0], 1024)
    whole = lambda array: pl.BlockSpec(array.shape, lambda head: (0, 0))
    count = keys.shape[0] + new_keys.shape[0]
    return pl.pallas_call(
        functools.partial(attend_kernel, span, row_step, chunk),
        grid=(heads,),
        out_shape=jax.ShapeDtypeStruct((rows, heads * HD), jnp.bfloat16),
        in_specs=[
            pl.BlockSpec((1, owners, None, row_step, HD), lambda head: (head, 0, chunk, 0, 0)),
            whole(keys),
            whole(values),
            whole(new_keys),
            whole(new_values),
        ],
        out_specs=pl.BlockSpec((rows, HD), lambda head: (0, head)),
        compiler_params=pltpu.CompilerParams(vmem_limit_bytes=VMEM_LIMIT),
        cost_estimate=pl.CostEstimate(
            flops=heads * rows * count * HD * 8,
            bytes_accessed=2 * (count * 3 * HD + 2 * heads * rows * HD),
            transcendentals=heads * rows * count,
        ),
        name="attend",
    )(queries, keys, values, new_keys, new_values)


def on_device(
    n_model,
    n_pool,
    states,
    norm_gain,
    w_query,
    q_bias,
    w_key,
    w_value,
    k_bias,
    v_bias,
    w_out,
    kv_pool,
    hit_holder,
    hit_slot,
    prefix_len,
):
    my_model = lax.axis_index("mp")
    my_pool = lax.axis_index("pool")
    row_count, width = states.shape[1:]
    suffix = row_count * n_model
    q_width = w_query.shape[1]
    q_local = q_width // HD
    kv_local = w_key.shape[1]
    kv_heads = kv_local * n_model // HD
    group_size = QH // kv_heads
    blocks_total = hit_holder.shape[1]
    block_len = kv_pool.shape[2]
    holders = n_model * n_pool
    capacity = 2 * blocks_total // holders
    sharers = HD // kv_local
    dest_heads = tuple(dest * q_local // group_size for dest in range(n_model))

    self_holder = my_model * n_pool + my_pool
    chosen = listing(hit_holder == self_holder, capacity)
    slot_ids = jnp.sum(jnp.where(chosen, hit_slot[:, None, :], 0), -1)
    outgoing = pack_blocks(kv_pool[0], slot_ids, dest_heads)
    arrived = lax.all_to_all(
        outgoing.reshape(holders, capacity * block_len, 2 * HD),
        ("mp", "pool"),
        split_axis=0,
        concat_axis=0,
        tiled=True,
    ).reshape(holders * capacity, block_len, 2 * HD)
    my_holder = hit_holder[my_pool]
    block_ids = jnp.arange(blocks_total, dtype=jnp.int32)
    earlier = (my_holder[:, None] == my_holder[None, :]) & (block_ids[None, :] < block_ids[:, None])
    where = my_holder * capacity + jnp.sum(earlier.astype(jnp.int32), -1)
    prefix_count = prefix_len[my_pool]

    positions = prefix_count + jnp.arange(suffix, dtype=jnp.int32)
    cosine, sine = angle_tables(positions)
    tables = (jnp.concatenate([cosine, cosine], 1), jnp.concatenate([-sine, sine], 1))
    normed = normalize(states[0], norm_gain)
    if sharers == 1:
        pieces = GATHER_PIECES
        place = jnp.stack([my_model // 2, my_model % 2]).astype(jnp.int32)
        biases = [bias.reshape(1, -1) for bias in (q_bias, k_bias, v_bias)]
        weights = (w_query, w_key, w_value)
        result = None
        for piece in range(pieces):
            own = normed[:, piece * width // pieces : (piece + 1) * width // pieces]
            if n_model == LINE_MODELS:
                blocks = line_gather(own, n_model)
            else:
                blocks = [lax.all_gather(own, "mp", axis=0, tiled=True)]
            result = project(place, blocks, weights, piece, pieces, result, biases, tables)
        queries, new_keys, new_values, pairs = result
        pairs = pairs.reshape(n_model, row_count, 2 * HD)
    else:
        tokens = lax.all_gather(normed, "mp", axis=0, tiled=True)
        linear, key_raw, value_raw = (
            jnp.dot(tokens, weight, preferred_element_type=jnp.float32) + bias.astype(jnp.float32)
            for weight, bias in ((w_query, q_bias), (w_key, k_bias), (w_value, v_bias))
        )
        queries = rotate(linear.reshape(suffix, q_local, HD), cosine, sine)
        queries = queries.astype(jnp.bfloat16).transpose(1, 0, 2)
        key_raw, value_raw = key_raw.astype(jnp.bfloat16), value_raw.astype(jnp.bfloat16)
        together = [
            [first + other for other in range(sharers)] for first in range(0, n_model, sharers)
        ]
        key_whole, value_whole = (
            lax.all_gather(part, "mp", axis=1, tiled=True, axis_index_groups=together)
            for part in (key_raw, value_raw)
        )
        new_keys = rotate(key_whole.astype(jnp.float32)[:, None, :], cosine, sine)
        new_keys = new_keys.astype(jnp.bfloat16)[:, 0]
        new_values = jnp.concatenate([value_whole, jnp.ones_like(value_whole)], 1)
        first_col = (my_model % sharers) * kv_local
        key_cols = lax.dynamic_slice_in_dim(new_keys, first_col, kv_local, 1)
        pairs = jnp.stack([key_cols, value_raw], 1).reshape(n_model, row_count, 2 * kv_local)

    pairs = lax.all_to_all(pairs, "mp", split_axis=0, concat_axis=0, tiled=True)
    cache_rows = (
        pairs.reshape(kv_heads, sharers, row_count, 2, kv_local)
        .transpose(2, 0, 3, 1, 4)
        .reshape(1, row_count, kv_heads * 2 * HD)
    )

    prefix_keys, prefix_values = order_blocks(arrived, where, prefix_count.reshape(1))

    row_step = max(row_count // ROW_CHUNKS, 16)
    by_chunk = queries.reshape(q_local, n_model, row_count // row_step, row_step, HD)
    summed = []
    for chunk in range(row_count // row_step):
        mixed = attend(
            by_chunk, prefix_keys, prefix_values, new_keys, new_values, row_step, chunk
        )
        share = jnp.dot(mixed, w_out, preferred_element_type=jnp.float32).astype(jnp.bfloat16)
        share = share.reshape(n_model, row_step, share.shape[1])
        summed.append(ring_scatter(share, n_model, my_model))
    return (jnp.concatenate(summed, 0)[None], cache_rows)


def solution(mesh):
    placed = (
        P(("groups", "pool"), "mp", None),
        P(),
        P(None, "mp"),
        P("mp"),
        P(None, "mp"),
        P(None, "mp"),
        P("mp"),
        P("mp"),
        P("mp", None),
        P(("groups", "mp", "pool"), None, None, None),
        P("groups", None),
        P("groups", None),
        P("groups"),
    )
    return jax.shard_map(
        functools.partial(on_device, mesh.shape["mp"], mesh.shape["pool"]),
        mesh=mesh,
        in_specs=placed,
        out_specs=(P(("groups", "pool"), "mp", None), P(("groups", "pool"), "mp", None)),
        check_vma=False,
    )
```

```python
import functools
import math

import jax
import jax.numpy as jnp
from jax import lax
from jax.experimental import pallas as pl
from jax.experimental.pallas import tpu as pltpu
from jax.sharding import PartitionSpec as P

QH = 64
HD = 128
ROPE_BASE = 1000000.0
EPSILON = 1e-06
SCORE_SCALE = HD ** (-0.5) * math.log2(math.e)
VMEM_LIMIT = 56 * 1024 * 1024
ATTEND_VMEM = 28 * 1024 * 1024
GATHER_PIECES = 2
ROW_CHUNKS = 4
LINE_MODELS = 8


def angle_tables(positions):
    frequency = jnp.power(
        jnp.float32(ROPE_BASE), -2.0 * jnp.arange(HD // 2, dtype=jnp.float32) / HD
    )
    angles = positions.astype(jnp.float32)[:, None] * frequency[None, :]
    return jnp.cos(angles), jnp.sin(angles)


def rotate(vectors, cosine, sine):
    first_half = vectors[..., : HD // 2]
    second = vectors[..., HD // 2 :]
    cosine = cosine[:, None, :]
    sine = sine[:, None, :]
    return jnp.concatenate(
        [first_half * cosine - second * sine, second * cosine + first_half * sine], -1
    )


def normalize(states, gain_vec):
    values = states.astype(jnp.float32)
    inv_rms = lax.rsqrt(jnp.mean(values * values, axis=-1, keepdims=True) + EPSILON)
    return (values * inv_rms * gain_vec.astype(jnp.float32)).astype(jnp.bfloat16)


def listing(owned_mask, capacity):
    rank_order = jnp.cumsum(owned_mask.astype(jnp.int32), -1) - 1
    slot_index = jnp.arange(capacity, dtype=jnp.int32)
    return owned_mask[..., None, :] & (rank_order[..., None, :] == slot_index[:, None])


def line_gather(own, n_model):
    length = n_model // 2

    def across(block, low, high):
        pairs = [(2 * z + y, 2 * z + 1 - y) for z in range(low, high) for y in range(2)]
        return lax.ppermute(block, "mp", pairs)

    lower, upper = [], []
    here, there = [own], []
    rising = falling = own
    there.append(across(own, 0, length))
    for step in range(1, length):
        rising = lax.ppermute(
            rising,
            "mp",
            [(2 * z + y, 2 * z + 2 + y) for z in range(step - 1, length - 1) for y in range(2)],
        )
        falling = lax.ppermute(
            falling,
            "mp",
            [(2 * z + y, 2 * z - 2 + y) for z in range(1, length - step + 1) for y in range(2)],
        )
        lower.append((rising, across(rising, step, length)))
        upper.append((falling, across(falling, 0, length - step)))
    here += [pair[0] for pair in lower] + [pair[0] for pair in upper]
    there += [pair[1] for pair in lower] + [pair[1] for pair in upper]
    return here + there


def project_kernel(length, first, last, *refs):
    place_ref = refs[0]
    n_blocks = 2 * (2 * length - 1) if length else 1
    blocks = refs[1 : 1 + n_blocks]
    rest = list(refs[1 + n_blocks :])
    weights = [rest.pop(0) for _ in range(3)]
    if not first:
        partial_ref = rest.pop(0)
    if last:
        q_bias_ref, k_bias_ref, v_bias_ref, cos_ref, sin_ref = rest[:5]
        query_ref, key_ref, value_ref, pair_ref = rest[5:9]
        rest = rest[9:]
    else:
        sum_ref = rest.pop(0)
    tokens_ref, total_ref, sems = rest
    step = pl.program_id(0)
    depth = weights[0].shape[0]
    q_width = weights[0].shape[1]

    def each_copy(act):
        if not length:
            act(pltpu.make_async_copy(blocks[0], tokens_ref, sems.at[0]))
            return
        rows = tokens_ref.shape[0] // (2 * length)
        my_y = place_ref[1]
        for my_z in range(length):

            @pl.when(place_ref[0] == my_z)
            def _():
                for z in range(length):
                    source = abs(z - my_z) + (length - 1 if z > my_z else 0)
                    for side in range(2):
                        y = my_y if side == 0 else 1 - my_y
                        start = pl.multiple_of((2 * z + y) * rows, rows)
                        act(
                            pltpu.make_async_copy(
                                blocks[side * (2 * length - 1) + source],
                                tokens_ref.at[pl.ds(start, rows), :],
                                sems.at[2 * z + side],
                            )
                        )

    @pl.when(step == 0)
    def _():
        each_copy(lambda copy: copy.start())
        total_ref[...] = jnp.zeros_like(total_ref) if first else partial_ref[...]
        each_copy(lambda copy: copy.wait())

    tokens = tokens_ref[:, pl.ds(pl.multiple_of(step * depth, depth), depth)]
    total_ref[:, :q_width] += jnp.dot(
        tokens, weights[0][...], preferred_element_type=jnp.float32
    )
    both = jnp.concatenate([weights[1][...], weights[2][...]], axis=1)
    total_ref[:, q_width:] += jnp.dot(tokens, both, preferred_element_type=jnp.float32)

    @pl.when(step == pl.num_programs(0) - 1)
    def _():
        if not last:
            sum_ref[...] = total_ref[...]
            return
        cosine, sine = cos_ref[...], sin_ref[...]

        def turned(vectors):
            return vectors * cosine + pltpu.roll(vectors, HD // 2, 1) * sine

        for head in range(q_width // HD):
            cols = slice(head * HD, (head + 1) * HD)
            query = total_ref[:, cols] + q_bias_ref[:, cols].astype(jnp.float32)
            query_ref[head] = turned(query).astype(jnp.bfloat16)
        key = total_ref[:, q_width : q_width + HD] + k_bias_ref[...].astype(jnp.float32)
        key = turned(key.astype(jnp.bfloat16).astype(jnp.float32)).astype(jnp.bfloat16)
        value = total_ref[:, q_width + HD :] + v_bias_ref[...].astype(jnp.float32)
        value = value.astype(jnp.bfloat16)
        key_ref[...] = key
        value_ref[:, :HD] = value
        value_ref[:, HD:] = jnp.ones_like(value)
        pair_ref[:, :HD] = key
        pair_ref[:, HD:] = value


def project(place, blocks, weights, piece, pieces, partial, biases, tables):
    length = place_length(blocks)
    width = blocks[0].shape[1]
    rows = blocks[0].shape[0] * (2 * length if length else 1)
    depth = math.gcd(width, 1024)
    steps = width // depth
    out_width = sum(weight.shape[1] for weight in weights)
    q_width = weights[0].shape[1]
    first, last = piece == 0, piece == pieces - 1
    fixed = lambda array: pl.BlockSpec(array.shape, lambda step: (0,) * len(array.shape))
    in_specs = [pl.BlockSpec(memory_space=pltpu.SMEM)]
    in_specs += [pl.BlockSpec(memory_space=pl.ANY)] * len(blocks)
    in_specs += [
        pl.BlockSpec((depth, weight.shape[1]), lambda step: (piece * steps + step, 0))
        for weight in weights
    ]
    operands = [place, *blocks, *weights]
    if not first:
        operands.append(partial)
    if last:
        operands += [*biases, *tables]
        out_shape = (
            jax.ShapeDtypeStruct((q_width // HD, rows, HD), jnp.bfloat16),
            jax.ShapeDtypeStruct((rows, HD), jnp.bfloat16),
            jax.ShapeDtypeStruct((rows, 2 * HD), jnp.bfloat16),
            jax.ShapeDtypeStruct((rows, 2 * HD), jnp.bfloat16),
        )
        out_specs = tuple(fixed(shape) for shape in out_shape)
    else:
        out_shape = jax.ShapeDtypeStruct((rows, out_width), jnp.float32)
        out_specs = fixed(out_shape)
    in_specs += [fixed(array) for array in operands[len(in_specs) :]]
    return pl.pallas_call(
        functools.partial(project_kernel, length, first, last),
        grid=(steps,),
        out_shape=out_shape,
        in_specs=in_specs,
        out_specs=out_specs,
        scratch_shapes=[
            pltpu.VMEM((rows, width), jnp.bfloat16),
            pltpu.VMEM((rows, out_width), jnp.float32),
            pltpu.SemaphoreType.DMA((max(2 * length, 1),)),
        ],
        compiler_params=pltpu.CompilerParams(vmem_limit_bytes=VMEM_LIMIT),
        cost_estimate=pl.CostEstimate(
            flops=2 * rows * width * out_width,
            bytes_accessed=2 * width * (rows + out_width) + 4 * rows * out_width,
            transcendentals=0,
        ),
        name="project",
    )(*operands)


def place_length(blocks):
    return 0 if len(blocks) == 1 else (len(blocks) // 2 + 1) // 2


def ring_scatter(shares, n_model, my_model):
    order = [m for m in range(0, n_model, 2)] + [m for m in range(n_model - 1, 0, -2)]
    inverse = [order.index(m) for m in range(n_model)]
    spot = jnp.array(inverse, jnp.int32)[my_model]
    half = n_model // 2
    width = shares.shape[-1]

    def share_of(offset):
        owner = jnp.array(order, jnp.int32)[(spot + offset + n_model) % n_model]
        return lax.dynamic_index_in_dim(shares, owner, 0, keepdims=False)

    def added(left, right):
        return (left.astype(jnp.float32) + right.astype(jnp.float32)).astype(jnp.bfloat16)

    def pairs(way):
        return [(order[i], order[(i + way) % n_model]) for i in range(n_model)]

    far = share_of(half)
    onward = lax.ppermute(far[:, : width // 2], "mp", pairs(1))
    back = lax.ppermute(far[:, width // 2 :], "mp", pairs(-1))
    for distance in range(half - 1, 0, -1):
        ahead, behind = share_of(distance), share_of(-distance)
        if distance == half - 1:
            onward = jnp.concatenate(
                [added(ahead[:, : width // 2], onward), ahead[:, width // 2 :]], 1
            )
            back = jnp.concatenate(
                [behind[:, : width // 2], added(behind[:, width // 2 :], back)], 1
            )
        else:
            onward, back = added(ahead, onward), added(behind, back)
        onward = lax.ppermute(onward, "mp", pairs(1))
        back = lax.ppermute(back, "mp", pairs(-1))
    own = share_of(0).astype(jnp.float32)
    return (own + onward.astype(jnp.float32) + back.astype(jnp.float32)).astype(jnp.bfloat16)


def pack_kernel(dest_heads, slots_ref, pool_ref, out_ref):
    requests, capacity = slots_ref.shape

    def place(step, _):
        request = step // capacity
        rank = step % capacity
        block = pool_ref[slots_ref[request, rank]]
        for dest, head in enumerate(dest_heads):
            out_ref[dest, request, rank] = block[:, head * 2 * HD : (head + 1) * 2 * HD]
        return 0

    lax.fori_loop(0, requests * capacity, place, 0)


def pack_blocks(pool, slots, dest_heads):
    block_len = pool.shape[1]
    shape = (len(dest_heads), slots.shape[0], slots.shape[1], block_len, 2 * HD)
    return pl.pallas_call(
        functools.partial(pack_kernel, dest_heads),
        out_shape=jax.ShapeDtypeStruct(shape, jnp.bfloat16),
        in_specs=[
            pl.BlockSpec(memory_space=pltpu.SMEM),
            pl.BlockSpec(memory_space=pltpu.VMEM),
        ],
        out_specs=pl.BlockSpec(memory_space=pltpu.VMEM),
        compiler_params=pltpu.CompilerParams(vmem_limit_bytes=VMEM_LIMIT),
        name="pack_blocks",
    )(slots, pool)


def order_kernel(length_ref, where_ref, arrived_ref, key_ref, value_ref):
    block_len = arrived_ref.shape[1]
    length = length_ref[0]
    first = arrived_ref[where_ref[0]][:1, :HD].astype(jnp.float32)
    row = lax.broadcasted_iota(jnp.int32, (block_len, HD), 0)

    def place(block_id, _):
        block = arrived_ref[where_ref[block_id]].astype(jnp.float32)
        start = pl.multiple_of(block_id * block_len, block_len)
        seen = row + start < length
        rows = pl.ds(start, block_len)
        key_ref[rows, :] = jnp.where(seen, block[:, :HD], first).astype(jnp.bfloat16)
        value_ref[rows, :HD] = jnp.where(seen, block[:, HD:], 0.0).astype(jnp.bfloat16)
        value_ref[rows, HD:] = jnp.where(seen, 1.0, 0.0).astype(jnp.bfloat16)
        return 0

    lax.fori_loop(0, where_ref.shape[0], place, 0)


def order_blocks(arrived, where, length):
    tokens = where.shape[0] * arrived.shape[1]
    return pl.pallas_call(
        order_kernel,
        out_shape=(
            jax.ShapeDtypeStruct((tokens, HD), jnp.bfloat16),
            jax.ShapeDtypeStruct((tokens, 2 * HD), jnp.bfloat16),
        ),
        in_specs=[
            pl.BlockSpec(memory_space=pltpu.SMEM),
            pl.BlockSpec(memory_space=pltpu.SMEM),
            pl.BlockSpec(memory_space=pltpu.VMEM),
        ],
        out_specs=(
            pl.BlockSpec(memory_space=pltpu.VMEM),
            pl.BlockSpec(memory_space=pltpu.VMEM),
        ),
        compiler_params=pltpu.CompilerParams(vmem_limit_bytes=VMEM_LIMIT),
        name="order_blocks",
    )(length, where, arrived)


def dot_keys(queries, keys):
    return lax.dot_general(
        queries, keys, (((1,), (1,)), ((), ())), preferred_element_type=jnp.float32
    )


def attend_kernel(
    span, row_step, chunk, query_ref, key_ref, value_ref, new_key_ref, new_value_ref, out_ref
):
    rows = out_ref.shape[0]
    queries = query_ref[0].reshape(rows, HD)
    spans = key_ref.shape[0] // span
    suffix = new_key_ref.shape[0]
    stride = suffix * row_step // rows
    local = lax.broadcasted_iota(jnp.int32, (rows, suffix), 0)
    token = (local // row_step) * stride + chunk * row_step + local % row_step
    causal = lax.broadcasted_iota(jnp.int32, (rows, suffix), 1) <= token
    scores = jnp.where(causal, dot_keys(queries, new_key_ref[...]), -jnp.inf)
    peak = jnp.max(scores, axis=1, keepdims=True)
    total = None
    values = new_value_ref[...]
    for step in range(spans + 1):
        if step < spans:
            next_scores = dot_keys(queries, key_ref[step * span : (step + 1) * span, :])
            next_peak = jnp.maximum(peak, jnp.max(next_scores, axis=1, keepdims=True))
        weights = jnp.exp2((scores - peak) * SCORE_SCALE).astype(jnp.bfloat16)
        product = jnp.dot(weights, values, preferred_element_type=jnp.float32)
        total = product if total is None else total + product
        if step < spans:
            total = total * jnp.exp2((peak - next_peak) * SCORE_SCALE)
            scores, peak = next_scores, next_peak
            values = value_ref[step * span : (step + 1) * span, :]
    out_ref[...] = (total[:, :HD] / total[:, HD:]).astype(jnp.bfloat16)


def attend(queries, keys, values, new_keys, new_values, row_step, chunk):
    heads, owners = queries.shape[:2]
    rows = owners * row_step
    span = math.gcd(keys.shape[0], 1024)
    whole = lambda array: pl.BlockSpec(array.shape, lambda head: (0, 0))
    count = keys.shape[0] + new_keys.shape[0]
    return pl.pallas_call(
        functools.partial(attend_kernel, span, row_step, chunk),
        grid=(heads,),
        out_shape=jax.ShapeDtypeStruct((rows, heads * HD), jnp.bfloat16),
        in_specs=[
            pl.BlockSpec((1, owners, None, row_step, HD), lambda head: (head, 0, chunk, 0, 0)),
            whole(keys),
            whole(values),
            whole(new_keys),
            whole(new_values),
        ],
        out_specs=pl.BlockSpec((rows, HD), lambda head: (0, head)),
        compiler_params=pltpu.CompilerParams(vmem_limit_bytes=ATTEND_VMEM),
        cost_estimate=pl.CostEstimate(
            flops=heads * rows * count * HD * 8,
            bytes_accessed=2 * (count * 3 * HD + 2 * heads * rows * HD),
            transcendentals=heads * rows * count,
        ),
        name="attend",
    )(queries, keys, values, new_keys, new_values)


def on_device(
    n_model,
    n_pool,
    states,
    norm_gain,
    w_query,
    q_bias,
    w_key,
    w_value,
    k_bias,
    v_bias,
    w_out,
    kv_pool,
    hit_holder,
    hit_slot,
    prefix_len,
):
    my_model = lax.axis_index("mp")
    my_pool = lax.axis_index("pool")
    row_count, width = states.shape[1:]
    suffix = row_count * n_model
    q_width = w_query.shape[1]
    q_local = q_width // HD
    kv_local = w_key.shape[1]
    kv_heads = kv_local * n_model // HD
    group_size = QH // kv_heads
    blocks_total = hit_holder.shape[1]
    block_len = kv_pool.shape[2]
    holders = n_model * n_pool
    capacity = 2 * blocks_total // holders
    sharers = HD // kv_local
    dest_heads = tuple(dest * q_local // group_size for dest in range(n_model))

    self_holder = my_model * n_pool + my_pool
    chosen = listing(hit_holder == self_holder, capacity)
    slot_ids = jnp.sum(jnp.where(chosen, hit_slot[:, None, :], 0), -1)
    outgoing = pack_blocks(kv_pool[0], slot_ids, dest_heads)
    arrived = lax.all_to_all(
        outgoing.reshape(holders, capacity * block_len, 2 * HD),
        ("mp", "pool"),
        split_axis=0,
        concat_axis=0,
        tiled=True,
    ).reshape(holders * capacity, block_len, 2 * HD)
    my_holder = hit_holder[my_pool]
    block_ids = jnp.arange(blocks_total, dtype=jnp.int32)
    earlier = (my_holder[:, None] == my_holder[None, :]) & (block_ids[None, :] < block_ids[:, None])
    where = my_holder * capacity + jnp.sum(earlier.astype(jnp.int32), -1)
    prefix_count = prefix_len[my_pool]

    positions = prefix_count + jnp.arange(suffix, dtype=jnp.int32)
    cosine, sine = angle_tables(positions)
    tables = (jnp.concatenate([cosine, cosine], 1), jnp.concatenate([-sine, sine], 1))
    normed = normalize(states[0], norm_gain)
    if sharers == 1:
        pieces = GATHER_PIECES
        place = jnp.stack([my_model // 2, my_model % 2]).astype(jnp.int32)
        biases = [bias.reshape(1, -1) for bias in (q_bias, k_bias, v_bias)]
        weights = (w_query, w_key, w_value)
        result = None
        for piece in range(pieces):
            own = normed[:, piece * width // pieces : (piece + 1) * width // pieces]
            if n_model == LINE_MODELS:
                blocks = line_gather(own, n_model)
            else:
                blocks = [lax.all_gather(own, "mp", axis=0, tiled=True)]
            if piece == pieces - 1:
                (prefix_keys, prefix_values), blocks[0] = lax.optimization_barrier(
                    (order_blocks(arrived, where, prefix_count.reshape(1)), blocks[0])
                )
            result = project(place, blocks, weights, piece, pieces, result, biases, tables)
        queries, new_keys, new_values, pairs = result
        pairs = pairs.reshape(n_model, row_count, 2 * HD)
    else:
        tokens = lax.all_gather(normed, "mp", axis=0, tiled=True)
        linear, key_raw, value_raw = (
            jnp.dot(tokens, weight, preferred_element_type=jnp.float32) + bias.astype(jnp.float32)
            for weight, bias in ((w_query, q_bias), (w_key, k_bias), (w_value, v_bias))
        )
        queries = rotate(linear.reshape(suffix, q_local, HD), cosine, sine)
        queries = queries.astype(jnp.bfloat16).transpose(1, 0, 2)
        key_raw, value_raw = key_raw.astype(jnp.bfloat16), value_raw.astype(jnp.bfloat16)
        together = [
            [first + other for other in range(sharers)] for first in range(0, n_model, sharers)
        ]
        key_whole, value_whole = (
            lax.all_gather(part, "mp", axis=1, tiled=True, axis_index_groups=together)
            for part in (key_raw, value_raw)
        )
        new_keys = rotate(key_whole.astype(jnp.float32)[:, None, :], cosine, sine)
        new_keys = new_keys.astype(jnp.bfloat16)[:, 0]
        new_values = jnp.concatenate([value_whole, jnp.ones_like(value_whole)], 1)
        first_col = (my_model % sharers) * kv_local
        key_cols = lax.dynamic_slice_in_dim(new_keys, first_col, kv_local, 1)
        pairs = jnp.stack([key_cols, value_raw], 1).reshape(n_model, row_count, 2 * kv_local)
        prefix_keys, prefix_values = order_blocks(arrived, where, prefix_count.reshape(1))

    row_step = max(row_count // ROW_CHUNKS, 16)
    by_chunk = queries.reshape(q_local, n_model, row_count // row_step, row_step, HD)
    summed = []
    for chunk in range(row_count // row_step):
        mixed = attend(
            by_chunk, prefix_keys, prefix_values, new_keys, new_values, row_step, chunk
        )
        share = jnp.dot(mixed, w_out, preferred_element_type=jnp.float32).astype(jnp.bfloat16)
        share, by_chunk, pairs = lax.optimization_barrier((share, by_chunk, pairs))
        share = share.reshape(n_model, row_step, share.shape[1])
        summed.append(ring_scatter(share, n_model, my_model))
    pairs = lax.all_to_all(pairs, "mp", split_axis=0, concat_axis=0, tiled=True)
    cache_rows = (
        pairs.reshape(kv_heads, sharers, row_count, 2, kv_local)
        .transpose(2, 0, 3, 1, 4)
        .reshape(1, row_count, kv_heads * 2 * HD)
    )
    return (jnp.concatenate(summed, 0)[None], cache_rows)


def solution(mesh):
    placed = (
        P(("groups", "pool"), "mp", None),
        P(),
        P(None, "mp"),
        P("mp"),
        P(None, "mp"),
        P(None, "mp"),
        P("mp"),
        P("mp"),
        P("mp", None),
        P(("groups", "mp", "pool"), None, None, None),
        P("groups", None),
        P("groups", None),
        P("groups"),
    )
    return jax.shard_map(
        functools.partial(on_device, mesh.shape["mp"], mesh.shape["pool"]),
        mesh=mesh,
        in_specs=placed,
        out_specs=(P(("groups", "pool"), "mp", None), P(("groups", "pool"), "mp", None)),
        check_vma=False,
    )
```

```python
import functools
import math

import jax
import jax.numpy as jnp
from jax import lax
from jax.experimental import pallas as pl
from jax.experimental.pallas import tpu as pltpu
from jax.sharding import PartitionSpec as P

QH = 64
HD = 128
ROPE_BASE = 1000000.0
EPSILON = 1e-06
SCORE_SCALE = HD ** (-0.5) * math.log2(math.e)
VMEM_LIMIT = 56 * 1024 * 1024
ATTEND_VMEM = 28 * 1024 * 1024
ROW_STEP = 32
LINE_MODELS = 8


def angle_tables(positions):
    frequency = jnp.power(
        jnp.float32(ROPE_BASE), -2.0 * jnp.arange(HD // 2, dtype=jnp.float32) / HD
    )
    angles = positions.astype(jnp.float32)[:, None] * frequency[None, :]
    return jnp.cos(angles), jnp.sin(angles)


def rotate(vectors, cosine, sine):
    first_half = vectors[..., : HD // 2]
    second = vectors[..., HD // 2 :]
    cosine = cosine[:, None, :]
    sine = sine[:, None, :]
    return jnp.concatenate(
        [first_half * cosine - second * sine, second * cosine + first_half * sine], -1
    )


def normalize(states, gain_vec):
    values = states.astype(jnp.float32)
    inv_rms = lax.rsqrt(jnp.mean(values * values, axis=-1, keepdims=True) + EPSILON)
    return (values * inv_rms * gain_vec.astype(jnp.float32)).astype(jnp.bfloat16)


def listing(owned_mask, capacity):
    rank_order = jnp.cumsum(owned_mask.astype(jnp.int32), -1) - 1
    slot_index = jnp.arange(capacity, dtype=jnp.int32)
    return owned_mask[..., None, :] & (rank_order[..., None, :] == slot_index[:, None])


def line_gather(own, upper_half, middle):
    def swap(block, mask):
        return lax.ppermute(block, "mp", [(index, index ^ mask) for index in range(LINE_MODELS)])

    def cross(block):
        return lax.ppermute(
            block,
            "mp",
            [(index, index ^ 6 if 2 <= index < 6 else index) for index in range(LINE_MODELS)],
        )

    beside = swap(own, 2)
    over = cross(own)
    own_y = swap(own, 1)
    over_beside = cross(beside)
    over_passed = swap(over, 2)
    beside_y = swap(beside, 1)
    far_first = jnp.where(middle, over, over_passed)
    far_first_y = swap(far_first, 1)
    far_second = jnp.where(middle, over_beside, swap(over_beside, 2))
    far_second_y = swap(far_second, 1)
    return [own, beside, own_y, beside_y], [far_first, far_second, far_first_y, far_second_y]


def project_kernel(starts_ref, *refs):
    n_blocks = starts_ref.shape[0]
    blocks = refs[:n_blocks]
    weights = refs[n_blocks : n_blocks + 3]
    q_bias_ref, k_bias_ref, v_bias_ref, cos_ref, sin_ref = refs[n_blocks + 3 : n_blocks + 8]
    query_ref, key_ref, value_ref, pair_ref, tokens_ref, total_ref, sems = refs[n_blocks + 8 :]
    step = pl.program_id(0)
    depth, q_width = weights[0].shape
    rows = blocks[0].shape[0]

    @pl.when(step == 0)
    def _():
        copies = [
            pltpu.make_async_copy(
                block,
                tokens_ref.at[pl.ds(pl.multiple_of(starts_ref[index], rows), rows), :],
                sems.at[index],
            )
            for index, block in enumerate(blocks)
        ]
        for copy in copies:
            copy.start()
        total_ref[...] = jnp.zeros_like(total_ref)
        for copy in copies:
            copy.wait()

    tokens = tokens_ref[:, pl.ds(pl.multiple_of(step * depth, depth), depth)]
    total_ref[:, :q_width] += jnp.dot(
        tokens, weights[0][...], preferred_element_type=jnp.float32
    )
    both = jnp.concatenate([weights[1][...], weights[2][...]], axis=1)
    total_ref[:, q_width:] += jnp.dot(tokens, both, preferred_element_type=jnp.float32)

    @pl.when(step == pl.num_programs(0) - 1)
    def _():
        cosine, sine = cos_ref[...], sin_ref[...]

        def turned(vectors):
            return vectors * cosine + pltpu.roll(vectors, HD // 2, 1) * sine

        for head in range(q_width // HD):
            cols = slice(head * HD, (head + 1) * HD)
            query = total_ref[:, cols] + q_bias_ref[:, cols].astype(jnp.float32)
            query_ref[head] = turned(query).astype(jnp.bfloat16)
        key = total_ref[:, q_width : q_width + HD] + k_bias_ref[...].astype(jnp.float32)
        key = turned(key.astype(jnp.bfloat16).astype(jnp.float32)).astype(jnp.bfloat16)
        value = total_ref[:, q_width + HD :] + v_bias_ref[...].astype(jnp.float32)
        value = value.astype(jnp.bfloat16)
        key_ref[...] = key
        value_ref[:, :HD] = value
        value_ref[:, HD:] = jnp.ones_like(value)
        pair_ref[:, :HD] = key
        pair_ref[:, HD:] = value


def project(starts, blocks, weights, biases, tables):
    width = blocks[0].shape[1]
    rows = sum(block.shape[0] for block in blocks)
    depth = math.gcd(width, 1024)
    q_width = weights[0].shape[1]
    out_width = q_width + 2 * HD
    fixed = lambda array: pl.BlockSpec(array.shape, lambda step: (0,) * len(array.shape))
    in_specs = [pl.BlockSpec(memory_space=pltpu.SMEM)]
    in_specs += [pl.BlockSpec(memory_space=pl.ANY)] * len(blocks)
    in_specs += [pl.BlockSpec((depth, weight.shape[1]), lambda step: (step, 0)) for weight in weights]
    in_specs += [fixed(array) for array in (*biases, *tables)]
    out_shape = (
        jax.ShapeDtypeStruct((q_width // HD, rows, HD), jnp.bfloat16),
        jax.ShapeDtypeStruct((rows, HD), jnp.bfloat16),
        jax.ShapeDtypeStruct((rows, 2 * HD), jnp.bfloat16),
        jax.ShapeDtypeStruct((rows, 2 * HD), jnp.bfloat16),
    )
    return pl.pallas_call(
        project_kernel,
        grid=(width // depth,),
        out_shape=out_shape,
        in_specs=in_specs,
        out_specs=tuple(fixed(shape) for shape in out_shape),
        scratch_shapes=[
            pltpu.VMEM((rows, width), jnp.bfloat16),
            pltpu.VMEM((rows, out_width), jnp.float32),
            pltpu.SemaphoreType.DMA((len(blocks),)),
        ],
        compiler_params=pltpu.CompilerParams(vmem_limit_bytes=ATTEND_VMEM),
        cost_estimate=pl.CostEstimate(
            flops=2 * rows * width * out_width,
            bytes_accessed=2 * width * (rows + out_width) + 4 * rows * out_width,
            transcendentals=0,
        ),
        name="project",
    )(starts, *blocks, *weights, *biases, *tables)


class RingScatter:
    def __init__(self, shares, n_model, my_model, first, way):
        order = [m for m in range(0, n_model, 2)] + [m for m in range(n_model - 1, 0, -2)]
        self.order = order
        self.n_model = n_model
        self.way = way
        spot = jnp.array([order.index(m) for m in range(n_model)], jnp.int32)[my_model]
        self.shares, self.spot, self.first = shares, spot, first
        self.distance = {way: n_model // 2, -way: n_model // 2 - 1}
        self.moving = {}

    def share_of(self, offset):
        table = jnp.array(self.order, jnp.int32)
        owner = table[(self.spot + offset + self.n_model) % self.n_model]
        owner = (owner - self.first + self.n_model) % self.n_model
        return lax.dynamic_index_in_dim(self.shares, owner, 0, keepdims=False)

    def advance(self):
        started = []
        for way in (self.way, -self.way):
            if not self.distance[way]:
                continue
            block = self.share_of(way * self.distance[way])
            if way in self.moving:
                arrived = self.moving[way].astype(jnp.float32)
                block = (block.astype(jnp.float32) + arrived).astype(jnp.bfloat16)
            started.append(way)
            self.moving[way] = block
            self.distance[way] -= 1
        return started

    def send(self, started):
        for way in started:
            pairs = [
                (self.order[i], self.order[(i + way) % self.n_model]) for i in range(self.n_model)
            ]
            self.moving[way] = lax.ppermute(self.moving[way], "mp", pairs)

    def step(self, *held):
        started = self.advance()
        blocks, held = lax.optimization_barrier(([self.moving[way] for way in started], held))
        for way, block in zip(started, blocks):
            self.moving[way] = block
        self.send(started)
        return held

    def finish(self):
        while any(self.distance.values()):
            self.send(self.advance())
        total = self.share_of(0).astype(jnp.float32)
        for way in (1, -1):
            total = total + self.moving[way].astype(jnp.float32)
        return total.astype(jnp.bfloat16)


def pack_kernel(slots_ref, heads_ref, pool_ref, *out_refs):
    capacity = slots_ref.shape[1]
    dests = heads_ref.shape[0]

    def place(rank, _):
        for listed, out_ref in enumerate(out_refs):
            slot = slots_ref[listed, rank]
            for dest in range(dests):
                first = pl.multiple_of(heads_ref[dest] * 2 * HD, 2 * HD)
                out_ref[dest, rank] = pool_ref[slot, :, pl.ds(first, 2 * HD)]
        return 0

    lax.fori_loop(0, capacity, place, 0)


def pack_blocks(pool, slots, heads):
    shape = (heads.shape[0], slots.shape[1], pool.shape[1], 2 * HD)
    return pl.pallas_call(
        pack_kernel,
        out_shape=[jax.ShapeDtypeStruct(shape, jnp.bfloat16)] * slots.shape[0],
        in_specs=[
            pl.BlockSpec(memory_space=pltpu.SMEM),
            pl.BlockSpec(memory_space=pltpu.SMEM),
            pl.BlockSpec(memory_space=pltpu.VMEM),
        ],
        out_specs=[pl.BlockSpec(memory_space=pltpu.VMEM)] * slots.shape[0],
        compiler_params=pltpu.CompilerParams(vmem_limit_bytes=VMEM_LIMIT),
        name="pack_blocks",
    )(slots, heads, pool)


def merge_kernel(kept_ref, got_ref, *refs):
    *out_refs, sems = refs
    copies = []
    for dest, out_ref in enumerate(out_refs):
        for side, source in enumerate((kept_ref, got_ref)):
            copies.append(
                pltpu.make_async_copy(source.at[dest], out_ref.at[side], sems.at[dest, side])
            )
    for copy in copies:
        copy.start()
    for copy in copies:
        copy.wait()


def merge_blocks(kept, got):
    dests = kept.shape[0]
    shape = jax.ShapeDtypeStruct((2, *kept.shape[1:]), kept.dtype)
    return pl.pallas_call(
        merge_kernel,
        out_shape=[shape] * dests,
        in_specs=[pl.BlockSpec(memory_space=pl.ANY)] * 2,
        out_specs=[pl.BlockSpec(memory_space=pl.ANY)] * dests,
        scratch_shapes=[pltpu.SemaphoreType.DMA((dests, 2))],
        name="merge_blocks",
    )(kept, got)


def order_kernel(length_ref, where_ref, *refs):
    *arrived_refs, key_ref, value_ref, held_ref, sems = refs
    block_len = held_ref.shape[1]
    count = held_ref.shape[0] // len(arrived_refs)
    copies = [
        pltpu.make_async_copy(
            arrived, held_ref.at[index * count : (index + 1) * count], sems.at[index]
        )
        for index, arrived in enumerate(arrived_refs)
    ]
    for copy in copies:
        copy.start()
    for copy in copies:
        copy.wait()
    length = length_ref[0]
    first = held_ref[where_ref[0]][:1, :HD].astype(jnp.float32)
    row = lax.broadcasted_iota(jnp.int32, (block_len, HD), 0)

    def place(block_id, _):
        block = held_ref[where_ref[block_id]].astype(jnp.float32)
        start = pl.multiple_of(block_id * block_len, block_len)
        seen = row + start < length
        rows = pl.ds(start, block_len)
        key_ref[rows, :] = jnp.where(seen, block[:, :HD], first).astype(jnp.bfloat16)
        value_ref[rows, :HD] = jnp.where(seen, block[:, HD:], 0.0).astype(jnp.bfloat16)
        value_ref[rows, HD:] = jnp.where(seen, 1.0, 0.0).astype(jnp.bfloat16)
        return 0

    lax.fori_loop(0, where_ref.shape[0], place, 0, unroll=8)


def order_blocks(arrived, where, length):
    count, block_len, _ = arrived[0].shape
    tokens = where.shape[0] * block_len
    return pl.pallas_call(
        order_kernel,
        out_shape=(
            jax.ShapeDtypeStruct((tokens, HD), jnp.bfloat16),
            jax.ShapeDtypeStruct((tokens, 2 * HD), jnp.bfloat16),
        ),
        in_specs=[pl.BlockSpec(memory_space=pltpu.SMEM)] * 2
        + [pl.BlockSpec(memory_space=pl.ANY)] * len(arrived),
        out_specs=(
            pl.BlockSpec(memory_space=pltpu.VMEM),
            pl.BlockSpec(memory_space=pltpu.VMEM),
        ),
        scratch_shapes=[
            pltpu.VMEM((len(arrived) * count, block_len, 2 * HD), jnp.bfloat16),
            pltpu.SemaphoreType.DMA((len(arrived),)),
        ],
        compiler_params=pltpu.CompilerParams(vmem_limit_bytes=ATTEND_VMEM),
        name="order_blocks",
    )(length, where, *arrived)


def dot_keys(queries, keys):
    return lax.dot_general(
        queries, keys, (((1,), (1,)), ((), ())), preferred_element_type=jnp.float32
    )


def attend_kernel(span, row_step, chunk, half_ref, *refs):
    query_refs, (key_ref, value_ref), new_key_refs, new_value_refs, out_ref = (
        refs[:2],
        refs[2:4],
        refs[4:6],
        refs[6:8],
        refs[8],
    )
    rows = out_ref.shape[0]
    half = new_key_refs[0].shape[0]
    queries = jnp.concatenate([ref[0].reshape(rows // 2, HD) for ref in query_refs], 0)
    spans = key_ref.shape[0] // span
    stride = 2 * half * row_step // rows
    turn = half_ref[0] * half
    local = lax.broadcasted_iota(jnp.int32, (rows, half), 0)
    token = (local // row_step) * stride + chunk * row_step + local % row_step
    token = lax.rem(token + turn, 2 * half)
    column = lax.broadcasted_iota(jnp.int32, (rows, half), 1)
    parts = []
    for side, ref in enumerate(new_key_refs):
        causal = column + lax.rem(turn + side * half, 2 * half) <= token
        parts.append(jnp.where(causal, dot_keys(queries, ref[...]), -jnp.inf))
    scores = jnp.concatenate(parts, 1)
    peak = jnp.max(scores, axis=1, keepdims=True)
    total = None
    values = jnp.concatenate([ref[...] for ref in new_value_refs], 0)
    for step in range(spans + 1):
        if step < spans:
            next_scores = dot_keys(queries, key_ref[step * span : (step + 1) * span, :])
            next_peak = jnp.maximum(peak, jnp.max(next_scores, axis=1, keepdims=True))
        weights = jnp.exp2((scores - peak) * SCORE_SCALE).astype(jnp.bfloat16)
        product = jnp.dot(weights, values, preferred_element_type=jnp.float32)
        total = product if total is None else total + product
        if step < spans:
            total = total * jnp.exp2((peak - next_peak) * SCORE_SCALE)
            scores, peak = next_scores, next_peak
            values = value_ref[step * span : (step + 1) * span, :]
    out_ref[...] = (total[:, :HD] / total[:, HD:]).astype(jnp.bfloat16)


def attend(half, queries, prefix, new_keys, new_values, row_step, chunk, first_head, heads):
    owners = queries[0].shape[1]
    rows = 2 * owners * row_step
    span = math.gcd(prefix[0].shape[0], 1024)
    whole = lambda array: pl.BlockSpec(array.shape, lambda head: (0, 0))
    count = prefix[0].shape[0] + 2 * new_keys[0].shape[0]
    query_spec = pl.BlockSpec(
        (1, owners, None, row_step, HD), lambda head: (first_head + head, 0, chunk, 0, 0)
    )
    fixed = (*prefix, *new_keys, *new_values)
    return pl.pallas_call(
        functools.partial(attend_kernel, span, row_step, chunk),
        grid=(heads,),
        out_shape=jax.ShapeDtypeStruct((rows, heads * HD), jnp.bfloat16),
        in_specs=[pl.BlockSpec(memory_space=pltpu.SMEM), query_spec, query_spec]
        + [whole(array) for array in fixed],
        out_specs=pl.BlockSpec((rows, HD), lambda head: (0, head)),
        compiler_params=pltpu.CompilerParams(vmem_limit_bytes=ATTEND_VMEM),
        cost_estimate=pl.CostEstimate(
            flops=heads * rows * count * HD * 8,
            bytes_accessed=2 * (count * 3 * HD + 2 * heads * rows * HD),
            transcendentals=heads * rows * count,
        ),
        name="attend",
    )(half, *queries, *fixed)


def on_device(
    n_model,
    n_pool,
    states,
    norm_gain,
    w_query,
    q_bias,
    w_key,
    w_value,
    k_bias,
    v_bias,
    w_out,
    kv_pool,
    hit_holder,
    hit_slot,
    prefix_len,
):
    my_model = lax.axis_index("mp")
    my_pool = lax.axis_index("pool")
    row_count = states.shape[1]
    suffix = row_count * n_model
    q_width = w_query.shape[1]
    q_local = q_width // HD
    kv_local = w_key.shape[1]
    kv_heads = kv_local * n_model // HD
    group_size = QH // kv_heads
    blocks_total = hit_holder.shape[1]
    block_len = kv_pool.shape[2]
    holders = n_model * n_pool
    capacity = 2 * blocks_total // holders
    sharers = HD // kv_local

    lined = n_model == LINE_MODELS

    self_holder = my_model * n_pool + my_pool
    chosen = listing(hit_holder == self_holder, capacity)
    slot_ids = jnp.sum(jnp.where(chosen, hit_slot[:, None, :], 0), -1)
    models = jnp.arange(n_model, dtype=jnp.int32)
    my_holder = hit_holder[my_pool]
    if lined:
        slot_ids = jnp.where(my_pool == 0, slot_ids, slot_ids[::-1])
        kept, given = pack_blocks(kv_pool[0], slot_ids, (models ^ my_model) * q_local // group_size)
        got = lax.ppermute(given, "pool", [(0, 1), (1, 0)])
        outgoing = merge_blocks(kept, got)
        arrived = [
            lax.ppermute(block, "mp", [(index, index ^ apart) for index in range(n_model)])
            if apart
            else block
            for apart, block in enumerate(outgoing)
        ]
        arrived = [block.reshape(-1, block_len, 2 * HD) for block in arrived]
        from_holder = ((my_holder // n_pool) ^ my_model) * n_pool + (my_holder % n_pool ^ my_pool)
    else:
        outgoing = jnp.stack(pack_blocks(kv_pool[0], slot_ids, models * q_local // group_size), 1)
        outgoing = outgoing.reshape(holders, capacity * block_len, 2 * HD)
        arrived = lax.all_to_all(outgoing, ("mp", "pool"), split_axis=0, concat_axis=0, tiled=True)
        arrived = [arrived.reshape(holders * capacity, block_len, 2 * HD)]
        from_holder = my_holder
    block_ids = jnp.arange(blocks_total, dtype=jnp.int32)
    earlier = (my_holder[:, None] == my_holder[None, :]) & (block_ids[None, :] < block_ids[:, None])
    where = from_holder * capacity + jnp.sum(earlier.astype(jnp.int32), -1)
    prefix_count = prefix_len[my_pool]

    upper_half = (my_model // (n_model // 2)).astype(jnp.int32) if lined else jnp.int32(0)
    half_rows = suffix // 2
    order = (jnp.arange(suffix, dtype=jnp.int32) + upper_half * half_rows) % suffix
    cosine, sine = angle_tables(prefix_count + order)
    cosine, sine = jnp.concatenate([cosine, cosine], 1), jnp.concatenate([-sine, sine], 1)
    normed = normalize(states[0], norm_gain)
    halves = [slice(0, half_rows), slice(half_rows, suffix)]
    biases = [bias.reshape(1, -1) for bias in (q_bias, k_bias, v_bias)]
    weights = (w_query, w_key, w_value)
    if lined:
        my_z, my_y = my_model // 2, my_model % 2
        middle = (my_z == 1) | (my_z == 2)
        near, far = line_gather(normed, upper_half, middle)
        results = []
        for blocks, inner in ((near, my_z % 2), (far, upper_half)):
            starts = jnp.stack(
                [
                    2 * (inner ^ other) + (my_y ^ side)
                    for side in range(2)
                    for other in range(2)
                ]
            )
            table = [part[halves[len(results)]] for part in (cosine, sine)]
            results.append(
                project(starts.astype(jnp.int32) * row_count, blocks, weights, biases, table)
            )
        queries, new_keys, new_values, pairs = zip(*results)
        pairs = jnp.where(
            upper_half == 0, jnp.concatenate(pairs, 0), jnp.concatenate(pairs[::-1], 0)
        ).reshape(n_model, row_count, 2 * HD)
    else:
        tokens = lax.all_gather(normed, "mp", axis=0, tiled=True)
        linear, key_raw, value_raw = (
            jnp.dot(tokens, weight, preferred_element_type=jnp.float32) + bias.astype(jnp.float32)
            for weight, bias in zip(weights, biases)
        )
        cosine, sine = cosine[:, : HD // 2], sine[:, HD // 2 :]
        queries = rotate(linear.reshape(suffix, q_local, HD), cosine, sine)
        queries = queries.astype(jnp.bfloat16).transpose(1, 0, 2)
        key_raw, value_raw = key_raw.astype(jnp.bfloat16), value_raw.astype(jnp.bfloat16)
        together = [
            [first + other for other in range(sharers)] for first in range(0, n_model, sharers)
        ]
        key_whole, value_whole = (
            lax.all_gather(part, "mp", axis=1, tiled=True, axis_index_groups=together)
            for part in (key_raw, value_raw)
        )
        key_whole = rotate(key_whole.astype(jnp.float32)[:, None, :], cosine, sine)
        key_whole = key_whole.astype(jnp.bfloat16)[:, 0]
        value_ones = jnp.concatenate([value_whole, jnp.ones_like(value_whole)], 1)
        first_col = (my_model % sharers) * kv_local
        key_cols = lax.dynamic_slice_in_dim(key_whole, first_col, kv_local, 1)
        pairs = jnp.stack([key_cols, value_raw], 1).reshape(n_model, row_count, 2 * kv_local)
        queries = [queries[:, part] for part in halves]
        new_keys = [key_whole[part] for part in halves]
        new_values = [value_ones[part] for part in halves]

    prefix = order_blocks(arrived, where, prefix_count.reshape(1))

    row_step = min(row_count, ROW_STEP)
    chunks = row_count // row_step
    queries = [
        part.reshape(q_local, n_model // 2, chunks, row_step, HD) for part in queries
    ]
    half_index = upper_half.reshape(1)
    scatters = []
    for chunk in range(chunks):
        calls = 1 if chunk == 0 else 2
        heads = q_local // calls
        mixed = []
        for call in range(calls):
            mixed.append(
                attend(
                    half_index,
                    queries,
                    prefix,
                    new_keys,
                    new_values,
                    row_step,
                    chunk,
                    call * heads,
                    heads,
                )
            )
            for scatter in scatters:
                queries, mixed = scatter.step(queries, mixed)
        mixed = jnp.concatenate(mixed, 1)
        share = jnp.dot(mixed, w_out, preferred_element_type=jnp.float32).astype(jnp.bfloat16)
        share = share.reshape(n_model, row_step, share.shape[1])
        scatters.append(
            RingScatter(
                share, n_model, my_model, upper_half * (n_model // 2), 1 if chunk % 2 == 0 else -1
            )
        )
        queries, pairs = scatters[-1].step(queries, pairs)
    pairs = lax.all_to_all(pairs, "mp", split_axis=0, concat_axis=0, tiled=True)
    cache_rows = (
        pairs.reshape(kv_heads, sharers, row_count, 2, kv_local)
        .transpose(2, 0, 3, 1, 4)
        .reshape(1, row_count, kv_heads * 2 * HD)
    )
    return (jnp.concatenate([scatter.finish() for scatter in scatters], 0)[None], cache_rows)


def solution(mesh):
    placed = (
        P(("groups", "pool"), "mp", None),
        P(),
        P(None, "mp"),
        P("mp"),
        P(None, "mp"),
        P(None, "mp"),
        P("mp"),
        P("mp"),
        P("mp", None),
        P(("groups", "mp", "pool"), None, None, None),
        P("groups", None),
        P("groups", None),
        P("groups"),
    )
    return jax.shard_map(
        functools.partial(on_device, mesh.shape["mp"], mesh.shape["pool"]),
        mesh=mesh,
        in_specs=placed,
        out_specs=(P(("groups", "pool"), "mp", None), P(("groups", "pool"), "mp", None)),
        check_vma=False,
    )
```

```python
import functools
import math

import jax
import jax.numpy as jnp
from jax import lax
from jax.experimental import pallas as pl
from jax.experimental.pallas import tpu as pltpu
from jax.sharding import PartitionSpec as P

QH = 64
HD = 128
ROPE_BASE = 1000000.0
EPSILON = 1e-06
SCORE_SCALE = HD ** (-0.5) * math.log2(math.e)
VMEM_LIMIT = 56 * 1024 * 1024
ATTEND_VMEM = 28 * 1024 * 1024
ROW_STEP = 32
LINE_MODELS = 8
IN_FLIGHT = 4


def angle_tables(positions):
    frequency = jnp.power(
        jnp.float32(ROPE_BASE), -2.0 * jnp.arange(HD // 2, dtype=jnp.float32) / HD
    )
    angles = positions.astype(jnp.float32)[:, None] * frequency[None, :]
    return jnp.cos(angles), jnp.sin(angles)


def rotate(vectors, cosine, sine):
    first_half = vectors[..., : HD // 2]
    second = vectors[..., HD // 2 :]
    cosine = cosine[:, None, :]
    sine = sine[:, None, :]
    return jnp.concatenate(
        [first_half * cosine - second * sine, second * cosine + first_half * sine], -1
    )


def normalize(states, gain_vec):
    values = states.astype(jnp.float32)
    inv_rms = lax.rsqrt(jnp.mean(values * values, axis=-1, keepdims=True) + EPSILON)
    return (values * inv_rms * gain_vec.astype(jnp.float32)).astype(jnp.bfloat16)


def listing(owned_mask, capacity):
    rank_order = jnp.cumsum(owned_mask.astype(jnp.int32), -1) - 1
    slot_index = jnp.arange(capacity, dtype=jnp.int32)
    return owned_mask[..., None, :] & (rank_order[..., None, :] == slot_index[:, None])


def swap(block, mask):
    return lax.ppermute(block, "mp", [(index, index ^ mask) for index in range(LINE_MODELS)])


def cross(block):
    pairs = []
    for index in range(LINE_MODELS):
        for core in range(2):
            if 2 <= index < 6:
                pairs.append((index * 2 + core, (index ^ 6) * 2 + core))
            else:
                pairs.append((index * 2 + core, index * 2 + 1 - core))
    return lax.ppermute(block, ("mp", "pool"), pairs)


def gather_and_exchange(own, outgoing, middle):
    done = []
    arrived = {0: outgoing[0]}

    def go(block, move):
        if len(done) >= IN_FLIGHT:
            block, done[-IN_FLIGHT] = lax.optimization_barrier((block, done[-IN_FLIGHT]))
        done.append(move(block))
        return done[-1]

    def exchange(apart):
        arrived[apart] = go(outgoing[apart], lambda block: swap(block, apart))

    along = lambda block: swap(block, 2)
    across = lambda block: swap(block, 1)
    beside = go(own, along)
    over = go(own, cross)
    own_y = go(own, across)
    over_beside = go(beside, cross)
    over_passed = go(over, along)
    beside_y = go(beside, across)
    exchange(4)
    over_beside_passed = go(over_beside, along)
    far_first = jnp.where(middle, over, over_passed)
    far_first_y = go(far_first, across)
    exchange(6)
    far_second = jnp.where(middle, over_beside, over_beside_passed)
    far_second_y = go(far_second, across)
    for apart in (5, 2, 7, 3, 1):
        exchange(apart)
    near = [own, beside, own_y, beside_y]
    far = [far_first, far_second, far_first_y, far_second_y]
    near[0], far[0] = lax.optimization_barrier((own, far_first, far_second_y))[:2]
    return near, far, [arrived[apart] for apart in range(LINE_MODELS)]


def project_kernel(starts_ref, *refs):
    n_blocks = starts_ref.shape[0]
    blocks = refs[:n_blocks]
    weights = refs[n_blocks : n_blocks + 3]
    q_bias_ref, k_bias_ref, v_bias_ref, cos_ref, sin_ref = refs[n_blocks + 3 : n_blocks + 8]
    query_ref, key_ref, value_ref, pair_ref, tokens_ref, total_ref, sems = refs[n_blocks + 8 :]
    step = pl.program_id(0)
    depth, q_width = weights[0].shape
    rows = blocks[0].shape[0]

    @pl.when(step == 0)
    def _():
        copies = [
            pltpu.make_async_copy(
                block,
                tokens_ref.at[pl.ds(pl.multiple_of(starts_ref[index], rows), rows), :],
                sems.at[index],
            )
            for index, block in enumerate(blocks)
        ]
        for copy in copies:
            copy.start()
        total_ref[...] = jnp.zeros_like(total_ref)
        for copy in copies:
            copy.wait()

    tokens = tokens_ref[:, pl.ds(pl.multiple_of(step * depth, depth), depth)]
    total_ref[:, :q_width] += jnp.dot(
        tokens, weights[0][...], preferred_element_type=jnp.float32
    )
    both = jnp.concatenate([weights[1][...], weights[2][...]], axis=1)
    total_ref[:, q_width:] += jnp.dot(tokens, both, preferred_element_type=jnp.float32)

    @pl.when(step == pl.num_programs(0) - 1)
    def _():
        cosine, sine = cos_ref[...], sin_ref[...]

        def turned(vectors):
            return vectors * cosine + pltpu.roll(vectors, HD // 2, 1) * sine

        for head in range(q_width // HD):
            cols = slice(head * HD, (head + 1) * HD)
            query = total_ref[:, cols] + q_bias_ref[:, cols].astype(jnp.float32)
            query_ref[head] = turned(query).astype(jnp.bfloat16)
        key = total_ref[:, q_width : q_width + HD] + k_bias_ref[...].astype(jnp.float32)
        key = turned(key.astype(jnp.bfloat16).astype(jnp.float32)).astype(jnp.bfloat16)
        value = total_ref[:, q_width + HD :] + v_bias_ref[...].astype(jnp.float32)
        value = value.astype(jnp.bfloat16)
        key_ref[...] = key
        value_ref[:, :HD] = value
        value_ref[:, HD:] = jnp.ones_like(value)
        pair_ref[:, :HD] = key
        pair_ref[:, HD:] = value


def project(starts, blocks, weights, biases, tables):
    width = blocks[0].shape[1]
    rows = sum(block.shape[0] for block in blocks)
    depth = math.gcd(width, 1024)
    q_width = weights[0].shape[1]
    out_width = q_width + 2 * HD
    fixed = lambda array: pl.BlockSpec(array.shape, lambda step: (0,) * len(array.shape))
    in_specs = [pl.BlockSpec(memory_space=pltpu.SMEM)]
    in_specs += [pl.BlockSpec(memory_space=pl.ANY)] * len(blocks)
    in_specs += [pl.BlockSpec((depth, weight.shape[1]), lambda step: (step, 0)) for weight in weights]
    in_specs += [fixed(array) for array in (*biases, *tables)]
    out_shape = (
        jax.ShapeDtypeStruct((q_width // HD, rows, HD), jnp.bfloat16),
        jax.ShapeDtypeStruct((rows, HD), jnp.bfloat16),
        jax.ShapeDtypeStruct((rows, 2 * HD), jnp.bfloat16),
        jax.ShapeDtypeStruct((rows, 2 * HD), jnp.bfloat16),
    )
    return pl.pallas_call(
        project_kernel,
        grid=(width // depth,),
        out_shape=out_shape,
        in_specs=in_specs,
        out_specs=tuple(fixed(shape) for shape in out_shape),
        scratch_shapes=[
            pltpu.VMEM((rows, width), jnp.bfloat16),
            pltpu.VMEM((rows, out_width), jnp.float32),
            pltpu.SemaphoreType.DMA((len(blocks),)),
        ],
        compiler_params=pltpu.CompilerParams(vmem_limit_bytes=ATTEND_VMEM),
        cost_estimate=pl.CostEstimate(
            flops=2 * rows * width * out_width,
            bytes_accessed=2 * width * (rows + out_width) + 4 * rows * out_width,
            transcendentals=0,
        ),
        name="project",
    )(starts, *blocks, *weights, *biases, *tables)


class RingScatter:
    def __init__(self, shares, n_model, my_model, first, way):
        order = [m for m in range(0, n_model, 2)] + [m for m in range(n_model - 1, 0, -2)]
        self.order = order
        self.n_model = n_model
        self.way = way
        spot = jnp.array([order.index(m) for m in range(n_model)], jnp.int32)[my_model]
        self.shares, self.spot, self.first = shares, spot, first
        self.distance = {way: n_model // 2, -way: n_model // 2 - 1}
        self.moving = {}

    def share_of(self, offset):
        table = jnp.array(self.order, jnp.int32)
        owner = table[(self.spot + offset + self.n_model) % self.n_model]
        owner = (owner - self.first + self.n_model) % self.n_model
        return lax.dynamic_index_in_dim(self.shares, owner, 0, keepdims=False)

    def advance(self):
        started = []
        for way in (self.way, -self.way):
            if not self.distance[way]:
                continue
            block = self.share_of(way * self.distance[way])
            if way in self.moving:
                arrived = self.moving[way].astype(jnp.float32)
                block = (block.astype(jnp.float32) + arrived).astype(jnp.bfloat16)
            started.append(way)
            self.moving[way] = block
            self.distance[way] -= 1
        return started

    def send(self, started):
        for way in started:
            pairs = [
                (self.order[i], self.order[(i + way) % self.n_model]) for i in range(self.n_model)
            ]
            self.moving[way] = lax.ppermute(self.moving[way], "mp", pairs)

    def step(self, *held):
        started = self.advance()
        blocks, held = lax.optimization_barrier(([self.moving[way] for way in started], held))
        for way, block in zip(started, blocks):
            self.moving[way] = block
        self.send(started)
        return held

    def finish(self):
        while any(self.distance.values()):
            self.send(self.advance())
        total = self.share_of(0).astype(jnp.float32)
        for way in (1, -1):
            total = total + self.moving[way].astype(jnp.float32)
        return total.astype(jnp.bfloat16)


def pick_kernel(slots_ref, pool_ref, out_ref):
    def place(rank, _):
        out_ref[rank] = pool_ref[slots_ref[rank]]
        return 0

    lax.fori_loop(0, slots_ref.shape[0], place, 0)


def pick_blocks(pool, slots):
    return pl.pallas_call(
        pick_kernel,
        out_shape=jax.ShapeDtypeStruct((*slots.shape, *pool.shape[1:]), pool.dtype),
        in_specs=[
            pl.BlockSpec(memory_space=pltpu.SMEM),
            pl.BlockSpec(memory_space=pltpu.VMEM),
        ],
        out_specs=pl.BlockSpec(memory_space=pltpu.VMEM),
        compiler_params=pltpu.CompilerParams(vmem_limit_bytes=ATTEND_VMEM),
        name="pick_blocks",
    )(slots, pool)


def pack_kernel(lists, slots_ref, heads_ref, *refs):
    sources, out_refs = refs[: len(lists)], refs[len(lists) :]

    def place(rank, _):
        for listed, source_ref in zip(lists, sources):
            slot = slots_ref[listed, rank]
            for dest, out_ref in enumerate(out_refs):
                first = pl.multiple_of(heads_ref[dest] * 2 * HD, 2 * HD)
                out_ref[listed, rank] = source_ref[slot, :, pl.ds(first, 2 * HD)]
        return 0

    lax.fori_loop(0, slots_ref.shape[1], place, 0)


def pack_blocks(sources, slots, heads):
    dests = heads.shape[0]
    block_len = sources[0].shape[1]
    shape = jax.ShapeDtypeStruct((*slots.shape, block_len, 2 * HD), jnp.bfloat16)
    return pl.pallas_call(
        functools.partial(pack_kernel, range(len(sources))),
        out_shape=[shape] * dests,
        in_specs=[pl.BlockSpec(memory_space=pltpu.SMEM)] * 2
        + [pl.BlockSpec(memory_space=pltpu.VMEM)] * len(sources),
        out_specs=[pl.BlockSpec(memory_space=pltpu.VMEM)] * dests,
        compiler_params=pltpu.CompilerParams(vmem_limit_bytes=ATTEND_VMEM),
        name="pack_blocks",
    )(slots, heads, *sources)


def order_kernel(length_ref, where_ref, *refs):
    *arrived_refs, key_ref, value_ref, held_ref, sems = refs
    block_len = held_ref.shape[1]
    copies = []
    begin = 0
    for index, source in enumerate(arrived_refs):
        end = begin + source.shape[0]
        copies.append(pltpu.make_async_copy(source, held_ref.at[begin:end], sems.at[index]))
        begin = end
    for copy in copies:
        copy.start()
    for copy in copies:
        copy.wait()
    length = length_ref[0]
    first = held_ref[where_ref[0]][:1, :HD].astype(jnp.float32)
    row = lax.broadcasted_iota(jnp.int32, (block_len, HD), 0)

    def place(block_id, _):
        block = held_ref[where_ref[block_id]].astype(jnp.float32)
        start = pl.multiple_of(block_id * block_len, block_len)
        seen = row + start < length
        rows = pl.ds(start, block_len)
        key_ref[rows, :] = jnp.where(seen, block[:, :HD], first).astype(jnp.bfloat16)
        value_ref[rows, :HD] = jnp.where(seen, block[:, HD:], 0.0).astype(jnp.bfloat16)
        value_ref[rows, HD:] = jnp.where(seen, 1.0, 0.0).astype(jnp.bfloat16)
        return 0

    lax.fori_loop(0, where_ref.shape[0], place, 0, unroll=8)


def order_blocks(arrived, where, length):
    count = sum(array.shape[-3] for array in arrived)
    block_len = arrived[0].shape[-2]
    tokens = where.shape[0] * block_len
    return pl.pallas_call(
        order_kernel,
        out_shape=(
            jax.ShapeDtypeStruct((tokens, HD), jnp.bfloat16),
            jax.ShapeDtypeStruct((tokens, 2 * HD), jnp.bfloat16),
        ),
        in_specs=[pl.BlockSpec(memory_space=pltpu.SMEM)] * 2
        + [pl.BlockSpec(memory_space=pl.ANY)] * len(arrived),
        out_specs=(
            pl.BlockSpec(memory_space=pltpu.VMEM),
            pl.BlockSpec(memory_space=pltpu.VMEM),
        ),
        scratch_shapes=[
            pltpu.VMEM((count, block_len, 2 * HD), jnp.bfloat16),
            pltpu.SemaphoreType.DMA((len(arrived),)),
        ],
        compiler_params=pltpu.CompilerParams(vmem_limit_bytes=ATTEND_VMEM),
        name="order_blocks",
    )(length, where, *arrived)


def dot_keys(queries, keys):
    return lax.dot_general(
        queries, keys, (((1,), (1,)), ((), ())), preferred_element_type=jnp.float32
    )


def attend_kernel(span, row_step, chunk, half_ref, *refs):
    query_refs, (key_ref, value_ref), new_key_refs, new_value_refs, out_ref = (
        refs[:2],
        refs[2:4],
        refs[4:6],
        refs[6:8],
        refs[8],
    )
    rows = out_ref.shape[0]
    half = new_key_refs[0].shape[0]
    queries = jnp.concatenate([ref[0].reshape(rows // 2, HD) for ref in query_refs], 0)
    spans = key_ref.shape[0] // span
    stride = 2 * half * row_step // rows
    turn = half_ref[0] * half
    local = lax.broadcasted_iota(jnp.int32, (rows, half), 0)
    token = (local // row_step) * stride + chunk * row_step + local % row_step
    token = lax.rem(token + turn, 2 * half)
    column = lax.broadcasted_iota(jnp.int32, (rows, half), 1)
    parts = []
    for side, ref in enumerate(new_key_refs):
        causal = column + lax.rem(turn + side * half, 2 * half) <= token
        parts.append(jnp.where(causal, dot_keys(queries, ref[...]), -jnp.inf))
    scores = jnp.concatenate(parts, 1)
    peak = jnp.max(scores, axis=1, keepdims=True)
    total = None
    values = jnp.concatenate([ref[...] for ref in new_value_refs], 0)
    for step in range(spans + 1):
        if step < spans:
            next_scores = dot_keys(queries, key_ref[step * span : (step + 1) * span, :])
            next_peak = jnp.maximum(peak, jnp.max(next_scores, axis=1, keepdims=True))
        weights = jnp.exp2((scores - peak) * SCORE_SCALE).astype(jnp.bfloat16)
        product = jnp.dot(weights, values, preferred_element_type=jnp.float32)
        total = product if total is None else total + product
        if step < spans:
            total = total * jnp.exp2((peak - next_peak) * SCORE_SCALE)
            scores, peak = next_scores, next_peak
            values = value_ref[step * span : (step + 1) * span, :]
    out_ref[...] = (total[:, :HD] / total[:, HD:]).astype(jnp.bfloat16)


def attend(half, queries, prefix, new_keys, new_values, row_step, chunk, first_head, heads):
    owners = queries[0].shape[1]
    rows = 2 * owners * row_step
    span = math.gcd(prefix[0].shape[0], 1024)
    whole = lambda array: pl.BlockSpec(array.shape, lambda head: (0, 0))
    count = prefix[0].shape[0] + 2 * new_keys[0].shape[0]
    query_spec = pl.BlockSpec(
        (1, owners, None, row_step, HD), lambda head: (first_head + head, 0, chunk, 0, 0)
    )
    fixed = (*prefix, *new_keys, *new_values)
    return pl.pallas_call(
        functools.partial(attend_kernel, span, row_step, chunk),
        grid=(heads,),
        out_shape=jax.ShapeDtypeStruct((rows, heads * HD), jnp.bfloat16),
        in_specs=[pl.BlockSpec(memory_space=pltpu.SMEM), query_spec, query_spec]
        + [whole(array) for array in fixed],
        out_specs=pl.BlockSpec((rows, HD), lambda head: (0, head)),
        compiler_params=pltpu.CompilerParams(vmem_limit_bytes=ATTEND_VMEM),
        cost_estimate=pl.CostEstimate(
            flops=heads * rows * count * HD * 8,
            bytes_accessed=2 * (count * 3 * HD + 2 * heads * rows * HD),
            transcendentals=heads * rows * count,
        ),
        name="attend",
    )(half, *queries, *fixed)


def output_kernel(mixed_ref, weight_ref, out_ref):
    out_ref[...] = jnp.dot(
        mixed_ref[...], weight_ref[...], preferred_element_type=jnp.float32
    ).astype(jnp.bfloat16)


def output_product(mixed, weight):
    rows, depth = mixed.shape
    width = weight.shape[1]
    tile = math.gcd(width, 1024)
    return pl.pallas_call(
        output_kernel,
        grid=(width // tile,),
        out_shape=jax.ShapeDtypeStruct((rows, width), jnp.bfloat16),
        in_specs=[
            pl.BlockSpec((rows, depth), lambda col: (0, 0)),
            pl.BlockSpec((depth, tile), lambda col: (0, col)),
        ],
        out_specs=pl.BlockSpec((rows, tile), lambda col: (0, col)),
        compiler_params=pltpu.CompilerParams(vmem_limit_bytes=ATTEND_VMEM),
        cost_estimate=pl.CostEstimate(
            flops=2 * rows * depth * width,
            bytes_accessed=2 * (rows * depth + depth * width + rows * width),
            transcendentals=0,
        ),
        name="output_product",
    )(mixed, weight)


def on_device(
    n_model,
    n_pool,
    states,
    norm_gain,
    w_query,
    q_bias,
    w_key,
    w_value,
    k_bias,
    v_bias,
    w_out,
    kv_pool,
    hit_holder,
    hit_slot,
    prefix_len,
):
    my_model = lax.axis_index("mp")
    my_pool = lax.axis_index("pool")
    row_count = states.shape[1]
    suffix = row_count * n_model
    q_width = w_query.shape[1]
    q_local = q_width // HD
    kv_local = w_key.shape[1]
    kv_heads = kv_local * n_model // HD
    group_size = QH // kv_heads
    blocks_total = hit_holder.shape[1]
    block_len = kv_pool.shape[2]
    holders = n_model * n_pool
    capacity = 2 * blocks_total // holders
    sharers = HD // kv_local

    lined = n_model == LINE_MODELS

    self_holder = my_model * n_pool + my_pool
    chosen = listing(hit_holder == self_holder, capacity)
    slot_ids = jnp.sum(jnp.where(chosen, hit_slot[:, None, :], 0), -1)
    models = jnp.arange(n_model, dtype=jnp.int32)
    my_holder = hit_holder[my_pool]
    prefix_count = prefix_len[my_pool]
    block_ids = jnp.arange(blocks_total, dtype=jnp.int32)
    earlier = (my_holder[:, None] == my_holder[None, :]) & (block_ids[None, :] < block_ids[:, None])
    rank = jnp.sum(earlier.astype(jnp.int32), -1)
    normed = normalize(states[0], norm_gain)
    if lined:
        mine, others = (
            lax.dynamic_index_in_dim(slot_ids, pool, 0, keepdims=False)
            for pool in (my_pool, 1 - my_pool)
        )
        pool_blocks = kv_pool[0]
        got = lax.ppermute(pick_blocks(pool_blocks, others), "pool", [(0, 1), (1, 0)])
        slots = jnp.stack([mine, jnp.arange(capacity, dtype=jnp.int32)])
        outgoing = pack_blocks((pool_blocks, got), slots, (models ^ my_model) * q_local // group_size)
        my_z, my_y = my_model // 2, my_model % 2
        near, far, arrived = gather_and_exchange(normed, outgoing, (my_z == 1) | (my_z == 2))
        arrived = [block.reshape(-1, block_len, 2 * HD) for block in arrived]
        distance = (my_holder // n_pool) ^ my_model
        where = (distance * n_pool + (my_holder % n_pool ^ my_pool)) * capacity + rank
    else:
        outgoing = pack_blocks((kv_pool[0],) * 2, slot_ids, models * q_local // group_size)
        outgoing = jnp.stack(outgoing).reshape(holders, capacity * block_len, 2 * HD)
        arrived = lax.all_to_all(outgoing, ("mp", "pool"), split_axis=0, concat_axis=0, tiled=True)
        arrived = [arrived.reshape(holders * capacity, block_len, 2 * HD)]
        where = my_holder * capacity + rank

    upper_half = (my_model // (n_model // 2)).astype(jnp.int32) if lined else jnp.int32(0)
    half_rows = suffix // 2
    order = (jnp.arange(suffix, dtype=jnp.int32) + upper_half * half_rows) % suffix
    cosine, sine = angle_tables(prefix_count + order)
    cosine, sine = jnp.concatenate([cosine, cosine], 1), jnp.concatenate([-sine, sine], 1)
    halves = [slice(0, half_rows), slice(half_rows, suffix)]
    biases = [bias.reshape(1, -1) for bias in (q_bias, k_bias, v_bias)]
    weights = (w_query, w_key, w_value)
    if lined:
        results = []
        for blocks, inner in ((near, my_z % 2), (far, upper_half)):
            starts = jnp.stack(
                [
                    2 * (inner ^ other) + (my_y ^ side)
                    for side in range(2)
                    for other in range(2)
                ]
            )
            table = [part[halves[len(results)]] for part in (cosine, sine)]
            results.append(
                project(starts.astype(jnp.int32) * row_count, blocks, weights, biases, table)
            )
        queries, new_keys, new_values, pairs = zip(*results)
        pairs = jnp.where(
            upper_half == 0, jnp.concatenate(pairs, 0), jnp.concatenate(pairs[::-1], 0)
        ).reshape(n_model, row_count, 2 * HD)
    else:
        tokens = lax.all_gather(normed, "mp", axis=0, tiled=True)
        linear, key_raw, value_raw = (
            jnp.dot(tokens, weight, preferred_element_type=jnp.float32) + bias.astype(jnp.float32)
            for weight, bias in zip(weights, biases)
        )
        cosine, sine = cosine[:, : HD // 2], sine[:, HD // 2 :]
        queries = rotate(linear.reshape(suffix, q_local, HD), cosine, sine)
        queries = queries.astype(jnp.bfloat16).transpose(1, 0, 2)
        key_raw, value_raw = key_raw.astype(jnp.bfloat16), value_raw.astype(jnp.bfloat16)
        together = [
            [first + other for other in range(sharers)] for first in range(0, n_model, sharers)
        ]
        key_whole, value_whole = (
            lax.all_gather(part, "mp", axis=1, tiled=True, axis_index_groups=together)
            for part in (key_raw, value_raw)
        )
        key_whole = rotate(key_whole.astype(jnp.float32)[:, None, :], cosine, sine)
        key_whole = key_whole.astype(jnp.bfloat16)[:, 0]
        value_ones = jnp.concatenate([value_whole, jnp.ones_like(value_whole)], 1)
        first_col = (my_model % sharers) * kv_local
        key_cols = lax.dynamic_slice_in_dim(key_whole, first_col, kv_local, 1)
        pairs = jnp.stack([key_cols, value_raw], 1).reshape(n_model, row_count, 2 * kv_local)
        queries = [queries[:, part] for part in halves]
        new_keys = [key_whole[part] for part in halves]
        new_values = [value_ones[part] for part in halves]

    prefix = order_blocks(arrived, where, prefix_count.reshape(1))

    row_step = min(row_count, ROW_STEP)
    chunks = row_count // row_step
    queries = [
        part.reshape(q_local, n_model // 2, chunks, row_step, HD) for part in queries
    ]
    half_index = upper_half.reshape(1)
    scatters = []
    for chunk in range(chunks):
        calls = 1 if chunk == 0 else 2
        heads = q_local // calls
        mixed = []
        for call in range(calls):
            mixed.append(
                attend(
                    half_index,
                    queries,
                    prefix,
                    new_keys,
                    new_values,
                    row_step,
                    chunk,
                    call * heads,
                    heads,
                )
            )
            for scatter in scatters:
                queries, mixed = scatter.step(queries, mixed)
        mixed = jnp.concatenate(mixed, 1)
        if chunk == 0:
            pairs = lax.all_to_all(pairs, "mp", split_axis=0, concat_axis=0, tiled=True)
            mixed, pairs = lax.optimization_barrier((mixed, pairs))
        share = output_product(mixed, w_out)
        share = share.reshape(n_model, row_step, share.shape[1])
        scatters.append(
            RingScatter(
                share, n_model, my_model, upper_half * (n_model // 2), 1 if chunk % 2 == 0 else -1
            )
        )
        queries = scatters[-1].step(queries)[0]
    cache_rows = (
        pairs.reshape(kv_heads, sharers, row_count, 2, kv_local)
        .transpose(2, 0, 3, 1, 4)
        .reshape(1, row_count, kv_heads * 2 * HD)
    )
    return (jnp.concatenate([scatter.finish() for scatter in scatters], 0)[None], cache_rows)


def solution(mesh):
    placed = (
        P(("groups", "pool"), "mp", None),
        P(),
        P(None, "mp"),
        P("mp"),
        P(None, "mp"),
        P(None, "mp"),
        P("mp"),
        P("mp"),
        P("mp", None),
        P(("groups", "mp", "pool"), None, None, None),
        P("groups", None),
        P("groups", None),
        P("groups"),
    )
    return jax.shard_map(
        functools.partial(on_device, mesh.shape["mp"], mesh.shape["pool"]),
        mesh=mesh,
        in_specs=placed,
        out_specs=(P(("groups", "pool"), "mp", None), P(("groups", "pool"), "mp", None)),
        check_vma=False,
    )
```

```python
import functools
import math

import jax
import jax.numpy as jnp
from jax import lax
from jax.experimental import pallas as pl
from jax.experimental.pallas import tpu as pltpu
from jax.sharding import PartitionSpec as P

QH = 64
HD = 128
ROPE_BASE = 1000000.0
EPSILON = 1e-06
SCORE_SCALE = HD ** (-0.5) * math.log2(math.e)
VMEM_LIMIT = 56 * 1024 * 1024
ATTEND_VMEM = 28 * 1024 * 1024
COLUMN_CHUNKS = 2
LINE_MODELS = 8


def angle_tables(positions):
    frequency = jnp.power(
        jnp.float32(ROPE_BASE), -2.0 * jnp.arange(HD // 2, dtype=jnp.float32) / HD
    )
    angles = positions.astype(jnp.float32)[:, None] * frequency[None, :]
    return jnp.cos(angles), jnp.sin(angles)


def rotate(vectors, cosine, sine):
    first_half = vectors[..., : HD // 2]
    second = vectors[..., HD // 2 :]
    cosine = cosine[:, None, :]
    sine = sine[:, None, :]
    return jnp.concatenate(
        [first_half * cosine - second * sine, second * cosine + first_half * sine], -1
    )


def normalize(states, gain_vec):
    values = states.astype(jnp.float32)
    inv_rms = lax.rsqrt(jnp.mean(values * values, axis=-1, keepdims=True) + EPSILON)
    return (values * inv_rms * gain_vec.astype(jnp.float32)).astype(jnp.bfloat16)


def listing(owned_mask, capacity):
    rank_order = jnp.cumsum(owned_mask.astype(jnp.int32), -1) - 1
    slot_index = jnp.arange(capacity, dtype=jnp.int32)
    return owned_mask[..., None, :] & (rank_order[..., None, :] == slot_index[:, None])


def swap(block, mask):
    return lax.ppermute(block, "mp", [(index, index ^ mask) for index in range(LINE_MODELS)])


def cross(block):
    pairs = []
    for index in range(LINE_MODELS):
        for core in range(2):
            if 2 <= index < 6:
                pairs.append((index * 2 + core, (index ^ 6) * 2 + core))
            else:
                pairs.append((index * 2 + core, index * 2 + 1 - core))
    return lax.ppermute(block, ("mp", "pool"), pairs)


def gather_and_exchange(own, outgoing, middle):
    arrived = {0: outgoing[0]}

    def after(block, *events):
        return lax.optimization_barrier((block, events))[0]

    def exchange(apart, *events):
        block = after(outgoing[apart], *events) if events else outgoing[apart]
        arrived[apart] = swap(block, apart)

    beside = swap(own, 2)
    over = cross(own)
    own_y = swap(own, 1)
    exchange(6)
    beside = after(beside, outgoing[6])
    over_beside = cross(beside)
    over_passed = swap(over, 2)
    beside_y = swap(beside, 1)
    exchange(4, over)
    over_beside_passed = swap(over_beside, 2)
    far_first = jnp.where(middle, over, over_passed)
    far_first_y = swap(far_first, 1)
    exchange(5, arrived[6], over_beside)
    exchange(2, over_passed, beside_y)
    far_second = jnp.where(middle, over_beside, over_beside_passed)
    far_second_y = swap(far_second, 1)
    exchange(7, arrived[4], far_second)
    exchange(3, far_first_y)
    exchange(1, far_first_y, arrived[2])
    near = [after(own, far_second, arrived[4], arrived[6]), beside, own_y, beside_y]
    far = [after(far_first, arrived[5], arrived[2]), far_second, far_first_y, far_second_y]
    return near, far, [arrived[apart] for apart in range(LINE_MODELS)]


def project_kernel(starts_ref, *refs):
    n_blocks = starts_ref.shape[0]
    blocks = refs[:n_blocks]
    weights = refs[n_blocks : n_blocks + 3]
    q_bias_ref, k_bias_ref, v_bias_ref, cos_ref, sin_ref = refs[n_blocks + 3 : n_blocks + 8]
    query_ref, key_ref, value_ref, pair_ref, tokens_ref, total_ref, sems = refs[n_blocks + 8 :]
    step = pl.program_id(0)
    depth, q_width = weights[0].shape
    rows = blocks[0].shape[0]

    @pl.when(step == 0)
    def _():
        copies = [
            pltpu.make_async_copy(
                block,
                tokens_ref.at[pl.ds(pl.multiple_of(starts_ref[index], rows), rows), :],
                sems.at[index],
            )
            for index, block in enumerate(blocks)
        ]
        for copy in copies:
            copy.start()
        total_ref[...] = jnp.zeros_like(total_ref)
        for copy in copies:
            copy.wait()

    tokens = tokens_ref[:, pl.ds(pl.multiple_of(step * depth, depth), depth)]
    total_ref[:, :q_width] += jnp.dot(
        tokens, weights[0][...], preferred_element_type=jnp.float32
    )
    both = jnp.concatenate([weights[1][...], weights[2][...]], axis=1)
    total_ref[:, q_width:] += jnp.dot(tokens, both, preferred_element_type=jnp.float32)

    @pl.when(step == pl.num_programs(0) - 1)
    def _():
        cosine, sine = cos_ref[...], sin_ref[...]

        def turned(vectors):
            return vectors * cosine + pltpu.roll(vectors, HD // 2, 1) * sine

        for head in range(q_width // HD):
            cols = slice(head * HD, (head + 1) * HD)
            query = total_ref[:, cols] + q_bias_ref[:, cols].astype(jnp.float32)
            query_ref[head] = turned(query).astype(jnp.bfloat16)
        key = total_ref[:, q_width : q_width + HD] + k_bias_ref[...].astype(jnp.float32)
        key = turned(key.astype(jnp.bfloat16).astype(jnp.float32)).astype(jnp.bfloat16)
        value = total_ref[:, q_width + HD :] + v_bias_ref[...].astype(jnp.float32)
        value = value.astype(jnp.bfloat16)
        key_ref[...] = key
        value_ref[:, :HD] = value
        value_ref[:, HD:] = jnp.ones_like(value)
        pair_ref[:, :HD] = key
        pair_ref[:, HD:] = value


def project(starts, blocks, weights, biases, tables):
    width = blocks[0].shape[1]
    rows = sum(block.shape[0] for block in blocks)
    depth = math.gcd(width, 1024)
    q_width = weights[0].shape[1]
    out_width = q_width + 2 * HD
    fixed = lambda array: pl.BlockSpec(array.shape, lambda step: (0,) * len(array.shape))
    in_specs = [pl.BlockSpec(memory_space=pltpu.SMEM)]
    in_specs += [pl.BlockSpec(memory_space=pl.ANY)] * len(blocks)
    in_specs += [pl.BlockSpec((depth, weight.shape[1]), lambda step: (step, 0)) for weight in weights]
    in_specs += [fixed(array) for array in (*biases, *tables)]
    out_shape = (
        jax.ShapeDtypeStruct((q_width // HD, rows, HD), jnp.bfloat16),
        jax.ShapeDtypeStruct((rows, HD), jnp.bfloat16),
        jax.ShapeDtypeStruct((rows, 2 * HD), jnp.bfloat16),
        jax.ShapeDtypeStruct((rows, 2 * HD), jnp.bfloat16),
    )
    return pl.pallas_call(
        project_kernel,
        grid=(width // depth,),
        out_shape=out_shape,
        in_specs=in_specs,
        out_specs=tuple(fixed(shape) for shape in out_shape),
        scratch_shapes=[
            pltpu.VMEM((rows, width), jnp.bfloat16),
            pltpu.VMEM((rows, out_width), jnp.float32),
            pltpu.SemaphoreType.DMA((len(blocks),)),
        ],
        compiler_params=pltpu.CompilerParams(vmem_limit_bytes=VMEM_LIMIT),
        cost_estimate=pl.CostEstimate(
            flops=2 * rows * width * out_width,
            bytes_accessed=2 * width * (rows + out_width) + 4 * rows * out_width,
            transcendentals=0,
        ),
        name="project",
    )(starts, *blocks, *weights, *biases, *tables)


class RingScatter:
    def __init__(self, shares, n_model, my_model, first, way):
        order = [m for m in range(0, n_model, 2)] + [m for m in range(n_model - 1, 0, -2)]
        self.order = order
        self.n_model = n_model
        self.way = way
        spot = jnp.array([order.index(m) for m in range(n_model)], jnp.int32)[my_model]
        self.shares, self.spot, self.first = shares, spot, first
        self.distance = {way: n_model // 2, -way: n_model // 2 - 1}
        self.moving = {}

    def share_of(self, offset):
        table = jnp.array(self.order, jnp.int32)
        owner = table[(self.spot + offset + self.n_model) % self.n_model]
        owner = (owner - self.first + self.n_model) % self.n_model
        return lax.dynamic_index_in_dim(self.shares, owner, 0, keepdims=False)

    def advance(self):
        started = []
        for way in (self.way, -self.way):
            if not self.distance[way]:
                continue
            block = self.share_of(way * self.distance[way])
            if way in self.moving:
                arrived = self.moving[way].astype(jnp.float32)
                block = (block.astype(jnp.float32) + arrived).astype(jnp.bfloat16)
            started.append(way)
            self.moving[way] = block
            self.distance[way] -= 1
        return started

    def send(self, started):
        for way in started:
            pairs = [
                (self.order[i], self.order[(i + way) % self.n_model]) for i in range(self.n_model)
            ]
            self.moving[way] = lax.ppermute(self.moving[way], "mp", pairs)

    def step(self, *held):
        started = self.advance()
        blocks, held = lax.optimization_barrier(([self.moving[way] for way in started], held))
        for way, block in zip(started, blocks):
            self.moving[way] = block
        self.send(started)
        return held

    def finish(self):
        while any(self.distance.values()):
            self.send(self.advance())
        total = self.share_of(0).astype(jnp.float32)
        for way in (1, -1):
            total = total + self.moving[way].astype(jnp.float32)
        return total.astype(jnp.bfloat16)


def pick_kernel(slots_ref, pool_ref, out_ref):
    def place(rank, _):
        out_ref[rank] = pool_ref[slots_ref[rank]]
        return 0

    lax.fori_loop(0, slots_ref.shape[0], place, 0)


def pick_blocks(pool, slots):
    return pl.pallas_call(
        pick_kernel,
        out_shape=jax.ShapeDtypeStruct((*slots.shape, *pool.shape[1:]), pool.dtype),
        in_specs=[
            pl.BlockSpec(memory_space=pltpu.SMEM),
            pl.BlockSpec(memory_space=pltpu.VMEM),
        ],
        out_specs=pl.BlockSpec(memory_space=pltpu.VMEM),
        compiler_params=pltpu.CompilerParams(vmem_limit_bytes=ATTEND_VMEM),
        name="pick_blocks",
    )(slots, pool)


def pack_kernel(lists, slots_ref, heads_ref, *refs):
    sources, out_refs = refs[: len(lists)], refs[len(lists) :]

    def place(rank, _):
        for listed, source_ref in zip(lists, sources):
            slot = slots_ref[listed, rank]
            for dest, out_ref in enumerate(out_refs):
                first = pl.multiple_of(heads_ref[dest] * 2 * HD, 2 * HD)
                out_ref[listed, rank] = source_ref[slot, :, pl.ds(first, 2 * HD)]
        return 0

    lax.fori_loop(0, slots_ref.shape[1], place, 0)


def pack_blocks(sources, slots, heads):
    dests = heads.shape[0]
    block_len = sources[0].shape[1]
    shape = jax.ShapeDtypeStruct((*slots.shape, block_len, 2 * HD), jnp.bfloat16)
    return pl.pallas_call(
        functools.partial(pack_kernel, range(len(sources))),
        out_shape=[shape] * dests,
        in_specs=[pl.BlockSpec(memory_space=pltpu.SMEM)] * 2
        + [pl.BlockSpec(memory_space=pltpu.VMEM)] * len(sources),
        out_specs=[pl.BlockSpec(memory_space=pltpu.VMEM)] * dests,
        compiler_params=pltpu.CompilerParams(vmem_limit_bytes=ATTEND_VMEM),
        name="pack_blocks",
    )(slots, heads, *sources)


def order_kernel(length_ref, where_ref, *refs):
    *arrived_refs, key_ref, value_ref, held_ref, sems = refs
    block_len = held_ref.shape[1]
    copies = []
    begin = 0
    for index, source in enumerate(arrived_refs):
        end = begin + source.shape[0]
        copies.append(pltpu.make_async_copy(source, held_ref.at[begin:end], sems.at[index]))
        begin = end
    for copy in copies:
        copy.start()
    for copy in copies:
        copy.wait()
    length = length_ref[0]
    first = held_ref[where_ref[0]][:1, :HD].astype(jnp.float32)
    row = lax.broadcasted_iota(jnp.int32, (block_len, HD), 0)

    def place(block_id, _):
        block = held_ref[where_ref[block_id]].astype(jnp.float32)
        start = pl.multiple_of(block_id * block_len, block_len)
        seen = row + start < length
        rows = pl.ds(start, block_len)
        key_ref[rows, :] = jnp.where(seen, block[:, :HD], first).astype(jnp.bfloat16)
        value_ref[rows, :HD] = jnp.where(seen, block[:, HD:], 0.0).astype(jnp.bfloat16)
        value_ref[rows, HD:] = jnp.where(seen, 1.0, 0.0).astype(jnp.bfloat16)
        return 0

    lax.fori_loop(0, where_ref.shape[0], place, 0, unroll=8)


def order_blocks(arrived, where, length):
    count = sum(array.shape[-3] for array in arrived)
    block_len = arrived[0].shape[-2]
    tokens = where.shape[0] * block_len
    return pl.pallas_call(
        order_kernel,
        out_shape=(
            jax.ShapeDtypeStruct((tokens, HD), jnp.bfloat16),
            jax.ShapeDtypeStruct((tokens, 2 * HD), jnp.bfloat16),
        ),
        in_specs=[pl.BlockSpec(memory_space=pltpu.SMEM)] * 2
        + [pl.BlockSpec(memory_space=pl.ANY)] * len(arrived),
        out_specs=(
            pl.BlockSpec(memory_space=pltpu.VMEM),
            pl.BlockSpec(memory_space=pltpu.VMEM),
        ),
        scratch_shapes=[
            pltpu.VMEM((count, block_len, 2 * HD), jnp.bfloat16),
            pltpu.SemaphoreType.DMA((len(arrived),)),
        ],
        compiler_params=pltpu.CompilerParams(vmem_limit_bytes=ATTEND_VMEM),
        name="order_blocks",
    )(length, where, *arrived)


def dot_keys(queries, keys):
    return lax.dot_general(
        queries, keys, (((1,), (1,)), ((), ())), preferred_element_type=jnp.float32
    )


def attend_kernel(span, row_step, chunk, half_ref, *refs):
    query_refs, (key_ref, value_ref), new_key_refs, new_value_refs, out_ref = (
        refs[:2],
        refs[2:4],
        refs[4:6],
        refs[6:8],
        refs[8],
    )
    rows = out_ref.shape[0]
    half = new_key_refs[0].shape[0]
    queries = jnp.concatenate([ref[0].reshape(rows // 2, HD) for ref in query_refs], 0)
    spans = key_ref.shape[0] // span
    stride = 2 * half * row_step // rows
    turn = half_ref[0] * half
    local = lax.broadcasted_iota(jnp.int32, (rows, half), 0)
    token = (local // row_step) * stride + chunk * row_step + local % row_step
    token = lax.rem(token + turn, 2 * half)
    column = lax.broadcasted_iota(jnp.int32, (rows, half), 1)
    parts = []
    for side, ref in enumerate(new_key_refs):
        causal = column + lax.rem(turn + side * half, 2 * half) <= token
        parts.append(jnp.where(causal, dot_keys(queries, ref[...]), -jnp.inf))
    scores = jnp.concatenate(parts, 1)
    peak = jnp.max(scores, axis=1, keepdims=True)
    total = None
    values = jnp.concatenate([ref[...] for ref in new_value_refs], 0)
    for step in range(spans + 1):
        if step < spans:
            next_scores = dot_keys(queries, key_ref[step * span : (step + 1) * span, :])
            next_peak = jnp.maximum(peak, jnp.max(next_scores, axis=1, keepdims=True))
        weights = jnp.exp2((scores - peak) * SCORE_SCALE).astype(jnp.bfloat16)
        product = jnp.dot(weights, values, preferred_element_type=jnp.float32)
        total = product if total is None else total + product
        if step < spans:
            total = total * jnp.exp2((peak - next_peak) * SCORE_SCALE)
            scores, peak = next_scores, next_peak
            values = value_ref[step * span : (step + 1) * span, :]
    out_ref[...] = (total[:, :HD] / total[:, HD:]).astype(jnp.bfloat16)


def attend(half, queries, prefix, new_keys, new_values, row_step, chunk, first_head, heads):
    owners = queries[0].shape[1]
    rows = 2 * owners * row_step
    span = math.gcd(prefix[0].shape[0], 1024)
    whole = lambda array: pl.BlockSpec(array.shape, lambda head: (0, 0))
    count = prefix[0].shape[0] + 2 * new_keys[0].shape[0]
    query_spec = pl.BlockSpec(
        (1, owners, None, row_step, HD), lambda head: (first_head + head, 0, chunk, 0, 0)
    )
    fixed = (*prefix, *new_keys, *new_values)
    return pl.pallas_call(
        functools.partial(attend_kernel, span, row_step, chunk),
        grid=(heads,),
        out_shape=jax.ShapeDtypeStruct((rows, heads * HD), jnp.bfloat16),
        in_specs=[pl.BlockSpec(memory_space=pltpu.SMEM), query_spec, query_spec]
        + [whole(array) for array in fixed],
        out_specs=pl.BlockSpec((rows, HD), lambda head: (0, head)),
        compiler_params=pltpu.CompilerParams(vmem_limit_bytes=ATTEND_VMEM),
        cost_estimate=pl.CostEstimate(
            flops=heads * rows * count * HD * 8,
            bytes_accessed=2 * (count * 3 * HD + 2 * heads * rows * HD),
            transcendentals=heads * rows * count,
        ),
        name="attend",
    )(half, *queries, *fixed)


def output_kernel(mixed_ref, weight_ref, out_ref):
    out_ref[...] = jnp.dot(
        mixed_ref[...], weight_ref[...], preferred_element_type=jnp.float32
    ).astype(jnp.bfloat16)


def output_product(mixed, weight, chunk, chunks):
    rows, depth = mixed.shape
    width = weight.shape[1] // chunks
    tile = math.gcd(width, 1024)
    tiles = width // tile
    return pl.pallas_call(
        output_kernel,
        grid=(tiles,),
        out_shape=jax.ShapeDtypeStruct((rows, width), jnp.bfloat16),
        in_specs=[
            pl.BlockSpec((rows, depth), lambda col: (0, 0)),
            pl.BlockSpec((depth, tile), lambda col: (0, chunk * tiles + col)),
        ],
        out_specs=pl.BlockSpec((rows, tile), lambda col: (0, col)),
        compiler_params=pltpu.CompilerParams(vmem_limit_bytes=VMEM_LIMIT),
        cost_estimate=pl.CostEstimate(
            flops=2 * rows * depth * width,
            bytes_accessed=2 * (rows * depth + depth * width + rows * width),
            transcendentals=0,
        ),
        name="output_product",
    )(mixed, weight)


def on_device(
    n_model,
    n_pool,
    states,
    norm_gain,
    w_query,
    q_bias,
    w_key,
    w_value,
    k_bias,
    v_bias,
    w_out,
    kv_pool,
    hit_holder,
    hit_slot,
    prefix_len,
):
    my_model = lax.axis_index("mp")
    my_pool = lax.axis_index("pool")
    row_count = states.shape[1]
    suffix = row_count * n_model
    q_width = w_query.shape[1]
    q_local = q_width // HD
    kv_local = w_key.shape[1]
    kv_heads = kv_local * n_model // HD
    group_size = QH // kv_heads
    blocks_total = hit_holder.shape[1]
    block_len = kv_pool.shape[2]
    holders = n_model * n_pool
    capacity = 2 * blocks_total // holders
    sharers = HD // kv_local

    lined = n_model == LINE_MODELS

    self_holder = my_model * n_pool + my_pool
    chosen = listing(hit_holder == self_holder, capacity)
    slot_ids = jnp.sum(jnp.where(chosen, hit_slot[:, None, :], 0), -1)
    models = jnp.arange(n_model, dtype=jnp.int32)
    my_holder = hit_holder[my_pool]
    prefix_count = prefix_len[my_pool]
    block_ids = jnp.arange(blocks_total, dtype=jnp.int32)
    earlier = (my_holder[:, None] == my_holder[None, :]) & (block_ids[None, :] < block_ids[:, None])
    rank = jnp.sum(earlier.astype(jnp.int32), -1)
    normed = normalize(states[0], norm_gain)
    if lined:
        mine, others = (
            lax.dynamic_index_in_dim(slot_ids, pool, 0, keepdims=False)
            for pool in (my_pool, 1 - my_pool)
        )
        pool_blocks = kv_pool[0]
        got = lax.ppermute(pick_blocks(pool_blocks, others), "pool", [(0, 1), (1, 0)])
        slots = jnp.stack([mine, jnp.arange(capacity, dtype=jnp.int32)])
        outgoing = pack_blocks((pool_blocks, got), slots, (models ^ my_model) * q_local // group_size)
        my_z, my_y = my_model // 2, my_model % 2
        near, far, arrived = gather_and_exchange(normed, outgoing, (my_z == 1) | (my_z == 2))
        arrived = [block.reshape(-1, block_len, 2 * HD) for block in arrived]
        distance = (my_holder // n_pool) ^ my_model
        where = (distance * n_pool + (my_holder % n_pool ^ my_pool)) * capacity + rank
    else:
        outgoing = pack_blocks((kv_pool[0],) * 2, slot_ids, models * q_local // group_size)
        outgoing = jnp.stack(outgoing).reshape(holders, capacity * block_len, 2 * HD)
        arrived = lax.all_to_all(outgoing, ("mp", "pool"), split_axis=0, concat_axis=0, tiled=True)
        arrived = [arrived.reshape(holders * capacity, block_len, 2 * HD)]
        where = my_holder * capacity + rank

    upper_half = (my_model // (n_model // 2)).astype(jnp.int32) if lined else jnp.int32(0)
    half_rows = suffix // 2
    order = (jnp.arange(suffix, dtype=jnp.int32) + upper_half * half_rows) % suffix
    cosine, sine = angle_tables(prefix_count + order)
    cosine, sine = jnp.concatenate([cosine, cosine], 1), jnp.concatenate([-sine, sine], 1)
    halves = [slice(0, half_rows), slice(half_rows, suffix)]
    biases = [bias.reshape(1, -1) for bias in (q_bias, k_bias, v_bias)]
    weights = (w_query, w_key, w_value)
    if lined:
        results = []
        for blocks, inner in ((near, my_z % 2), (far, upper_half)):
            starts = jnp.stack(
                [
                    2 * (inner ^ other) + (my_y ^ side)
                    for side in range(2)
                    for other in range(2)
                ]
            )
            table = [part[halves[len(results)]] for part in (cosine, sine)]
            results.append(
                project(starts.astype(jnp.int32) * row_count, blocks, weights, biases, table)
            )
        queries, new_keys, new_values, pairs = zip(*results)
        pairs = jnp.where(
            upper_half == 0, jnp.concatenate(pairs, 0), jnp.concatenate(pairs[::-1], 0)
        ).reshape(n_model, row_count, 2 * HD)
    else:
        tokens = lax.all_gather(normed, "mp", axis=0, tiled=True)
        linear, key_raw, value_raw = (
            jnp.dot(tokens, weight, preferred_element_type=jnp.float32) + bias.astype(jnp.float32)
            for weight, bias in zip(weights, biases)
        )
        cosine, sine = cosine[:, : HD // 2], sine[:, HD // 2 :]
        queries = rotate(linear.reshape(suffix, q_local, HD), cosine, sine)
        queries = queries.astype(jnp.bfloat16).transpose(1, 0, 2)
        key_raw, value_raw = key_raw.astype(jnp.bfloat16), value_raw.astype(jnp.bfloat16)
        together = [
            [first + other for other in range(sharers)] for first in range(0, n_model, sharers)
        ]
        key_whole, value_whole = (
            lax.all_gather(part, "mp", axis=1, tiled=True, axis_index_groups=together)
            for part in (key_raw, value_raw)
        )
        key_whole = rotate(key_whole.astype(jnp.float32)[:, None, :], cosine, sine)
        key_whole = key_whole.astype(jnp.bfloat16)[:, 0]
        value_ones = jnp.concatenate([value_whole, jnp.ones_like(value_whole)], 1)
        first_col = (my_model % sharers) * kv_local
        key_cols = lax.dynamic_slice_in_dim(key_whole, first_col, kv_local, 1)
        pairs = jnp.stack([key_cols, value_raw], 1).reshape(n_model, row_count, 2 * kv_local)
        queries = [queries[:, part] for part in halves]
        new_keys = [key_whole[part] for part in halves]
        new_values = [value_ones[part] for part in halves]

    arrived, new_keys = lax.optimization_barrier((arrived, list(new_keys)))
    prefix = order_blocks(arrived, where, prefix_count.reshape(1))

    queries = [part.reshape(q_local, -1, 1, row_count, HD) for part in queries]
    mixed = attend(
        upper_half.reshape(1), queries, prefix, new_keys, new_values, row_count, 0, 0, q_local
    )
    pairs = lax.all_to_all(pairs, "mp", split_axis=0, concat_axis=0, tiled=True)
    mixed, pairs = lax.optimization_barrier((mixed, pairs))
    cache_rows = (
        pairs.reshape(kv_heads, sharers, row_count, 2, kv_local)
        .transpose(2, 0, 3, 1, 4)
        .reshape(1, row_count, kv_heads * 2 * HD)
    )

    width = w_out.shape[1]
    first = upper_half * (n_model // 2)
    scatters = []
    for chunk in range(COLUMN_CHUNKS):
        share = output_product(mixed, w_out, chunk, COLUMN_CHUNKS)
        share = share.reshape(n_model, row_count, width // COLUMN_CHUNKS)
        scatters.append(
            RingScatter(share, n_model, my_model, first, 1 if chunk % 2 == 0 else -1)
        )
        (mixed,) = scatters[-1].step(mixed)
    return (jnp.concatenate([scatter.finish() for scatter in scatters], 1)[None], cache_rows)


def solution(mesh):
    placed = (
        P(("groups", "pool"), "mp", None),
        P(),
        P(None, "mp"),
        P("mp"),
        P(None, "mp"),
        P(None, "mp"),
        P("mp"),
        P("mp"),
        P("mp", None),
        P(("groups", "mp", "pool"), None, None, None),
        P("groups", None),
        P("groups", None),
        P("groups"),
    )
    return jax.shard_map(
        functools.partial(on_device, mesh.shape["mp"], mesh.shape["pool"]),
        mesh=mesh,
        in_specs=placed,
        out_specs=(P(("groups", "pool"), "mp", None), P(("groups", "pool"), "mp", None)),
        check_vma=False,
    )
```

```python
import functools
import math

import jax
import jax.numpy as jnp
from jax import lax
from jax.experimental import pallas as pl
from jax.experimental.pallas import tpu as pltpu
from jax.sharding import PartitionSpec as P

QH = 64
HD = 128
ROPE_BASE = 1000000.0
EPSILON = 1e-06
SCORE_SCALE = HD ** (-0.5) * math.log2(math.e)
VMEM_LIMIT = 56 * 1024 * 1024
ATTEND_VMEM = 28 * 1024 * 1024
COLUMN_CHUNKS = 2
STREAMS = 4
LINE_MODELS = 8


def angle_tables(positions):
    frequency = jnp.power(
        jnp.float32(ROPE_BASE), -2.0 * jnp.arange(HD // 2, dtype=jnp.float32) / HD
    )
    angles = positions.astype(jnp.float32)[:, None] * frequency[None, :]
    return jnp.cos(angles), jnp.sin(angles)


def rotate(vectors, cosine, sine):
    first_half = vectors[..., : HD // 2]
    second = vectors[..., HD // 2 :]
    cosine = cosine[:, None, :]
    sine = sine[:, None, :]
    return jnp.concatenate(
        [first_half * cosine - second * sine, second * cosine + first_half * sine], -1
    )


def normalize(states, gain_vec):
    values = states.astype(jnp.float32)
    inv_rms = lax.rsqrt(jnp.mean(values * values, axis=-1, keepdims=True) + EPSILON)
    return (values * inv_rms * gain_vec.astype(jnp.float32)).astype(jnp.bfloat16)


def listing(owned_mask, capacity):
    rank_order = jnp.cumsum(owned_mask.astype(jnp.int32), -1) - 1
    slot_index = jnp.arange(capacity, dtype=jnp.int32)
    return owned_mask[..., None, :] & (rank_order[..., None, :] == slot_index[:, None])


def swap(block, mask):
    return lax.ppermute(block, "mp", [(index, index ^ mask) for index in range(LINE_MODELS)])


def cross(block):
    pairs = []
    for index in range(LINE_MODELS):
        for core in range(2):
            if 2 <= index < 6:
                pairs.append((index * 2 + core, (index ^ 6) * 2 + core))
            else:
                pairs.append((index * 2 + core, index * 2 + 1 - core))
    return lax.ppermute(block, ("mp", "pool"), pairs)


def gather_and_exchange(own, outgoing, middle):
    arrived = {0: outgoing[0]}

    def after(block, *events):
        return lax.optimization_barrier((block, events))[0]

    def exchange(apart, *events):
        block = after(outgoing[apart], *events) if events else outgoing[apart]
        arrived[apart] = swap(block, apart)

    beside = swap(own, 2)
    over = cross(own)
    own_y = swap(own, 1)
    over_beside = cross(beside)
    over_passed = swap(over, 2)
    beside_y = swap(beside, 1)
    far_first = jnp.where(middle, over, over_passed)
    far_first_y = swap(far_first, 1)
    over_beside_passed = swap(over_beside, 2)
    exchange(4, over_beside)
    exchange(6, over_beside, far_first)
    far_second = jnp.where(middle, over_beside, over_beside_passed)
    far_second_y = swap(far_second, 1)
    exchange(5, arrived[4], far_second)
    exchange(2, arrived[4], far_second)
    exchange(7, arrived[6], far_first_y)
    exchange(3, arrived[6], far_first_y)
    exchange(1, arrived[6], far_first_y)
    near = [after(own, far_second, arrived[4]), beside, own_y, beside_y]
    far = [after(far_first, arrived[6]), far_second, far_first_y, far_second_y]
    return near, far, [arrived[apart] for apart in range(LINE_MODELS)]


def project_kernel(starts_ref, *refs):
    n_blocks = starts_ref.shape[0]
    blocks, refs = refs[:n_blocks], refs[n_blocks:]
    q_weights, (k_weight_ref, v_weight_ref), refs = refs[:STREAMS], refs[STREAMS:][:2], refs[STREAMS + 2 :]
    q_bias_ref, k_bias_ref, v_bias_ref, cos_ref, sin_ref = refs[:5]
    query_ref, key_ref, value_ref, pair_ref, tokens_ref, total_ref, sems = refs[5:]
    step = pl.program_id(0)
    depth = k_weight_ref.shape[0]
    q_width = q_weights[0].shape[1]
    rows = blocks[0].shape[0]

    @pl.when(step == 0)
    def _():
        copies = [
            pltpu.make_async_copy(
                block,
                tokens_ref.at[pl.ds(pl.multiple_of(starts_ref[index], rows), rows), :],
                sems.at[index],
            )
            for index, block in enumerate(blocks)
        ]
        for copy in copies:
            copy.start()
        total_ref[...] = jnp.zeros_like(total_ref)
        for copy in copies:
            copy.wait()

    tokens = tokens_ref[:, pl.ds(pl.multiple_of(step * depth, depth), depth)]
    q_weight = jnp.concatenate([ref[...] for ref in q_weights], axis=0)
    total_ref[:, :q_width] += jnp.dot(tokens, q_weight, preferred_element_type=jnp.float32)
    both = jnp.concatenate([k_weight_ref[...], v_weight_ref[...]], axis=1)
    total_ref[:, q_width:] += jnp.dot(tokens, both, preferred_element_type=jnp.float32)

    @pl.when(step == pl.num_programs(0) - 1)
    def _():
        cosine, sine = cos_ref[...], sin_ref[...]

        def turned(vectors):
            return vectors * cosine + pltpu.roll(vectors, HD // 2, 1) * sine

        for head in range(q_width // HD):
            cols = slice(head * HD, (head + 1) * HD)
            query = total_ref[:, cols] + q_bias_ref[:, cols].astype(jnp.float32)
            query_ref[head] = turned(query).astype(jnp.bfloat16)
        key = total_ref[:, q_width : q_width + HD] + k_bias_ref[...].astype(jnp.float32)
        key = turned(key.astype(jnp.bfloat16).astype(jnp.float32)).astype(jnp.bfloat16)
        value = total_ref[:, q_width + HD :] + v_bias_ref[...].astype(jnp.float32)
        value = value.astype(jnp.bfloat16)
        key_ref[...] = key
        value_ref[:, :HD] = value
        value_ref[:, HD:] = jnp.ones_like(value)
        pair_ref[:, :HD] = key
        pair_ref[:, HD:] = value


def project(starts, blocks, weights, biases, tables):
    width = blocks[0].shape[1]
    rows = sum(block.shape[0] for block in blocks)
    depth = math.gcd(width, 1024)
    q_width = weights[0].shape[1]
    out_width = q_width + 2 * HD
    fixed = lambda array: pl.BlockSpec(array.shape, lambda step: (0,) * len(array.shape))
    in_specs = [pl.BlockSpec(memory_space=pltpu.SMEM)]
    in_specs += [pl.BlockSpec(memory_space=pl.ANY)] * len(blocks)
    in_specs += [
        pl.BlockSpec((depth // STREAMS, q_width), lambda step, part=part: (step * STREAMS + part, 0))
        for part in range(STREAMS)
    ]
    in_specs += [pl.BlockSpec((depth, HD), lambda step: (step, 0))] * 2
    in_specs += [fixed(array) for array in (*biases, *tables)]
    out_shape = (
        jax.ShapeDtypeStruct((q_width // HD, rows, HD), jnp.bfloat16),
        jax.ShapeDtypeStruct((rows, HD), jnp.bfloat16),
        jax.ShapeDtypeStruct((rows, 2 * HD), jnp.bfloat16),
        jax.ShapeDtypeStruct((rows, 2 * HD), jnp.bfloat16),
    )
    return pl.pallas_call(
        project_kernel,
        grid=(width // depth,),
        out_shape=out_shape,
        in_specs=in_specs,
        out_specs=tuple(fixed(shape) for shape in out_shape),
        scratch_shapes=[
            pltpu.VMEM((rows, width), jnp.bfloat16),
            pltpu.VMEM((rows, out_width), jnp.float32),
            pltpu.SemaphoreType.DMA((len(blocks),)),
        ],
        compiler_params=pltpu.CompilerParams(vmem_limit_bytes=VMEM_LIMIT),
        cost_estimate=pl.CostEstimate(
            flops=2 * rows * width * out_width,
            bytes_accessed=2 * width * (rows + out_width) + 4 * rows * out_width,
            transcendentals=0,
        ),
        name="project",
    )(starts, *blocks, *weights[:1] * STREAMS, *weights[1:], *biases, *tables)


class RingScatter:
    def __init__(self, shares, n_model, my_model, first, way):
        order = [m for m in range(0, n_model, 2)] + [m for m in range(n_model - 1, 0, -2)]
        self.order = order
        self.n_model = n_model
        self.way = way
        spot = jnp.array([order.index(m) for m in range(n_model)], jnp.int32)[my_model]
        self.shares, self.spot, self.first = shares, spot, first
        self.distance = {way: n_model // 2, -way: n_model // 2 - 1}
        self.moving = {}

    def share_of(self, offset):
        table = jnp.array(self.order, jnp.int32)
        owner = table[(self.spot + offset + self.n_model) % self.n_model]
        owner = (owner - self.first + self.n_model) % self.n_model
        return lax.dynamic_index_in_dim(self.shares, owner, 0, keepdims=False)

    def advance(self):
        started = []
        for way in (self.way, -self.way):
            if not self.distance[way]:
                continue
            block = self.share_of(way * self.distance[way])
            if way in self.moving:
                arrived = self.moving[way].astype(jnp.float32)
                block = (block.astype(jnp.float32) + arrived).astype(jnp.bfloat16)
            started.append(way)
            self.moving[way] = block
            self.distance[way] -= 1
        return started

    def send(self, started):
        for way in started:
            pairs = [
                (self.order[i], self.order[(i + way) % self.n_model]) for i in range(self.n_model)
            ]
            self.moving[way] = lax.ppermute(self.moving[way], "mp", pairs)

    def step(self, *held):
        started = self.advance()
        blocks, held = lax.optimization_barrier(([self.moving[way] for way in started], held))
        for way, block in zip(started, blocks):
            self.moving[way] = block
        self.send(started)
        return held

    def finish(self):
        while any(self.distance.values()):
            self.send(self.advance())
        total = self.share_of(0).astype(jnp.float32)
        for way in (1, -1):
            total = total + self.moving[way].astype(jnp.float32)
        return total.astype(jnp.bfloat16)


def pick_kernel(slots_ref, pool_ref, out_ref):
    def place(rank, _):
        out_ref[rank] = pool_ref[slots_ref[rank]]
        return 0

    lax.fori_loop(0, slots_ref.shape[0], place, 0)


def pick_blocks(pool, slots):
    return pl.pallas_call(
        pick_kernel,
        out_shape=jax.ShapeDtypeStruct((*slots.shape, *pool.shape[1:]), pool.dtype),
        in_specs=[
            pl.BlockSpec(memory_space=pltpu.SMEM),
            pl.BlockSpec(memory_space=pltpu.VMEM),
        ],
        out_specs=pl.BlockSpec(memory_space=pltpu.VMEM),
        compiler_params=pltpu.CompilerParams(vmem_limit_bytes=ATTEND_VMEM),
        name="pick_blocks",
    )(slots, pool)


def pack_kernel(lists, slots_ref, heads_ref, *refs):
    sources, out_refs = refs[: len(lists)], refs[len(lists) :]

    def place(rank, _):
        for listed, source_ref in zip(lists, sources):
            slot = slots_ref[listed, rank]
            for dest, out_ref in enumerate(out_refs):
                first = pl.multiple_of(heads_ref[dest] * 2 * HD, 2 * HD)
                out_ref[listed, rank] = source_ref[slot, :, pl.ds(first, 2 * HD)]
        return 0

    lax.fori_loop(0, slots_ref.shape[1], place, 0)


def pack_blocks(sources, slots, heads):
    dests = heads.shape[0]
    block_len = sources[0].shape[1]
    shape = jax.ShapeDtypeStruct((*slots.shape, block_len, 2 * HD), jnp.bfloat16)
    return pl.pallas_call(
        functools.partial(pack_kernel, range(len(sources))),
        out_shape=[shape] * dests,
        in_specs=[pl.BlockSpec(memory_space=pltpu.SMEM)] * 2
        + [pl.BlockSpec(memory_space=pltpu.VMEM)] * len(sources),
        out_specs=[pl.BlockSpec(memory_space=pltpu.VMEM)] * dests,
        compiler_params=pltpu.CompilerParams(vmem_limit_bytes=ATTEND_VMEM),
        name="pack_blocks",
    )(slots, heads, *sources)


def order_kernel(length_ref, where_ref, *refs):
    *arrived_refs, key_ref, value_ref, held_ref, sems = refs
    block_len = held_ref.shape[1]
    copies = []
    begin = 0
    for index, source in enumerate(arrived_refs):
        end = begin + source.shape[0]
        copies.append(pltpu.make_async_copy(source, held_ref.at[begin:end], sems.at[index]))
        begin = end
    for copy in copies:
        copy.start()
    for copy in copies:
        copy.wait()
    length = length_ref[0]
    first = held_ref[where_ref[0]][:1, :HD].astype(jnp.float32)
    row = lax.broadcasted_iota(jnp.int32, (block_len, HD), 0)

    def place(block_id, _):
        block = held_ref[where_ref[block_id]].astype(jnp.float32)
        start = pl.multiple_of(block_id * block_len, block_len)
        seen = row + start < length
        rows = pl.ds(start, block_len)
        key_ref[rows, :] = jnp.where(seen, block[:, :HD], first).astype(jnp.bfloat16)
        value_ref[rows, :HD] = jnp.where(seen, block[:, HD:], 0.0).astype(jnp.bfloat16)
        value_ref[rows, HD:] = jnp.where(seen, 1.0, 0.0).astype(jnp.bfloat16)
        return 0

    lax.fori_loop(0, where_ref.shape[0], place, 0, unroll=8)


def order_blocks(arrived, where, length):
    count = sum(array.shape[-3] for array in arrived)
    block_len = arrived[0].shape[-2]
    tokens = where.shape[0] * block_len
    return pl.pallas_call(
        order_kernel,
        out_shape=(
            jax.ShapeDtypeStruct((tokens, HD), jnp.bfloat16),
            jax.ShapeDtypeStruct((tokens, 2 * HD), jnp.bfloat16),
        ),
        in_specs=[pl.BlockSpec(memory_space=pltpu.SMEM)] * 2
        + [pl.BlockSpec(memory_space=pl.ANY)] * len(arrived),
        out_specs=(
            pl.BlockSpec(memory_space=pltpu.VMEM),
            pl.BlockSpec(memory_space=pltpu.VMEM),
        ),
        scratch_shapes=[
            pltpu.VMEM((count, block_len, 2 * HD), jnp.bfloat16),
            pltpu.SemaphoreType.DMA((len(arrived),)),
        ],
        compiler_params=pltpu.CompilerParams(vmem_limit_bytes=ATTEND_VMEM),
        name="order_blocks",
    )(length, where, *arrived)


def dot_keys(queries, keys):
    return lax.dot_general(
        queries, keys, (((1,), (1,)), ((), ())), preferred_element_type=jnp.float32
    )


def attend_kernel(span, row_step, chunk, half_ref, *refs):
    query_refs, (key_ref, value_ref), new_key_refs, new_value_refs, out_ref = (
        refs[:2],
        refs[2:4],
        refs[4:6],
        refs[6:8],
        refs[8],
    )
    rows = out_ref.shape[0]
    half = new_key_refs[0].shape[0]
    queries = jnp.concatenate([ref[0].reshape(rows // 2, HD) for ref in query_refs], 0)
    spans = key_ref.shape[0] // span
    stride = 2 * half * row_step // rows
    turn = half_ref[0] * half
    local = lax.broadcasted_iota(jnp.int32, (rows, half), 0)
    token = (local // row_step) * stride + chunk * row_step + local % row_step
    token = lax.rem(token + turn, 2 * half)
    column = lax.broadcasted_iota(jnp.int32, (rows, half), 1)
    parts = []
    for side, ref in enumerate(new_key_refs):
        causal = column + lax.rem(turn + side * half, 2 * half) <= token
        parts.append(jnp.where(causal, dot_keys(queries, ref[...]), -jnp.inf))
    scores = jnp.concatenate(parts, 1)
    peak = jnp.max(scores, axis=1, keepdims=True)
    total = None
    values = jnp.concatenate([ref[...] for ref in new_value_refs], 0)
    for step in range(spans + 1):
        if step < spans:
            next_scores = dot_keys(queries, key_ref[step * span : (step + 1) * span, :])
            next_peak = jnp.maximum(peak, jnp.max(next_scores, axis=1, keepdims=True))
        weights = jnp.exp2((scores - peak) * SCORE_SCALE).astype(jnp.bfloat16)
        product = jnp.dot(weights, values, preferred_element_type=jnp.float32)
        total = product if total is None else total + product
        if step < spans:
            total = total * jnp.exp2((peak - next_peak) * SCORE_SCALE)
            scores, peak = next_scores, next_peak
            values = value_ref[step * span : (step + 1) * span, :]
    out_ref[...] = (total[:, :HD] / total[:, HD:]).astype(jnp.bfloat16)


def attend(half, queries, prefix, new_keys, new_values, row_step, chunk, first_head, heads):
    owners = queries[0].shape[1]
    rows = 2 * owners * row_step
    span = math.gcd(prefix[0].shape[0], 1024)
    whole = lambda array: pl.BlockSpec(array.shape, lambda head: (0, 0))
    count = prefix[0].shape[0] + 2 * new_keys[0].shape[0]
    query_spec = pl.BlockSpec(
        (1, owners, None, row_step, HD), lambda head: (first_head + head, 0, chunk, 0, 0)
    )
    fixed = (*prefix, *new_keys, *new_values)
    return pl.pallas_call(
        functools.partial(attend_kernel, span, row_step, chunk),
        grid=(heads,),
        out_shape=jax.ShapeDtypeStruct((rows, heads * HD), jnp.bfloat16),
        in_specs=[pl.BlockSpec(memory_space=pltpu.SMEM), query_spec, query_spec]
        + [whole(array) for array in fixed],
        out_specs=pl.BlockSpec((rows, HD), lambda head: (0, head)),
        compiler_params=pltpu.CompilerParams(vmem_limit_bytes=ATTEND_VMEM),
        cost_estimate=pl.CostEstimate(
            flops=heads * rows * count * HD * 8,
            bytes_accessed=2 * (count * 3 * HD + 2 * heads * rows * HD),
            transcendentals=heads * rows * count,
        ),
        name="attend",
    )(half, *queries, *fixed)


def output_kernel(mixed_ref, *refs):
    *weight_refs, out_ref = refs
    weight = jnp.concatenate([ref[...] for ref in weight_refs], axis=0)
    out_ref[...] = jnp.dot(
        mixed_ref[...], weight, preferred_element_type=jnp.float32
    ).astype(jnp.bfloat16)


def output_product(mixed, weight, chunk, chunks):
    rows, depth = mixed.shape
    width = weight.shape[1] // chunks
    tile = math.gcd(width, 1024)
    tiles = width // tile
    return pl.pallas_call(
        output_kernel,
        grid=(tiles,),
        out_shape=jax.ShapeDtypeStruct((rows, width), jnp.bfloat16),
        in_specs=[pl.BlockSpec((rows, depth), lambda col: (0, 0))]
        + [
            pl.BlockSpec((depth // STREAMS, tile), lambda col, part=part: (part, chunk * tiles + col))
            for part in range(STREAMS)
        ],
        out_specs=pl.BlockSpec((rows, tile), lambda col: (0, col)),
        compiler_params=pltpu.CompilerParams(vmem_limit_bytes=VMEM_LIMIT),
        cost_estimate=pl.CostEstimate(
            flops=2 * rows * depth * width,
            bytes_accessed=2 * (rows * depth + depth * width + rows * width),
            transcendentals=0,
        ),
        name="output_product",
    )(mixed, *[weight] * STREAMS)


def on_device(
    n_model,
    n_pool,
    states,
    norm_gain,
    w_query,
    q_bias,
    w_key,
    w_value,
    k_bias,
    v_bias,
    w_out,
    kv_pool,
    hit_holder,
    hit_slot,
    prefix_len,
):
    my_model = lax.axis_index("mp")
    my_pool = lax.axis_index("pool")
    row_count = states.shape[1]
    suffix = row_count * n_model
    q_width = w_query.shape[1]
    q_local = q_width // HD
    kv_local = w_key.shape[1]
    kv_heads = kv_local * n_model // HD
    group_size = QH // kv_heads
    blocks_total = hit_holder.shape[1]
    block_len = kv_pool.shape[2]
    holders = n_model * n_pool
    capacity = 2 * blocks_total // holders
    sharers = HD // kv_local

    lined = n_model == LINE_MODELS

    self_holder = my_model * n_pool + my_pool
    chosen = listing(hit_holder == self_holder, capacity)
    slot_ids = jnp.sum(jnp.where(chosen, hit_slot[:, None, :], 0), -1)
    models = jnp.arange(n_model, dtype=jnp.int32)
    my_holder = hit_holder[my_pool]
    prefix_count = prefix_len[my_pool]
    block_ids = jnp.arange(blocks_total, dtype=jnp.int32)
    earlier = (my_holder[:, None] == my_holder[None, :]) & (block_ids[None, :] < block_ids[:, None])
    rank = jnp.sum(earlier.astype(jnp.int32), -1)
    normed = normalize(states[0], norm_gain)
    if lined:
        mine, others = (
            lax.dynamic_index_in_dim(slot_ids, pool, 0, keepdims=False)
            for pool in (my_pool, 1 - my_pool)
        )
        pool_blocks = kv_pool[0]
        got = lax.ppermute(pick_blocks(pool_blocks, others), "pool", [(0, 1), (1, 0)])
        slots = jnp.stack([mine, jnp.arange(capacity, dtype=jnp.int32)])
        outgoing = pack_blocks((pool_blocks, got), slots, (models ^ my_model) * q_local // group_size)
        my_z, my_y = my_model // 2, my_model % 2
        near, far, arrived = gather_and_exchange(normed, outgoing, (my_z == 1) | (my_z == 2))
        arrived = [block.reshape(-1, block_len, 2 * HD) for block in arrived]
        distance = (my_holder // n_pool) ^ my_model
        where = (distance * n_pool + (my_holder % n_pool ^ my_pool)) * capacity + rank
    else:
        outgoing = pack_blocks((kv_pool[0],) * 2, slot_ids, models * q_local // group_size)
        outgoing = jnp.stack(outgoing).reshape(holders, capacity * block_len, 2 * HD)
        arrived = lax.all_to_all(outgoing, ("mp", "pool"), split_axis=0, concat_axis=0, tiled=True)
        arrived = [arrived.reshape(holders * capacity, block_len, 2 * HD)]
        where = my_holder * capacity + rank

    upper_half = (my_model // (n_model // 2)).astype(jnp.int32) if lined else jnp.int32(0)
    half_rows = suffix // 2
    order = (jnp.arange(suffix, dtype=jnp.int32) + upper_half * half_rows) % suffix
    cosine, sine = angle_tables(prefix_count + order)
    cosine, sine = jnp.concatenate([cosine, cosine], 1), jnp.concatenate([-sine, sine], 1)
    halves = [slice(0, half_rows), slice(half_rows, suffix)]
    biases = [bias.reshape(1, -1) for bias in (q_bias, k_bias, v_bias)]
    weights = (w_query, w_key, w_value)
    if lined:
        results = []
        for blocks, inner in ((near, my_z % 2), (far, upper_half)):
            starts = jnp.stack(
                [
                    2 * (inner ^ other) + (my_y ^ side)
                    for side in range(2)
                    for other in range(2)
                ]
            )
            table = [part[halves[len(results)]] for part in (cosine, sine)]
            results.append(
                project(starts.astype(jnp.int32) * row_count, blocks, weights, biases, table)
            )
        queries, new_keys, new_values, pairs = zip(*results)
        pairs = jnp.where(
            upper_half == 0, jnp.concatenate(pairs, 0), jnp.concatenate(pairs[::-1], 0)
        ).reshape(n_model, row_count, 2 * HD)
    else:
        tokens = lax.all_gather(normed, "mp", axis=0, tiled=True)
        linear, key_raw, value_raw = (
            jnp.dot(tokens, weight, preferred_element_type=jnp.float32) + bias.astype(jnp.float32)
            for weight, bias in zip(weights, biases)
        )
        cosine, sine = cosine[:, : HD // 2], sine[:, HD // 2 :]
        queries = rotate(linear.reshape(suffix, q_local, HD), cosine, sine)
        queries = queries.astype(jnp.bfloat16).transpose(1, 0, 2)
        key_raw, value_raw = key_raw.astype(jnp.bfloat16), value_raw.astype(jnp.bfloat16)
        together = [
            [first + other for other in range(sharers)] for first in range(0, n_model, sharers)
        ]
        key_whole, value_whole = (
            lax.all_gather(part, "mp", axis=1, tiled=True, axis_index_groups=together)
            for part in (key_raw, value_raw)
        )
        key_whole = rotate(key_whole.astype(jnp.float32)[:, None, :], cosine, sine)
        key_whole = key_whole.astype(jnp.bfloat16)[:, 0]
        value_ones = jnp.concatenate([value_whole, jnp.ones_like(value_whole)], 1)
        first_col = (my_model % sharers) * kv_local
        key_cols = lax.dynamic_slice_in_dim(key_whole, first_col, kv_local, 1)
        pairs = jnp.stack([key_cols, value_raw], 1).reshape(n_model, row_count, 2 * kv_local)
        queries = [queries[:, part] for part in halves]
        new_keys = [key_whole[part] for part in halves]
        new_values = [value_ones[part] for part in halves]

    arrived, new_keys = lax.optimization_barrier((arrived, list(new_keys)))
    prefix = order_blocks(arrived, where, prefix_count.reshape(1))

    queries = [part.reshape(q_local, -1, 1, row_count, HD) for part in queries]
    mixed = attend(
        upper_half.reshape(1), queries, prefix, new_keys, new_values, row_count, 0, 0, q_local
    )
    pairs = lax.all_to_all(pairs, "mp", split_axis=0, concat_axis=0, tiled=True)
    mixed, pairs = lax.optimization_barrier((mixed, pairs))
    cache_rows = (
        pairs.reshape(kv_heads, sharers, row_count, 2, kv_local)
        .transpose(2, 0, 3, 1, 4)
        .reshape(1, row_count, kv_heads * 2 * HD)
    )

    width = w_out.shape[1]
    first = upper_half * (n_model // 2)
    scatters = []
    for chunk in range(COLUMN_CHUNKS):
        share = output_product(mixed, w_out, chunk, COLUMN_CHUNKS)
        share = share.reshape(n_model, row_count, width // COLUMN_CHUNKS)
        scatters.append(
            RingScatter(share, n_model, my_model, first, 1 if chunk % 2 == 0 else -1)
        )
        (mixed,) = scatters[-1].step(mixed)
    return (jnp.concatenate([scatter.finish() for scatter in scatters], 1)[None], cache_rows)


def solution(mesh):
    placed = (
        P(("groups", "pool"), "mp", None),
        P(),
        P(None, "mp"),
        P("mp"),
        P(None, "mp"),
        P(None, "mp"),
        P("mp"),
        P("mp"),
        P("mp", None),
        P(("groups", "mp", "pool"), None, None, None),
        P("groups", None),
        P("groups", None),
        P("groups"),
    )
    return jax.shard_map(
        functools.partial(on_device, mesh.shape["mp"], mesh.shape["pool"]),
        mesh=mesh,
        in_specs=placed,
        out_specs=(P(("groups", "pool"), "mp", None), P(("groups", "pool"), "mp", None)),
        check_vma=False,
    )
```

```python
import functools
import math

import jax
import jax.numpy as jnp
from jax import lax
from jax.experimental import pallas as pl
from jax.experimental.pallas import tpu as pltpu
from jax.sharding import PartitionSpec as P

QH = 64
HD = 128
ROPE_BASE = 1000000.0
EPSILON = 1e-06
SCORE_SCALE = HD ** (-0.5) * math.log2(math.e)
VMEM_LIMIT = 56 * 1024 * 1024
ATTEND_VMEM = 28 * 1024 * 1024
COLUMN_CHUNKS = 2
STREAMS = 4
LINE_MODELS = 8


def angle_tables(positions):
    frequency = jnp.power(
        jnp.float32(ROPE_BASE), -2.0 * jnp.arange(HD // 2, dtype=jnp.float32) / HD
    )
    angles = positions.astype(jnp.float32)[:, None] * frequency[None, :]
    return jnp.cos(angles), jnp.sin(angles)


def rotate(vectors, cosine, sine):
    first_half = vectors[..., : HD // 2]
    second = vectors[..., HD // 2 :]
    cosine = cosine[:, None, :]
    sine = sine[:, None, :]
    return jnp.concatenate(
        [first_half * cosine - second * sine, second * cosine + first_half * sine], -1
    )


def normalize(states, gain_vec):
    values = states.astype(jnp.float32)
    inv_rms = lax.rsqrt(jnp.mean(values * values, axis=-1, keepdims=True) + EPSILON)
    return (values * inv_rms * gain_vec.astype(jnp.float32)).astype(jnp.bfloat16)


def listing(owned_mask, capacity):
    rank_order = jnp.cumsum(owned_mask.astype(jnp.int32), -1) - 1
    slot_index = jnp.arange(capacity, dtype=jnp.int32)
    return owned_mask[..., None, :] & (rank_order[..., None, :] == slot_index[:, None])


def swap(block, mask):
    return lax.ppermute(block, "mp", [(index, index ^ mask) for index in range(LINE_MODELS)])


def cross(block):
    pairs = []
    for index in range(LINE_MODELS):
        for core in range(2):
            if 2 <= index < 6:
                pairs.append((index * 2 + core, (index ^ 6) * 2 + core))
            else:
                pairs.append((index * 2 + core, index * 2 + 1 - core))
    return lax.ppermute(block, ("mp", "pool"), pairs)


def gather_and_exchange(own, outgoing, middle):
    arrived = {0: outgoing[0]}

    def after(block, *events):
        return lax.optimization_barrier((block, events))[0]

    def exchange(apart, *events):
        block = after(outgoing[apart], *events) if events else outgoing[apart]
        arrived[apart] = swap(block, apart)

    beside = swap(own, 2)
    over = cross(own)
    own_y = swap(own, 1)
    over_beside = cross(beside)
    over_passed = swap(over, 2)
    beside_y = swap(beside, 1)
    far_first = jnp.where(middle, over, over_passed)
    far_first_y = swap(far_first, 1)
    over_beside_passed = swap(after(over_beside, outgoing[4]), 2)
    exchange(4, over_beside)
    exchange(6, over_beside)
    far_second = jnp.where(middle, over_beside, over_beside_passed)
    far_second_y = swap(far_second, 1)
    exchange(5, far_first_y, far_second)
    exchange(2, far_first_y, far_second)
    exchange(7, arrived[4], far_first_y)
    exchange(3, arrived[4], far_first_y)
    exchange(1, arrived[4], far_first_y)
    near = [after(own, far_second, arrived[4], arrived[6]), beside, own_y, beside_y]
    far = [far_first, far_second, far_first_y, far_second_y]
    return near, far, [arrived[apart] for apart in range(LINE_MODELS)]


def project_kernel(starts_ref, *refs):
    n_blocks = starts_ref.shape[0]
    blocks, refs = refs[:n_blocks], refs[n_blocks:]
    q_weights, (k_weight_ref, v_weight_ref), refs = refs[:STREAMS], refs[STREAMS:][:2], refs[STREAMS + 2 :]
    q_bias_ref, k_bias_ref, v_bias_ref, cos_ref, sin_ref = refs[:5]
    query_ref, key_ref, value_ref, pair_ref, tokens_ref, total_ref, sems = refs[5:]
    step = pl.program_id(0)
    depth = k_weight_ref.shape[0]
    q_width = q_weights[0].shape[1]
    rows = blocks[0].shape[0]

    @pl.when(step == 0)
    def _():
        copies = [
            pltpu.make_async_copy(
                block,
                tokens_ref.at[pl.ds(pl.multiple_of(starts_ref[index], rows), rows), :],
                sems.at[index],
            )
            for index, block in enumerate(blocks)
        ]
        for copy in copies:
            copy.start()
        total_ref[...] = jnp.zeros_like(total_ref)
        for copy in copies:
            copy.wait()

    tokens = tokens_ref[:, pl.ds(pl.multiple_of(step * depth, depth), depth)]
    q_weight = jnp.concatenate([ref[...] for ref in q_weights], axis=0)
    total_ref[:, :q_width] += jnp.dot(tokens, q_weight, preferred_element_type=jnp.float32)
    both = jnp.concatenate([k_weight_ref[...], v_weight_ref[...]], axis=1)
    total_ref[:, q_width:] += jnp.dot(tokens, both, preferred_element_type=jnp.float32)

    @pl.when(step == pl.num_programs(0) - 1)
    def _():
        cosine, sine = cos_ref[...], sin_ref[...]

        def turned(vectors):
            return vectors * cosine + pltpu.roll(vectors, HD // 2, 1) * sine

        for head in range(q_width // HD):
            cols = slice(head * HD, (head + 1) * HD)
            query = total_ref[:, cols] + q_bias_ref[:, cols].astype(jnp.float32)
            query_ref[head] = turned(query).astype(jnp.bfloat16)
        key = total_ref[:, q_width : q_width + HD] + k_bias_ref[...].astype(jnp.float32)
        key = turned(key.astype(jnp.bfloat16).astype(jnp.float32)).astype(jnp.bfloat16)
        value = total_ref[:, q_width + HD :] + v_bias_ref[...].astype(jnp.float32)
        value = value.astype(jnp.bfloat16)
        key_ref[...] = key
        value_ref[:, :HD] = value
        value_ref[:, HD:] = jnp.ones_like(value)
        pair_ref[:, :HD] = key
        pair_ref[:, HD:] = value


def project(starts, blocks, weights, biases, tables):
    width = blocks[0].shape[1]
    rows = sum(block.shape[0] for block in blocks)
    depth = math.gcd(width, 1024)
    q_width = weights[0].shape[1]
    out_width = q_width + 2 * HD
    fixed = lambda array: pl.BlockSpec(array.shape, lambda step: (0,) * len(array.shape))
    in_specs = [pl.BlockSpec(memory_space=pltpu.SMEM)]
    in_specs += [pl.BlockSpec(memory_space=pl.ANY)] * len(blocks)
    in_specs += [
        pl.BlockSpec((depth // STREAMS, q_width), lambda step, part=part: (step * STREAMS + part, 0))
        for part in range(STREAMS)
    ]
    in_specs += [pl.BlockSpec((depth, HD), lambda step: (step, 0))] * 2
    in_specs += [fixed(array) for array in (*biases, *tables)]
    out_shape = (
        jax.ShapeDtypeStruct((q_width // HD, rows, HD), jnp.bfloat16),
        jax.ShapeDtypeStruct((rows, HD), jnp.bfloat16),
        jax.ShapeDtypeStruct((rows, 2 * HD), jnp.bfloat16),
        jax.ShapeDtypeStruct((rows, 2 * HD), jnp.bfloat16),
    )
    return pl.pallas_call(
        project_kernel,
        grid=(width // depth,),
        out_shape=out_shape,
        in_specs=in_specs,
        out_specs=tuple(fixed(shape) for shape in out_shape),
        scratch_shapes=[
            pltpu.VMEM((rows, width), jnp.bfloat16),
            pltpu.VMEM((rows, out_width), jnp.float32),
            pltpu.SemaphoreType.DMA((len(blocks),)),
        ],
        compiler_params=pltpu.CompilerParams(vmem_limit_bytes=VMEM_LIMIT),
        cost_estimate=pl.CostEstimate(
            flops=2 * rows * width * out_width,
            bytes_accessed=2 * width * (rows + out_width) + 4 * rows * out_width,
            transcendentals=0,
        ),
        name="project",
    )(starts, *blocks, *weights[:1] * STREAMS, *weights[1:], *biases, *tables)


class RingScatter:
    def __init__(self, shares, n_model, my_model, first, way):
        order = [m for m in range(0, n_model, 2)] + [m for m in range(n_model - 1, 0, -2)]
        self.order = order
        self.n_model = n_model
        self.way = way
        spot = jnp.array([order.index(m) for m in range(n_model)], jnp.int32)[my_model]
        self.shares, self.spot, self.first = shares, spot, first
        self.distance = {way: n_model // 2, -way: n_model // 2 - 1}
        self.moving = {}

    def share_of(self, offset):
        table = jnp.array(self.order, jnp.int32)
        owner = table[(self.spot + offset + self.n_model) % self.n_model]
        owner = (owner - self.first + self.n_model) % self.n_model
        return lax.dynamic_index_in_dim(self.shares, owner, 0, keepdims=False)

    def advance(self):
        started = []
        for way in (self.way, -self.way):
            if not self.distance[way]:
                continue
            block = self.share_of(way * self.distance[way])
            if way in self.moving:
                arrived = self.moving[way].astype(jnp.float32)
                block = (block.astype(jnp.float32) + arrived).astype(jnp.bfloat16)
            started.append(way)
            self.moving[way] = block
            self.distance[way] -= 1
        return started

    def send(self, started):
        for way in started:
            pairs = [
                (self.order[i], self.order[(i + way) % self.n_model]) for i in range(self.n_model)
            ]
            self.moving[way] = lax.ppermute(self.moving[way], "mp", pairs)

    def finish(self):
        while any(self.distance.values()):
            self.send(self.advance())
        total = self.share_of(0).astype(jnp.float32)
        for way in (1, -1):
            total = total + self.moving[way].astype(jnp.float32)
        return total.astype(jnp.bfloat16)


def pick_kernel(slots_ref, pool_ref, out_ref):
    def place(rank, _):
        out_ref[rank] = pool_ref[slots_ref[rank]]
        return 0

    lax.fori_loop(0, slots_ref.shape[0], place, 0)


def pick_blocks(pool, slots):
    return pl.pallas_call(
        pick_kernel,
        out_shape=jax.ShapeDtypeStruct((*slots.shape, *pool.shape[1:]), pool.dtype),
        in_specs=[
            pl.BlockSpec(memory_space=pltpu.SMEM),
            pl.BlockSpec(memory_space=pltpu.VMEM),
        ],
        out_specs=pl.BlockSpec(memory_space=pltpu.VMEM),
        compiler_params=pltpu.CompilerParams(vmem_limit_bytes=ATTEND_VMEM),
        name="pick_blocks",
    )(slots, pool)


def pack_kernel(lists, slots_ref, heads_ref, *refs):
    sources, out_refs = refs[: len(lists)], refs[len(lists) :]

    def place(rank, _):
        for listed, source_ref in zip(lists, sources):
            slot = slots_ref[listed, rank]
            for dest, out_ref in enumerate(out_refs):
                first = pl.multiple_of(heads_ref[dest] * 2 * HD, 2 * HD)
                out_ref[listed, rank] = source_ref[slot, :, pl.ds(first, 2 * HD)]
        return 0

    lax.fori_loop(0, slots_ref.shape[1], place, 0)


def pack_blocks(sources, slots, heads):
    dests = heads.shape[0]
    block_len = sources[0].shape[1]
    shape = jax.ShapeDtypeStruct((*slots.shape, block_len, 2 * HD), jnp.bfloat16)
    return pl.pallas_call(
        functools.partial(pack_kernel, range(len(sources))),
        out_shape=[shape] * dests,
        in_specs=[pl.BlockSpec(memory_space=pltpu.SMEM)] * 2
        + [pl.BlockSpec(memory_space=pltpu.VMEM)] * len(sources),
        out_specs=[pl.BlockSpec(memory_space=pltpu.VMEM)] * dests,
        compiler_params=pltpu.CompilerParams(vmem_limit_bytes=ATTEND_VMEM),
        name="pack_blocks",
    )(slots, heads, *sources)


def order_kernel(length_ref, where_ref, *refs):
    *arrived_refs, key_ref, value_ref, held_ref, sems = refs
    block_len = held_ref.shape[1]
    copies = []
    begin = 0
    for index, source in enumerate(arrived_refs):
        end = begin + source.shape[0]
        copies.append(pltpu.make_async_copy(source, held_ref.at[begin:end], sems.at[index]))
        begin = end
    for copy in copies:
        copy.start()
    for copy in copies:
        copy.wait()
    length = length_ref[0]
    first = held_ref[where_ref[0]][:1, :HD].astype(jnp.float32)
    row = lax.broadcasted_iota(jnp.int32, (block_len, HD), 0)

    def place(block_id, _):
        block = held_ref[where_ref[block_id]].astype(jnp.float32)
        start = pl.multiple_of(block_id * block_len, block_len)
        seen = row + start < length
        rows = pl.ds(start, block_len)
        key_ref[rows, :] = jnp.where(seen, block[:, :HD], first).astype(jnp.bfloat16)
        value_ref[rows, :HD] = jnp.where(seen, block[:, HD:], 0.0).astype(jnp.bfloat16)
        value_ref[rows, HD:] = jnp.where(seen, 1.0, 0.0).astype(jnp.bfloat16)
        return 0

    lax.fori_loop(0, where_ref.shape[0], place, 0, unroll=8)


def order_blocks(arrived, where, length):
    count = sum(array.shape[-3] for array in arrived)
    block_len = arrived[0].shape[-2]
    tokens = where.shape[0] * block_len
    return pl.pallas_call(
        order_kernel,
        out_shape=(
            jax.ShapeDtypeStruct((tokens, HD), jnp.bfloat16),
            jax.ShapeDtypeStruct((tokens, 2 * HD), jnp.bfloat16),
        ),
        in_specs=[pl.BlockSpec(memory_space=pltpu.SMEM)] * 2
        + [pl.BlockSpec(memory_space=pl.ANY)] * len(arrived),
        out_specs=(
            pl.BlockSpec(memory_space=pltpu.VMEM),
            pl.BlockSpec(memory_space=pltpu.VMEM),
        ),
        scratch_shapes=[
            pltpu.VMEM((count, block_len, 2 * HD), jnp.bfloat16),
            pltpu.SemaphoreType.DMA((len(arrived),)),
        ],
        compiler_params=pltpu.CompilerParams(vmem_limit_bytes=ATTEND_VMEM),
        name="order_blocks",
    )(length, where, *arrived)


def dot_keys(queries, keys):
    return lax.dot_general(
        queries, keys, (((1,), (1,)), ((), ())), preferred_element_type=jnp.float32
    )


def attend_kernel(span, heads, half_ref, *refs):
    query_refs, (key_ref, value_ref), new_key_refs, new_value_refs = (
        refs[:2],
        refs[2:4],
        refs[4:6],
        refs[6:8],
    )
    weight_ref, *out_refs = refs[8 : 9 + COLUMN_CHUNKS]
    mixed_ref, held_ref, sems = refs[9 + COLUMN_CHUNKS :]
    step = pl.program_id(0)
    rows = mixed_ref.shape[0]
    half = rows // 2
    depth = held_ref.shape[0] // STREAMS
    copies = [
        pltpu.make_async_copy(
            weight_ref.at[part * depth : (part + 1) * depth, :],
            held_ref.at[part * depth : (part + 1) * depth, :],
            sems.at[part],
        )
        for part in range(STREAMS)
    ]

    @pl.when(step == 0)
    def _():
        for copy in copies:
            copy.start()

    @pl.when(step < heads)
    def _():
        queries = jnp.concatenate([ref[0] for ref in query_refs], 0)
        spans = key_ref.shape[0] // span
        turn = half_ref[0] * half
        token = lax.rem(lax.broadcasted_iota(jnp.int32, (rows, half), 0) + turn, rows)
        column = lax.broadcasted_iota(jnp.int32, (rows, half), 1)
        parts = []
        for side, ref in enumerate(new_key_refs):
            causal = column + lax.rem(turn + side * half, rows) <= token
            parts.append(jnp.where(causal, dot_keys(queries, ref[...]), -jnp.inf))
        scores = jnp.concatenate(parts, 1)
        peak = jnp.max(scores, axis=1, keepdims=True)
        total = None
        values = jnp.concatenate([ref[...] for ref in new_value_refs], 0)
        for index in range(spans + 1):
            if index < spans:
                next_scores = dot_keys(queries, key_ref[index * span : (index + 1) * span, :])
                next_peak = jnp.maximum(peak, jnp.max(next_scores, axis=1, keepdims=True))
            weights = jnp.exp2((scores - peak) * SCORE_SCALE).astype(jnp.bfloat16)
            product = jnp.dot(weights, values, preferred_element_type=jnp.float32)
            total = product if total is None else total + product
            if index < spans:
                total = total * jnp.exp2((peak - next_peak) * SCORE_SCALE)
                scores, peak = next_scores, next_peak
                values = value_ref[index * span : (index + 1) * span, :]
        mixed_ref[:, pl.ds(pl.multiple_of(step * HD, HD), HD)] = (
            total[:, :HD] / total[:, HD:]
        ).astype(jnp.bfloat16)

    @pl.when(step == heads)
    def _():
        for copy in copies:
            copy.wait()

    tile = out_refs[0].shape[1]
    tiles = held_ref.shape[1] // tile // len(out_refs)
    for chunk, out_ref in enumerate(out_refs):
        begin = heads + chunk * tiles

        @pl.when((step >= begin) & (step < begin + tiles))
        def _(out_ref=out_ref):
            columns = pl.ds(pl.multiple_of((step - heads) * tile, tile), tile)
            out_ref[...] = jnp.dot(
                mixed_ref[...], held_ref[:, columns], preferred_element_type=jnp.float32
            ).astype(jnp.bfloat16)


def attend(half, queries, prefix, new_keys, new_values, weight):
    heads = queries[0].shape[0]
    rows = 2 * new_keys[0].shape[0]
    depth, width = weight.shape
    tile = math.gcd(width // COLUMN_CHUNKS, 1024)
    tiles = width // COLUMN_CHUNKS // tile
    span = math.gcd(prefix[0].shape[0], 1024)
    whole = lambda array: pl.BlockSpec(array.shape, lambda step: (0, 0))
    count = prefix[0].shape[0] + rows
    query_spec = pl.BlockSpec(
        (1, rows // 2, HD), lambda step: (jnp.minimum(step, heads - 1), 0, 0)
    )
    fixed = (*prefix, *new_keys, *new_values)
    return pl.pallas_call(
        functools.partial(attend_kernel, span, heads),
        grid=(heads + width // tile,),
        out_shape=[jax.ShapeDtypeStruct((rows, tiles * tile), jnp.bfloat16)] * COLUMN_CHUNKS,
        in_specs=[pl.BlockSpec(memory_space=pltpu.SMEM), query_spec, query_spec]
        + [whole(array) for array in fixed]
        + [pl.BlockSpec(memory_space=pl.ANY)],
        out_specs=[
            pl.BlockSpec(
                (rows, tile),
                lambda step, begin=heads + chunk * tiles: (0, jnp.clip(step - begin, 0, tiles - 1)),
            )
            for chunk in range(COLUMN_CHUNKS)
        ],
        scratch_shapes=[
            pltpu.VMEM((rows, depth), jnp.bfloat16),
            pltpu.VMEM((depth, width), jnp.bfloat16),
            pltpu.SemaphoreType.DMA((STREAMS,)),
        ],
        compiler_params=pltpu.CompilerParams(vmem_limit_bytes=VMEM_LIMIT),
        cost_estimate=pl.CostEstimate(
            flops=heads * rows * count * HD * 8 + 2 * rows * depth * width,
            bytes_accessed=2 * (count * 3 * HD + 2 * heads * rows * HD + depth * width),
            transcendentals=heads * rows * count,
        ),
        name="attend",
    )(half, *queries, *fixed, weight)


def on_device(
    n_model,
    n_pool,
    states,
    norm_gain,
    w_query,
    q_bias,
    w_key,
    w_value,
    k_bias,
    v_bias,
    w_out,
    kv_pool,
    hit_holder,
    hit_slot,
    prefix_len,
):
    my_model = lax.axis_index("mp")
    my_pool = lax.axis_index("pool")
    row_count = states.shape[1]
    suffix = row_count * n_model
    q_width = w_query.shape[1]
    q_local = q_width // HD
    kv_local = w_key.shape[1]
    kv_heads = kv_local * n_model // HD
    group_size = QH // kv_heads
    blocks_total = hit_holder.shape[1]
    block_len = kv_pool.shape[2]
    holders = n_model * n_pool
    capacity = 2 * blocks_total // holders
    sharers = HD // kv_local

    lined = n_model == LINE_MODELS

    self_holder = my_model * n_pool + my_pool
    chosen = listing(hit_holder == self_holder, capacity)
    slot_ids = jnp.sum(jnp.where(chosen, hit_slot[:, None, :], 0), -1)
    models = jnp.arange(n_model, dtype=jnp.int32)
    my_holder = hit_holder[my_pool]
    prefix_count = prefix_len[my_pool]
    block_ids = jnp.arange(blocks_total, dtype=jnp.int32)
    earlier = (my_holder[:, None] == my_holder[None, :]) & (block_ids[None, :] < block_ids[:, None])
    rank = jnp.sum(earlier.astype(jnp.int32), -1)
    normed = normalize(states[0], norm_gain)
    if lined:
        mine, others = (
            lax.dynamic_index_in_dim(slot_ids, pool, 0, keepdims=False)
            for pool in (my_pool, 1 - my_pool)
        )
        pool_blocks = kv_pool[0]
        got = lax.ppermute(pick_blocks(pool_blocks, others), "pool", [(0, 1), (1, 0)])
        slots = jnp.stack([mine, jnp.arange(capacity, dtype=jnp.int32)])
        outgoing = pack_blocks((pool_blocks, got), slots, (models ^ my_model) * q_local // group_size)
        my_z, my_y = my_model // 2, my_model % 2
        near, far, arrived = gather_and_exchange(normed, outgoing, (my_z == 1) | (my_z == 2))
        arrived = [block.reshape(-1, block_len, 2 * HD) for block in arrived]
        distance = (my_holder // n_pool) ^ my_model
        where = (distance * n_pool + (my_holder % n_pool ^ my_pool)) * capacity + rank
    else:
        outgoing = pack_blocks((kv_pool[0],) * 2, slot_ids, models * q_local // group_size)
        outgoing = jnp.stack(outgoing).reshape(holders, capacity * block_len, 2 * HD)
        arrived = lax.all_to_all(outgoing, ("mp", "pool"), split_axis=0, concat_axis=0, tiled=True)
        arrived = [arrived.reshape(holders * capacity, block_len, 2 * HD)]
        where = my_holder * capacity + rank

    upper_half = (my_model // (n_model // 2)).astype(jnp.int32) if lined else jnp.int32(0)
    half_rows = suffix // 2
    order = (jnp.arange(suffix, dtype=jnp.int32) + upper_half * half_rows) % suffix
    cosine, sine = angle_tables(prefix_count + order)
    cosine, sine = jnp.concatenate([cosine, cosine], 1), jnp.concatenate([-sine, sine], 1)
    halves = [slice(0, half_rows), slice(half_rows, suffix)]
    biases = [bias.reshape(1, -1) for bias in (q_bias, k_bias, v_bias)]
    weights = (w_query, w_key, w_value)
    if lined:
        results = []
        for blocks, inner in ((near, my_z % 2), (far, upper_half)):
            starts = jnp.stack(
                [
                    2 * (inner ^ other) + (my_y ^ side)
                    for side in range(2)
                    for other in range(2)
                ]
            )
            table = [part[halves[len(results)]] for part in (cosine, sine)]
            results.append(
                project(starts.astype(jnp.int32) * row_count, blocks, weights, biases, table)
            )
        queries, new_keys, new_values, pairs = zip(*results)
        pairs = jnp.where(
            upper_half == 0, jnp.concatenate(pairs, 0), jnp.concatenate(pairs[::-1], 0)
        ).reshape(n_model, row_count, 2 * HD)
    else:
        tokens = lax.all_gather(normed, "mp", axis=0, tiled=True)
        linear, key_raw, value_raw = (
            jnp.dot(tokens, weight, preferred_element_type=jnp.float32) + bias.astype(jnp.float32)
            for weight, bias in zip(weights, biases)
        )
        cosine, sine = cosine[:, : HD // 2], sine[:, HD // 2 :]
        queries = rotate(linear.reshape(suffix, q_local, HD), cosine, sine)
        queries = queries.astype(jnp.bfloat16).transpose(1, 0, 2)
        key_raw, value_raw = key_raw.astype(jnp.bfloat16), value_raw.astype(jnp.bfloat16)
        together = [
            [first + other for other in range(sharers)] for first in range(0, n_model, sharers)
        ]
        key_whole, value_whole = (
            lax.all_gather(part, "mp", axis=1, tiled=True, axis_index_groups=together)
            for part in (key_raw, value_raw)
        )
        key_whole = rotate(key_whole.astype(jnp.float32)[:, None, :], cosine, sine)
        key_whole = key_whole.astype(jnp.bfloat16)[:, 0]
        value_ones = jnp.concatenate([value_whole, jnp.ones_like(value_whole)], 1)
        first_col = (my_model % sharers) * kv_local
        key_cols = lax.dynamic_slice_in_dim(key_whole, first_col, kv_local, 1)
        pairs = jnp.stack([key_cols, value_raw], 1).reshape(n_model, row_count, 2 * kv_local)
        queries = [queries[:, part] for part in halves]
        new_keys = [key_whole[part] for part in halves]
        new_values = [value_ones[part] for part in halves]

    pairs = lax.all_to_all(pairs, "mp", split_axis=0, concat_axis=0, tiled=True)
    arrived, new_keys, pairs = lax.optimization_barrier((arrived, list(new_keys), pairs))
    cache_rows = (
        pairs.reshape(kv_heads, sharers, row_count, 2, kv_local)
        .transpose(2, 0, 3, 1, 4)
        .reshape(1, row_count, kv_heads * 2 * HD)
    )
    prefix = order_blocks(arrived, where, prefix_count.reshape(1))
    shares = attend(upper_half.reshape(1), queries, prefix, new_keys, new_values, w_out)

    first = upper_half * (n_model // 2)
    scatters = [
        RingScatter(
            share.reshape(n_model, row_count, -1),
            n_model,
            my_model,
            first,
            1 if chunk % 2 == 0 else -1,
        )
        for chunk, share in enumerate(shares)
    ]
    return (jnp.concatenate([scatter.finish() for scatter in scatters], 1)[None], cache_rows)


def solution(mesh):
    placed = (
        P(("groups", "pool"), "mp", None),
        P(),
        P(None, "mp"),
        P("mp"),
        P(None, "mp"),
        P(None, "mp"),
        P("mp"),
        P("mp"),
        P("mp", None),
        P(("groups", "mp", "pool"), None, None, None),
        P("groups", None),
        P("groups", None),
        P("groups"),
    )
    return jax.shard_map(
        functools.partial(on_device, mesh.shape["mp"], mesh.shape["pool"]),
        mesh=mesh,
        in_specs=placed,
        out_specs=(P(("groups", "pool"), "mp", None), P(("groups", "pool"), "mp", None)),
        check_vma=False,
    )
```

```python
import functools
import math

import jax
import jax.numpy as jnp
from jax import lax
from jax.experimental import pallas as pl
from jax.experimental.pallas import tpu as pltpu
from jax.sharding import PartitionSpec as P

QH = 64
HD = 128
ROPE_BASE = 1000000.0
EPSILON = 1e-06
SCORE_SCALE = HD ** (-0.5) * math.log2(math.e)
VMEM_LIMIT = 56 * 1024 * 1024
ATTEND_VMEM = 28 * 1024 * 1024
COLUMN_CHUNKS = 2
STREAMS = 4
LINE_MODELS = 8


def angle_tables(positions):
    frequency = jnp.power(
        jnp.float32(ROPE_BASE), -2.0 * jnp.arange(HD // 2, dtype=jnp.float32) / HD
    )
    angles = positions.astype(jnp.float32)[:, None] * frequency[None, :]
    return jnp.cos(angles), jnp.sin(angles)


def rotate(vectors, cosine, sine):
    first_half = vectors[..., : HD // 2]
    second = vectors[..., HD // 2 :]
    cosine = cosine[:, None, :]
    sine = sine[:, None, :]
    return jnp.concatenate(
        [first_half * cosine - second * sine, second * cosine + first_half * sine], -1
    )


def normalize(states, gain_vec):
    values = states.astype(jnp.float32)
    inv_rms = lax.rsqrt(jnp.mean(values * values, axis=-1, keepdims=True) + EPSILON)
    return (values * inv_rms * gain_vec.astype(jnp.float32)).astype(jnp.bfloat16)


def listing(owned_mask, capacity):
    rank_order = jnp.cumsum(owned_mask.astype(jnp.int32), -1) - 1
    slot_index = jnp.arange(capacity, dtype=jnp.int32)
    return owned_mask[..., None, :] & (rank_order[..., None, :] == slot_index[:, None])


def swap(block, mask):
    return lax.ppermute(block, "mp", [(index, index ^ mask) for index in range(LINE_MODELS)])


def cross(block):
    pairs = []
    for index in range(LINE_MODELS):
        for core in range(2):
            if 2 <= index < 6:
                pairs.append((index * 2 + core, (index ^ 6) * 2 + core))
            else:
                pairs.append((index * 2 + core, index * 2 + 1 - core))
    return lax.ppermute(block, ("mp", "pool"), pairs)


def gather_and_exchange(own, outgoing, middle):
    arrived = {0: outgoing[0]}

    def after(block, *events):
        return lax.optimization_barrier((block, events))[0]

    def exchange(apart, *events):
        block = after(outgoing[apart], *events) if events else outgoing[apart]
        arrived[apart] = swap(block, apart)

    beside = swap(own, 2)
    over = cross(own)
    own_y = swap(own, 1)
    over_beside = cross(beside)
    over_passed = swap(over, 2)
    beside_y = swap(after(beside, own_y), 1)
    far_first = jnp.where(middle, over, over_passed)
    far_first_y = swap(after(far_first, beside_y), 1)
    over_beside_passed = swap(after(over_beside, outgoing[4]), 2)
    exchange(4, over_beside)
    exchange(6, over_beside)
    far_second = jnp.where(middle, over_beside, over_beside_passed)
    far_second_y = swap(after(far_second, far_first_y), 1)
    exchange(5, far_first_y, far_second)
    exchange(2, far_first_y, far_second)
    exchange(7, arrived[4], far_first_y)
    exchange(3, arrived[4], far_first_y)
    exchange(1, arrived[4], far_first_y)
    near = [after(own, far_second, arrived[4], arrived[6]), beside, own_y, beside_y]
    far = [far_first, far_second, far_first_y, far_second_y]
    return near, far, [arrived[apart] for apart in range(LINE_MODELS)]


def project_kernel(starts_ref, *refs):
    n_blocks = starts_ref.shape[0]
    blocks, refs = refs[:n_blocks], refs[n_blocks:]
    q_weights, (k_weight_ref, v_weight_ref), refs = refs[:STREAMS], refs[STREAMS:][:2], refs[STREAMS + 2 :]
    q_bias_ref, k_bias_ref, v_bias_ref, cos_ref, sin_ref = refs[:5]
    query_ref, key_ref, value_ref, pair_ref, tokens_ref, total_ref, sems = refs[5:]
    step = pl.program_id(0)
    depth = k_weight_ref.shape[0]
    q_width = q_weights[0].shape[1]
    rows = blocks[0].shape[0]

    @pl.when(step == 0)
    def _():
        copies = [
            pltpu.make_async_copy(
                block,
                tokens_ref.at[pl.ds(pl.multiple_of(starts_ref[index], rows), rows), :],
                sems.at[index],
            )
            for index, block in enumerate(blocks)
        ]
        for copy in copies:
            copy.start()
        total_ref[...] = jnp.zeros_like(total_ref)
        for copy in copies:
            copy.wait()

    tokens = tokens_ref[:, pl.ds(pl.multiple_of(step * depth, depth), depth)]
    q_weight = jnp.concatenate([ref[...] for ref in q_weights], axis=0)
    total_ref[:, :q_width] += jnp.dot(tokens, q_weight, preferred_element_type=jnp.float32)
    both = jnp.concatenate([k_weight_ref[...], v_weight_ref[...]], axis=1)
    total_ref[:, q_width:] += jnp.dot(tokens, both, preferred_element_type=jnp.float32)

    @pl.when(step == pl.num_programs(0) - 1)
    def _():
        cosine, sine = cos_ref[...], sin_ref[...]

        def turned(vectors):
            return vectors * cosine + pltpu.roll(vectors, HD // 2, 1) * sine

        for head in range(q_width // HD):
            cols = slice(head * HD, (head + 1) * HD)
            query = total_ref[:, cols] + q_bias_ref[:, cols].astype(jnp.float32)
            query_ref[head] = turned(query).astype(jnp.bfloat16)
        key = total_ref[:, q_width : q_width + HD] + k_bias_ref[...].astype(jnp.float32)
        key = turned(key.astype(jnp.bfloat16).astype(jnp.float32)).astype(jnp.bfloat16)
        value = total_ref[:, q_width + HD :] + v_bias_ref[...].astype(jnp.float32)
        value = value.astype(jnp.bfloat16)
        key_ref[...] = key
        value_ref[:, :HD] = value
        value_ref[:, HD:] = jnp.ones_like(value)
        pair_ref[:, :HD] = key
        pair_ref[:, HD:] = value


def project(starts, blocks, weights, biases, tables):
    width = blocks[0].shape[1]
    rows = sum(block.shape[0] for block in blocks)
    depth = math.gcd(width, 1024)
    q_width = weights[0].shape[1]
    out_width = q_width + 2 * HD
    fixed = lambda array: pl.BlockSpec(array.shape, lambda step: (0,) * len(array.shape))
    in_specs = [pl.BlockSpec(memory_space=pltpu.SMEM)]
    in_specs += [pl.BlockSpec(memory_space=pl.ANY)] * len(blocks)
    in_specs += [
        pl.BlockSpec((depth // STREAMS, q_width), lambda step, part=part: (step * STREAMS + part, 0))
        for part in range(STREAMS)
    ]
    in_specs += [pl.BlockSpec((depth, HD), lambda step: (step, 0))] * 2
    in_specs += [fixed(array) for array in (*biases, *tables)]
    out_shape = (
        jax.ShapeDtypeStruct((q_width // HD, rows, HD), jnp.bfloat16),
        jax.ShapeDtypeStruct((rows, HD), jnp.bfloat16),
        jax.ShapeDtypeStruct((rows, 2 * HD), jnp.bfloat16),
        jax.ShapeDtypeStruct((rows, 2 * HD), jnp.bfloat16),
    )
    return pl.pallas_call(
        project_kernel,
        grid=(width // depth,),
        out_shape=out_shape,
        in_specs=in_specs,
        out_specs=tuple(fixed(shape) for shape in out_shape),
        scratch_shapes=[
            pltpu.VMEM((rows, width), jnp.bfloat16),
            pltpu.VMEM((rows, out_width), jnp.float32),
            pltpu.SemaphoreType.DMA((len(blocks),)),
        ],
        compiler_params=pltpu.CompilerParams(vmem_limit_bytes=VMEM_LIMIT),
        cost_estimate=pl.CostEstimate(
            flops=2 * rows * width * out_width,
            bytes_accessed=2 * width * (rows + out_width) + 4 * rows * out_width,
            transcendentals=0,
        ),
        name="project",
    )(starts, *blocks, *weights[:1] * STREAMS, *weights[1:], *biases, *tables)


class RingScatter:
    def __init__(self, shares, n_model, my_model, first, way):
        order = [m for m in range(0, n_model, 2)] + [m for m in range(n_model - 1, 0, -2)]
        self.order = order
        self.n_model = n_model
        self.way = way
        spot = jnp.array([order.index(m) for m in range(n_model)], jnp.int32)[my_model]
        self.shares, self.spot, self.first = shares, spot, first
        self.distance = {way: n_model // 2, -way: n_model // 2 - 1}
        self.moving = {}

    def share_of(self, offset):
        table = jnp.array(self.order, jnp.int32)
        owner = table[(self.spot + offset + self.n_model) % self.n_model]
        owner = (owner - self.first + self.n_model) % self.n_model
        return lax.dynamic_index_in_dim(self.shares, owner, 0, keepdims=False)

    def advance(self):
        started = []
        for way in (self.way, -self.way):
            if not self.distance[way]:
                continue
            block = self.share_of(way * self.distance[way])
            if way in self.moving:
                arrived = self.moving[way].astype(jnp.float32)
                block = (block.astype(jnp.float32) + arrived).astype(jnp.bfloat16)
            started.append(way)
            self.moving[way] = block
            self.distance[way] -= 1
        return started

    def send(self, started):
        for way in started:
            pairs = [
                (self.order[i], self.order[(i + way) % self.n_model]) for i in range(self.n_model)
            ]
            self.moving[way] = lax.ppermute(self.moving[way], "mp", pairs)

    def finish(self):
        while any(self.distance.values()):
            self.send(self.advance())
        total = self.share_of(0).astype(jnp.float32)
        for way in (1, -1):
            total = total + self.moving[way].astype(jnp.float32)
        return total.astype(jnp.bfloat16)


def pick_kernel(slots_ref, pool_ref, out_ref):
    def place(rank, _):
        out_ref[rank] = pool_ref[slots_ref[rank]]
        return 0

    lax.fori_loop(0, slots_ref.shape[0], place, 0)


def pick_blocks(pool, slots):
    return pl.pallas_call(
        pick_kernel,
        out_shape=jax.ShapeDtypeStruct((*slots.shape, *pool.shape[1:]), pool.dtype),
        in_specs=[
            pl.BlockSpec(memory_space=pltpu.SMEM),
            pl.BlockSpec(memory_space=pltpu.VMEM),
        ],
        out_specs=pl.BlockSpec(memory_space=pltpu.VMEM),
        compiler_params=pltpu.CompilerParams(vmem_limit_bytes=ATTEND_VMEM),
        name="pick_blocks",
    )(slots, pool)


def pack_kernel(lists, slots_ref, heads_ref, *refs):
    sources, out_refs = refs[: len(lists)], refs[len(lists) :]

    def place(rank, _):
        for listed, source_ref in zip(lists, sources):
            slot = slots_ref[listed, rank]
            for dest, out_ref in enumerate(out_refs):
                first = pl.multiple_of(heads_ref[dest] * 2 * HD, 2 * HD)
                out_ref[listed, rank] = source_ref[slot, :, pl.ds(first, 2 * HD)]
        return 0

    lax.fori_loop(0, slots_ref.shape[1], place, 0)


def pack_blocks(sources, slots, heads):
    dests = heads.shape[0]
    block_len = sources[0].shape[1]
    shape = jax.ShapeDtypeStruct((*slots.shape, block_len, 2 * HD), jnp.bfloat16)
    return pl.pallas_call(
        functools.partial(pack_kernel, range(len(sources))),
        out_shape=[shape] * dests,
        in_specs=[pl.BlockSpec(memory_space=pltpu.SMEM)] * 2
        + [pl.BlockSpec(memory_space=pltpu.VMEM)] * len(sources),
        out_specs=[pl.BlockSpec(memory_space=pltpu.VMEM)] * dests,
        compiler_params=pltpu.CompilerParams(vmem_limit_bytes=ATTEND_VMEM),
        name="pack_blocks",
    )(slots, heads, *sources)


def order_kernel(length_ref, where_ref, *refs):
    *arrived_refs, key_ref, value_ref, held_ref, sems = refs
    block_len = held_ref.shape[1]
    copies = []
    begin = 0
    for index, source in enumerate(arrived_refs):
        end = begin + source.shape[0]
        copies.append(pltpu.make_async_copy(source, held_ref.at[begin:end], sems.at[index]))
        begin = end
    for copy in copies:
        copy.start()
    for copy in copies:
        copy.wait()
    length = length_ref[0]
    first = held_ref[where_ref[0]][:1, :HD].astype(jnp.float32)
    row = lax.broadcasted_iota(jnp.int32, (block_len, HD), 0)

    def place(block_id, _):
        block = held_ref[where_ref[block_id]].astype(jnp.float32)
        start = pl.multiple_of(block_id * block_len, block_len)
        seen = row + start < length
        rows = pl.ds(start, block_len)
        key_ref[rows, :] = jnp.where(seen, block[:, :HD], first).astype(jnp.bfloat16)
        value_ref[rows, :HD] = jnp.where(seen, block[:, HD:], 0.0).astype(jnp.bfloat16)
        value_ref[rows, HD:] = jnp.where(seen, 1.0, 0.0).astype(jnp.bfloat16)
        return 0

    lax.fori_loop(0, where_ref.shape[0], place, 0, unroll=8)


def order_blocks(arrived, where, length):
    count = sum(array.shape[-3] for array in arrived)
    block_len = arrived[0].shape[-2]
    tokens = where.shape[0] * block_len
    return pl.pallas_call(
        order_kernel,
        out_shape=(
            jax.ShapeDtypeStruct((tokens, HD), jnp.bfloat16),
            jax.ShapeDtypeStruct((tokens, 2 * HD), jnp.bfloat16),
        ),
        in_specs=[pl.BlockSpec(memory_space=pltpu.SMEM)] * 2
        + [pl.BlockSpec(memory_space=pl.ANY)] * len(arrived),
        out_specs=(
            pl.BlockSpec(memory_space=pltpu.VMEM),
            pl.BlockSpec(memory_space=pltpu.VMEM),
        ),
        scratch_shapes=[
            pltpu.VMEM((count, block_len, 2 * HD), jnp.bfloat16),
            pltpu.SemaphoreType.DMA((len(arrived),)),
        ],
        compiler_params=pltpu.CompilerParams(vmem_limit_bytes=ATTEND_VMEM),
        name="order_blocks",
    )(length, where, *arrived)


def dot_keys(queries, keys):
    return lax.dot_general(
        queries, keys, (((1,), (1,)), ((), ())), preferred_element_type=jnp.float32
    )


def attend_kernel(span, half_ref, *refs):
    query_refs, (key_ref, value_ref), new_key_refs, new_value_refs, out_ref = (
        refs[:2],
        refs[2:4],
        refs[4:6],
        refs[6:8],
        refs[8],
    )
    rows = out_ref.shape[0]
    half = rows // 2
    queries = jnp.concatenate([ref[0] for ref in query_refs], 0)
    spans = key_ref.shape[0] // span
    turn = half_ref[0] * half
    token = lax.rem(lax.broadcasted_iota(jnp.int32, (rows, half), 0) + turn, rows)
    column = lax.broadcasted_iota(jnp.int32, (rows, half), 1)
    parts = []
    for side, ref in enumerate(new_key_refs):
        causal = column + lax.rem(turn + side * half, rows) <= token
        parts.append(jnp.where(causal, dot_keys(queries, ref[...]), -jnp.inf))
    scores = jnp.concatenate(parts, 1)
    peak = jnp.max(scores, axis=1, keepdims=True)
    total = None
    values = jnp.concatenate([ref[...] for ref in new_value_refs], 0)
    for index in range(spans + 1):
        if index < spans:
            next_scores = dot_keys(queries, key_ref[index * span : (index + 1) * span, :])
            next_peak = jnp.maximum(peak, jnp.max(next_scores, axis=1, keepdims=True))
        weights = jnp.exp2((scores - peak) * SCORE_SCALE).astype(jnp.bfloat16)
        product = jnp.dot(weights, values, preferred_element_type=jnp.float32)
        total = product if total is None else total + product
        if index < spans:
            total = total * jnp.exp2((peak - next_peak) * SCORE_SCALE)
            scores, peak = next_scores, next_peak
            values = value_ref[index * span : (index + 1) * span, :]
    out_ref[...] = (total[:, :HD] / total[:, HD:]).astype(jnp.bfloat16)


def attend(half, queries, prefix, new_keys, new_values):
    heads = queries[0].shape[0]
    rows = 2 * new_keys[0].shape[0]
    span = math.gcd(prefix[0].shape[0], 1024)
    whole = lambda array: pl.BlockSpec(array.shape, lambda step: (0, 0))
    count = prefix[0].shape[0] + rows
    query_spec = pl.BlockSpec((1, rows // 2, HD), lambda step: (step, 0, 0))
    fixed = (*prefix, *new_keys, *new_values)
    return pl.pallas_call(
        functools.partial(attend_kernel, span),
        grid=(heads,),
        out_shape=jax.ShapeDtypeStruct((rows, heads * HD), jnp.bfloat16),
        in_specs=[pl.BlockSpec(memory_space=pltpu.SMEM), query_spec, query_spec]
        + [whole(array) for array in fixed],
        out_specs=pl.BlockSpec((rows, HD), lambda step: (0, step)),
        compiler_params=pltpu.CompilerParams(vmem_limit_bytes=ATTEND_VMEM),
        cost_estimate=pl.CostEstimate(
            flops=heads * rows * count * HD * 8,
            bytes_accessed=2 * (count * 3 * HD + 2 * heads * rows * HD),
            transcendentals=heads * rows * count,
        ),
        name="attend",
    )(half, *queries, *fixed)


def on_device(
    n_model,
    n_pool,
    states,
    norm_gain,
    w_query,
    q_bias,
    w_key,
    w_value,
    k_bias,
    v_bias,
    w_out,
    kv_pool,
    hit_holder,
    hit_slot,
    prefix_len,
):
    my_model = lax.axis_index("mp")
    my_pool = lax.axis_index("pool")
    row_count = states.shape[1]
    suffix = row_count * n_model
    q_width = w_query.shape[1]
    q_local = q_width // HD
    kv_local = w_key.shape[1]
    kv_heads = kv_local * n_model // HD
    group_size = QH // kv_heads
    blocks_total = hit_holder.shape[1]
    block_len = kv_pool.shape[2]
    holders = n_model * n_pool
    capacity = 2 * blocks_total // holders
    sharers = HD // kv_local

    lined = n_model == LINE_MODELS

    self_holder = my_model * n_pool + my_pool
    chosen = listing(hit_holder == self_holder, capacity)
    slot_ids = jnp.sum(jnp.where(chosen, hit_slot[:, None, :], 0), -1)
    models = jnp.arange(n_model, dtype=jnp.int32)
    my_holder = hit_holder[my_pool]
    prefix_count = prefix_len[my_pool]
    block_ids = jnp.arange(blocks_total, dtype=jnp.int32)
    earlier = (my_holder[:, None] == my_holder[None, :]) & (block_ids[None, :] < block_ids[:, None])
    rank = jnp.sum(earlier.astype(jnp.int32), -1)
    normed = normalize(states[0], norm_gain)
    if lined:
        mine, others = (
            lax.dynamic_index_in_dim(slot_ids, pool, 0, keepdims=False)
            for pool in (my_pool, 1 - my_pool)
        )
        pool_blocks = kv_pool[0]
        got = lax.ppermute(pick_blocks(pool_blocks, others), "pool", [(0, 1), (1, 0)])
        slots = jnp.stack([mine, jnp.arange(capacity, dtype=jnp.int32)])
        outgoing = pack_blocks((pool_blocks, got), slots, (models ^ my_model) * q_local // group_size)
        my_z, my_y = my_model // 2, my_model % 2
        near, far, arrived = gather_and_exchange(normed, outgoing, (my_z == 1) | (my_z == 2))
        arrived = [block.reshape(-1, block_len, 2 * HD) for block in arrived]
        distance = (my_holder // n_pool) ^ my_model
        where = (distance * n_pool + (my_holder % n_pool ^ my_pool)) * capacity + rank
    else:
        outgoing = pack_blocks((kv_pool[0],) * 2, slot_ids, models * q_local // group_size)
        outgoing = jnp.stack(outgoing).reshape(holders, capacity * block_len, 2 * HD)
        arrived = lax.all_to_all(outgoing, ("mp", "pool"), split_axis=0, concat_axis=0, tiled=True)
        arrived = [arrived.reshape(holders * capacity, block_len, 2 * HD)]
        where = my_holder * capacity + rank

    upper_half = (my_model // (n_model // 2)).astype(jnp.int32) if lined else jnp.int32(0)
    half_rows = suffix // 2
    order = (jnp.arange(suffix, dtype=jnp.int32) + upper_half * half_rows) % suffix
    cosine, sine = angle_tables(prefix_count + order)
    cosine, sine = jnp.concatenate([cosine, cosine], 1), jnp.concatenate([-sine, sine], 1)
    halves = [slice(0, half_rows), slice(half_rows, suffix)]
    biases = [bias.reshape(1, -1) for bias in (q_bias, k_bias, v_bias)]
    weights = (w_query, w_key, w_value)
    if lined:
        results = []
        for blocks, inner in ((near, my_z % 2), (far, upper_half)):
            starts = jnp.stack(
                [
                    2 * (inner ^ other) + (my_y ^ side)
                    for side in range(2)
                    for other in range(2)
                ]
            )
            table = [part[halves[len(results)]] for part in (cosine, sine)]
            results.append(
                project(starts.astype(jnp.int32) * row_count, blocks, weights, biases, table)
            )
        queries, new_keys, new_values, pairs = zip(*results)
        pairs = jnp.where(
            upper_half == 0, jnp.concatenate(pairs, 0), jnp.concatenate(pairs[::-1], 0)
        ).reshape(n_model, row_count, 2 * HD)
    else:
        tokens = lax.all_gather(normed, "mp", axis=0, tiled=True)
        linear, key_raw, value_raw = (
            jnp.dot(tokens, weight, preferred_element_type=jnp.float32) + bias.astype(jnp.float32)
            for weight, bias in zip(weights, biases)
        )
        cosine, sine = cosine[:, : HD // 2], sine[:, HD // 2 :]
        queries = rotate(linear.reshape(suffix, q_local, HD), cosine, sine)
        queries = queries.astype(jnp.bfloat16).transpose(1, 0, 2)
        key_raw, value_raw = key_raw.astype(jnp.bfloat16), value_raw.astype(jnp.bfloat16)
        together = [
            [first + other for other in range(sharers)] for first in range(0, n_model, sharers)
        ]
        key_whole, value_whole = (
            lax.all_gather(part, "mp", axis=1, tiled=True, axis_index_groups=together)
            for part in (key_raw, value_raw)
        )
        key_whole = rotate(key_whole.astype(jnp.float32)[:, None, :], cosine, sine)
        key_whole = key_whole.astype(jnp.bfloat16)[:, 0]
        value_ones = jnp.concatenate([value_whole, jnp.ones_like(value_whole)], 1)
        first_col = (my_model % sharers) * kv_local
        key_cols = lax.dynamic_slice_in_dim(key_whole, first_col, kv_local, 1)
        pairs = jnp.stack([key_cols, value_raw], 1).reshape(n_model, row_count, 2 * kv_local)
        queries = [queries[:, part] for part in halves]
        new_keys = [key_whole[part] for part in halves]
        new_values = [value_ones[part] for part in halves]

    pairs = lax.all_to_all(pairs, "mp", split_axis=0, concat_axis=0, tiled=True)
    arrived, new_keys, pairs = lax.optimization_barrier((arrived, list(new_keys), pairs))
    cache_rows = (
        pairs.reshape(kv_heads, sharers, row_count, 2, kv_local)
        .transpose(2, 0, 3, 1, 4)
        .reshape(1, row_count, kv_heads * 2 * HD)
    )
    prefix = order_blocks(arrived, where, prefix_count.reshape(1))
    mixed = attend(upper_half.reshape(1), queries, prefix, new_keys, new_values)
    width = w_out.shape[1] // COLUMN_CHUNKS
    shares = [
        jnp.dot(
            mixed,
            w_out[:, chunk * width : (chunk + 1) * width],
            preferred_element_type=jnp.float32,
        ).astype(jnp.bfloat16)
        for chunk in range(COLUMN_CHUNKS)
    ]

    first = upper_half * (n_model // 2)
    scatters = [
        RingScatter(
            share.reshape(n_model, row_count, -1),
            n_model,
            my_model,
            first,
            1 if chunk % 2 == 0 else -1,
        )
        for chunk, share in enumerate(shares)
    ]
    return (jnp.concatenate([scatter.finish() for scatter in scatters], 1)[None], cache_rows)


def solution(mesh):
    placed = (
        P(("groups", "pool"), "mp", None),
        P(),
        P(None, "mp"),
        P("mp"),
        P(None, "mp"),
        P(None, "mp"),
        P("mp"),
        P("mp"),
        P("mp", None),
        P(("groups", "mp", "pool"), None, None, None),
        P("groups", None),
        P("groups", None),
        P("groups"),
    )
    return jax.shard_map(
        functools.partial(on_device, mesh.shape["mp"], mesh.shape["pool"]),
        mesh=mesh,
        in_specs=placed,
        out_specs=(P(("groups", "pool"), "mp", None), P(("groups", "pool"), "mp", None)),
        check_vma=False,
    )
```

```python
import functools
import math

import jax
import jax.numpy as jnp
from jax import lax
from jax.experimental import pallas as pl
from jax.experimental.pallas import tpu as pltpu
from jax.sharding import PartitionSpec as P

QH = 64
HD = 128
ROPE_BASE = 1000000.0
EPSILON = 1e-06
SCORE_SCALE = HD ** (-0.5) * math.log2(math.e)
VMEM_LIMIT = 56 * 1024 * 1024
ATTEND_VMEM = 28 * 1024 * 1024
COLUMN_CHUNKS = 2
STREAMS = 4
LINE_MODELS = 8


def angle_tables(positions):
    frequency = jnp.power(
        jnp.float32(ROPE_BASE), -2.0 * jnp.arange(HD // 2, dtype=jnp.float32) / HD
    )
    angles = positions.astype(jnp.float32)[:, None] * frequency[None, :]
    return jnp.cos(angles), jnp.sin(angles)


def rotate(vectors, cosine, sine):
    first_half = vectors[..., : HD // 2]
    second = vectors[..., HD // 2 :]
    cosine = cosine[:, None, :]
    sine = sine[:, None, :]
    return jnp.concatenate(
        [first_half * cosine - second * sine, second * cosine + first_half * sine], -1
    )


def normalize(states, gain_vec):
    values = states.astype(jnp.float32)
    inv_rms = lax.rsqrt(jnp.mean(values * values, axis=-1, keepdims=True) + EPSILON)
    return (values * inv_rms * gain_vec.astype(jnp.float32)).astype(jnp.bfloat16)


def listing(owned_mask, capacity):
    rank_order = jnp.cumsum(owned_mask.astype(jnp.int32), -1) - 1
    slot_index = jnp.arange(capacity, dtype=jnp.int32)
    return owned_mask[..., None, :] & (rank_order[..., None, :] == slot_index[:, None])


def swap(block, mask):
    return lax.ppermute(block, "mp", [(index, index ^ mask) for index in range(LINE_MODELS)])


def cross(block):
    pairs = []
    for index in range(LINE_MODELS):
        for core in range(2):
            if 2 <= index < 6:
                pairs.append((index * 2 + core, (index ^ 6) * 2 + core))
            else:
                pairs.append((index * 2 + core, index * 2 + 1 - core))
    return lax.ppermute(block, ("mp", "pool"), pairs)


def gather_and_exchange(own, outgoing, middle):
    arrived = {0: outgoing[0]}

    def after(block, *events):
        return lax.optimization_barrier((block, events))[0]

    def exchange(apart, *events):
        block = after(outgoing[apart], *events) if events else outgoing[apart]
        arrived[apart] = swap(block, apart)

    beside = swap(own, 2)
    over = cross(own)
    own_y = swap(own, 1)
    over_beside = cross(beside)
    over_passed = swap(over, 2)
    beside_y = swap(after(beside, own_y), 1)
    far_first = jnp.where(middle, over, over_passed)
    far_first_y = swap(after(far_first, beside_y), 1)
    over_beside_passed = swap(after(over_beside, outgoing[4]), 2)
    exchange(4, over_beside)
    exchange(6, over_beside)
    far_second = jnp.where(middle, over_beside, over_beside_passed)
    far_second_y = swap(after(far_second, far_first_y), 1)
    exchange(5, far_first_y, far_second)
    exchange(2, far_first_y, far_second)
    exchange(7, arrived[4], far_first_y)
    exchange(3, arrived[4], far_first_y)
    exchange(1, arrived[4], far_first_y)
    near = [after(own, far_second, arrived[4], arrived[6]), beside, own_y, beside_y]
    far = [far_first, far_second, far_first_y, far_second_y]
    return near, far, [arrived[apart] for apart in range(LINE_MODELS)]


def project_kernel(starts_ref, *refs):
    n_blocks = starts_ref.shape[0]
    blocks, refs = refs[:n_blocks], refs[n_blocks:]
    q_weights, (k_weight_ref, v_weight_ref), refs = refs[:STREAMS], refs[STREAMS:][:2], refs[STREAMS + 2 :]
    q_bias_ref, k_bias_ref, v_bias_ref, cos_ref, sin_ref = refs[:5]
    query_ref, key_ref, value_ref, pair_ref, tokens_ref, total_ref, sems = refs[5:]
    step = pl.program_id(0)
    depth = k_weight_ref.shape[0]
    q_width = q_weights[0].shape[1]
    rows = blocks[0].shape[0]

    @pl.when(step == 0)
    def _():
        copies = [
            pltpu.make_async_copy(
                block,
                tokens_ref.at[pl.ds(pl.multiple_of(starts_ref[index], rows), rows), :],
                sems.at[index],
            )
            for index, block in enumerate(blocks)
        ]
        for copy in copies:
            copy.start()
        total_ref[...] = jnp.zeros_like(total_ref)
        for copy in copies:
            copy.wait()

    tokens = tokens_ref[:, pl.ds(pl.multiple_of(step * depth, depth), depth)]
    q_weight = jnp.concatenate([ref[...] for ref in q_weights], axis=0)
    total_ref[:, :q_width] += jnp.dot(tokens, q_weight, preferred_element_type=jnp.float32)
    both = jnp.concatenate([k_weight_ref[...], v_weight_ref[...]], axis=1)
    total_ref[:, q_width:] += jnp.dot(tokens, both, preferred_element_type=jnp.float32)

    @pl.when(step == pl.num_programs(0) - 1)
    def _():
        cosine, sine = cos_ref[...], sin_ref[...]

        def turned(vectors):
            return vectors * cosine + pltpu.roll(vectors, HD // 2, 1) * sine

        for head in range(q_width // HD):
            cols = slice(head * HD, (head + 1) * HD)
            query = total_ref[:, cols] + q_bias_ref[:, cols].astype(jnp.float32)
            query_ref[head] = turned(query).astype(jnp.bfloat16)
        key = total_ref[:, q_width : q_width + HD] + k_bias_ref[...].astype(jnp.float32)
        key = turned(key.astype(jnp.bfloat16).astype(jnp.float32)).astype(jnp.bfloat16)
        value = total_ref[:, q_width + HD :] + v_bias_ref[...].astype(jnp.float32)
        value = value.astype(jnp.bfloat16)
        key_ref[...] = key
        value_ref[:, :HD] = value
        value_ref[:, HD:] = jnp.ones_like(value)
        pair_ref[:, :HD] = key
        pair_ref[:, HD:] = value


def project(starts, blocks, weights, biases, tables):
    width = blocks[0].shape[1]
    rows = sum(block.shape[0] for block in blocks)
    depth = math.gcd(width, 1024)
    q_width = weights[0].shape[1]
    out_width = q_width + 2 * HD
    fixed = lambda array: pl.BlockSpec(array.shape, lambda step: (0,) * len(array.shape))
    in_specs = [pl.BlockSpec(memory_space=pltpu.SMEM)]
    in_specs += [pl.BlockSpec(memory_space=pl.ANY)] * len(blocks)
    in_specs += [
        pl.BlockSpec((depth // STREAMS, q_width), lambda step, part=part: (step * STREAMS + part, 0))
        for part in range(STREAMS)
    ]
    in_specs += [pl.BlockSpec((depth, HD), lambda step: (step, 0))] * 2
    in_specs += [fixed(array) for array in (*biases, *tables)]
    out_shape = (
        jax.ShapeDtypeStruct((q_width // HD, rows, HD), jnp.bfloat16),
        jax.ShapeDtypeStruct((rows, HD), jnp.bfloat16),
        jax.ShapeDtypeStruct((rows, 2 * HD), jnp.bfloat16),
        jax.ShapeDtypeStruct((rows, 2 * HD), jnp.bfloat16),
    )
    return pl.pallas_call(
        project_kernel,
        grid=(width // depth,),
        out_shape=out_shape,
        in_specs=in_specs,
        out_specs=tuple(fixed(shape) for shape in out_shape),
        scratch_shapes=[
            pltpu.VMEM((rows, width), jnp.bfloat16),
            pltpu.VMEM((rows, out_width), jnp.float32),
            pltpu.SemaphoreType.DMA((len(blocks),)),
        ],
        compiler_params=pltpu.CompilerParams(vmem_limit_bytes=VMEM_LIMIT),
        cost_estimate=pl.CostEstimate(
            flops=2 * rows * width * out_width,
            bytes_accessed=2 * width * (rows + out_width) + 4 * rows * out_width,
            transcendentals=0,
        ),
        name="project",
    )(starts, *blocks, *weights[:1] * STREAMS, *weights[1:], *biases, *tables)


class RingScatter:
    def __init__(self, shares, n_model, my_model, first, way):
        order = [m for m in range(0, n_model, 2)] + [m for m in range(n_model - 1, 0, -2)]
        self.order = order
        self.n_model = n_model
        self.way = way
        spot = jnp.array([order.index(m) for m in range(n_model)], jnp.int32)[my_model]
        self.shares, self.spot, self.first = shares, spot, first
        self.distance = {way: n_model // 2, -way: n_model // 2 - 1}
        self.moving = {}

    def share_of(self, offset):
        table = jnp.array(self.order, jnp.int32)
        owner = table[(self.spot + offset + self.n_model) % self.n_model]
        owner = (owner - self.first + self.n_model) % self.n_model
        return lax.dynamic_index_in_dim(self.shares, owner, 0, keepdims=False)

    def step(self, *before):
        ways = [way for way in (self.way, -self.way) if self.distance[way]]
        blocks = []
        for way in ways:
            block = self.share_of(way * self.distance[way])
            if way in self.moving:
                arrived = self.moving[way].astype(jnp.float32)
                block = (block.astype(jnp.float32) + arrived).astype(jnp.bfloat16)
            blocks.append(block)
            self.distance[way] -= 1
        blocks, _ = lax.optimization_barrier((blocks, (before, list(self.moving.values()))))
        for way, block in zip(ways, blocks):
            pairs = [
                (self.order[i], self.order[(i + way) % self.n_model]) for i in range(self.n_model)
            ]
            self.moving[way] = lax.ppermute(block, "mp", pairs)
        return blocks

    def finish(self):
        total = self.share_of(0).astype(jnp.float32)
        for way in (1, -1):
            total = total + self.moving[way].astype(jnp.float32)
        return total.astype(jnp.bfloat16)


def pick_kernel(slots_ref, pool_ref, out_ref):
    def place(rank, _):
        out_ref[rank] = pool_ref[slots_ref[rank]]
        return 0

    lax.fori_loop(0, slots_ref.shape[0], place, 0)


def pick_blocks(pool, slots):
    return pl.pallas_call(
        pick_kernel,
        out_shape=jax.ShapeDtypeStruct((*slots.shape, *pool.shape[1:]), pool.dtype),
        in_specs=[
            pl.BlockSpec(memory_space=pltpu.SMEM),
            pl.BlockSpec(memory_space=pltpu.VMEM),
        ],
        out_specs=pl.BlockSpec(memory_space=pltpu.VMEM),
        compiler_params=pltpu.CompilerParams(vmem_limit_bytes=ATTEND_VMEM),
        name="pick_blocks",
    )(slots, pool)


def pack_kernel(lists, slots_ref, heads_ref, *refs):
    sources, out_refs = refs[: len(lists)], refs[len(lists) :]

    def place(rank, _):
        for listed, source_ref in zip(lists, sources):
            slot = slots_ref[listed, rank]
            for dest, out_ref in enumerate(out_refs):
                first = pl.multiple_of(heads_ref[dest] * 2 * HD, 2 * HD)
                out_ref[listed, rank] = source_ref[slot, :, pl.ds(first, 2 * HD)]
        return 0

    lax.fori_loop(0, slots_ref.shape[1], place, 0)


def pack_blocks(sources, slots, heads):
    dests = heads.shape[0]
    block_len = sources[0].shape[1]
    shape = jax.ShapeDtypeStruct((*slots.shape, block_len, 2 * HD), jnp.bfloat16)
    return pl.pallas_call(
        functools.partial(pack_kernel, range(len(sources))),
        out_shape=[shape] * dests,
        in_specs=[pl.BlockSpec(memory_space=pltpu.SMEM)] * 2
        + [pl.BlockSpec(memory_space=pltpu.VMEM)] * len(sources),
        out_specs=[pl.BlockSpec(memory_space=pltpu.VMEM)] * dests,
        compiler_params=pltpu.CompilerParams(vmem_limit_bytes=ATTEND_VMEM),
        name="pack_blocks",
    )(slots, heads, *sources)


def order_kernel(length_ref, where_ref, *refs):
    *arrived_refs, key_ref, value_ref, held_ref, sems = refs
    block_len = held_ref.shape[1]
    copies = []
    begin = 0
    for index, source in enumerate(arrived_refs):
        end = begin + source.shape[0]
        copies.append(pltpu.make_async_copy(source, held_ref.at[begin:end], sems.at[index]))
        begin = end
    for copy in copies:
        copy.start()
    for copy in copies:
        copy.wait()
    length = length_ref[0]
    first = held_ref[where_ref[0]][:1, :HD].astype(jnp.float32)
    row = lax.broadcasted_iota(jnp.int32, (block_len, HD), 0)

    def place(block_id, _):
        block = held_ref[where_ref[block_id]].astype(jnp.float32)
        start = pl.multiple_of(block_id * block_len, block_len)
        seen = row + start < length
        rows = pl.ds(start, block_len)
        key_ref[rows, :] = jnp.where(seen, block[:, :HD], first).astype(jnp.bfloat16)
        value_ref[rows, :HD] = jnp.where(seen, block[:, HD:], 0.0).astype(jnp.bfloat16)
        value_ref[rows, HD:] = jnp.where(seen, 1.0, 0.0).astype(jnp.bfloat16)
        return 0

    lax.fori_loop(0, where_ref.shape[0], place, 0, unroll=8)


def order_blocks(arrived, where, length):
    count = sum(array.shape[-3] for array in arrived)
    block_len = arrived[0].shape[-2]
    tokens = where.shape[0] * block_len
    return pl.pallas_call(
        order_kernel,
        out_shape=(
            jax.ShapeDtypeStruct((tokens, HD), jnp.bfloat16),
            jax.ShapeDtypeStruct((tokens, 2 * HD), jnp.bfloat16),
        ),
        in_specs=[pl.BlockSpec(memory_space=pltpu.SMEM)] * 2
        + [pl.BlockSpec(memory_space=pl.ANY)] * len(arrived),
        out_specs=(
            pl.BlockSpec(memory_space=pltpu.VMEM),
            pl.BlockSpec(memory_space=pltpu.VMEM),
        ),
        scratch_shapes=[
            pltpu.VMEM((count, block_len, 2 * HD), jnp.bfloat16),
            pltpu.SemaphoreType.DMA((len(arrived),)),
        ],
        compiler_params=pltpu.CompilerParams(vmem_limit_bytes=ATTEND_VMEM),
        name="order_blocks",
    )(length, where, *arrived)


def dot_keys(queries, keys):
    return lax.dot_general(
        queries, keys, (((1,), (1,)), ((), ())), preferred_element_type=jnp.float32
    )


def attend_kernel(span, half_ref, *refs):
    query_refs, (key_ref, value_ref), new_key_refs, new_value_refs, out_ref = (
        refs[:2],
        refs[2:4],
        refs[4:6],
        refs[6:8],
        refs[8],
    )
    rows = out_ref.shape[0]
    half = rows // 2
    queries = jnp.concatenate([ref[0] for ref in query_refs], 0)
    spans = key_ref.shape[0] // span
    turn = half_ref[0] * half
    token = lax.rem(lax.broadcasted_iota(jnp.int32, (rows, half), 0) + turn, rows)
    column = lax.broadcasted_iota(jnp.int32, (rows, half), 1)
    parts = []
    for side, ref in enumerate(new_key_refs):
        causal = column + lax.rem(turn + side * half, rows) <= token
        parts.append(jnp.where(causal, dot_keys(queries, ref[...]), -jnp.inf))
    scores = jnp.concatenate(parts, 1)
    peak = jnp.max(scores, axis=1, keepdims=True)
    total = None
    values = jnp.concatenate([ref[...] for ref in new_value_refs], 0)
    for index in range(spans + 1):
        if index < spans:
            next_scores = dot_keys(queries, key_ref[index * span : (index + 1) * span, :])
            next_peak = jnp.maximum(peak, jnp.max(next_scores, axis=1, keepdims=True))
        weights = jnp.exp2((scores - peak) * SCORE_SCALE).astype(jnp.bfloat16)
        product = jnp.dot(weights, values, preferred_element_type=jnp.float32)
        total = product if total is None else total + product
        if index < spans:
            total = total * jnp.exp2((peak - next_peak) * SCORE_SCALE)
            scores, peak = next_scores, next_peak
            values = value_ref[index * span : (index + 1) * span, :]
    out_ref[...] = (total[:, :HD] / total[:, HD:]).astype(jnp.bfloat16)


def attend(half, queries, prefix, new_keys, new_values):
    heads = queries[0].shape[0]
    rows = 2 * new_keys[0].shape[0]
    span = math.gcd(prefix[0].shape[0], 1024)
    whole = lambda array: pl.BlockSpec(array.shape, lambda step: (0, 0))
    count = prefix[0].shape[0] + rows
    query_spec = pl.BlockSpec((1, rows // 2, HD), lambda step: (step, 0, 0))
    fixed = (*prefix, *new_keys, *new_values)
    return pl.pallas_call(
        functools.partial(attend_kernel, span),
        grid=(heads,),
        out_shape=jax.ShapeDtypeStruct((rows, heads * HD), jnp.bfloat16),
        in_specs=[pl.BlockSpec(memory_space=pltpu.SMEM), query_spec, query_spec]
        + [whole(array) for array in fixed],
        out_specs=pl.BlockSpec((rows, HD), lambda step: (0, step)),
        compiler_params=pltpu.CompilerParams(vmem_limit_bytes=ATTEND_VMEM),
        cost_estimate=pl.CostEstimate(
            flops=heads * rows * count * HD * 8,
            bytes_accessed=2 * (count * 3 * HD + 2 * heads * rows * HD),
            transcendentals=heads * rows * count,
        ),
        name="attend",
    )(half, *queries, *fixed)


def on_device(
    n_model,
    n_pool,
    states,
    norm_gain,
    w_query,
    q_bias,
    w_key,
    w_value,
    k_bias,
    v_bias,
    w_out,
    kv_pool,
    hit_holder,
    hit_slot,
    prefix_len,
):
    my_model = lax.axis_index("mp")
    my_pool = lax.axis_index("pool")
    row_count = states.shape[1]
    suffix = row_count * n_model
    q_width = w_query.shape[1]
    q_local = q_width // HD
    kv_local = w_key.shape[1]
    kv_heads = kv_local * n_model // HD
    group_size = QH // kv_heads
    blocks_total = hit_holder.shape[1]
    block_len = kv_pool.shape[2]
    holders = n_model * n_pool
    capacity = 2 * blocks_total // holders
    sharers = HD // kv_local

    lined = n_model == LINE_MODELS

    self_holder = my_model * n_pool + my_pool
    chosen = listing(hit_holder == self_holder, capacity)
    slot_ids = jnp.sum(jnp.where(chosen, hit_slot[:, None, :], 0), -1)
    models = jnp.arange(n_model, dtype=jnp.int32)
    my_holder = hit_holder[my_pool]
    prefix_count = prefix_len[my_pool]
    block_ids = jnp.arange(blocks_total, dtype=jnp.int32)
    earlier = (my_holder[:, None] == my_holder[None, :]) & (block_ids[None, :] < block_ids[:, None])
    rank = jnp.sum(earlier.astype(jnp.int32), -1)
    normed = normalize(states[0], norm_gain)
    if lined:
        mine, others = (
            lax.dynamic_index_in_dim(slot_ids, pool, 0, keepdims=False)
            for pool in (my_pool, 1 - my_pool)
        )
        pool_blocks = kv_pool[0]
        got = lax.ppermute(pick_blocks(pool_blocks, others), "pool", [(0, 1), (1, 0)])
        slots = jnp.stack([mine, jnp.arange(capacity, dtype=jnp.int32)])
        outgoing = pack_blocks((pool_blocks, got), slots, (models ^ my_model) * q_local // group_size)
        my_z, my_y = my_model // 2, my_model % 2
        near, far, arrived = gather_and_exchange(normed, outgoing, (my_z == 1) | (my_z == 2))
        arrived = [block.reshape(-1, block_len, 2 * HD) for block in arrived]
        distance = (my_holder // n_pool) ^ my_model
        where = (distance * n_pool + (my_holder % n_pool ^ my_pool)) * capacity + rank
    else:
        outgoing = pack_blocks((kv_pool[0],) * 2, slot_ids, models * q_local // group_size)
        outgoing = jnp.stack(outgoing).reshape(holders, capacity * block_len, 2 * HD)
        arrived = lax.all_to_all(outgoing, ("mp", "pool"), split_axis=0, concat_axis=0, tiled=True)
        arrived = [arrived.reshape(holders * capacity, block_len, 2 * HD)]
        where = my_holder * capacity + rank

    upper_half = (my_model // (n_model // 2)).astype(jnp.int32) if lined else jnp.int32(0)
    half_rows = suffix // 2
    order = (jnp.arange(suffix, dtype=jnp.int32) + upper_half * half_rows) % suffix
    cosine, sine = angle_tables(prefix_count + order)
    cosine, sine = jnp.concatenate([cosine, cosine], 1), jnp.concatenate([-sine, sine], 1)
    halves = [slice(0, half_rows), slice(half_rows, suffix)]
    biases = [bias.reshape(1, -1) for bias in (q_bias, k_bias, v_bias)]
    weights = (w_query, w_key, w_value)
    if lined:
        results = []
        for blocks, inner in ((near, my_z % 2), (far, upper_half)):
            starts = jnp.stack(
                [
                    2 * (inner ^ other) + (my_y ^ side)
                    for side in range(2)
                    for other in range(2)
                ]
            )
            table = [part[halves[len(results)]] for part in (cosine, sine)]
            results.append(
                project(starts.astype(jnp.int32) * row_count, blocks, weights, biases, table)
            )
        queries, new_keys, new_values, pairs = zip(*results)
        pairs = jnp.where(
            upper_half == 0, jnp.concatenate(pairs, 0), jnp.concatenate(pairs[::-1], 0)
        ).reshape(n_model, row_count, 2 * HD)
    else:
        tokens = lax.all_gather(normed, "mp", axis=0, tiled=True)
        linear, key_raw, value_raw = (
            jnp.dot(tokens, weight, preferred_element_type=jnp.float32) + bias.astype(jnp.float32)
            for weight, bias in zip(weights, biases)
        )
        cosine, sine = cosine[:, : HD // 2], sine[:, HD // 2 :]
        queries = rotate(linear.reshape(suffix, q_local, HD), cosine, sine)
        queries = queries.astype(jnp.bfloat16).transpose(1, 0, 2)
        key_raw, value_raw = key_raw.astype(jnp.bfloat16), value_raw.astype(jnp.bfloat16)
        together = [
            [first + other for other in range(sharers)] for first in range(0, n_model, sharers)
        ]
        key_whole, value_whole = (
            lax.all_gather(part, "mp", axis=1, tiled=True, axis_index_groups=together)
            for part in (key_raw, value_raw)
        )
        key_whole = rotate(key_whole.astype(jnp.float32)[:, None, :], cosine, sine)
        key_whole = key_whole.astype(jnp.bfloat16)[:, 0]
        value_ones = jnp.concatenate([value_whole, jnp.ones_like(value_whole)], 1)
        first_col = (my_model % sharers) * kv_local
        key_cols = lax.dynamic_slice_in_dim(key_whole, first_col, kv_local, 1)
        pairs = jnp.stack([key_cols, value_raw], 1).reshape(n_model, row_count, 2 * kv_local)
        queries = [queries[:, part] for part in halves]
        new_keys = [key_whole[part] for part in halves]
        new_values = [value_ones[part] for part in halves]

    pairs = lax.all_to_all(pairs, "mp", split_axis=0, concat_axis=0, tiled=True)
    arrived, new_keys, pairs = lax.optimization_barrier((arrived, list(new_keys), pairs))
    cache_rows = (
        pairs.reshape(kv_heads, sharers, row_count, 2, kv_local)
        .transpose(2, 0, 3, 1, 4)
        .reshape(1, row_count, kv_heads * 2 * HD)
    )
    prefix = order_blocks(arrived, where, prefix_count.reshape(1))
    mixed = attend(upper_half.reshape(1), queries, prefix, new_keys, new_values)
    width = w_out.shape[1] // COLUMN_CHUNKS
    shares = [
        jnp.dot(
            mixed,
            w_out[:, chunk * width : (chunk + 1) * width],
            preferred_element_type=jnp.float32,
        ).astype(jnp.bfloat16)
        for chunk in range(COLUMN_CHUNKS)
    ]

    first = upper_half * (n_model // 2)
    scatters = [
        RingScatter(
            share.reshape(n_model, row_count, -1),
            n_model,
            my_model,
            first,
            1 if chunk % 2 == 0 else -1,
        )
        for chunk, share in enumerate(shares)
    ]
    sent = []
    for _ in range(n_model // 2):
        for scatter in scatters:
            sent = scatter.step(*sent)
    return (jnp.concatenate([scatter.finish() for scatter in scatters], 1)[None], cache_rows)


def solution(mesh):
    placed = (
        P(("groups", "pool"), "mp", None),
        P(),
        P(None, "mp"),
        P("mp"),
        P(None, "mp"),
        P(None, "mp"),
        P("mp"),
        P("mp"),
        P("mp", None),
        P(("groups", "mp", "pool"), None, None, None),
        P("groups", None),
        P("groups", None),
        P("groups"),
    )
    return jax.shard_map(
        functools.partial(on_device, mesh.shape["mp"], mesh.shape["pool"]),
        mesh=mesh,
        in_specs=placed,
        out_specs=(P(("groups", "pool"), "mp", None), P(("groups", "pool"), "mp", None)),
        check_vma=False,
    )
```

```python
import functools
import math

import jax
import jax.numpy as jnp
from jax import lax
from jax.experimental import pallas as pl
from jax.experimental.pallas import tpu as pltpu
from jax.sharding import PartitionSpec as P

QH = 64
HD = 128
ROPE_BASE = 1000000.0
EPSILON = 1e-06
SCORE_SCALE = HD ** (-0.5) * math.log2(math.e)
VMEM_LIMIT = 56 * 1024 * 1024
ATTEND_VMEM = 28 * 1024 * 1024
ROW_CHUNKS = 2
STREAMS = 4
LINE_MODELS = 8


def angle_tables(positions):
    frequency = jnp.power(
        jnp.float32(ROPE_BASE), -2.0 * jnp.arange(HD // 2, dtype=jnp.float32) / HD
    )
    angles = positions.astype(jnp.float32)[:, None] * frequency[None, :]
    return jnp.cos(angles), jnp.sin(angles)


def rotate(vectors, cosine, sine):
    first_half = vectors[..., : HD // 2]
    second = vectors[..., HD // 2 :]
    cosine = cosine[:, None, :]
    sine = sine[:, None, :]
    return jnp.concatenate(
        [first_half * cosine - second * sine, second * cosine + first_half * sine], -1
    )


def normalize(states, gain_vec):
    values = states.astype(jnp.float32)
    inv_rms = lax.rsqrt(jnp.mean(values * values, axis=-1, keepdims=True) + EPSILON)
    return (values * inv_rms * gain_vec.astype(jnp.float32)).astype(jnp.bfloat16)


def listing(owned_mask, capacity):
    rank_order = jnp.cumsum(owned_mask.astype(jnp.int32), -1) - 1
    slot_index = jnp.arange(capacity, dtype=jnp.int32)
    return owned_mask[..., None, :] & (rank_order[..., None, :] == slot_index[:, None])


def swap(block, mask):
    return lax.ppermute(block, "mp", [(index, index ^ mask) for index in range(LINE_MODELS)])


def cross(block):
    pairs = []
    for index in range(LINE_MODELS):
        for core in range(2):
            if 2 <= index < 6:
                pairs.append((index * 2 + core, (index ^ 6) * 2 + core))
            else:
                pairs.append((index * 2 + core, index * 2 + 1 - core))
    return lax.ppermute(block, ("mp", "pool"), pairs)


def gather_and_exchange(own, outgoing, middle):
    arrived = {0: outgoing[0]}

    def after(block, *events):
        return lax.optimization_barrier((block, events))[0]

    def exchange(apart, *events):
        block = after(outgoing[apart], *events) if events else outgoing[apart]
        arrived[apart] = swap(block, apart)

    beside = swap(own, 2)
    over = cross(own)
    own_y = swap(own, 1)
    over_beside = cross(beside)
    over_passed = swap(over, 2)
    beside_y = swap(after(beside, own_y), 1)
    far_first = jnp.where(middle, over, over_passed)
    far_first_y = swap(after(far_first, beside_y), 1)
    over_beside_passed = swap(after(over_beside, outgoing[4]), 2)
    exchange(4, over_beside)
    exchange(6, over_beside)
    far_second = jnp.where(middle, over_beside, over_beside_passed)
    far_second_y = swap(after(far_second, far_first_y), 1)
    exchange(5, far_first_y, far_second)
    exchange(2, far_first_y, far_second)
    exchange(7, arrived[4], far_first_y)
    exchange(3, arrived[4], far_first_y)
    exchange(1, arrived[4], far_first_y)
    near = [after(own, far_second, arrived[4], arrived[6]), beside, own_y, beside_y]
    far = [far_first, far_second, far_first_y, far_second_y]
    return near, far, [arrived[apart] for apart in range(LINE_MODELS)]


def project_kernel(starts_ref, *refs):
    n_blocks = starts_ref.shape[0]
    blocks, refs = refs[:n_blocks], refs[n_blocks:]
    q_weights, (k_weight_ref, v_weight_ref), refs = refs[:STREAMS], refs[STREAMS:][:2], refs[STREAMS + 2 :]
    q_bias_ref, k_bias_ref, v_bias_ref, cos_ref, sin_ref = refs[:5]
    query_ref, key_ref, value_ref, pair_ref, tokens_ref, total_ref, sems = refs[5:]
    step = pl.program_id(0)
    depth = k_weight_ref.shape[0]
    q_width = q_weights[0].shape[1]
    rows = blocks[0].shape[0]

    @pl.when(step == 0)
    def _():
        copies = [
            pltpu.make_async_copy(
                block,
                tokens_ref.at[pl.ds(pl.multiple_of(starts_ref[index], rows), rows), :],
                sems.at[index],
            )
            for index, block in enumerate(blocks)
        ]
        for copy in copies:
            copy.start()
        total_ref[...] = jnp.zeros_like(total_ref)
        for copy in copies:
            copy.wait()

    tokens = tokens_ref[:, pl.ds(pl.multiple_of(step * depth, depth), depth)]
    q_weight = jnp.concatenate([ref[...] for ref in q_weights], axis=0)
    total_ref[:, :q_width] += jnp.dot(tokens, q_weight, preferred_element_type=jnp.float32)
    both = jnp.concatenate([k_weight_ref[...], v_weight_ref[...]], axis=1)
    total_ref[:, q_width:] += jnp.dot(tokens, both, preferred_element_type=jnp.float32)

    @pl.when(step == pl.num_programs(0) - 1)
    def _():
        cosine, sine = cos_ref[...], sin_ref[...]

        def turned(vectors):
            return vectors * cosine + pltpu.roll(vectors, HD // 2, 1) * sine

        for head in range(q_width // HD):
            cols = slice(head * HD, (head + 1) * HD)
            query = total_ref[:, cols] + q_bias_ref[:, cols].astype(jnp.float32)
            query_ref[head] = turned(query).astype(jnp.bfloat16)
        key = total_ref[:, q_width : q_width + HD] + k_bias_ref[...].astype(jnp.float32)
        key = turned(key.astype(jnp.bfloat16).astype(jnp.float32)).astype(jnp.bfloat16)
        value = total_ref[:, q_width + HD :] + v_bias_ref[...].astype(jnp.float32)
        value = value.astype(jnp.bfloat16)
        key_ref[...] = key
        value_ref[:, :HD] = value
        value_ref[:, HD:] = jnp.ones_like(value)
        pair_ref[:, :HD] = key
        pair_ref[:, HD:] = value


def project(starts, blocks, weights, biases, tables):
    width = blocks[0].shape[1]
    rows = sum(block.shape[0] for block in blocks)
    depth = math.gcd(width, 1024)
    q_width = weights[0].shape[1]
    out_width = q_width + 2 * HD
    fixed = lambda array: pl.BlockSpec(array.shape, lambda step: (0,) * len(array.shape))
    in_specs = [pl.BlockSpec(memory_space=pltpu.SMEM)]
    in_specs += [pl.BlockSpec(memory_space=pl.ANY)] * len(blocks)
    in_specs += [
        pl.BlockSpec((depth // STREAMS, q_width), lambda step, part=part: (step * STREAMS + part, 0))
        for part in range(STREAMS)
    ]
    in_specs += [pl.BlockSpec((depth, HD), lambda step: (step, 0))] * 2
    in_specs += [fixed(array) for array in (*biases, *tables)]
    out_shape = (
        jax.ShapeDtypeStruct((q_width // HD, rows, HD), jnp.bfloat16),
        jax.ShapeDtypeStruct((rows, HD), jnp.bfloat16),
        jax.ShapeDtypeStruct((rows, 2 * HD), jnp.bfloat16),
        jax.ShapeDtypeStruct((rows, 2 * HD), jnp.bfloat16),
    )
    return pl.pallas_call(
        project_kernel,
        grid=(width // depth,),
        out_shape=out_shape,
        in_specs=in_specs,
        out_specs=tuple(fixed(shape) for shape in out_shape),
        scratch_shapes=[
            pltpu.VMEM((rows, width), jnp.bfloat16),
            pltpu.VMEM((rows, out_width), jnp.float32),
            pltpu.SemaphoreType.DMA((len(blocks),)),
        ],
        compiler_params=pltpu.CompilerParams(vmem_limit_bytes=VMEM_LIMIT),
        cost_estimate=pl.CostEstimate(
            flops=2 * rows * width * out_width,
            bytes_accessed=2 * width * (rows + out_width) + 4 * rows * out_width,
            transcendentals=0,
        ),
        name="project",
    )(starts, *blocks, *weights[:1] * STREAMS, *weights[1:], *biases, *tables)


class RingScatter:
    def __init__(self, shares, n_model, my_model, first, way):
        order = [m for m in range(0, n_model, 2)] + [m for m in range(n_model - 1, 0, -2)]
        self.order = order
        self.n_model = n_model
        self.way = way
        spot = jnp.array([order.index(m) for m in range(n_model)], jnp.int32)[my_model]
        self.shares, self.spot, self.first = shares, spot, first
        self.distance = {way: n_model // 2, -way: n_model // 2 - 1}
        self.moving = {}

    def share_of(self, offset):
        table = jnp.array(self.order, jnp.int32)
        owner = table[(self.spot + offset + self.n_model) % self.n_model]
        owner = (owner - self.first + self.n_model) % self.n_model
        return lax.dynamic_index_in_dim(self.shares, owner, 0, keepdims=False)

    def step(self, *before):
        ways = [way for way in (self.way, -self.way) if self.distance[way]]
        blocks = []
        for way in ways:
            block = self.share_of(way * self.distance[way])
            if way in self.moving:
                arrived = self.moving[way].astype(jnp.float32)
                block = (block.astype(jnp.float32) + arrived).astype(jnp.bfloat16)
            blocks.append(block)
            self.distance[way] -= 1
        blocks, _ = lax.optimization_barrier((blocks, (before, list(self.moving.values()))))
        for way, block in zip(ways, blocks):
            pairs = [
                (self.order[i], self.order[(i + way) % self.n_model]) for i in range(self.n_model)
            ]
            self.moving[way] = lax.ppermute(block, "mp", pairs)
        return blocks

    def finish(self):
        total = self.share_of(0).astype(jnp.float32)
        for way in (1, -1):
            total = total + self.moving[way].astype(jnp.float32)
        return total.astype(jnp.bfloat16)


def pick_kernel(slots_ref, pool_ref, out_ref):
    def place(rank, _):
        out_ref[rank] = pool_ref[slots_ref[rank]]
        return 0

    lax.fori_loop(0, slots_ref.shape[0], place, 0)


def pick_blocks(pool, slots):
    return pl.pallas_call(
        pick_kernel,
        out_shape=jax.ShapeDtypeStruct((*slots.shape, *pool.shape[1:]), pool.dtype),
        in_specs=[
            pl.BlockSpec(memory_space=pltpu.SMEM),
            pl.BlockSpec(memory_space=pltpu.VMEM),
        ],
        out_specs=pl.BlockSpec(memory_space=pltpu.VMEM),
        compiler_params=pltpu.CompilerParams(vmem_limit_bytes=ATTEND_VMEM),
        name="pick_blocks",
    )(slots, pool)


def pack_kernel(lists, slots_ref, heads_ref, *refs):
    sources, out_refs = refs[: len(lists)], refs[len(lists) :]

    def place(rank, _):
        for listed, source_ref in zip(lists, sources):
            slot = slots_ref[listed, rank]
            for dest, out_ref in enumerate(out_refs):
                first = pl.multiple_of(heads_ref[dest] * 2 * HD, 2 * HD)
                out_ref[listed, rank] = source_ref[slot, :, pl.ds(first, 2 * HD)]
        return 0

    lax.fori_loop(0, slots_ref.shape[1], place, 0)


def pack_blocks(sources, slots, heads):
    dests = heads.shape[0]
    block_len = sources[0].shape[1]
    shape = jax.ShapeDtypeStruct((*slots.shape, block_len, 2 * HD), jnp.bfloat16)
    return pl.pallas_call(
        functools.partial(pack_kernel, range(len(sources))),
        out_shape=[shape] * dests,
        in_specs=[pl.BlockSpec(memory_space=pltpu.SMEM)] * 2
        + [pl.BlockSpec(memory_space=pltpu.VMEM)] * len(sources),
        out_specs=[pl.BlockSpec(memory_space=pltpu.VMEM)] * dests,
        compiler_params=pltpu.CompilerParams(vmem_limit_bytes=ATTEND_VMEM),
        name="pack_blocks",
    )(slots, heads, *sources)


def order_kernel(length_ref, where_ref, *refs):
    *arrived_refs, key_ref, value_ref, held_ref, sems = refs
    block_len = held_ref.shape[1]
    copies = []
    begin = 0
    for index, source in enumerate(arrived_refs):
        end = begin + source.shape[0]
        copies.append(pltpu.make_async_copy(source, held_ref.at[begin:end], sems.at[index]))
        begin = end
    for copy in copies:
        copy.start()
    for copy in copies:
        copy.wait()
    length = length_ref[0]
    first = held_ref[where_ref[0]][:1, :HD].astype(jnp.float32)
    row = lax.broadcasted_iota(jnp.int32, (block_len, HD), 0)

    def place(block_id, _):
        block = held_ref[where_ref[block_id]].astype(jnp.float32)
        start = pl.multiple_of(block_id * block_len, block_len)
        seen = row + start < length
        rows = pl.ds(start, block_len)
        key_ref[rows, :] = jnp.where(seen, block[:, :HD], first).astype(jnp.bfloat16)
        value_ref[rows, :HD] = jnp.where(seen, block[:, HD:], 0.0).astype(jnp.bfloat16)
        value_ref[rows, HD:] = jnp.where(seen, 1.0, 0.0).astype(jnp.bfloat16)
        return 0

    lax.fori_loop(0, where_ref.shape[0], place, 0, unroll=8)


def order_blocks(arrived, where, length):
    count = sum(array.shape[-3] for array in arrived)
    block_len = arrived[0].shape[-2]
    tokens = where.shape[0] * block_len
    return pl.pallas_call(
        order_kernel,
        out_shape=(
            jax.ShapeDtypeStruct((tokens, HD), jnp.bfloat16),
            jax.ShapeDtypeStruct((tokens, 2 * HD), jnp.bfloat16),
        ),
        in_specs=[pl.BlockSpec(memory_space=pltpu.SMEM)] * 2
        + [pl.BlockSpec(memory_space=pl.ANY)] * len(arrived),
        out_specs=(
            pl.BlockSpec(memory_space=pltpu.VMEM),
            pl.BlockSpec(memory_space=pltpu.VMEM),
        ),
        scratch_shapes=[
            pltpu.VMEM((count, block_len, 2 * HD), jnp.bfloat16),
            pltpu.SemaphoreType.DMA((len(arrived),)),
        ],
        compiler_params=pltpu.CompilerParams(vmem_limit_bytes=ATTEND_VMEM),
        name="order_blocks",
    )(length, where, *arrived)


def dot_keys(queries, keys):
    return lax.dot_general(
        queries, keys, (((1,), (1,)), ((), ())), preferred_element_type=jnp.float32
    )


def attend_kernel(span, row_step, chunk, half_ref, *refs):
    query_refs, (key_ref, value_ref), new_key_refs, new_value_refs, out_ref = (
        refs[:2],
        refs[2:4],
        refs[4:6],
        refs[6:8],
        refs[8],
    )
    rows = out_ref.shape[0]
    half = new_key_refs[0].shape[0]
    queries = jnp.concatenate([ref[0].reshape(rows // 2, HD) for ref in query_refs], 0)
    spans = key_ref.shape[0] // span
    stride = 2 * half * row_step // rows
    turn = half_ref[0] * half
    local = lax.broadcasted_iota(jnp.int32, (rows, half), 0)
    token = (local // row_step) * stride + chunk * row_step + local % row_step
    token = lax.rem(token + turn, 2 * half)
    column = lax.broadcasted_iota(jnp.int32, (rows, half), 1)
    parts = []
    for side, ref in enumerate(new_key_refs):
        causal = column + lax.rem(turn + side * half, 2 * half) <= token
        parts.append(jnp.where(causal, dot_keys(queries, ref[...]), -jnp.inf))
    scores = jnp.concatenate(parts, 1)
    peak = jnp.max(scores, axis=1, keepdims=True)
    total = None
    values = jnp.concatenate([ref[...] for ref in new_value_refs], 0)
    for index in range(spans + 1):
        if index < spans:
            next_scores = dot_keys(queries, key_ref[index * span : (index + 1) * span, :])
            next_peak = jnp.maximum(peak, jnp.max(next_scores, axis=1, keepdims=True))
        weights = jnp.exp2((scores - peak) * SCORE_SCALE).astype(jnp.bfloat16)
        product = jnp.dot(weights, values, preferred_element_type=jnp.float32)
        total = product if total is None else total + product
        if index < spans:
            total = total * jnp.exp2((peak - next_peak) * SCORE_SCALE)
            scores, peak = next_scores, next_peak
            values = value_ref[index * span : (index + 1) * span, :]
    out_ref[...] = (total[:, :HD] / total[:, HD:]).astype(jnp.bfloat16)


def attend(half, queries, prefix, new_keys, new_values, chunk):
    heads, owners, _, row_step, _ = queries[0].shape
    rows = 2 * owners * row_step
    span = math.gcd(prefix[0].shape[0], 1024)
    whole = lambda array: pl.BlockSpec(array.shape, lambda step: (0, 0))
    count = prefix[0].shape[0] + 2 * new_keys[0].shape[0]
    query_spec = pl.BlockSpec(
        (1, owners, None, row_step, HD), lambda step: (step, 0, chunk, 0, 0)
    )
    fixed = (*prefix, *new_keys, *new_values)
    return pl.pallas_call(
        functools.partial(attend_kernel, span, row_step, chunk),
        grid=(heads,),
        out_shape=jax.ShapeDtypeStruct((rows, heads * HD), jnp.bfloat16),
        in_specs=[pl.BlockSpec(memory_space=pltpu.SMEM), query_spec, query_spec]
        + [whole(array) for array in fixed],
        out_specs=pl.BlockSpec((rows, HD), lambda step: (0, step)),
        compiler_params=pltpu.CompilerParams(vmem_limit_bytes=ATTEND_VMEM),
        cost_estimate=pl.CostEstimate(
            flops=heads * rows * count * HD * 8,
            bytes_accessed=2 * (count * 3 * HD + 2 * heads * rows * HD),
            transcendentals=heads * rows * count,
        ),
        name="attend",
    )(half, *queries, *fixed)


def on_device(
    n_model,
    n_pool,
    states,
    norm_gain,
    w_query,
    q_bias,
    w_key,
    w_value,
    k_bias,
    v_bias,
    w_out,
    kv_pool,
    hit_holder,
    hit_slot,
    prefix_len,
):
    my_model = lax.axis_index("mp")
    my_pool = lax.axis_index("pool")
    row_count = states.shape[1]
    suffix = row_count * n_model
    q_width = w_query.shape[1]
    q_local = q_width // HD
    kv_local = w_key.shape[1]
    kv_heads = kv_local * n_model // HD
    group_size = QH // kv_heads
    blocks_total = hit_holder.shape[1]
    block_len = kv_pool.shape[2]
    holders = n_model * n_pool
    capacity = 2 * blocks_total // holders
    sharers = HD // kv_local

    lined = n_model == LINE_MODELS

    self_holder = my_model * n_pool + my_pool
    chosen = listing(hit_holder == self_holder, capacity)
    slot_ids = jnp.sum(jnp.where(chosen, hit_slot[:, None, :], 0), -1)
    models = jnp.arange(n_model, dtype=jnp.int32)
    my_holder = hit_holder[my_pool]
    prefix_count = prefix_len[my_pool]
    block_ids = jnp.arange(blocks_total, dtype=jnp.int32)
    earlier = (my_holder[:, None] == my_holder[None, :]) & (block_ids[None, :] < block_ids[:, None])
    rank = jnp.sum(earlier.astype(jnp.int32), -1)
    normed = normalize(states[0], norm_gain)
    if lined:
        mine, others = (
            lax.dynamic_index_in_dim(slot_ids, pool, 0, keepdims=False)
            for pool in (my_pool, 1 - my_pool)
        )
        pool_blocks = kv_pool[0]
        got = lax.ppermute(pick_blocks(pool_blocks, others), "pool", [(0, 1), (1, 0)])
        slots = jnp.stack([mine, jnp.arange(capacity, dtype=jnp.int32)])
        outgoing = pack_blocks((pool_blocks, got), slots, (models ^ my_model) * q_local // group_size)
        my_z, my_y = my_model // 2, my_model % 2
        near, far, arrived = gather_and_exchange(normed, outgoing, (my_z == 1) | (my_z == 2))
        arrived = [block.reshape(-1, block_len, 2 * HD) for block in arrived]
        distance = (my_holder // n_pool) ^ my_model
        where = (distance * n_pool + (my_holder % n_pool ^ my_pool)) * capacity + rank
    else:
        outgoing = pack_blocks((kv_pool[0],) * 2, slot_ids, models * q_local // group_size)
        outgoing = jnp.stack(outgoing).reshape(holders, capacity * block_len, 2 * HD)
        arrived = lax.all_to_all(outgoing, ("mp", "pool"), split_axis=0, concat_axis=0, tiled=True)
        arrived = [arrived.reshape(holders * capacity, block_len, 2 * HD)]
        where = my_holder * capacity + rank

    upper_half = (my_model // (n_model // 2)).astype(jnp.int32) if lined else jnp.int32(0)
    half_rows = suffix // 2
    order = (jnp.arange(suffix, dtype=jnp.int32) + upper_half * half_rows) % suffix
    cosine, sine = angle_tables(prefix_count + order)
    cosine, sine = jnp.concatenate([cosine, cosine], 1), jnp.concatenate([-sine, sine], 1)
    halves = [slice(0, half_rows), slice(half_rows, suffix)]
    biases = [bias.reshape(1, -1) for bias in (q_bias, k_bias, v_bias)]
    weights = (w_query, w_key, w_value)
    if lined:
        results = []
        for blocks, inner in ((near, my_z % 2), (far, upper_half)):
            starts = jnp.stack(
                [
                    2 * (inner ^ other) + (my_y ^ side)
                    for side in range(2)
                    for other in range(2)
                ]
            )
            table = [part[halves[len(results)]] for part in (cosine, sine)]
            results.append(
                project(starts.astype(jnp.int32) * row_count, blocks, weights, biases, table)
            )
        queries, new_keys, new_values, pairs = zip(*results)
        pairs = jnp.where(
            upper_half == 0, jnp.concatenate(pairs, 0), jnp.concatenate(pairs[::-1], 0)
        ).reshape(n_model, row_count, 2 * HD)
    else:
        tokens = lax.all_gather(normed, "mp", axis=0, tiled=True)
        linear, key_raw, value_raw = (
            jnp.dot(tokens, weight, preferred_element_type=jnp.float32) + bias.astype(jnp.float32)
            for weight, bias in zip(weights, biases)
        )
        cosine, sine = cosine[:, : HD // 2], sine[:, HD // 2 :]
        queries = rotate(linear.reshape(suffix, q_local, HD), cosine, sine)
        queries = queries.astype(jnp.bfloat16).transpose(1, 0, 2)
        key_raw, value_raw = key_raw.astype(jnp.bfloat16), value_raw.astype(jnp.bfloat16)
        together = [
            [first + other for other in range(sharers)] for first in range(0, n_model, sharers)
        ]
        key_whole, value_whole = (
            lax.all_gather(part, "mp", axis=1, tiled=True, axis_index_groups=together)
            for part in (key_raw, value_raw)
        )
        key_whole = rotate(key_whole.astype(jnp.float32)[:, None, :], cosine, sine)
        key_whole = key_whole.astype(jnp.bfloat16)[:, 0]
        value_ones = jnp.concatenate([value_whole, jnp.ones_like(value_whole)], 1)
        first_col = (my_model % sharers) * kv_local
        key_cols = lax.dynamic_slice_in_dim(key_whole, first_col, kv_local, 1)
        pairs = jnp.stack([key_cols, value_raw], 1).reshape(n_model, row_count, 2 * kv_local)
        queries = [queries[:, part] for part in halves]
        new_keys = [key_whole[part] for part in halves]
        new_values = [value_ones[part] for part in halves]

    pairs = lax.all_to_all(pairs, "mp", split_axis=0, concat_axis=0, tiled=True)
    arrived, new_keys, pairs = lax.optimization_barrier((arrived, list(new_keys), pairs))
    cache_rows = (
        pairs.reshape(kv_heads, sharers, row_count, 2, kv_local)
        .transpose(2, 0, 3, 1, 4)
        .reshape(1, row_count, kv_heads * 2 * HD)
    )
    prefix = order_blocks(arrived, where, prefix_count.reshape(1))

    row_step = max(row_count // ROW_CHUNKS, 16)
    chunks = row_count // row_step
    queries = [part.reshape(q_local, -1, chunks, row_step, HD) for part in queries]
    first = upper_half * (n_model // 2)
    steps = n_model // 2
    scatters, taken, sums, sent = [], [], [], []
    for chunk in range(chunks):
        queries, _ = lax.optimization_barrier((queries, sent))
        mixed = attend(upper_half.reshape(1), queries, prefix, new_keys, new_values, chunk)
        if scatters:
            mixed, _ = lax.optimization_barrier((mixed, scatters[-1].step()))
            taken[-1] += 1
        share = jnp.dot(mixed, w_out, preferred_element_type=jnp.float32).astype(jnp.bfloat16)
        share = share.reshape(n_model, row_step, -1)
        way = 1 if chunk % 2 == 0 else -1
        scatters.append(RingScatter(share, n_model, my_model, first, way))
        sent = scatters[-1].step()
        taken.append(1)
    while len(sums) < chunks:
        for chunk, scatter in enumerate(scatters):
            if taken[chunk] < steps:
                sent = scatter.step(sent, sums)
                taken[chunk] += 1
            elif len(sums) == chunk:
                sums.append(scatter.finish())
    return (jnp.concatenate(sums, 0)[None], cache_rows)


def solution(mesh):
    placed = (
        P(("groups", "pool"), "mp", None),
        P(),
        P(None, "mp"),
        P("mp"),
        P(None, "mp"),
        P(None, "mp"),
        P("mp"),
        P("mp"),
        P("mp", None),
        P(("groups", "mp", "pool"), None, None, None),
        P("groups", None),
        P("groups", None),
        P("groups"),
    )
    return jax.shard_map(
        functools.partial(on_device, mesh.shape["mp"], mesh.shape["pool"]),
        mesh=mesh,
        in_specs=placed,
        out_specs=(P(("groups", "pool"), "mp", None), P(("groups", "pool"), "mp", None)),
        check_vma=False,
    )
```

```python
import functools
import math

import jax
import jax.numpy as jnp
from jax import lax
from jax.experimental import pallas as pl
from jax.experimental.pallas import tpu as pltpu
from jax.sharding import PartitionSpec as P

QH = 64
HD = 128
ROPE_BASE = 1000000.0
EPSILON = 1e-06
SCORE_SCALE = HD ** (-0.5) * math.log2(math.e)
VMEM_LIMIT = 56 * 1024 * 1024
ATTEND_VMEM = 28 * 1024 * 1024
ROW_CHUNKS = 2
DOT_ROWS = 128
STREAMS = 4
LINE_MODELS = 8


def angle_tables(positions):
    frequency = jnp.power(
        jnp.float32(ROPE_BASE), -2.0 * jnp.arange(HD // 2, dtype=jnp.float32) / HD
    )
    angles = positions.astype(jnp.float32)[:, None] * frequency[None, :]
    return jnp.cos(angles), jnp.sin(angles)


def rotate(vectors, cosine, sine):
    first_half = vectors[..., : HD // 2]
    second = vectors[..., HD // 2 :]
    cosine = cosine[:, None, :]
    sine = sine[:, None, :]
    return jnp.concatenate(
        [first_half * cosine - second * sine, second * cosine + first_half * sine], -1
    )


def normalize(states, gain_vec):
    values = states.astype(jnp.float32)
    inv_rms = lax.rsqrt(jnp.mean(values * values, axis=-1, keepdims=True) + EPSILON)
    return (values * inv_rms * gain_vec.astype(jnp.float32)).astype(jnp.bfloat16)


def listing(owned_mask, capacity):
    rank_order = jnp.cumsum(owned_mask.astype(jnp.int32), -1) - 1
    slot_index = jnp.arange(capacity, dtype=jnp.int32)
    return owned_mask[..., None, :] & (rank_order[..., None, :] == slot_index[:, None])


def swap(block, mask):
    return lax.ppermute(block, "mp", [(index, index ^ mask) for index in range(LINE_MODELS)])


def cross(block):
    pairs = []
    for index in range(LINE_MODELS):
        for core in range(2):
            if 2 <= index < 6:
                pairs.append((index * 2 + core, (index ^ 6) * 2 + core))
            else:
                pairs.append((index * 2 + core, index * 2 + 1 - core))
    return lax.ppermute(block, ("mp", "pool"), pairs)


def gather_and_exchange(own, outgoing, middle):
    arrived = {0: outgoing[0]}

    def after(block, *events):
        return lax.optimization_barrier((block, events))[0]

    def exchange(apart, *events):
        block = after(outgoing[apart], *events) if events else outgoing[apart]
        arrived[apart] = swap(block, apart)

    beside = swap(own, 2)
    over = cross(own)
    own_y = swap(own, 1)
    over_beside = cross(beside)
    over_passed = swap(over, 2)
    beside_y = swap(after(beside, own_y), 1)
    far_first = jnp.where(middle, over, over_passed)
    far_first_y = swap(after(far_first, beside_y), 1)
    over_beside_passed = swap(after(over_beside, outgoing[4]), 2)
    exchange(4, over_beside)
    exchange(6, over_beside)
    exchange(1, over_beside)
    far_second = jnp.where(middle, over_beside, over_beside_passed)
    far_second_y = swap(after(far_second, far_first_y), 1)
    exchange(5, far_first_y, far_second)
    exchange(2, far_first_y, far_second)
    exchange(7, arrived[4], far_first_y)
    exchange(3, arrived[4], far_first_y)
    near = [after(own, far_second, arrived[4], arrived[6]), beside, own_y, beside_y]
    far = [far_first, far_second, far_first_y, far_second_y]
    return near, far, [arrived[apart] for apart in range(LINE_MODELS)]


def project_kernel(starts_ref, *refs):
    n_blocks = starts_ref.shape[0]
    blocks, refs = refs[:n_blocks], refs[n_blocks:]
    q_weights, (k_weight_ref, v_weight_ref), refs = refs[:STREAMS], refs[STREAMS:][:2], refs[STREAMS + 2 :]
    q_bias_ref, k_bias_ref, v_bias_ref, cos_ref, sin_ref = refs[:5]
    query_ref, key_ref, value_ref, pair_ref, tokens_ref, total_ref, sems = refs[5:]
    step = pl.program_id(0)
    depth = k_weight_ref.shape[0]
    q_width = q_weights[0].shape[1]
    rows = blocks[0].shape[0]

    @pl.when(step == 0)
    def _():
        copies = [
            pltpu.make_async_copy(
                block,
                tokens_ref.at[pl.ds(pl.multiple_of(starts_ref[index], rows), rows), :],
                sems.at[index],
            )
            for index, block in enumerate(blocks)
        ]
        for copy in copies:
            copy.start()
        total_ref[...] = jnp.zeros_like(total_ref)
        for copy in copies:
            copy.wait()

    tokens = tokens_ref[:, pl.ds(pl.multiple_of(step * depth, depth), depth)]
    q_weight = jnp.concatenate([ref[...] for ref in q_weights], axis=0)
    total_ref[:, :q_width] += jnp.dot(tokens, q_weight, preferred_element_type=jnp.float32)
    both = jnp.concatenate([k_weight_ref[...], v_weight_ref[...]], axis=1)
    total_ref[:, q_width:] += jnp.dot(tokens, both, preferred_element_type=jnp.float32)

    @pl.when(step == pl.num_programs(0) - 1)
    def _():
        cosine, sine = cos_ref[...], sin_ref[...]

        def turned(vectors):
            return vectors * cosine + pltpu.roll(vectors, HD // 2, 1) * sine

        for head in range(q_width // HD):
            cols = slice(head * HD, (head + 1) * HD)
            query = total_ref[:, cols] + q_bias_ref[:, cols].astype(jnp.float32)
            query_ref[head] = turned(query).astype(jnp.bfloat16)
        key = total_ref[:, q_width : q_width + HD] + k_bias_ref[...].astype(jnp.float32)
        key = turned(key.astype(jnp.bfloat16).astype(jnp.float32)).astype(jnp.bfloat16)
        value = total_ref[:, q_width + HD :] + v_bias_ref[...].astype(jnp.float32)
        value = value.astype(jnp.bfloat16)
        key_ref[...] = key
        value_ref[:, :HD] = value
        value_ref[:, HD:] = jnp.ones_like(value)
        pair_ref[:, :HD] = key
        pair_ref[:, HD:] = value


def project(starts, blocks, weights, biases, tables):
    width = blocks[0].shape[1]
    rows = sum(block.shape[0] for block in blocks)
    depth = math.gcd(width, 1024)
    q_width = weights[0].shape[1]
    out_width = q_width + 2 * HD
    fixed = lambda array: pl.BlockSpec(array.shape, lambda step: (0,) * len(array.shape))
    in_specs = [pl.BlockSpec(memory_space=pltpu.SMEM)]
    in_specs += [pl.BlockSpec(memory_space=pl.ANY)] * len(blocks)
    in_specs += [
        pl.BlockSpec((depth // STREAMS, q_width), lambda step, part=part: (step * STREAMS + part, 0))
        for part in range(STREAMS)
    ]
    in_specs += [pl.BlockSpec((depth, HD), lambda step: (step, 0))] * 2
    in_specs += [fixed(array) for array in (*biases, *tables)]
    out_shape = (
        jax.ShapeDtypeStruct((q_width // HD, rows, HD), jnp.bfloat16),
        jax.ShapeDtypeStruct((rows, HD), jnp.bfloat16),
        jax.ShapeDtypeStruct((rows, 2 * HD), jnp.bfloat16),
        jax.ShapeDtypeStruct((rows, 2 * HD), jnp.bfloat16),
    )
    return pl.pallas_call(
        project_kernel,
        grid=(width // depth,),
        out_shape=out_shape,
        in_specs=in_specs,
        out_specs=tuple(fixed(shape) for shape in out_shape),
        scratch_shapes=[
            pltpu.VMEM((rows, width), jnp.bfloat16),
            pltpu.VMEM((rows, out_width), jnp.float32),
            pltpu.SemaphoreType.DMA((len(blocks),)),
        ],
        compiler_params=pltpu.CompilerParams(vmem_limit_bytes=VMEM_LIMIT),
        cost_estimate=pl.CostEstimate(
            flops=2 * rows * width * out_width,
            bytes_accessed=2 * width * (rows + out_width) + 4 * rows * out_width,
            transcendentals=0,
        ),
        name="project",
    )(starts, *blocks, *weights[:1] * STREAMS, *weights[1:], *biases, *tables)


class RingScatter:
    def __init__(self, shares, n_model, my_model, first, way):
        order = [m for m in range(0, n_model, 2)] + [m for m in range(n_model - 1, 0, -2)]
        self.order = order
        self.n_model = n_model
        self.way = way
        spot = jnp.array([order.index(m) for m in range(n_model)], jnp.int32)[my_model]
        self.shares, self.spot, self.first = shares, spot, first
        self.distance = {way: n_model // 2, -way: n_model // 2 - 1}
        self.moving = {}

    def share_of(self, offset):
        table = jnp.array(self.order, jnp.int32)
        owner = table[(self.spot + offset + self.n_model) % self.n_model]
        owner = (owner - self.first + self.n_model) % self.n_model
        size = self.shares[0].shape[0]
        block = None
        for index, part in enumerate(self.shares):
            place = jnp.clip(owner - index * size, 0, size - 1)
            found = lax.dynamic_index_in_dim(part, place, 0, keepdims=False)
            block = found if block is None else jnp.where(owner >= index * size, found, block)
        return block

    def step(self, *before):
        ways = [way for way in (self.way, -self.way) if self.distance[way]]
        blocks = []
        for way in ways:
            block = self.share_of(way * self.distance[way])
            if way in self.moving:
                arrived = self.moving[way].astype(jnp.float32)
                block = (block.astype(jnp.float32) + arrived).astype(jnp.bfloat16)
            blocks.append(block)
            self.distance[way] -= 1
        blocks, _ = lax.optimization_barrier((blocks, (before, list(self.moving.values()))))
        for way, block in zip(ways, blocks):
            pairs = [
                (self.order[i], self.order[(i + way) % self.n_model]) for i in range(self.n_model)
            ]
            self.moving[way] = lax.ppermute(block, "mp", pairs)
        return blocks

    def finish(self):
        total = self.share_of(0).astype(jnp.float32)
        for way in (1, -1):
            total = total + self.moving[way].astype(jnp.float32)
        return total.astype(jnp.bfloat16)


def pick_kernel(slots_ref, pool_ref, out_ref):
    def place(rank, _):
        out_ref[rank] = pool_ref[slots_ref[rank]]
        return 0

    lax.fori_loop(0, slots_ref.shape[0], place, 0)


def pick_blocks(pool, slots):
    return pl.pallas_call(
        pick_kernel,
        out_shape=jax.ShapeDtypeStruct((*slots.shape, *pool.shape[1:]), pool.dtype),
        in_specs=[
            pl.BlockSpec(memory_space=pltpu.SMEM),
            pl.BlockSpec(memory_space=pltpu.VMEM),
        ],
        out_specs=pl.BlockSpec(memory_space=pltpu.VMEM),
        compiler_params=pltpu.CompilerParams(vmem_limit_bytes=ATTEND_VMEM),
        name="pick_blocks",
    )(slots, pool)


def pack_kernel(lists, slots_ref, heads_ref, *refs):
    sources, out_refs = refs[: len(lists)], refs[len(lists) :]

    def place(rank, _):
        for listed, source_ref in zip(lists, sources):
            slot = slots_ref[listed, rank]
            for dest, out_ref in enumerate(out_refs):
                first = pl.multiple_of(heads_ref[dest] * 2 * HD, 2 * HD)
                out_ref[listed, rank] = source_ref[slot, :, pl.ds(first, 2 * HD)]
        return 0

    lax.fori_loop(0, slots_ref.shape[1], place, 0)


def pack_blocks(sources, slots, heads):
    dests = heads.shape[0]
    block_len = sources[0].shape[1]
    shape = jax.ShapeDtypeStruct((*slots.shape, block_len, 2 * HD), jnp.bfloat16)
    return pl.pallas_call(
        functools.partial(pack_kernel, range(len(sources))),
        out_shape=[shape] * dests,
        in_specs=[pl.BlockSpec(memory_space=pltpu.SMEM)] * 2
        + [pl.BlockSpec(memory_space=pltpu.VMEM)] * len(sources),
        out_specs=[pl.BlockSpec(memory_space=pltpu.VMEM)] * dests,
        compiler_params=pltpu.CompilerParams(vmem_limit_bytes=ATTEND_VMEM),
        name="pack_blocks",
    )(slots, heads, *sources)


def order_kernel(length_ref, where_ref, *refs):
    *arrived_refs, key_ref, value_ref, held_ref, sems = refs
    block_len = held_ref.shape[1]
    copies = []
    begin = 0
    for index, source in enumerate(arrived_refs):
        end = begin + source.shape[0]
        copies.append(pltpu.make_async_copy(source, held_ref.at[begin:end], sems.at[index]))
        begin = end
    for copy in copies:
        copy.start()
    for copy in copies:
        copy.wait()
    length = length_ref[0]
    first = held_ref[where_ref[0]][:1, :HD].astype(jnp.float32)
    row = lax.broadcasted_iota(jnp.int32, (block_len, HD), 0)

    def place(block_id, _):
        block = held_ref[where_ref[block_id]].astype(jnp.float32)
        start = pl.multiple_of(block_id * block_len, block_len)
        seen = row + start < length
        rows = pl.ds(start, block_len)
        key_ref[rows, :] = jnp.where(seen, block[:, :HD], first).astype(jnp.bfloat16)
        value_ref[rows, :HD] = jnp.where(seen, block[:, HD:], 0.0).astype(jnp.bfloat16)
        value_ref[rows, HD:] = jnp.where(seen, 1.0, 0.0).astype(jnp.bfloat16)
        return 0

    lax.fori_loop(0, where_ref.shape[0], place, 0, unroll=8)


def order_blocks(arrived, where, length):
    count = sum(array.shape[-3] for array in arrived)
    block_len = arrived[0].shape[-2]
    tokens = where.shape[0] * block_len
    return pl.pallas_call(
        order_kernel,
        out_shape=(
            jax.ShapeDtypeStruct((tokens, HD), jnp.bfloat16),
            jax.ShapeDtypeStruct((tokens, 2 * HD), jnp.bfloat16),
        ),
        in_specs=[pl.BlockSpec(memory_space=pltpu.SMEM)] * 2
        + [pl.BlockSpec(memory_space=pl.ANY)] * len(arrived),
        out_specs=(
            pl.BlockSpec(memory_space=pltpu.VMEM),
            pl.BlockSpec(memory_space=pltpu.VMEM),
        ),
        scratch_shapes=[
            pltpu.VMEM((count, block_len, 2 * HD), jnp.bfloat16),
            pltpu.SemaphoreType.DMA((len(arrived),)),
        ],
        compiler_params=pltpu.CompilerParams(vmem_limit_bytes=ATTEND_VMEM),
        name="order_blocks",
    )(length, where, *arrived)


def dot_keys(queries, keys):
    return lax.dot_general(
        queries, keys, (((1,), (1,)), ((), ())), preferred_element_type=jnp.float32
    )


def attend_kernel(span, row_step, chunk, half_ref, *refs):
    query_refs, (key_ref, value_ref), new_key_refs, new_value_refs, out_ref = (
        refs[:2],
        refs[2:4],
        refs[4:6],
        refs[6:8],
        refs[8],
    )
    rows = out_ref.shape[0]
    half = new_key_refs[0].shape[0]
    queries = jnp.concatenate([ref[0].reshape(rows // 2, HD) for ref in query_refs], 0)
    spans = key_ref.shape[0] // span
    stride = 2 * half * row_step // rows
    turn = half_ref[0] * half
    local = lax.broadcasted_iota(jnp.int32, (rows, half), 0)
    token = (local // row_step) * stride + chunk * row_step + local % row_step
    token = lax.rem(token + turn, 2 * half)
    column = lax.broadcasted_iota(jnp.int32, (rows, half), 1)
    parts = []
    for side, ref in enumerate(new_key_refs):
        causal = column + lax.rem(turn + side * half, 2 * half) <= token
        parts.append(jnp.where(causal, dot_keys(queries, ref[...]), -jnp.inf))
    scores = jnp.concatenate(parts, 1)
    peak = jnp.max(scores, axis=1, keepdims=True)
    total = None
    values = jnp.concatenate([ref[...] for ref in new_value_refs], 0)
    for index in range(spans + 1):
        if index < spans:
            next_scores = dot_keys(queries, key_ref[index * span : (index + 1) * span, :])
            next_peak = jnp.maximum(peak, jnp.max(next_scores, axis=1, keepdims=True))
        weights = jnp.exp2((scores - peak) * SCORE_SCALE).astype(jnp.bfloat16)
        product = jnp.dot(weights, values, preferred_element_type=jnp.float32)
        total = product if total is None else total + product
        if index < spans:
            total = total * jnp.exp2((peak - next_peak) * SCORE_SCALE)
            scores, peak = next_scores, next_peak
            values = value_ref[index * span : (index + 1) * span, :]
    out_ref[...] = (total[:, :HD] / total[:, HD:]).astype(jnp.bfloat16)


def attend(half, queries, prefix, new_keys, new_values, chunk):
    heads, owners, _, row_step, _ = queries[0].shape
    rows = 2 * owners * row_step
    span = math.gcd(prefix[0].shape[0], 1024)
    whole = lambda array: pl.BlockSpec(array.shape, lambda step: (0, 0))
    count = prefix[0].shape[0] + 2 * new_keys[0].shape[0]
    query_spec = pl.BlockSpec(
        (1, owners, None, row_step, HD), lambda step: (step, 0, chunk, 0, 0)
    )
    fixed = (*prefix, *new_keys, *new_values)
    return pl.pallas_call(
        functools.partial(attend_kernel, span, row_step, chunk),
        grid=(heads,),
        out_shape=jax.ShapeDtypeStruct((rows, heads * HD), jnp.bfloat16),
        in_specs=[pl.BlockSpec(memory_space=pltpu.SMEM), query_spec, query_spec]
        + [whole(array) for array in fixed],
        out_specs=pl.BlockSpec((rows, HD), lambda step: (0, step)),
        compiler_params=pltpu.CompilerParams(vmem_limit_bytes=ATTEND_VMEM),
        cost_estimate=pl.CostEstimate(
            flops=heads * rows * count * HD * 8,
            bytes_accessed=2 * (count * 3 * HD + 2 * heads * rows * HD),
            transcendentals=heads * rows * count,
        ),
        name="attend",
    )(half, *queries, *fixed)


def on_device(
    n_model,
    n_pool,
    states,
    norm_gain,
    w_query,
    q_bias,
    w_key,
    w_value,
    k_bias,
    v_bias,
    w_out,
    kv_pool,
    hit_holder,
    hit_slot,
    prefix_len,
):
    my_model = lax.axis_index("mp")
    my_pool = lax.axis_index("pool")
    row_count = states.shape[1]
    suffix = row_count * n_model
    q_width = w_query.shape[1]
    q_local = q_width // HD
    kv_local = w_key.shape[1]
    kv_heads = kv_local * n_model // HD
    group_size = QH // kv_heads
    blocks_total = hit_holder.shape[1]
    block_len = kv_pool.shape[2]
    holders = n_model * n_pool
    capacity = 2 * blocks_total // holders
    sharers = HD // kv_local

    lined = n_model == LINE_MODELS

    self_holder = my_model * n_pool + my_pool
    chosen = listing(hit_holder == self_holder, capacity)
    slot_ids = jnp.sum(jnp.where(chosen, hit_slot[:, None, :], 0), -1)
    models = jnp.arange(n_model, dtype=jnp.int32)
    my_holder = hit_holder[my_pool]
    prefix_count = prefix_len[my_pool]
    block_ids = jnp.arange(blocks_total, dtype=jnp.int32)
    earlier = (my_holder[:, None] == my_holder[None, :]) & (block_ids[None, :] < block_ids[:, None])
    rank = jnp.sum(earlier.astype(jnp.int32), -1)
    normed = normalize(states[0], norm_gain)
    if lined:
        mine, others = (
            lax.dynamic_index_in_dim(slot_ids, pool, 0, keepdims=False)
            for pool in (my_pool, 1 - my_pool)
        )
        others, normed = lax.optimization_barrier((others, normed))
        pool_blocks = kv_pool[0]
        got = lax.ppermute(pick_blocks(pool_blocks, others), "pool", [(0, 1), (1, 0)])
        slots = jnp.stack([mine, jnp.arange(capacity, dtype=jnp.int32)])
        outgoing = pack_blocks((pool_blocks, got), slots, (models ^ my_model) * q_local // group_size)
        my_z, my_y = my_model // 2, my_model % 2
        near, far, arrived = gather_and_exchange(normed, outgoing, (my_z == 1) | (my_z == 2))
        arrived = [block.reshape(-1, block_len, 2 * HD) for block in arrived]
        distance = (my_holder // n_pool) ^ my_model
        where = (distance * n_pool + (my_holder % n_pool ^ my_pool)) * capacity + rank
    else:
        outgoing = pack_blocks((kv_pool[0],) * 2, slot_ids, models * q_local // group_size)
        outgoing = jnp.stack(outgoing).reshape(holders, capacity * block_len, 2 * HD)
        arrived = lax.all_to_all(outgoing, ("mp", "pool"), split_axis=0, concat_axis=0, tiled=True)
        arrived = [arrived.reshape(holders * capacity, block_len, 2 * HD)]
        where = my_holder * capacity + rank

    upper_half = (my_model // (n_model // 2)).astype(jnp.int32) if lined else jnp.int32(0)
    half_rows = suffix // 2
    order = (jnp.arange(suffix, dtype=jnp.int32) + upper_half * half_rows) % suffix
    cosine, sine = angle_tables(prefix_count + order)
    cosine, sine = jnp.concatenate([cosine, cosine], 1), jnp.concatenate([-sine, sine], 1)
    halves = [slice(0, half_rows), slice(half_rows, suffix)]
    biases = [bias.reshape(1, -1) for bias in (q_bias, k_bias, v_bias)]
    weights = (w_query, w_key, w_value)
    if lined:
        results = []
        for blocks, inner in ((near, my_z % 2), (far, upper_half)):
            starts = jnp.stack(
                [
                    2 * (inner ^ other) + (my_y ^ side)
                    for side in range(2)
                    for other in range(2)
                ]
            )
            table = [part[halves[len(results)]] for part in (cosine, sine)]
            results.append(
                project(starts.astype(jnp.int32) * row_count, blocks, weights, biases, table)
            )
        queries, new_keys, new_values, pairs = zip(*results)
        pairs = jnp.where(
            upper_half == 0, jnp.concatenate(pairs, 0), jnp.concatenate(pairs[::-1], 0)
        ).reshape(n_model, row_count, 2 * HD)
    else:
        tokens = lax.all_gather(normed, "mp", axis=0, tiled=True)
        linear, key_raw, value_raw = (
            jnp.dot(tokens, weight, preferred_element_type=jnp.float32) + bias.astype(jnp.float32)
            for weight, bias in zip(weights, biases)
        )
        cosine, sine = cosine[:, : HD // 2], sine[:, HD // 2 :]
        queries = rotate(linear.reshape(suffix, q_local, HD), cosine, sine)
        queries = queries.astype(jnp.bfloat16).transpose(1, 0, 2)
        key_raw, value_raw = key_raw.astype(jnp.bfloat16), value_raw.astype(jnp.bfloat16)
        together = [
            [first + other for other in range(sharers)] for first in range(0, n_model, sharers)
        ]
        key_whole, value_whole = (
            lax.all_gather(part, "mp", axis=1, tiled=True, axis_index_groups=together)
            for part in (key_raw, value_raw)
        )
        key_whole = rotate(key_whole.astype(jnp.float32)[:, None, :], cosine, sine)
        key_whole = key_whole.astype(jnp.bfloat16)[:, 0]
        value_ones = jnp.concatenate([value_whole, jnp.ones_like(value_whole)], 1)
        first_col = (my_model % sharers) * kv_local
        key_cols = lax.dynamic_slice_in_dim(key_whole, first_col, kv_local, 1)
        pairs = jnp.stack([key_cols, value_raw], 1).reshape(n_model, row_count, 2 * kv_local)
        queries = [queries[:, part] for part in halves]
        new_keys = [key_whole[part] for part in halves]
        new_values = [value_ones[part] for part in halves]

    pairs = lax.all_to_all(pairs, "mp", split_axis=0, concat_axis=0, tiled=True)
    arrived, new_keys, pairs = lax.optimization_barrier((arrived, list(new_keys), pairs))
    cache_rows = (
        pairs.reshape(kv_heads, sharers, row_count, 2, kv_local)
        .transpose(2, 0, 3, 1, 4)
        .reshape(1, row_count, kv_heads * 2 * HD)
    )
    prefix = order_blocks(arrived, where, prefix_count.reshape(1))

    row_step = max(row_count // ROW_CHUNKS, 16)
    chunks = row_count // row_step
    queries = [part.reshape(q_local, -1, chunks, row_step, HD) for part in queries]
    first = upper_half * (n_model // 2)
    steps = n_model // 2
    scatters, taken, sums, sent = [], [], [], []
    for chunk in range(chunks):
        queries, _ = lax.optimization_barrier((queries, sent))
        mixed = attend(upper_half.reshape(1), queries, prefix, new_keys, new_values, chunk)
        if scatters:
            mixed, _ = lax.optimization_barrier((mixed, scatters[-1].step()))
            taken[-1] += 1
        count = max(row_step, DOT_ROWS)
        share = [
            jnp.dot(
                mixed[start : start + count], w_out, preferred_element_type=jnp.float32
            ).astype(jnp.bfloat16)
            for start in range(0, mixed.shape[0], count)
        ]
        share = [part.reshape(-1, row_step, part.shape[1]) for part in share]
        way = 1 if chunk % 2 == 0 else -1
        scatters.append(RingScatter(share, n_model, my_model, first, way))
        sent = scatters[-1].step()
        taken.append(1)
    while len(sums) < chunks:
        for chunk, scatter in enumerate(scatters):
            if taken[chunk] < steps:
                sent = scatter.step(sent, sums)
                taken[chunk] += 1
            elif len(sums) == chunk:
                sums.append(scatter.finish())
    return (jnp.concatenate(sums, 0)[None], cache_rows)


def solution(mesh):
    placed = (
        P(("groups", "pool"), "mp", None),
        P(),
        P(None, "mp"),
        P("mp"),
        P(None, "mp"),
        P(None, "mp"),
        P("mp"),
        P("mp"),
        P("mp", None),
        P(("groups", "mp", "pool"), None, None, None),
        P("groups", None),
        P("groups", None),
        P("groups"),
    )
    return jax.shard_map(
        functools.partial(on_device, mesh.shape["mp"], mesh.shape["pool"]),
        mesh=mesh,
        in_specs=placed,
        out_specs=(P(("groups", "pool"), "mp", None), P(("groups", "pool"), "mp", None)),
        check_vma=False,
    )
```

```python
import functools
import math

import jax
import jax.numpy as jnp
from jax import lax
from jax.experimental import pallas as pl
from jax.experimental.pallas import tpu as pltpu
from jax.sharding import PartitionSpec as P

QH = 64
HD = 128
ROPE_BASE = 1000000.0
EPSILON = 1e-06
SCORE_SCALE = HD ** (-0.5) * math.log2(math.e)
VMEM_LIMIT = 56 * 1024 * 1024
ATTEND_VMEM = 28 * 1024 * 1024
COLUMN_CHUNKS = 2
STREAMS = 4
LINE_MODELS = 8


def angle_tables(positions):
    frequency = jnp.power(
        jnp.float32(ROPE_BASE), -2.0 * jnp.arange(HD // 2, dtype=jnp.float32) / HD
    )
    angles = positions.astype(jnp.float32)[:, None] * frequency[None, :]
    return jnp.cos(angles), jnp.sin(angles)


def rotate(vectors, cosine, sine):
    first_half = vectors[..., : HD // 2]
    second = vectors[..., HD // 2 :]
    cosine = cosine[:, None, :]
    sine = sine[:, None, :]
    return jnp.concatenate(
        [first_half * cosine - second * sine, second * cosine + first_half * sine], -1
    )


def normalize(states, gain_vec):
    values = states.astype(jnp.float32)
    inv_rms = lax.rsqrt(jnp.mean(values * values, axis=-1, keepdims=True) + EPSILON)
    return (values * inv_rms * gain_vec.astype(jnp.float32)).astype(jnp.bfloat16)


def listing(owned_mask, capacity):
    rank_order = jnp.cumsum(owned_mask.astype(jnp.int32), -1) - 1
    slot_index = jnp.arange(capacity, dtype=jnp.int32)
    return owned_mask[..., None, :] & (rank_order[..., None, :] == slot_index[:, None])


def swap(block, mask):
    return lax.ppermute(block, "mp", [(index, index ^ mask) for index in range(LINE_MODELS)])


def cross(block):
    pairs = []
    for index in range(LINE_MODELS):
        for core in range(2):
            if 2 <= index < 6:
                pairs.append((index * 2 + core, (index ^ 6) * 2 + core))
            else:
                pairs.append((index * 2 + core, index * 2 + 1 - core))
    return lax.ppermute(block, ("mp", "pool"), pairs)


def gather_and_exchange(own, outgoing, middle, project_near):
    arrived = {0: outgoing[0]}

    def after(block, *events):
        return lax.optimization_barrier((block, events))[0]

    def exchange(apart, *events):
        block = after(outgoing[apart], *events) if events else outgoing[apart]
        arrived[apart] = swap(block, apart)

    beside = swap(own, 2)
    over = cross(own)
    own_y = swap(own, 1)
    over_beside = cross(beside)
    over_passed = swap(over, 2)
    beside_y = swap(after(beside, own_y), 1)
    far_first = jnp.where(middle, over, over_passed)
    far_first_y = swap(after(far_first, beside_y), 1)
    over_beside_passed = swap(after(over_beside, outgoing[4]), 2)
    exchange(4, over_beside)
    exchange(6, over_beside)
    near = project_near([after(own, far_first), beside, own_y, beside_y])
    far_second = jnp.where(middle, over_beside, over_beside_passed)
    far_second, near, _ = lax.optimization_barrier((far_second, near, arrived[4]))
    far_second_y = swap(after(far_second, far_first_y), 1)
    exchange(2, arrived[4], far_first_y)
    exchange(5, arrived[6], far_first_y)
    exchange(7, arrived[6], far_first_y)
    exchange(3, arrived[6], far_first_y)
    exchange(1, arrived[6], far_first_y)
    far_first = after(far_first, arrived[2], arrived[6])
    far = [far_first, far_second, far_first_y, far_second_y]
    return near, far, [arrived[apart] for apart in range(LINE_MODELS)]


def project_kernel(starts_ref, *refs):
    n_blocks = starts_ref.shape[0]
    blocks, refs = refs[:n_blocks], refs[n_blocks:]
    q_weights, (k_weight_ref, v_weight_ref), refs = refs[:STREAMS], refs[STREAMS:][:2], refs[STREAMS + 2 :]
    q_bias_ref, k_bias_ref, v_bias_ref, cos_ref, sin_ref = refs[:5]
    query_ref, key_ref, value_ref, pair_ref, tokens_ref, total_ref, sems = refs[5:]
    step = pl.program_id(0)
    depth = k_weight_ref.shape[0]
    q_width = q_weights[0].shape[1]
    rows = blocks[0].shape[0]

    @pl.when(step == 0)
    def _():
        copies = [
            pltpu.make_async_copy(
                block,
                tokens_ref.at[pl.ds(pl.multiple_of(starts_ref[index], rows), rows), :],
                sems.at[index],
            )
            for index, block in enumerate(blocks)
        ]
        for copy in copies:
            copy.start()
        total_ref[...] = jnp.zeros_like(total_ref)
        for copy in copies:
            copy.wait()

    tokens = tokens_ref[:, pl.ds(pl.multiple_of(step * depth, depth), depth)]
    q_weight = jnp.concatenate([ref[...] for ref in q_weights], axis=0)
    total_ref[:, :q_width] += jnp.dot(tokens, q_weight, preferred_element_type=jnp.float32)
    both = jnp.concatenate([k_weight_ref[...], v_weight_ref[...]], axis=1)
    total_ref[:, q_width:] += jnp.dot(tokens, both, preferred_element_type=jnp.float32)

    @pl.when(step == pl.num_programs(0) - 1)
    def _():
        cosine, sine = cos_ref[...], sin_ref[...]

        def turned(vectors):
            return vectors * cosine + pltpu.roll(vectors, HD // 2, 1) * sine

        for head in range(q_width // HD):
            cols = slice(head * HD, (head + 1) * HD)
            query = total_ref[:, cols] + q_bias_ref[:, cols].astype(jnp.float32)
            query_ref[head] = turned(query).astype(jnp.bfloat16)
        key = total_ref[:, q_width : q_width + HD] + k_bias_ref[...].astype(jnp.float32)
        key = turned(key.astype(jnp.bfloat16).astype(jnp.float32)).astype(jnp.bfloat16)
        value = total_ref[:, q_width + HD :] + v_bias_ref[...].astype(jnp.float32)
        value = value.astype(jnp.bfloat16)
        key_ref[...] = key
        value_ref[:, :HD] = value
        value_ref[:, HD:] = jnp.ones_like(value)
        pair_ref[:, :HD] = key
        pair_ref[:, HD:] = value


def project(starts, blocks, weights, biases, tables):
    width = blocks[0].shape[1]
    rows = sum(block.shape[0] for block in blocks)
    depth = math.gcd(width, 1024)
    q_width = weights[0].shape[1]
    out_width = q_width + 2 * HD
    fixed = lambda array: pl.BlockSpec(array.shape, lambda step: (0,) * len(array.shape))
    in_specs = [pl.BlockSpec(memory_space=pltpu.SMEM)]
    in_specs += [pl.BlockSpec(memory_space=pl.ANY)] * len(blocks)
    in_specs += [
        pl.BlockSpec((depth // STREAMS, q_width), lambda step, part=part: (step * STREAMS + part, 0))
        for part in range(STREAMS)
    ]
    in_specs += [pl.BlockSpec((depth, HD), lambda step: (step, 0))] * 2
    in_specs += [fixed(array) for array in (*biases, *tables)]
    out_shape = (
        jax.ShapeDtypeStruct((q_width // HD, rows, HD), jnp.bfloat16),
        jax.ShapeDtypeStruct((rows, HD), jnp.bfloat16),
        jax.ShapeDtypeStruct((rows, 2 * HD), jnp.bfloat16),
        jax.ShapeDtypeStruct((rows, 2 * HD), jnp.bfloat16),
    )
    return pl.pallas_call(
        project_kernel,
        grid=(width // depth,),
        out_shape=out_shape,
        in_specs=in_specs,
        out_specs=tuple(fixed(shape) for shape in out_shape),
        scratch_shapes=[
            pltpu.VMEM((rows, width), jnp.bfloat16),
            pltpu.VMEM((rows, out_width), jnp.float32),
            pltpu.SemaphoreType.DMA((len(blocks),)),
        ],
        compiler_params=pltpu.CompilerParams(vmem_limit_bytes=VMEM_LIMIT),
        cost_estimate=pl.CostEstimate(
            flops=2 * rows * width * out_width,
            bytes_accessed=2 * width * (rows + out_width) + 4 * rows * out_width,
            transcendentals=0,
        ),
        name="project",
    )(starts, *blocks, *weights[:1] * STREAMS, *weights[1:], *biases, *tables)


class RingScatter:
    def __init__(self, shares, n_model, my_model, first, way):
        order = [m for m in range(0, n_model, 2)] + [m for m in range(n_model - 1, 0, -2)]
        self.order = order
        self.n_model = n_model
        self.way = way
        spot = jnp.array([order.index(m) for m in range(n_model)], jnp.int32)[my_model]
        self.shares, self.spot, self.first = shares, spot, first
        self.distance = {way: n_model // 2, -way: n_model // 2 - 1}
        self.moving = {}

    def share_of(self, offset):
        table = jnp.array(self.order, jnp.int32)
        owner = table[(self.spot + offset + self.n_model) % self.n_model]
        owner = (owner - self.first + self.n_model) % self.n_model
        return lax.dynamic_index_in_dim(self.shares, owner, 0, keepdims=False)

    def step(self, *before):
        ways = [way for way in (self.way, -self.way) if self.distance[way]]
        blocks = []
        for way in ways:
            block = self.share_of(way * self.distance[way])
            if way in self.moving:
                arrived = self.moving[way].astype(jnp.float32)
                block = (block.astype(jnp.float32) + arrived).astype(jnp.bfloat16)
            blocks.append(block)
            self.distance[way] -= 1
        blocks, _ = lax.optimization_barrier((blocks, (before, list(self.moving.values()))))
        for way, block in zip(ways, blocks):
            pairs = [
                (self.order[i], self.order[(i + way) % self.n_model]) for i in range(self.n_model)
            ]
            self.moving[way] = lax.ppermute(block, "mp", pairs)
        return blocks

    def finish(self):
        total = self.share_of(0).astype(jnp.float32)
        for way in (1, -1):
            total = total + self.moving[way].astype(jnp.float32)
        return total.astype(jnp.bfloat16)


def pick_kernel(slots_ref, pool_ref, out_ref):
    def place(rank, _):
        out_ref[rank] = pool_ref[slots_ref[rank]]
        return 0

    lax.fori_loop(0, slots_ref.shape[0], place, 0)


def pick_blocks(pool, slots):
    return pl.pallas_call(
        pick_kernel,
        out_shape=jax.ShapeDtypeStruct((*slots.shape, *pool.shape[1:]), pool.dtype),
        in_specs=[
            pl.BlockSpec(memory_space=pltpu.SMEM),
            pl.BlockSpec(memory_space=pltpu.VMEM),
        ],
        out_specs=pl.BlockSpec(memory_space=pltpu.VMEM),
        compiler_params=pltpu.CompilerParams(vmem_limit_bytes=ATTEND_VMEM),
        name="pick_blocks",
    )(slots, pool)


def pack_kernel(lists, slots_ref, heads_ref, *refs):
    sources, out_refs = refs[: len(lists)], refs[len(lists) :]

    def place(rank, _):
        for listed, source_ref in zip(lists, sources):
            slot = slots_ref[listed, rank]
            for dest, out_ref in enumerate(out_refs):
                first = pl.multiple_of(heads_ref[dest] * 2 * HD, 2 * HD)
                out_ref[listed, rank] = source_ref[slot, :, pl.ds(first, 2 * HD)]
        return 0

    lax.fori_loop(0, slots_ref.shape[1], place, 0)


def pack_blocks(sources, slots, heads):
    dests = heads.shape[0]
    block_len = sources[0].shape[1]
    shape = jax.ShapeDtypeStruct((*slots.shape, block_len, 2 * HD), jnp.bfloat16)
    return pl.pallas_call(
        functools.partial(pack_kernel, range(len(sources))),
        out_shape=[shape] * dests,
        in_specs=[pl.BlockSpec(memory_space=pltpu.SMEM)] * 2
        + [pl.BlockSpec(memory_space=pltpu.VMEM)] * len(sources),
        out_specs=[pl.BlockSpec(memory_space=pltpu.VMEM)] * dests,
        compiler_params=pltpu.CompilerParams(vmem_limit_bytes=ATTEND_VMEM),
        name="pack_blocks",
    )(slots, heads, *sources)


def order_kernel(length_ref, where_ref, *refs):
    *arrived_refs, key_ref, value_ref, held_ref, sems = refs
    block_len = held_ref.shape[1]
    copies = []
    begin = 0
    for index, source in enumerate(arrived_refs):
        end = begin + source.shape[0]
        copies.append(pltpu.make_async_copy(source, held_ref.at[begin:end], sems.at[index]))
        begin = end
    for copy in copies:
        copy.start()
    for copy in copies:
        copy.wait()
    length = length_ref[0]
    first = held_ref[where_ref[0]][:1, :HD].astype(jnp.float32)
    row = lax.broadcasted_iota(jnp.int32, (block_len, HD), 0)

    def place(block_id, _):
        block = held_ref[where_ref[block_id]].astype(jnp.float32)
        start = pl.multiple_of(block_id * block_len, block_len)
        seen = row + start < length
        rows = pl.ds(start, block_len)
        key_ref[rows, :] = jnp.where(seen, block[:, :HD], first).astype(jnp.bfloat16)
        value_ref[rows, :HD] = jnp.where(seen, block[:, HD:], 0.0).astype(jnp.bfloat16)
        value_ref[rows, HD:] = jnp.where(seen, 1.0, 0.0).astype(jnp.bfloat16)
        return 0

    lax.fori_loop(0, where_ref.shape[0], place, 0, unroll=8)


def order_blocks(arrived, where, length):
    count = sum(array.shape[-3] for array in arrived)
    block_len = arrived[0].shape[-2]
    tokens = where.shape[0] * block_len
    return pl.pallas_call(
        order_kernel,
        out_shape=(
            jax.ShapeDtypeStruct((tokens, HD), jnp.bfloat16),
            jax.ShapeDtypeStruct((tokens, 2 * HD), jnp.bfloat16),
        ),
        in_specs=[pl.BlockSpec(memory_space=pltpu.SMEM)] * 2
        + [pl.BlockSpec(memory_space=pl.ANY)] * len(arrived),
        out_specs=(
            pl.BlockSpec(memory_space=pltpu.VMEM),
            pl.BlockSpec(memory_space=pltpu.VMEM),
        ),
        scratch_shapes=[
            pltpu.VMEM((count, block_len, 2 * HD), jnp.bfloat16),
            pltpu.SemaphoreType.DMA((len(arrived),)),
        ],
        compiler_params=pltpu.CompilerParams(vmem_limit_bytes=ATTEND_VMEM),
        name="order_blocks",
    )(length, where, *arrived)


def dot_keys(queries, keys):
    return lax.dot_general(
        queries, keys, (((1,), (1,)), ((), ())), preferred_element_type=jnp.float32
    )


def attend_kernel(span, half_ref, *refs):
    query_refs, (key_ref, value_ref), new_key_refs, new_value_refs, out_ref = (
        refs[:2],
        refs[2:4],
        refs[4:6],
        refs[6:8],
        refs[8],
    )
    rows = out_ref.shape[0]
    half = rows // 2
    queries = jnp.concatenate([ref[0] for ref in query_refs], 0)
    spans = key_ref.shape[0] // span
    turn = half_ref[0] * half
    token = lax.rem(lax.broadcasted_iota(jnp.int32, (rows, half), 0) + turn, rows)
    column = lax.broadcasted_iota(jnp.int32, (rows, half), 1)
    parts = []
    for side, ref in enumerate(new_key_refs):
        causal = column + lax.rem(turn + side * half, rows) <= token
        parts.append(jnp.where(causal, dot_keys(queries, ref[...]), -jnp.inf))
    scores = jnp.concatenate(parts, 1)
    peak = jnp.max(scores, axis=1, keepdims=True)
    total = None
    values = jnp.concatenate([ref[...] for ref in new_value_refs], 0)
    for index in range(spans + 1):
        if index < spans:
            next_scores = dot_keys(queries, key_ref[index * span : (index + 1) * span, :])
            next_peak = jnp.maximum(peak, jnp.max(next_scores, axis=1, keepdims=True))
        weights = jnp.exp2((scores - peak) * SCORE_SCALE).astype(jnp.bfloat16)
        product = jnp.dot(weights, values, preferred_element_type=jnp.float32)
        total = product if total is None else total + product
        if index < spans:
            total = total * jnp.exp2((peak - next_peak) * SCORE_SCALE)
            scores, peak = next_scores, next_peak
            values = value_ref[index * span : (index + 1) * span, :]
    out_ref[...] = (total[:, :HD] / total[:, HD:]).astype(jnp.bfloat16)


def attend(half, queries, prefix, new_keys, new_values):
    heads = queries[0].shape[0]
    rows = 2 * new_keys[0].shape[0]
    span = math.gcd(prefix[0].shape[0], 1024)
    whole = lambda array: pl.BlockSpec(array.shape, lambda step: (0, 0))
    count = prefix[0].shape[0] + rows
    query_spec = pl.BlockSpec((1, rows // 2, HD), lambda step: (step, 0, 0))
    fixed = (*prefix, *new_keys, *new_values)
    return pl.pallas_call(
        functools.partial(attend_kernel, span),
        grid=(heads,),
        out_shape=jax.ShapeDtypeStruct((rows, heads * HD), jnp.bfloat16),
        in_specs=[pl.BlockSpec(memory_space=pltpu.SMEM), query_spec, query_spec]
        + [whole(array) for array in fixed],
        out_specs=pl.BlockSpec((rows, HD), lambda step: (0, step)),
        compiler_params=pltpu.CompilerParams(vmem_limit_bytes=ATTEND_VMEM),
        cost_estimate=pl.CostEstimate(
            flops=heads * rows * count * HD * 8,
            bytes_accessed=2 * (count * 3 * HD + 2 * heads * rows * HD),
            transcendentals=heads * rows * count,
        ),
        name="attend",
    )(half, *queries, *fixed)


def on_device(
    n_model,
    n_pool,
    states,
    norm_gain,
    w_query,
    q_bias,
    w_key,
    w_value,
    k_bias,
    v_bias,
    w_out,
    kv_pool,
    hit_holder,
    hit_slot,
    prefix_len,
):
    my_model = lax.axis_index("mp")
    my_pool = lax.axis_index("pool")
    row_count = states.shape[1]
    suffix = row_count * n_model
    q_width = w_query.shape[1]
    q_local = q_width // HD
    kv_local = w_key.shape[1]
    kv_heads = kv_local * n_model // HD
    group_size = QH // kv_heads
    blocks_total = hit_holder.shape[1]
    block_len = kv_pool.shape[2]
    holders = n_model * n_pool
    capacity = 2 * blocks_total // holders
    sharers = HD // kv_local

    lined = n_model == LINE_MODELS

    self_holder = my_model * n_pool + my_pool
    chosen = listing(hit_holder == self_holder, capacity)
    slot_ids = jnp.sum(jnp.where(chosen, hit_slot[:, None, :], 0), -1)
    models = jnp.arange(n_model, dtype=jnp.int32)
    my_holder = hit_holder[my_pool]
    prefix_count = prefix_len[my_pool]
    block_ids = jnp.arange(blocks_total, dtype=jnp.int32)
    earlier = (my_holder[:, None] == my_holder[None, :]) & (block_ids[None, :] < block_ids[:, None])
    rank = jnp.sum(earlier.astype(jnp.int32), -1)
    normed = normalize(states[0], norm_gain)
    upper_half = (my_model // (n_model // 2)).astype(jnp.int32) if lined else jnp.int32(0)
    half_rows = suffix // 2
    order = (jnp.arange(suffix, dtype=jnp.int32) + upper_half * half_rows) % suffix
    cosine, sine = angle_tables(prefix_count + order)
    cosine, sine = jnp.concatenate([cosine, cosine], 1), jnp.concatenate([-sine, sine], 1)
    halves = [slice(0, half_rows), slice(half_rows, suffix)]
    biases = [bias.reshape(1, -1) for bias in (q_bias, k_bias, v_bias)]
    weights = (w_query, w_key, w_value)
    if lined:
        mine, others = (
            lax.dynamic_index_in_dim(slot_ids, pool, 0, keepdims=False)
            for pool in (my_pool, 1 - my_pool)
        )
        pool_blocks = kv_pool[0]
        got = lax.ppermute(pick_blocks(pool_blocks, others), "pool", [(0, 1), (1, 0)])
        slots = jnp.stack([mine, jnp.arange(capacity, dtype=jnp.int32)])
        outgoing = pack_blocks((pool_blocks, got), slots, (models ^ my_model) * q_local // group_size)
        my_z, my_y = my_model // 2, my_model % 2

        def project_half(blocks, inner, part):
            starts = jnp.stack(
                [2 * (inner ^ other) + (my_y ^ side) for side in range(2) for other in range(2)]
            )
            table = [values[halves[part]] for values in (cosine, sine)]
            return project(starts.astype(jnp.int32) * row_count, blocks, weights, biases, table)

        near, far, arrived = gather_and_exchange(
            normed,
            outgoing,
            (my_z == 1) | (my_z == 2),
            lambda blocks: project_half(blocks, my_z % 2, 0),
        )
        results = near, project_half(far, upper_half, 1)
        arrived = [block.reshape(-1, block_len, 2 * HD) for block in arrived]
        distance = (my_holder // n_pool) ^ my_model
        where = (distance * n_pool + (my_holder % n_pool ^ my_pool)) * capacity + rank
    else:
        outgoing = pack_blocks((kv_pool[0],) * 2, slot_ids, models * q_local // group_size)
        outgoing = jnp.stack(outgoing).reshape(holders, capacity * block_len, 2 * HD)
        arrived = lax.all_to_all(outgoing, ("mp", "pool"), split_axis=0, concat_axis=0, tiled=True)
        arrived = [arrived.reshape(holders * capacity, block_len, 2 * HD)]
        where = my_holder * capacity + rank

    if lined:
        queries, new_keys, new_values, pairs = zip(*results)
        pairs = jnp.where(
            upper_half == 0, jnp.concatenate(pairs, 0), jnp.concatenate(pairs[::-1], 0)
        ).reshape(n_model, row_count, 2 * HD)
    else:
        tokens = lax.all_gather(normed, "mp", axis=0, tiled=True)
        linear, key_raw, value_raw = (
            jnp.dot(tokens, weight, preferred_element_type=jnp.float32) + bias.astype(jnp.float32)
            for weight, bias in zip(weights, biases)
        )
        cosine, sine = cosine[:, : HD // 2], sine[:, HD // 2 :]
        queries = rotate(linear.reshape(suffix, q_local, HD), cosine, sine)
        queries = queries.astype(jnp.bfloat16).transpose(1, 0, 2)
        key_raw, value_raw = key_raw.astype(jnp.bfloat16), value_raw.astype(jnp.bfloat16)
        together = [
            [first + other for other in range(sharers)] for first in range(0, n_model, sharers)
        ]
        key_whole, value_whole = (
            lax.all_gather(part, "mp", axis=1, tiled=True, axis_index_groups=together)
            for part in (key_raw, value_raw)
        )
        key_whole = rotate(key_whole.astype(jnp.float32)[:, None, :], cosine, sine)
        key_whole = key_whole.astype(jnp.bfloat16)[:, 0]
        value_ones = jnp.concatenate([value_whole, jnp.ones_like(value_whole)], 1)
        first_col = (my_model % sharers) * kv_local
        key_cols = lax.dynamic_slice_in_dim(key_whole, first_col, kv_local, 1)
        pairs = jnp.stack([key_cols, value_raw], 1).reshape(n_model, row_count, 2 * kv_local)
        queries = [queries[:, part] for part in halves]
        new_keys = [key_whole[part] for part in halves]
        new_values = [value_ones[part] for part in halves]

    pairs = lax.all_to_all(pairs, "mp", split_axis=0, concat_axis=0, tiled=True)
    arrived, new_keys, pairs = lax.optimization_barrier((arrived, list(new_keys), pairs))
    cache_rows = (
        pairs.reshape(kv_heads, sharers, row_count, 2, kv_local)
        .transpose(2, 0, 3, 1, 4)
        .reshape(1, row_count, kv_heads * 2 * HD)
    )
    prefix = order_blocks(arrived, where, prefix_count.reshape(1))
    mixed = attend(upper_half.reshape(1), queries, prefix, new_keys, new_values)
    width = w_out.shape[1] // COLUMN_CHUNKS
    shares = [
        jnp.dot(
            mixed,
            w_out[:, chunk * width : (chunk + 1) * width],
            preferred_element_type=jnp.float32,
        ).astype(jnp.bfloat16)
        for chunk in range(COLUMN_CHUNKS)
    ]

    first = upper_half * (n_model // 2)
    scatters = [
        RingScatter(
            share.reshape(n_model, row_count, -1),
            n_model,
            my_model,
            first,
            1 if chunk % 2 == 0 else -1,
        )
        for chunk, share in enumerate(shares)
    ]
    sent, sums = [], []
    steps = n_model // 2
    for step in range(steps):
        for scatter in scatters:
            sent = scatter.step(sent, sums)
            if step == steps - 1:
                sums.append(scatter.finish())
    return (jnp.concatenate(sums, 1)[None], cache_rows)


def solution(mesh):
    placed = (
        P(("groups", "pool"), "mp", None),
        P(),
        P(None, "mp"),
        P("mp"),
        P(None, "mp"),
        P(None, "mp"),
        P("mp"),
        P("mp"),
        P("mp", None),
        P(("groups", "mp", "pool"), None, None, None),
        P("groups", None),
        P("groups", None),
        P("groups"),
    )
    return jax.shard_map(
        functools.partial(on_device, mesh.shape["mp"], mesh.shape["pool"]),
        mesh=mesh,
        in_specs=placed,
        out_specs=(P(("groups", "pool"), "mp", None), P(("groups", "pool"), "mp", None)),
        check_vma=False,
    )
```

```python
import functools
import math

import jax
import jax.numpy as jnp
from jax import lax
from jax.experimental import pallas as pl
from jax.experimental.pallas import tpu as pltpu
from jax.sharding import PartitionSpec as P

QH = 64
HD = 128
ROPE_BASE = 1000000.0
EPSILON = 1e-06
SCORE_SCALE = HD ** (-0.5) * math.log2(math.e)
VMEM_LIMIT = 56 * 1024 * 1024
ATTEND_VMEM = 20 * 1024 * 1024
COLUMN_CHUNKS = 2
STREAMS = 4
LINE_MODELS = 8


def angle_tables(positions):
    frequency = jnp.power(
        jnp.float32(ROPE_BASE), -2.0 * jnp.arange(HD // 2, dtype=jnp.float32) / HD
    )
    angles = positions.astype(jnp.float32)[:, None] * frequency[None, :]
    return jnp.cos(angles), jnp.sin(angles)


def rotate(vectors, cosine, sine):
    first_half = vectors[..., : HD // 2]
    second = vectors[..., HD // 2 :]
    cosine = cosine[:, None, :]
    sine = sine[:, None, :]
    return jnp.concatenate(
        [first_half * cosine - second * sine, second * cosine + first_half * sine], -1
    )


def normalize(states, gain_vec):
    values = states.astype(jnp.float32)
    inv_rms = lax.rsqrt(jnp.mean(values * values, axis=-1, keepdims=True) + EPSILON)
    return (values * inv_rms * gain_vec.astype(jnp.float32)).astype(jnp.bfloat16)


def listing(owned_mask, capacity):
    rank_order = jnp.cumsum(owned_mask.astype(jnp.int32), -1) - 1
    slot_index = jnp.arange(capacity, dtype=jnp.int32)
    return owned_mask[..., None, :] & (rank_order[..., None, :] == slot_index[:, None])


def swap(block, mask):
    return lax.ppermute(block, "mp", [(index, index ^ mask) for index in range(LINE_MODELS)])


def cross(block):
    pairs = []
    for index in range(LINE_MODELS):
        for core in range(2):
            if 2 <= index < 6:
                pairs.append((index * 2 + core, (index ^ 6) * 2 + core))
            else:
                pairs.append((index * 2 + core, index * 2 + 1 - core))
    return lax.ppermute(block, ("mp", "pool"), pairs)


def gather_and_exchange(own, outgoing, middle, project_near):
    arrived = {0: outgoing[0]}

    def after(block, *events):
        return lax.optimization_barrier((block, events))[0]

    def exchange(apart, *events):
        block = after(outgoing[apart], *events) if events else outgoing[apart]
        arrived[apart] = swap(block, apart)

    beside = swap(own, 2)
    over = cross(own)
    own_y = swap(own, 1)
    over_beside = cross(beside)
    over_passed = swap(over, 2)
    beside_y = swap(after(beside, own_y), 1)
    far_first = jnp.where(middle, over, over_passed)
    far_first_y = swap(after(far_first, beside_y), 1)
    over_beside_passed = swap(after(over_beside, outgoing[4]), 2)
    exchange(4, over_beside)
    exchange(6, over_beside)
    exchange(1, far_first_y)
    exchange(3, far_first_y)
    near = project_near([after(own, far_first), beside, own_y, beside_y])
    far_second = jnp.where(middle, over_beside, over_beside_passed)
    first_sent = [arrived[apart] for apart in (4, 6, 1, 3)]
    far_second, near, _ = lax.optimization_barrier((far_second, near, first_sent))
    far_second_y = swap(after(far_second, far_first_y), 1)
    for apart in (5, 7, 2):
        exchange(apart, arrived[4], arrived[6])
    far = [far_first, far_second, far_first_y, far_second_y]
    return near, far, [arrived[apart] for apart in range(LINE_MODELS)]


def project_kernel(starts_ref, *refs):
    n_blocks = starts_ref.shape[0]
    blocks, refs = refs[:n_blocks], refs[n_blocks:]
    q_weights, (k_weight_ref, v_weight_ref), refs = refs[:STREAMS], refs[STREAMS:][:2], refs[STREAMS + 2 :]
    q_bias_ref, k_bias_ref, v_bias_ref, cos_ref, sin_ref = refs[:5]
    query_ref, key_ref, value_ref, pair_ref, tokens_ref, total_ref, sems = refs[5:]
    step = pl.program_id(0)
    depth = k_weight_ref.shape[0]
    q_width = q_weights[0].shape[1]
    rows = blocks[0].shape[0]

    @pl.when(step == 0)
    def _():
        copies = [
            pltpu.make_async_copy(
                block,
                tokens_ref.at[pl.ds(pl.multiple_of(starts_ref[index], rows), rows), :],
                sems.at[index],
            )
            for index, block in enumerate(blocks)
        ]
        for copy in copies:
            copy.start()
        total_ref[...] = jnp.zeros_like(total_ref)
        for copy in copies:
            copy.wait()

    tokens = tokens_ref[:, pl.ds(pl.multiple_of(step * depth, depth), depth)]
    q_weight = jnp.concatenate([ref[...] for ref in q_weights], axis=0)
    total_ref[:, :q_width] += jnp.dot(tokens, q_weight, preferred_element_type=jnp.float32)
    both = jnp.concatenate([k_weight_ref[...], v_weight_ref[...]], axis=1)
    total_ref[:, q_width:] += jnp.dot(tokens, both, preferred_element_type=jnp.float32)

    @pl.when(step == pl.num_programs(0) - 1)
    def _():
        cosine, sine = cos_ref[...], sin_ref[...]

        def turned(vectors):
            return vectors * cosine + pltpu.roll(vectors, HD // 2, 1) * sine

        for head in range(q_width // HD):
            cols = slice(head * HD, (head + 1) * HD)
            query = total_ref[:, cols] + q_bias_ref[:, cols].astype(jnp.float32)
            query_ref[head] = turned(query).astype(jnp.bfloat16)
        key = total_ref[:, q_width : q_width + HD] + k_bias_ref[...].astype(jnp.float32)
        key = turned(key.astype(jnp.bfloat16).astype(jnp.float32)).astype(jnp.bfloat16)
        value = total_ref[:, q_width + HD :] + v_bias_ref[...].astype(jnp.float32)
        value = value.astype(jnp.bfloat16)
        key_ref[...] = key
        value_ref[:, :HD] = value
        value_ref[:, HD:] = jnp.ones_like(value)
        pair_ref[:, :HD] = key
        pair_ref[:, HD:] = value


def project(starts, blocks, weights, biases, tables):
    width = blocks[0].shape[1]
    rows = sum(block.shape[0] for block in blocks)
    depth = math.gcd(width, 1024)
    q_width = weights[0].shape[1]
    out_width = q_width + 2 * HD
    fixed = lambda array: pl.BlockSpec(array.shape, lambda step: (0,) * len(array.shape))
    in_specs = [pl.BlockSpec(memory_space=pltpu.SMEM)]
    in_specs += [pl.BlockSpec(memory_space=pl.ANY)] * len(blocks)
    in_specs += [
        pl.BlockSpec((depth // STREAMS, q_width), lambda step, part=part: (step * STREAMS + part, 0))
        for part in range(STREAMS)
    ]
    in_specs += [pl.BlockSpec((depth, HD), lambda step: (step, 0))] * 2
    in_specs += [fixed(array) for array in (*biases, *tables)]
    out_shape = (
        jax.ShapeDtypeStruct((q_width // HD, rows, HD), jnp.bfloat16),
        jax.ShapeDtypeStruct((rows, HD), jnp.bfloat16),
        jax.ShapeDtypeStruct((rows, 2 * HD), jnp.bfloat16),
        jax.ShapeDtypeStruct((rows, 2 * HD), jnp.bfloat16),
    )
    return pl.pallas_call(
        project_kernel,
        grid=(width // depth,),
        out_shape=out_shape,
        in_specs=in_specs,
        out_specs=tuple(fixed(shape) for shape in out_shape),
        scratch_shapes=[
            pltpu.VMEM((rows, width), jnp.bfloat16),
            pltpu.VMEM((rows, out_width), jnp.float32),
            pltpu.SemaphoreType.DMA((len(blocks),)),
        ],
        compiler_params=pltpu.CompilerParams(vmem_limit_bytes=VMEM_LIMIT),
        cost_estimate=pl.CostEstimate(
            flops=2 * rows * width * out_width,
            bytes_accessed=2 * width * (rows + out_width) + 4 * rows * out_width,
            transcendentals=0,
        ),
        name="project",
    )(starts, *blocks, *weights[:1] * STREAMS, *weights[1:], *biases, *tables)


class RingScatter:
    def __init__(self, shares, n_model, my_model, first, way):
        order = [m for m in range(0, n_model, 2)] + [m for m in range(n_model - 1, 0, -2)]
        self.order = order
        self.n_model = n_model
        self.way = way
        spot = jnp.array([order.index(m) for m in range(n_model)], jnp.int32)[my_model]
        self.shares, self.spot, self.first = shares, spot, first
        self.distance = {way: n_model // 2, -way: n_model // 2 - 1}
        self.moving = {}

    def share_of(self, offset):
        table = jnp.array(self.order, jnp.int32)
        owner = table[(self.spot + offset + self.n_model) % self.n_model]
        owner = (owner - self.first + self.n_model) % self.n_model
        return lax.dynamic_index_in_dim(self.shares, owner, 0, keepdims=False)

    def step(self, *before):
        ways = [way for way in (self.way, -self.way) if self.distance[way]]
        blocks = []
        for way in ways:
            block = self.share_of(way * self.distance[way])
            if way in self.moving:
                arrived = self.moving[way].astype(jnp.float32)
                block = (block.astype(jnp.float32) + arrived).astype(jnp.bfloat16)
            blocks.append(block)
            self.distance[way] -= 1
        blocks, _ = lax.optimization_barrier((blocks, (before, list(self.moving.values()))))
        for way, block in zip(ways, blocks):
            pairs = [
                (self.order[i], self.order[(i + way) % self.n_model]) for i in range(self.n_model)
            ]
            self.moving[way] = lax.ppermute(block, "mp", pairs)
        return blocks

    def finish(self):
        total = self.share_of(0).astype(jnp.float32)
        for way in (1, -1):
            total = total + self.moving[way].astype(jnp.float32)
        return total.astype(jnp.bfloat16)


def pick_kernel(slots_ref, pool_ref, out_ref):
    def place(rank, _):
        out_ref[rank] = pool_ref[slots_ref[rank]]
        return 0

    lax.fori_loop(0, slots_ref.shape[0], place, 0)


def pick_blocks(pool, slots):
    return pl.pallas_call(
        pick_kernel,
        out_shape=jax.ShapeDtypeStruct((*slots.shape, *pool.shape[1:]), pool.dtype),
        in_specs=[
            pl.BlockSpec(memory_space=pltpu.SMEM),
            pl.BlockSpec(memory_space=pltpu.VMEM),
        ],
        out_specs=pl.BlockSpec(memory_space=pltpu.VMEM),
        compiler_params=pltpu.CompilerParams(vmem_limit_bytes=ATTEND_VMEM),
        name="pick_blocks",
    )(slots, pool)


def pack_kernel(lists, slots_ref, heads_ref, *refs):
    sources, out_refs = refs[: len(lists)], refs[len(lists) :]

    def place(rank, _):
        for listed, source_ref in zip(lists, sources):
            slot = slots_ref[listed, rank]
            for dest, out_ref in enumerate(out_refs):
                first = pl.multiple_of(heads_ref[dest] * 2 * HD, 2 * HD)
                out_ref[listed, rank] = source_ref[slot, :, pl.ds(first, 2 * HD)]
        return 0

    lax.fori_loop(0, slots_ref.shape[1], place, 0)


def pack_blocks(sources, slots, heads):
    dests = heads.shape[0]
    block_len = sources[0].shape[1]
    shape = jax.ShapeDtypeStruct((*slots.shape, block_len, 2 * HD), jnp.bfloat16)
    return pl.pallas_call(
        functools.partial(pack_kernel, range(len(sources))),
        out_shape=[shape] * dests,
        in_specs=[pl.BlockSpec(memory_space=pltpu.SMEM)] * 2
        + [pl.BlockSpec(memory_space=pltpu.VMEM)] * len(sources),
        out_specs=[pl.BlockSpec(memory_space=pltpu.VMEM)] * dests,
        compiler_params=pltpu.CompilerParams(vmem_limit_bytes=ATTEND_VMEM),
        name="pack_blocks",
    )(slots, heads, *sources)


def order_kernel(length_ref, where_ref, *refs):
    *arrived_refs, key_ref, value_ref, held_ref, sems = refs
    block_len = held_ref.shape[1]
    copies = []
    begin = 0
    for index, source in enumerate(arrived_refs):
        end = begin + source.shape[0]
        copies.append(pltpu.make_async_copy(source, held_ref.at[begin:end], sems.at[index]))
        begin = end
    for copy in copies:
        copy.start()
    for copy in copies:
        copy.wait()
    length = length_ref[0]
    first = held_ref[where_ref[0]][:1, :HD].astype(jnp.float32)
    row = lax.broadcasted_iota(jnp.int32, (block_len, HD), 0)

    def place(block_id, _):
        block = held_ref[where_ref[block_id]].astype(jnp.float32)
        start = pl.multiple_of(block_id * block_len, block_len)
        seen = row + start < length
        rows = pl.ds(start, block_len)
        key_ref[rows, :] = jnp.where(seen, block[:, :HD], first).astype(jnp.bfloat16)
        value_ref[rows, :HD] = jnp.where(seen, block[:, HD:], 0.0).astype(jnp.bfloat16)
        value_ref[rows, HD:] = jnp.where(seen, 1.0, 0.0).astype(jnp.bfloat16)
        return 0

    lax.fori_loop(0, where_ref.shape[0], place, 0, unroll=8)


def order_blocks(arrived, where, length):
    count = sum(array.shape[-3] for array in arrived)
    block_len = arrived[0].shape[-2]
    tokens = where.shape[0] * block_len
    return pl.pallas_call(
        order_kernel,
        out_shape=(
            jax.ShapeDtypeStruct((tokens, HD), jnp.bfloat16),
            jax.ShapeDtypeStruct((tokens, 2 * HD), jnp.bfloat16),
        ),
        in_specs=[pl.BlockSpec(memory_space=pltpu.SMEM)] * 2
        + [pl.BlockSpec(memory_space=pl.ANY)] * len(arrived),
        out_specs=(
            pl.BlockSpec(memory_space=pltpu.VMEM),
            pl.BlockSpec(memory_space=pltpu.VMEM),
        ),
        scratch_shapes=[
            pltpu.VMEM((count, block_len, 2 * HD), jnp.bfloat16),
            pltpu.SemaphoreType.DMA((len(arrived),)),
        ],
        compiler_params=pltpu.CompilerParams(vmem_limit_bytes=ATTEND_VMEM),
        name="order_blocks",
    )(length, where, *arrived)


def dot_keys(queries, keys):
    return lax.dot_general(
        queries, keys, (((1,), (1,)), ((), ())), preferred_element_type=jnp.float32
    )


def attend_kernel(span, half_ref, *refs):
    query_refs, (key_ref, value_ref), new_key_refs, new_value_refs, out_ref = (
        refs[:2],
        refs[2:4],
        refs[4:6],
        refs[6:8],
        refs[8],
    )
    rows = out_ref.shape[0]
    half = rows // 2
    queries = jnp.concatenate([ref[0] for ref in query_refs], 0)
    spans = key_ref.shape[0] // span
    turn = half_ref[0] * half
    token = lax.rem(lax.broadcasted_iota(jnp.int32, (rows, half), 0) + turn, rows)
    column = lax.broadcasted_iota(jnp.int32, (rows, half), 1)
    parts = []
    for side, ref in enumerate(new_key_refs):
        causal = column + lax.rem(turn + side * half, rows) <= token
        parts.append(jnp.where(causal, dot_keys(queries, ref[...]), -jnp.inf))
    scores = jnp.concatenate(parts, 1)
    peak = jnp.max(scores, axis=1, keepdims=True)
    total = None
    values = jnp.concatenate([ref[...] for ref in new_value_refs], 0)
    for index in range(spans + 1):
        if index < spans:
            next_scores = dot_keys(queries, key_ref[index * span : (index + 1) * span, :])
            next_peak = jnp.maximum(peak, jnp.max(next_scores, axis=1, keepdims=True))
        weights = jnp.exp2((scores - peak) * SCORE_SCALE).astype(jnp.bfloat16)
        product = jnp.dot(weights, values, preferred_element_type=jnp.float32)
        total = product if total is None else total + product
        if index < spans:
            total = total * jnp.exp2((peak - next_peak) * SCORE_SCALE)
            scores, peak = next_scores, next_peak
            values = value_ref[index * span : (index + 1) * span, :]
    out_ref[...] = (total[:, :HD] / total[:, HD:]).astype(jnp.bfloat16)


def attend(half, queries, prefix, new_keys, new_values):
    heads = queries[0].shape[0]
    rows = 2 * new_keys[0].shape[0]
    span = math.gcd(prefix[0].shape[0], 1024)
    whole = lambda array: pl.BlockSpec(array.shape, lambda step: (0, 0))
    count = prefix[0].shape[0] + rows
    query_spec = pl.BlockSpec((1, rows // 2, HD), lambda step: (step, 0, 0))
    fixed = (*prefix, *new_keys, *new_values)
    return pl.pallas_call(
        functools.partial(attend_kernel, span),
        grid=(heads,),
        out_shape=jax.ShapeDtypeStruct((rows, heads * HD), jnp.bfloat16),
        in_specs=[pl.BlockSpec(memory_space=pltpu.SMEM), query_spec, query_spec]
        + [whole(array) for array in fixed],
        out_specs=pl.BlockSpec((rows, HD), lambda step: (0, step)),
        compiler_params=pltpu.CompilerParams(vmem_limit_bytes=ATTEND_VMEM),
        cost_estimate=pl.CostEstimate(
            flops=heads * rows * count * HD * 8,
            bytes_accessed=2 * (count * 3 * HD + 2 * heads * rows * HD),
            transcendentals=heads * rows * count,
        ),
        name="attend",
    )(half, *queries, *fixed)


def on_device(
    n_model,
    n_pool,
    states,
    norm_gain,
    w_query,
    q_bias,
    w_key,
    w_value,
    k_bias,
    v_bias,
    w_out,
    kv_pool,
    hit_holder,
    hit_slot,
    prefix_len,
):
    my_model = lax.axis_index("mp")
    my_pool = lax.axis_index("pool")
    row_count = states.shape[1]
    suffix = row_count * n_model
    q_width = w_query.shape[1]
    q_local = q_width // HD
    kv_local = w_key.shape[1]
    kv_heads = kv_local * n_model // HD
    group_size = QH // kv_heads
    blocks_total = hit_holder.shape[1]
    block_len = kv_pool.shape[2]
    holders = n_model * n_pool
    capacity = 2 * blocks_total // holders
    sharers = HD // kv_local

    lined = n_model == LINE_MODELS

    self_holder = my_model * n_pool + my_pool
    chosen = listing(hit_holder == self_holder, capacity)
    slot_ids = jnp.sum(jnp.where(chosen, hit_slot[:, None, :], 0), -1)
    models = jnp.arange(n_model, dtype=jnp.int32)
    my_holder = hit_holder[my_pool]
    prefix_count = prefix_len[my_pool]
    block_ids = jnp.arange(blocks_total, dtype=jnp.int32)
    earlier = (my_holder[:, None] == my_holder[None, :]) & (block_ids[None, :] < block_ids[:, None])
    rank = jnp.sum(earlier.astype(jnp.int32), -1)
    normed = normalize(states[0], norm_gain)
    upper_half = (my_model // (n_model // 2)).astype(jnp.int32) if lined else jnp.int32(0)
    half_rows = suffix // 2
    order = (jnp.arange(suffix, dtype=jnp.int32) + upper_half * half_rows) % suffix
    cosine, sine = angle_tables(prefix_count + order)
    cosine, sine = jnp.concatenate([cosine, cosine], 1), jnp.concatenate([-sine, sine], 1)
    halves = [slice(0, half_rows), slice(half_rows, suffix)]
    biases = [bias.reshape(1, -1) for bias in (q_bias, k_bias, v_bias)]
    weights = (w_query, w_key, w_value)
    if lined:
        mine, others = (
            lax.dynamic_index_in_dim(slot_ids, pool, 0, keepdims=False)
            for pool in (my_pool, 1 - my_pool)
        )
        pool_blocks = kv_pool[0]
        got = lax.ppermute(pick_blocks(pool_blocks, others), "pool", [(0, 1), (1, 0)])
        slots = jnp.stack([mine, jnp.arange(capacity, dtype=jnp.int32)])
        outgoing = pack_blocks((pool_blocks, got), slots, (models ^ my_model) * q_local // group_size)
        my_z, my_y = my_model // 2, my_model % 2

        def project_half(blocks, inner, part):
            starts = jnp.stack(
                [2 * (inner ^ other) + (my_y ^ side) for side in range(2) for other in range(2)]
            )
            table = [values[halves[part]] for values in (cosine, sine)]
            return project(starts.astype(jnp.int32) * row_count, blocks, weights, biases, table)

        near, far, arrived = gather_and_exchange(
            normed,
            outgoing,
            (my_z == 1) | (my_z == 2),
            lambda blocks: project_half(blocks, my_z % 2, 0),
        )
        results = near, project_half(far, upper_half, 1)
        arrived = [block.reshape(-1, block_len, 2 * HD) for block in arrived]
        distance = (my_holder // n_pool) ^ my_model
        where = (distance * n_pool + (my_holder % n_pool ^ my_pool)) * capacity + rank
    else:
        outgoing = pack_blocks((kv_pool[0],) * 2, slot_ids, models * q_local // group_size)
        outgoing = jnp.stack(outgoing).reshape(holders, capacity * block_len, 2 * HD)
        arrived = lax.all_to_all(outgoing, ("mp", "pool"), split_axis=0, concat_axis=0, tiled=True)
        arrived = [arrived.reshape(holders * capacity, block_len, 2 * HD)]
        where = my_holder * capacity + rank

    if lined:
        queries, new_keys, new_values, pairs = zip(*results)
        pairs = jnp.where(
            upper_half == 0, jnp.concatenate(pairs, 0), jnp.concatenate(pairs[::-1], 0)
        ).reshape(n_model, row_count, 2 * HD)
    else:
        tokens = lax.all_gather(normed, "mp", axis=0, tiled=True)
        linear, key_raw, value_raw = (
            jnp.dot(tokens, weight, preferred_element_type=jnp.float32) + bias.astype(jnp.float32)
            for weight, bias in zip(weights, biases)
        )
        cosine, sine = cosine[:, : HD // 2], sine[:, HD // 2 :]
        queries = rotate(linear.reshape(suffix, q_local, HD), cosine, sine)
        queries = queries.astype(jnp.bfloat16).transpose(1, 0, 2)
        key_raw, value_raw = key_raw.astype(jnp.bfloat16), value_raw.astype(jnp.bfloat16)
        together = [
            [first + other for other in range(sharers)] for first in range(0, n_model, sharers)
        ]
        key_whole, value_whole = (
            lax.all_gather(part, "mp", axis=1, tiled=True, axis_index_groups=together)
            for part in (key_raw, value_raw)
        )
        key_whole = rotate(key_whole.astype(jnp.float32)[:, None, :], cosine, sine)
        key_whole = key_whole.astype(jnp.bfloat16)[:, 0]
        value_ones = jnp.concatenate([value_whole, jnp.ones_like(value_whole)], 1)
        first_col = (my_model % sharers) * kv_local
        key_cols = lax.dynamic_slice_in_dim(key_whole, first_col, kv_local, 1)
        pairs = jnp.stack([key_cols, value_raw], 1).reshape(n_model, row_count, 2 * kv_local)
        queries = [queries[:, part] for part in halves]
        new_keys = [key_whole[part] for part in halves]
        new_values = [value_ones[part] for part in halves]

    pairs = lax.all_to_all(pairs, "mp", split_axis=0, concat_axis=0, tiled=True)
    arrived, new_keys, pairs = lax.optimization_barrier((arrived, list(new_keys), pairs))
    cache_rows = (
        pairs.reshape(kv_heads, sharers, row_count, 2, kv_local)
        .transpose(2, 0, 3, 1, 4)
        .reshape(1, row_count, kv_heads * 2 * HD)
    )
    prefix = order_blocks(arrived, where, prefix_count.reshape(1))
    mixed = attend(upper_half.reshape(1), queries, prefix, new_keys, new_values)
    width = w_out.shape[1] // COLUMN_CHUNKS
    shares = [
        jnp.dot(
            mixed,
            w_out[:, chunk * width : (chunk + 1) * width],
            preferred_element_type=jnp.float32,
        ).astype(jnp.bfloat16)
        for chunk in range(COLUMN_CHUNKS)
    ]

    first = upper_half * (n_model // 2)
    scatters = [
        RingScatter(
            share.reshape(n_model, row_count, -1),
            n_model,
            my_model,
            first,
            1 if chunk % 2 == 0 else -1,
        )
        for chunk, share in enumerate(shares)
    ]
    sent, sums = [], []
    steps = n_model // 2
    for step in range(steps):
        for scatter in scatters:
            sent = scatter.step(sent, sums)
            if step == steps - 1:
                sums.append(scatter.finish())
    return (jnp.concatenate(sums, 1)[None], cache_rows)


def solution(mesh):
    placed = (
        P(("groups", "pool"), "mp", None),
        P(),
        P(None, "mp"),
        P("mp"),
        P(None, "mp"),
        P(None, "mp"),
        P("mp"),
        P("mp"),
        P("mp", None),
        P(("groups", "mp", "pool"), None, None, None),
        P("groups", None),
        P("groups", None),
        P("groups"),
    )
    return jax.shard_map(
        functools.partial(on_device, mesh.shape["mp"], mesh.shape["pool"]),
        mesh=mesh,
        in_specs=placed,
        out_specs=(P(("groups", "pool"), "mp", None), P(("groups", "pool"), "mp", None)),
        check_vma=False,
    )
```

```python
import functools
import math

import jax
import jax.numpy as jnp
from jax import lax
from jax.experimental import pallas as pl
from jax.experimental.pallas import tpu as pltpu
from jax.sharding import PartitionSpec as P

QH = 64
HD = 128
ROPE_BASE = 1000000.0
EPSILON = 1e-06
SCORE_SCALE = HD ** (-0.5) * math.log2(math.e)
VMEM_LIMIT = 56 * 1024 * 1024
ATTEND_VMEM = 28 * 1024 * 1024
COLUMN_CHUNKS = 2
STREAMS = 4
LINE_MODELS = 8


def angle_tables(positions):
    frequency = jnp.power(
        jnp.float32(ROPE_BASE), -2.0 * jnp.arange(HD // 2, dtype=jnp.float32) / HD
    )
    angles = positions.astype(jnp.float32)[:, None] * frequency[None, :]
    return jnp.cos(angles), jnp.sin(angles)


def rotate(vectors, cosine, sine):
    first_half = vectors[..., : HD // 2]
    second = vectors[..., HD // 2 :]
    cosine = cosine[:, None, :]
    sine = sine[:, None, :]
    return jnp.concatenate(
        [first_half * cosine - second * sine, second * cosine + first_half * sine], -1
    )


def normalize(states, gain_vec):
    values = states.astype(jnp.float32)
    inv_rms = lax.rsqrt(jnp.mean(values * values, axis=-1, keepdims=True) + EPSILON)
    return (values * inv_rms * gain_vec.astype(jnp.float32)).astype(jnp.bfloat16)


def listing(owned_mask, capacity):
    rank_order = jnp.cumsum(owned_mask.astype(jnp.int32), -1) - 1
    slot_index = jnp.arange(capacity, dtype=jnp.int32)
    return owned_mask[..., None, :] & (rank_order[..., None, :] == slot_index[:, None])


def swap(block, mask):
    return lax.ppermute(block, "mp", [(index, index ^ mask) for index in range(LINE_MODELS)])


def cross(block):
    pairs = []
    for index in range(LINE_MODELS):
        for core in range(2):
            if 2 <= index < 6:
                pairs.append((index * 2 + core, (index ^ 6) * 2 + core))
            else:
                pairs.append((index * 2 + core, index * 2 + 1 - core))
    return lax.ppermute(block, ("mp", "pool"), pairs)


def gather_and_exchange(own, outgoing, middle):
    arrived = {0: outgoing[0]}

    def after(block, *events):
        return lax.optimization_barrier((block, events))[0]

    def exchange(apart, *events):
        block = after(outgoing[apart], *events) if events else outgoing[apart]
        arrived[apart] = swap(block, apart)

    beside = swap(own, 2)
    over = cross(own)
    own_y = swap(own, 1)
    over_beside = cross(beside)
    over_passed = swap(over, 2)
    beside_y = swap(after(beside, own_y), 1)
    far_first = jnp.where(middle, over, over_passed)
    far_first_y = swap(after(far_first, beside_y), 1)
    over_beside_passed = swap(after(over_beside, outgoing[4]), 2)
    exchange(4, over_beside)
    exchange(6, over_beside)
    far_second = jnp.where(middle, over_beside, over_beside_passed)
    far_second_y = swap(after(far_second, far_first_y), 1)
    exchange(5, far_first_y, far_second)
    exchange(2, far_first_y, far_second)
    exchange(7, arrived[4], far_first_y)
    exchange(3, arrived[4], far_first_y)
    exchange(1, far_first_y)
    near = [after(own, far_second, arrived[4], arrived[6], arrived[1]), beside, own_y, beside_y]
    far = [far_first, far_second, far_first_y, far_second_y]
    return near, far, [arrived[apart] for apart in range(LINE_MODELS)]


def project_kernel(starts_ref, *refs):
    n_blocks = starts_ref.shape[0]
    blocks, refs = refs[:n_blocks], refs[n_blocks:]
    q_weights, (k_weight_ref, v_weight_ref), refs = refs[:STREAMS], refs[STREAMS:][:2], refs[STREAMS + 2 :]
    q_bias_ref, k_bias_ref, v_bias_ref, cos_ref, sin_ref = refs[:5]
    query_ref, key_ref, value_ref, pair_ref, tokens_ref, total_ref, sems = refs[5:]
    step = pl.program_id(0)
    depth = k_weight_ref.shape[0]
    q_width = q_weights[0].shape[1]
    rows = blocks[0].shape[0]

    @pl.when(step == 0)
    def _():
        copies = [
            pltpu.make_async_copy(
                block,
                tokens_ref.at[pl.ds(pl.multiple_of(starts_ref[index], rows), rows), :],
                sems.at[index],
            )
            for index, block in enumerate(blocks)
        ]
        for copy in copies:
            copy.start()
        total_ref[...] = jnp.zeros_like(total_ref)
        for copy in copies:
            copy.wait()

    tokens = tokens_ref[:, pl.ds(pl.multiple_of(step * depth, depth), depth)]
    q_weight = jnp.concatenate([ref[...] for ref in q_weights], axis=0)
    total_ref[:, :q_width] += jnp.dot(tokens, q_weight, preferred_element_type=jnp.float32)
    both = jnp.concatenate([k_weight_ref[...], v_weight_ref[...]], axis=1)
    total_ref[:, q_width:] += jnp.dot(tokens, both, preferred_element_type=jnp.float32)

    @pl.when(step == pl.num_programs(0) - 1)
    def _():
        cosine, sine = cos_ref[...], sin_ref[...]

        def turned(vectors):
            return vectors * cosine + pltpu.roll(vectors, HD // 2, 1) * sine

        for head in range(q_width // HD):
            cols = slice(head * HD, (head + 1) * HD)
            query = total_ref[:, cols] + q_bias_ref[:, cols].astype(jnp.float32)
            query_ref[head] = turned(query).astype(jnp.bfloat16)
        key = total_ref[:, q_width : q_width + HD] + k_bias_ref[...].astype(jnp.float32)
        key = turned(key.astype(jnp.bfloat16).astype(jnp.float32)).astype(jnp.bfloat16)
        value = total_ref[:, q_width + HD :] + v_bias_ref[...].astype(jnp.float32)
        value = value.astype(jnp.bfloat16)
        key_ref[...] = key
        value_ref[:, :HD] = value
        value_ref[:, HD:] = jnp.ones_like(value)
        pair_ref[:, :HD] = key
        pair_ref[:, HD:] = value


def project(starts, blocks, weights, biases, tables):
    width = blocks[0].shape[1]
    rows = sum(block.shape[0] for block in blocks)
    depth = math.gcd(width, 1024)
    q_width = weights[0].shape[1]
    out_width = q_width + 2 * HD
    fixed = lambda array: pl.BlockSpec(array.shape, lambda step: (0,) * len(array.shape))
    in_specs = [pl.BlockSpec(memory_space=pltpu.SMEM)]
    in_specs += [pl.BlockSpec(memory_space=pl.ANY)] * len(blocks)
    in_specs += [
        pl.BlockSpec((depth // STREAMS, q_width), lambda step, part=part: (step * STREAMS + part, 0))
        for part in range(STREAMS)
    ]
    in_specs += [pl.BlockSpec((depth, HD), lambda step: (step, 0))] * 2
    in_specs += [fixed(array) for array in (*biases, *tables)]
    out_shape = (
        jax.ShapeDtypeStruct((q_width // HD, rows, HD), jnp.bfloat16),
        jax.ShapeDtypeStruct((rows, HD), jnp.bfloat16),
        jax.ShapeDtypeStruct((rows, 2 * HD), jnp.bfloat16),
        jax.ShapeDtypeStruct((rows, 2 * HD), jnp.bfloat16),
    )
    return pl.pallas_call(
        project_kernel,
        grid=(width // depth,),
        out_shape=out_shape,
        in_specs=in_specs,
        out_specs=tuple(fixed(shape) for shape in out_shape),
        scratch_shapes=[
            pltpu.VMEM((rows, width), jnp.bfloat16),
            pltpu.VMEM((rows, out_width), jnp.float32),
            pltpu.SemaphoreType.DMA((len(blocks),)),
        ],
        compiler_params=pltpu.CompilerParams(vmem_limit_bytes=VMEM_LIMIT),
        cost_estimate=pl.CostEstimate(
            flops=2 * rows * width * out_width,
            bytes_accessed=2 * width * (rows + out_width) + 4 * rows * out_width,
            transcendentals=0,
        ),
        name="project",
    )(starts, *blocks, *weights[:1] * STREAMS, *weights[1:], *biases, *tables)


class RingScatter:
    def __init__(self, shares, places, order, way):
        self.shares, self.places, self.order, self.way = shares, places, order, way
        self.n_model = len(order)
        self.distance = {way: self.n_model // 2, -way: self.n_model // 2 - 1}
        self.moving = {}

    def share_of(self, offset):
        place = self.places[offset % self.n_model]
        return lax.dynamic_index_in_dim(self.shares, place, 0, keepdims=False)

    def step(self, *before):
        ways = [way for way in (self.way, -self.way) if self.distance[way]]
        blocks = []
        for way in ways:
            block = self.share_of(way * self.distance[way])
            if way in self.moving:
                arrived = self.moving[way].astype(jnp.float32)
                block = (block.astype(jnp.float32) + arrived).astype(jnp.bfloat16)
            blocks.append(block)
            self.distance[way] -= 1
        blocks, _ = lax.optimization_barrier((blocks, (before, list(self.moving.values()))))
        for way, block in zip(ways, blocks):
            pairs = [
                (self.order[i], self.order[(i + way) % self.n_model]) for i in range(self.n_model)
            ]
            self.moving[way] = lax.ppermute(block, "mp", pairs)
        return blocks

    def finish(self):
        total = self.share_of(0).astype(jnp.float32)
        for way in (1, -1):
            total = total + self.moving[way].astype(jnp.float32)
        return total.astype(jnp.bfloat16)


def pick_kernel(slots_ref, pool_ref, out_ref):
    def place(rank, _):
        out_ref[rank] = pool_ref[slots_ref[rank]]
        return 0

    lax.fori_loop(0, slots_ref.shape[0], place, 0)


def pick_blocks(pool, slots):
    return pl.pallas_call(
        pick_kernel,
        out_shape=jax.ShapeDtypeStruct((*slots.shape, *pool.shape[1:]), pool.dtype),
        in_specs=[
            pl.BlockSpec(memory_space=pltpu.SMEM),
            pl.BlockSpec(memory_space=pltpu.VMEM),
        ],
        out_specs=pl.BlockSpec(memory_space=pltpu.VMEM),
        compiler_params=pltpu.CompilerParams(vmem_limit_bytes=ATTEND_VMEM),
        name="pick_blocks",
    )(slots, pool)


def pack_kernel(lists, slots_ref, heads_ref, *refs):
    sources, out_refs = refs[: len(lists)], refs[len(lists) :]

    def place(rank, _):
        for listed, source_ref in zip(lists, sources):
            slot = slots_ref[listed, rank]
            for dest, out_ref in enumerate(out_refs):
                first = pl.multiple_of(heads_ref[dest] * 2 * HD, 2 * HD)
                out_ref[listed, rank] = source_ref[slot, :, pl.ds(first, 2 * HD)]
        return 0

    lax.fori_loop(0, slots_ref.shape[1], place, 0)


def pack_blocks(sources, slots, heads):
    dests = heads.shape[0]
    block_len = sources[0].shape[1]
    shape = jax.ShapeDtypeStruct((*slots.shape, block_len, 2 * HD), jnp.bfloat16)
    return pl.pallas_call(
        functools.partial(pack_kernel, range(len(sources))),
        out_shape=[shape] * dests,
        in_specs=[pl.BlockSpec(memory_space=pltpu.SMEM)] * 2
        + [pl.BlockSpec(memory_space=pltpu.VMEM)] * len(sources),
        out_specs=[pl.BlockSpec(memory_space=pltpu.VMEM)] * dests,
        compiler_params=pltpu.CompilerParams(vmem_limit_bytes=ATTEND_VMEM),
        name="pack_blocks",
    )(slots, heads, *sources)


def order_kernel(length_ref, where_ref, *refs):
    *arrived_refs, key_ref, value_ref, held_ref, sems = refs
    block_len = held_ref.shape[1]
    copies = []
    begin = 0
    for index, source in enumerate(arrived_refs):
        end = begin + source.shape[0]
        copies.append(pltpu.make_async_copy(source, held_ref.at[begin:end], sems.at[index]))
        begin = end
    for copy in copies:
        copy.start()
    for copy in copies:
        copy.wait()
    length = length_ref[0]
    first = held_ref[where_ref[0]][:1, :HD].astype(jnp.float32)
    row = lax.broadcasted_iota(jnp.int32, (block_len, HD), 0)

    def place(block_id, _):
        block = held_ref[where_ref[block_id]].astype(jnp.float32)
        start = pl.multiple_of(block_id * block_len, block_len)
        seen = row + start < length
        rows = pl.ds(start, block_len)
        key_ref[rows, :] = jnp.where(seen, block[:, :HD], first).astype(jnp.bfloat16)
        value_ref[rows, :HD] = jnp.where(seen, block[:, HD:], 0.0).astype(jnp.bfloat16)
        value_ref[rows, HD:] = jnp.where(seen, 1.0, 0.0).astype(jnp.bfloat16)
        return 0

    lax.fori_loop(0, where_ref.shape[0], place, 0, unroll=8)


def order_blocks(arrived, where, length):
    count = sum(array.shape[-3] for array in arrived)
    block_len = arrived[0].shape[-2]
    tokens = where.shape[0] * block_len
    return pl.pallas_call(
        order_kernel,
        out_shape=(
            jax.ShapeDtypeStruct((tokens, HD), jnp.bfloat16),
            jax.ShapeDtypeStruct((tokens, 2 * HD), jnp.bfloat16),
        ),
        in_specs=[pl.BlockSpec(memory_space=pltpu.SMEM)] * 2
        + [pl.BlockSpec(memory_space=pl.ANY)] * len(arrived),
        out_specs=(
            pl.BlockSpec(memory_space=pltpu.VMEM),
            pl.BlockSpec(memory_space=pltpu.VMEM),
        ),
        scratch_shapes=[
            pltpu.VMEM((count, block_len, 2 * HD), jnp.bfloat16),
            pltpu.SemaphoreType.DMA((len(arrived),)),
        ],
        compiler_params=pltpu.CompilerParams(vmem_limit_bytes=ATTEND_VMEM),
        name="order_blocks",
    )(length, where, *arrived)


def dot_keys(queries, keys):
    return lax.dot_general(
        queries, keys, (((1,), (1,)), ((), ())), preferred_element_type=jnp.float32
    )


def attend_kernel(span, half_ref, *refs):
    query_refs, (key_ref, value_ref), new_key_refs, new_value_refs, out_ref = (
        refs[:2],
        refs[2:4],
        refs[4:6],
        refs[6:8],
        refs[8],
    )
    rows = out_ref.shape[0]
    half = rows // 2
    queries = jnp.concatenate([ref[0] for ref in query_refs], 0)
    spans = key_ref.shape[0] // span
    turn = half_ref[0] * half
    token = lax.rem(lax.broadcasted_iota(jnp.int32, (rows, half), 0) + turn, rows)
    column = lax.broadcasted_iota(jnp.int32, (rows, half), 1)
    parts = []
    for side, ref in enumerate(new_key_refs):
        causal = column + lax.rem(turn + side * half, rows) <= token
        parts.append(jnp.where(causal, dot_keys(queries, ref[...]), -jnp.inf))
    scores = jnp.concatenate(parts, 1)
    peak = jnp.max(scores, axis=1, keepdims=True)
    total = None
    values = jnp.concatenate([ref[...] for ref in new_value_refs], 0)
    for index in range(spans + 1):
        if index < spans:
            next_scores = dot_keys(queries, key_ref[index * span : (index + 1) * span, :])
            next_peak = jnp.maximum(peak, jnp.max(next_scores, axis=1, keepdims=True))
        weights = jnp.exp2((scores - peak) * SCORE_SCALE).astype(jnp.bfloat16)
        product = jnp.dot(weights, values, preferred_element_type=jnp.float32)
        total = product if total is None else total + product
        if index < spans:
            total = total * jnp.exp2((peak - next_peak) * SCORE_SCALE)
            scores, peak = next_scores, next_peak
            values = value_ref[index * span : (index + 1) * span, :]
    out_ref[...] = (total[:, :HD] / total[:, HD:]).astype(jnp.bfloat16)


def attend(half, queries, prefix, new_keys, new_values):
    heads = queries[0].shape[0]
    rows = 2 * new_keys[0].shape[0]
    span = math.gcd(prefix[0].shape[0], 2048)
    whole = lambda array: pl.BlockSpec(array.shape, lambda step: (0, 0))
    count = prefix[0].shape[0] + rows
    query_spec = pl.BlockSpec((1, rows // 2, HD), lambda step: (step, 0, 0))
    fixed = (*prefix, *new_keys, *new_values)
    return pl.pallas_call(
        functools.partial(attend_kernel, span),
        grid=(heads,),
        out_shape=jax.ShapeDtypeStruct((rows, heads * HD), jnp.bfloat16),
        in_specs=[pl.BlockSpec(memory_space=pltpu.SMEM), query_spec, query_spec]
        + [whole(array) for array in fixed],
        out_specs=pl.BlockSpec((rows, HD), lambda step: (0, step)),
        compiler_params=pltpu.CompilerParams(vmem_limit_bytes=ATTEND_VMEM),
        cost_estimate=pl.CostEstimate(
            flops=heads * rows * count * HD * 8,
            bytes_accessed=2 * (count * 3 * HD + 2 * heads * rows * HD),
            transcendentals=heads * rows * count,
        ),
        name="attend",
    )(half, *queries, *fixed)


def on_device(
    n_model,
    n_pool,
    states,
    norm_gain,
    w_query,
    q_bias,
    w_key,
    w_value,
    k_bias,
    v_bias,
    w_out,
    kv_pool,
    hit_holder,
    hit_slot,
    prefix_len,
):
    my_model = lax.axis_index("mp")
    my_pool = lax.axis_index("pool")
    row_count = states.shape[1]
    suffix = row_count * n_model
    q_width = w_query.shape[1]
    q_local = q_width // HD
    kv_local = w_key.shape[1]
    kv_heads = kv_local * n_model // HD
    group_size = QH // kv_heads
    blocks_total = hit_holder.shape[1]
    block_len = kv_pool.shape[2]
    holders = n_model * n_pool
    capacity = 2 * blocks_total // holders
    sharers = HD // kv_local

    lined = n_model == LINE_MODELS

    self_holder = my_model * n_pool + my_pool
    chosen = listing(hit_holder == self_holder, capacity)
    slot_ids = jnp.sum(jnp.where(chosen, hit_slot[:, None, :], 0), -1)
    models = jnp.arange(n_model, dtype=jnp.int32)
    my_holder = hit_holder[my_pool]
    prefix_count = prefix_len[my_pool]
    block_ids = jnp.arange(blocks_total, dtype=jnp.int32)
    earlier = (my_holder[:, None] == my_holder[None, :]) & (block_ids[None, :] < block_ids[:, None])
    rank = jnp.sum(earlier.astype(jnp.int32), -1)
    normed = normalize(states[0], norm_gain)
    if lined:
        mine, others = (
            lax.dynamic_index_in_dim(slot_ids, pool, 0, keepdims=False)
            for pool in (my_pool, 1 - my_pool)
        )
        pool_blocks = kv_pool[0]
        got = lax.ppermute(pick_blocks(pool_blocks, others), "pool", [(0, 1), (1, 0)])
        slots = jnp.stack([mine, jnp.arange(capacity, dtype=jnp.int32)])
        outgoing = pack_blocks((pool_blocks, got), slots, (models ^ my_model) * q_local // group_size)
        my_z, my_y = my_model // 2, my_model % 2
        near, far, arrived = gather_and_exchange(normed, outgoing, (my_z == 1) | (my_z == 2))
        arrived = [block.reshape(-1, block_len, 2 * HD) for block in arrived]
        distance = (my_holder // n_pool) ^ my_model
        where = (distance * n_pool + (my_holder % n_pool ^ my_pool)) * capacity + rank
    else:
        outgoing = pack_blocks((kv_pool[0],) * 2, slot_ids, models * q_local // group_size)
        outgoing = jnp.stack(outgoing).reshape(holders, capacity * block_len, 2 * HD)
        arrived = lax.all_to_all(outgoing, ("mp", "pool"), split_axis=0, concat_axis=0, tiled=True)
        arrived = [arrived.reshape(holders * capacity, block_len, 2 * HD)]
        where = my_holder * capacity + rank

    upper_half = (my_model // (n_model // 2)).astype(jnp.int32) if lined else jnp.int32(0)
    half_rows = suffix // 2
    order = (jnp.arange(suffix, dtype=jnp.int32) + upper_half * half_rows) % suffix
    cosine, sine = angle_tables(prefix_count + order)
    cosine, sine = jnp.concatenate([cosine, cosine], 1), jnp.concatenate([-sine, sine], 1)
    halves = [slice(0, half_rows), slice(half_rows, suffix)]
    biases = [bias.reshape(1, -1) for bias in (q_bias, k_bias, v_bias)]
    weights = (w_query, w_key, w_value)
    if lined:
        results = []
        for blocks, inner in ((near, my_z % 2), (far, upper_half)):
            starts = jnp.stack(
                [
                    2 * (inner ^ other) + (my_y ^ side)
                    for side in range(2)
                    for other in range(2)
                ]
            )
            table = [part[halves[len(results)]] for part in (cosine, sine)]
            results.append(
                project(starts.astype(jnp.int32) * row_count, blocks, weights, biases, table)
            )
        queries, new_keys, new_values, pairs = zip(*results)
        pairs = jnp.where(
            upper_half == 0, jnp.concatenate(pairs, 0), jnp.concatenate(pairs[::-1], 0)
        ).reshape(n_model, row_count, 2 * HD)
    else:
        tokens = lax.all_gather(normed, "mp", axis=0, tiled=True)
        linear, key_raw, value_raw = (
            jnp.dot(tokens, weight, preferred_element_type=jnp.float32) + bias.astype(jnp.float32)
            for weight, bias in zip(weights, biases)
        )
        cosine, sine = cosine[:, : HD // 2], sine[:, HD // 2 :]
        queries = rotate(linear.reshape(suffix, q_local, HD), cosine, sine)
        queries = queries.astype(jnp.bfloat16).transpose(1, 0, 2)
        key_raw, value_raw = key_raw.astype(jnp.bfloat16), value_raw.astype(jnp.bfloat16)
        together = [
            [first + other for other in range(sharers)] for first in range(0, n_model, sharers)
        ]
        key_whole, value_whole = (
            lax.all_gather(part, "mp", axis=1, tiled=True, axis_index_groups=together)
            for part in (key_raw, value_raw)
        )
        key_whole = rotate(key_whole.astype(jnp.float32)[:, None, :], cosine, sine)
        key_whole = key_whole.astype(jnp.bfloat16)[:, 0]
        value_ones = jnp.concatenate([value_whole, jnp.ones_like(value_whole)], 1)
        first_col = (my_model % sharers) * kv_local
        key_cols = lax.dynamic_slice_in_dim(key_whole, first_col, kv_local, 1)
        pairs = jnp.stack([key_cols, value_raw], 1).reshape(n_model, row_count, 2 * kv_local)
        queries = [queries[:, part] for part in halves]
        new_keys = [key_whole[part] for part in halves]
        new_values = [value_ones[part] for part in halves]

    pairs = lax.all_to_all(pairs, "mp", split_axis=0, concat_axis=0, tiled=True)
    arrived, new_keys, pairs = lax.optimization_barrier((arrived, list(new_keys), pairs))
    cache_rows = (
        pairs.reshape(kv_heads, sharers, row_count, 2, kv_local)
        .transpose(2, 0, 3, 1, 4)
        .reshape(1, row_count, kv_heads * 2 * HD)
    )
    prefix = order_blocks(arrived, where, prefix_count.reshape(1))
    mixed = attend(upper_half.reshape(1), queries, prefix, new_keys, new_values)
    width = w_out.shape[1] // COLUMN_CHUNKS
    shares = [
        jnp.dot(
            mixed,
            w_out[:, chunk * width : (chunk + 1) * width],
            preferred_element_type=jnp.float32,
        ).astype(jnp.bfloat16)
        for chunk in range(COLUMN_CHUNKS)
    ]

    order = [m for m in range(0, n_model, 2)] + [m for m in range(n_model - 1, 0, -2)]
    spot = jnp.array([order.index(m) for m in range(n_model)], jnp.int32)[my_model]
    places = jnp.array(order, jnp.int32)[(spot + models) % n_model]
    places = (places + n_model - upper_half * (n_model // 2)) % n_model
    scatters = [
        RingScatter(
            share.reshape(n_model, row_count, -1), places, order, 1 if chunk % 2 == 0 else -1
        )
        for chunk, share in enumerate(shares)
    ]
    sent, sums = [], []
    steps = n_model // 2
    for step in range(steps):
        for scatter in scatters:
            sent = scatter.step(sent, sums)
            if step == steps - 1:
                sums.append(scatter.finish())
    return (jnp.concatenate(sums, 1)[None], cache_rows)


def solution(mesh):
    placed = (
        P(("groups", "pool"), "mp", None),
        P(),
        P(None, "mp"),
        P("mp"),
        P(None, "mp"),
        P(None, "mp"),
        P("mp"),
        P("mp"),
        P("mp", None),
        P(("groups", "mp", "pool"), None, None, None),
        P("groups", None),
        P("groups", None),
        P("groups"),
    )
    return jax.shard_map(
        functools.partial(on_device, mesh.shape["mp"], mesh.shape["pool"]),
        mesh=mesh,
        in_specs=placed,
        out_specs=(P(("groups", "pool"), "mp", None), P(("groups", "pool"), "mp", None)),
        check_vma=False,
    )
```

```python
import functools
import math

import jax
import jax.numpy as jnp
from jax import lax
from jax.experimental import pallas as pl
from jax.experimental.pallas import tpu as pltpu
from jax.sharding import PartitionSpec as P

QH = 64
HD = 128
ROPE_BASE = 1000000.0
EPSILON = 1e-06
SCORE_SCALE = HD ** (-0.5) * math.log2(math.e)
VMEM_LIMIT = 56 * 1024 * 1024
ATTEND_VMEM = 28 * 1024 * 1024
COLUMN_CHUNKS = 2
STREAMS = 4
LINE_MODELS = 8


def angle_tables(positions):
    frequency = jnp.power(
        jnp.float32(ROPE_BASE), -2.0 * jnp.arange(HD // 2, dtype=jnp.float32) / HD
    )
    angles = positions.astype(jnp.float32)[:, None] * frequency[None, :]
    return jnp.cos(angles), jnp.sin(angles)


def rotate(vectors, cosine, sine):
    first_half = vectors[..., : HD // 2]
    second = vectors[..., HD // 2 :]
    cosine = cosine[:, None, :]
    sine = sine[:, None, :]
    return jnp.concatenate(
        [first_half * cosine - second * sine, second * cosine + first_half * sine], -1
    )


def normalize(states, gain_vec):
    values = states.astype(jnp.float32)
    inv_rms = lax.rsqrt(jnp.mean(values * values, axis=-1, keepdims=True) + EPSILON)
    return (values * inv_rms * gain_vec.astype(jnp.float32)).astype(jnp.bfloat16)


def listing(owned_mask, capacity):
    rank_order = jnp.cumsum(owned_mask.astype(jnp.int32), -1) - 1
    slot_index = jnp.arange(capacity, dtype=jnp.int32)
    return owned_mask[..., None, :] & (rank_order[..., None, :] == slot_index[:, None])


def swap(block, mask):
    return lax.ppermute(block, "mp", [(index, index ^ mask) for index in range(LINE_MODELS)])


def cross(block):
    pairs = []
    for index in range(LINE_MODELS):
        for core in range(2):
            if 2 <= index < 6:
                pairs.append((index * 2 + core, (index ^ 6) * 2 + core))
            else:
                pairs.append((index * 2 + core, index * 2 + 1 - core))
    return lax.ppermute(block, ("mp", "pool"), pairs)


def gather_and_exchange(own, outgoing, middle):
    arrived = {0: outgoing[0]}

    def after(block, *events):
        return lax.optimization_barrier((block, events))[0]

    def exchange(apart, *events):
        block = after(outgoing[apart], *events) if events else outgoing[apart]
        arrived[apart] = swap(block, apart)

    beside = swap(own, 2)
    over = cross(own)
    own_y = swap(own, 1)
    over_beside = cross(beside)
    over_passed = swap(over, 2)
    beside_y = swap(after(beside, own_y), 1)
    far_first = jnp.where(middle, over, over_passed)
    far_first_y = swap(after(far_first, beside_y), 1)
    over_beside_passed = swap(after(over_beside, outgoing[4]), 2)
    exchange(4, over_beside)
    exchange(6, over_beside)
    far_second = jnp.where(middle, over_beside, over_beside_passed)
    far_second_y = swap(after(far_second, far_first_y), 1)
    exchange(5, far_first_y, far_second)
    exchange(2, far_first_y, far_second)
    exchange(7, arrived[4], far_first_y)
    exchange(3, arrived[4], far_first_y)
    exchange(1, arrived[4], far_first_y)
    near = [after(own, far_second, arrived[4], arrived[6]), beside, own_y, beside_y]
    far = [far_first, far_second, far_first_y, far_second_y]
    return near, far, [arrived[apart] for apart in range(LINE_MODELS)]


def project_kernel(starts_ref, *refs):
    n_blocks = starts_ref.shape[0]
    blocks, refs = refs[:n_blocks], refs[n_blocks:]
    q_weights, (k_weight_ref, v_weight_ref), refs = refs[:STREAMS], refs[STREAMS:][:2], refs[STREAMS + 2 :]
    q_bias_ref, k_bias_ref, v_bias_ref, cos_ref, sin_ref = refs[:5]
    query_ref, key_ref, value_ref, pair_ref, tokens_ref, total_ref, sems = refs[5:]
    step = pl.program_id(0)
    depth = k_weight_ref.shape[0]
    q_width = q_weights[0].shape[1]
    rows = blocks[0].shape[0]

    @pl.when(step == 0)
    def _():
        copies = [
            pltpu.make_async_copy(
                block,
                tokens_ref.at[pl.ds(pl.multiple_of(starts_ref[index], rows), rows), :],
                sems.at[index],
            )
            for index, block in enumerate(blocks)
        ]
        for copy in copies:
            copy.start()
        total_ref[...] = jnp.zeros_like(total_ref)
        for copy in copies:
            copy.wait()

    tokens = tokens_ref[:, pl.ds(pl.multiple_of(step * depth, depth), depth)]
    q_weight = jnp.concatenate([ref[...] for ref in q_weights], axis=0)
    total_ref[:, :q_width] += jnp.dot(tokens, q_weight, preferred_element_type=jnp.float32)
    both = jnp.concatenate([k_weight_ref[...], v_weight_ref[...]], axis=1)
    total_ref[:, q_width:] += jnp.dot(tokens, both, preferred_element_type=jnp.float32)

    @pl.when(step == pl.num_programs(0) - 1)
    def _():
        cosine, sine = cos_ref[...], sin_ref[...]

        def turned(vectors):
            return vectors * cosine + pltpu.roll(vectors, HD // 2, 1) * sine

        for head in range(q_width // HD):
            cols = slice(head * HD, (head + 1) * HD)
            query = total_ref[:, cols] + q_bias_ref[:, cols].astype(jnp.float32)
            query_ref[head] = turned(query).astype(jnp.bfloat16)
        key = total_ref[:, q_width : q_width + HD] + k_bias_ref[...].astype(jnp.float32)
        key = turned(key.astype(jnp.bfloat16).astype(jnp.float32)).astype(jnp.bfloat16)
        value = total_ref[:, q_width + HD :] + v_bias_ref[...].astype(jnp.float32)
        value = value.astype(jnp.bfloat16)
        key_ref[...] = key
        value_ref[:, :HD] = value
        value_ref[:, HD:] = jnp.ones_like(value)
        pair_ref[:, :HD] = key
        pair_ref[:, HD:] = value


def project(starts, blocks, weights, biases, tables):
    width = blocks[0].shape[1]
    rows = sum(block.shape[0] for block in blocks)
    depth = math.gcd(width, 1024)
    q_width = weights[0].shape[1]
    out_width = q_width + 2 * HD
    fixed = lambda array: pl.BlockSpec(array.shape, lambda step: (0,) * len(array.shape))
    in_specs = [pl.BlockSpec(memory_space=pltpu.SMEM)]
    in_specs += [pl.BlockSpec(memory_space=pl.ANY)] * len(blocks)
    in_specs += [
        pl.BlockSpec((depth // STREAMS, q_width), lambda step, part=part: (step * STREAMS + part, 0))
        for part in range(STREAMS)
    ]
    in_specs += [pl.BlockSpec((depth, HD), lambda step: (step, 0))] * 2
    in_specs += [fixed(array) for array in (*biases, *tables)]
    out_shape = (
        jax.ShapeDtypeStruct((q_width // HD, rows, HD), jnp.bfloat16),
        jax.ShapeDtypeStruct((rows, HD), jnp.bfloat16),
        jax.ShapeDtypeStruct((rows, 2 * HD), jnp.bfloat16),
        jax.ShapeDtypeStruct((rows, 2 * HD), jnp.bfloat16),
    )
    return pl.pallas_call(
        project_kernel,
        grid=(width // depth,),
        out_shape=out_shape,
        in_specs=in_specs,
        out_specs=tuple(fixed(shape) for shape in out_shape),
        scratch_shapes=[
            pltpu.VMEM((rows, width), jnp.bfloat16),
            pltpu.VMEM((rows, out_width), jnp.float32),
            pltpu.SemaphoreType.DMA((len(blocks),)),
        ],
        compiler_params=pltpu.CompilerParams(vmem_limit_bytes=VMEM_LIMIT),
        cost_estimate=pl.CostEstimate(
            flops=2 * rows * width * out_width,
            bytes_accessed=2 * width * (rows + out_width) + 4 * rows * out_width,
            transcendentals=0,
        ),
        name="project",
    )(starts, *blocks, *weights[:1] * STREAMS, *weights[1:], *biases, *tables)


class RingScatter:
    def __init__(self, shares, places, order, way):
        self.shares, self.places, self.order, self.way = shares, places, order, way
        self.n_model = len(order)
        self.distance = {way: self.n_model // 2, -way: self.n_model // 2 - 1}
        self.moving = {}

    def share_of(self, offset):
        place = self.places[offset % self.n_model]
        return lax.dynamic_index_in_dim(self.shares, place, 0, keepdims=False)

    def step(self, *before):
        ways = [way for way in (self.way, -self.way) if self.distance[way]]
        blocks = []
        for way in ways:
            block = self.share_of(way * self.distance[way])
            if way in self.moving:
                arrived = self.moving[way].astype(jnp.float32)
                block = (block.astype(jnp.float32) + arrived).astype(jnp.bfloat16)
            blocks.append(block)
            self.distance[way] -= 1
        blocks, _ = lax.optimization_barrier((blocks, (before, list(self.moving.values()))))
        for way, block in zip(ways, blocks):
            pairs = [
                (self.order[i], self.order[(i + way) % self.n_model]) for i in range(self.n_model)
            ]
            self.moving[way] = lax.ppermute(block, "mp", pairs)
        return blocks

    def finish(self):
        total = self.share_of(0).astype(jnp.float32)
        for way in (1, -1):
            total = total + self.moving[way].astype(jnp.float32)
        return total.astype(jnp.bfloat16)


def pick_kernel(slots_ref, pool_ref, out_ref):
    def place(rank, _):
        out_ref[rank] = pool_ref[slots_ref[rank]]
        return 0

    lax.fori_loop(0, slots_ref.shape[0], place, 0)


def pick_blocks(pool, slots):
    return pl.pallas_call(
        pick_kernel,
        out_shape=jax.ShapeDtypeStruct((*slots.shape, *pool.shape[1:]), pool.dtype),
        in_specs=[
            pl.BlockSpec(memory_space=pltpu.SMEM),
            pl.BlockSpec(memory_space=pltpu.VMEM),
        ],
        out_specs=pl.BlockSpec(memory_space=pltpu.VMEM),
        compiler_params=pltpu.CompilerParams(vmem_limit_bytes=ATTEND_VMEM),
        name="pick_blocks",
    )(slots, pool)


def pack_kernel(lists, slots_ref, heads_ref, *refs):
    sources, out_refs = refs[: len(lists)], refs[len(lists) :]

    def place(rank, _):
        for listed, source_ref in zip(lists, sources):
            slot = slots_ref[listed, rank]
            for dest, out_ref in enumerate(out_refs):
                first = pl.multiple_of(heads_ref[dest] * 2 * HD, 2 * HD)
                out_ref[listed, rank] = source_ref[slot, :, pl.ds(first, 2 * HD)]
        return 0

    lax.fori_loop(0, slots_ref.shape[1], place, 0)


def pack_blocks(sources, slots, heads):
    dests = heads.shape[0]
    block_len = sources[0].shape[1]
    shape = jax.ShapeDtypeStruct((*slots.shape, block_len, 2 * HD), jnp.bfloat16)
    return pl.pallas_call(
        functools.partial(pack_kernel, range(len(sources))),
        out_shape=[shape] * dests,
        in_specs=[pl.BlockSpec(memory_space=pltpu.SMEM)] * 2
        + [pl.BlockSpec(memory_space=pltpu.VMEM)] * len(sources),
        out_specs=[pl.BlockSpec(memory_space=pltpu.VMEM)] * dests,
        compiler_params=pltpu.CompilerParams(vmem_limit_bytes=ATTEND_VMEM),
        name="pack_blocks",
    )(slots, heads, *sources)


def order_kernel(length_ref, where_ref, *refs):
    *arrived_refs, key_ref, value_ref, held_ref, sems = refs
    block_len = held_ref.shape[1]
    copies = []
    begin = 0
    for index, source in enumerate(arrived_refs):
        end = begin + source.shape[0]
        copies.append(pltpu.make_async_copy(source, held_ref.at[begin:end], sems.at[index]))
        begin = end
    for copy in copies:
        copy.start()
    for copy in copies:
        copy.wait()
    length = length_ref[0]
    first = held_ref[where_ref[0]][:1, :HD].astype(jnp.float32)
    row = lax.broadcasted_iota(jnp.int32, (block_len, HD), 0)

    def place(block_id, _):
        block = held_ref[where_ref[block_id]].astype(jnp.float32)
        start = pl.multiple_of(block_id * block_len, block_len)
        seen = row + start < length
        rows = pl.ds(start, block_len)
        key_ref[rows, :] = jnp.where(seen, block[:, :HD], first).astype(jnp.bfloat16)
        value_ref[rows, :HD] = jnp.where(seen, block[:, HD:], 0.0).astype(jnp.bfloat16)
        value_ref[rows, HD:] = jnp.where(seen, 1.0, 0.0).astype(jnp.bfloat16)
        return 0

    lax.fori_loop(0, where_ref.shape[0], place, 0, unroll=8)


def order_blocks(arrived, where, length):
    count = sum(array.shape[-3] for array in arrived)
    block_len = arrived[0].shape[-2]
    tokens = where.shape[0] * block_len
    return pl.pallas_call(
        order_kernel,
        out_shape=(
            jax.ShapeDtypeStruct((tokens, HD), jnp.bfloat16),
            jax.ShapeDtypeStruct((tokens, 2 * HD), jnp.bfloat16),
        ),
        in_specs=[pl.BlockSpec(memory_space=pltpu.SMEM)] * 2
        + [pl.BlockSpec(memory_space=pl.ANY)] * len(arrived),
        out_specs=(
            pl.BlockSpec(memory_space=pltpu.VMEM),
            pl.BlockSpec(memory_space=pltpu.VMEM),
        ),
        scratch_shapes=[
            pltpu.VMEM((count, block_len, 2 * HD), jnp.bfloat16),
            pltpu.SemaphoreType.DMA((len(arrived),)),
        ],
        compiler_params=pltpu.CompilerParams(vmem_limit_bytes=ATTEND_VMEM),
        name="order_blocks",
    )(length, where, *arrived)


def dot_keys(queries, keys):
    return lax.dot_general(
        queries, keys, (((1,), (1,)), ((), ())), preferred_element_type=jnp.float32
    )


def attend_kernel(span, half_ref, *refs):
    query_refs, (key_ref, value_ref), new_key_refs, new_value_refs, out_ref = (
        refs[:2],
        refs[2:4],
        refs[4:6],
        refs[6:8],
        refs[8],
    )
    rows = out_ref.shape[0]
    half = rows // 2
    queries = jnp.concatenate([ref[0] for ref in query_refs], 0)
    spans = key_ref.shape[0] // span
    turn = half_ref[0] * half
    token = lax.rem(lax.broadcasted_iota(jnp.int32, (rows, half), 0) + turn, rows)
    column = lax.broadcasted_iota(jnp.int32, (rows, half), 1)
    parts = []
    for side, ref in enumerate(new_key_refs):
        causal = column + lax.rem(turn + side * half, rows) <= token
        parts.append(jnp.where(causal, dot_keys(queries, ref[...]), -jnp.inf))
    scores = jnp.concatenate(parts, 1)
    peak = jnp.max(scores, axis=1, keepdims=True)
    total = None
    values = jnp.concatenate([ref[...] for ref in new_value_refs], 0)
    for index in range(spans + 1):
        if index < spans:
            next_scores = dot_keys(queries, key_ref[index * span : (index + 1) * span, :])
            next_peak = jnp.maximum(peak, jnp.max(next_scores, axis=1, keepdims=True))
        weights = jnp.exp2((scores - peak) * SCORE_SCALE).astype(jnp.bfloat16)
        product = jnp.dot(weights, values, preferred_element_type=jnp.float32)
        total = product if total is None else total + product
        if index < spans:
            total = total * jnp.exp2((peak - next_peak) * SCORE_SCALE)
            scores, peak = next_scores, next_peak
            values = value_ref[index * span : (index + 1) * span, :]
    out_ref[...] = (total[:, :HD] / total[:, HD:]).astype(jnp.bfloat16)


def attend(half, queries, prefix, new_keys, new_values):
    heads = queries[0].shape[0]
    rows = 2 * new_keys[0].shape[0]
    span = math.gcd(prefix[0].shape[0], 2048)
    whole = lambda array: pl.BlockSpec(array.shape, lambda step: (0, 0))
    count = prefix[0].shape[0] + rows
    query_spec = pl.BlockSpec((1, rows // 2, HD), lambda step: (step, 0, 0))
    fixed = (*prefix, *new_keys, *new_values)
    return pl.pallas_call(
        functools.partial(attend_kernel, span),
        grid=(heads,),
        out_shape=jax.ShapeDtypeStruct((rows, heads * HD), jnp.bfloat16),
        in_specs=[pl.BlockSpec(memory_space=pltpu.SMEM), query_spec, query_spec]
        + [whole(array) for array in fixed],
        out_specs=pl.BlockSpec((rows, HD), lambda step: (0, step)),
        compiler_params=pltpu.CompilerParams(vmem_limit_bytes=ATTEND_VMEM),
        cost_estimate=pl.CostEstimate(
            flops=heads * rows * count * HD * 8,
            bytes_accessed=2 * (count * 3 * HD + 2 * heads * rows * HD),
            transcendentals=heads * rows * count,
        ),
        name="attend",
    )(half, *queries, *fixed)


def on_device(
    n_model,
    n_pool,
    states,
    norm_gain,
    w_query,
    q_bias,
    w_key,
    w_value,
    k_bias,
    v_bias,
    w_out,
    kv_pool,
    hit_holder,
    hit_slot,
    prefix_len,
):
    my_model = lax.axis_index("mp")
    my_pool = lax.axis_index("pool")
    row_count = states.shape[1]
    suffix = row_count * n_model
    q_width = w_query.shape[1]
    q_local = q_width // HD
    kv_local = w_key.shape[1]
    kv_heads = kv_local * n_model // HD
    group_size = QH // kv_heads
    blocks_total = hit_holder.shape[1]
    block_len = kv_pool.shape[2]
    holders = n_model * n_pool
    capacity = 2 * blocks_total // holders
    sharers = HD // kv_local

    lined = n_model == LINE_MODELS

    self_holder = my_model * n_pool + my_pool
    chosen = listing(hit_holder == self_holder, capacity)
    slot_ids = jnp.sum(jnp.where(chosen, hit_slot[:, None, :], 0), -1)
    models = jnp.arange(n_model, dtype=jnp.int32)
    my_holder = hit_holder[my_pool]
    prefix_count = prefix_len[my_pool]
    block_ids = jnp.arange(blocks_total, dtype=jnp.int32)
    earlier = (my_holder[:, None] == my_holder[None, :]) & (block_ids[None, :] < block_ids[:, None])
    rank = jnp.sum(earlier.astype(jnp.int32), -1)
    normed = normalize(states[0], norm_gain)
    if lined:
        mine, others = (
            lax.dynamic_index_in_dim(slot_ids, pool, 0, keepdims=False)
            for pool in (my_pool, 1 - my_pool)
        )
        pool_blocks = kv_pool[0]
        picked, normed = lax.optimization_barrier((pick_blocks(pool_blocks, others), normed))
        got = lax.ppermute(picked, "pool", [(0, 1), (1, 0)])
        slots = jnp.stack([mine, jnp.arange(capacity, dtype=jnp.int32)])
        outgoing = pack_blocks((pool_blocks, got), slots, (models ^ my_model) * q_local // group_size)
        my_z, my_y = my_model // 2, my_model % 2
        near, far, arrived = gather_and_exchange(normed, outgoing, (my_z == 1) | (my_z == 2))
        arrived = [block.reshape(-1, block_len, 2 * HD) for block in arrived]
        distance = (my_holder // n_pool) ^ my_model
        where = (distance * n_pool + (my_holder % n_pool ^ my_pool)) * capacity + rank
    else:
        outgoing = pack_blocks((kv_pool[0],) * 2, slot_ids, models * q_local // group_size)
        outgoing = jnp.stack(outgoing).reshape(holders, capacity * block_len, 2 * HD)
        arrived = lax.all_to_all(outgoing, ("mp", "pool"), split_axis=0, concat_axis=0, tiled=True)
        arrived = [arrived.reshape(holders * capacity, block_len, 2 * HD)]
        where = my_holder * capacity + rank

    upper_half = (my_model // (n_model // 2)).astype(jnp.int32) if lined else jnp.int32(0)
    half_rows = suffix // 2
    order = (jnp.arange(suffix, dtype=jnp.int32) + upper_half * half_rows) % suffix
    cosine, sine = angle_tables(prefix_count + order)
    cosine, sine = jnp.concatenate([cosine, cosine], 1), jnp.concatenate([-sine, sine], 1)
    halves = [slice(0, half_rows), slice(half_rows, suffix)]
    biases = [bias.reshape(1, -1) for bias in (q_bias, k_bias, v_bias)]
    weights = (w_query, w_key, w_value)
    if lined:
        results = []
        for blocks, inner in ((near, my_z % 2), (far, upper_half)):
            starts = jnp.stack(
                [
                    2 * (inner ^ other) + (my_y ^ side)
                    for side in range(2)
                    for other in range(2)
                ]
            )
            table = [part[halves[len(results)]] for part in (cosine, sine)]
            results.append(
                project(starts.astype(jnp.int32) * row_count, blocks, weights, biases, table)
            )
        queries, new_keys, new_values, pairs = zip(*results)
        pairs = jnp.where(
            upper_half == 0, jnp.concatenate(pairs, 0), jnp.concatenate(pairs[::-1], 0)
        ).reshape(n_model, row_count, 2 * HD)
    else:
        tokens = lax.all_gather(normed, "mp", axis=0, tiled=True)
        linear, key_raw, value_raw = (
            jnp.dot(tokens, weight, preferred_element_type=jnp.float32) + bias.astype(jnp.float32)
            for weight, bias in zip(weights, biases)
        )
        cosine, sine = cosine[:, : HD // 2], sine[:, HD // 2 :]
        queries = rotate(linear.reshape(suffix, q_local, HD), cosine, sine)
        queries = queries.astype(jnp.bfloat16).transpose(1, 0, 2)
        key_raw, value_raw = key_raw.astype(jnp.bfloat16), value_raw.astype(jnp.bfloat16)
        together = [
            [first + other for other in range(sharers)] for first in range(0, n_model, sharers)
        ]
        key_whole, value_whole = (
            lax.all_gather(part, "mp", axis=1, tiled=True, axis_index_groups=together)
            for part in (key_raw, value_raw)
        )
        key_whole = rotate(key_whole.astype(jnp.float32)[:, None, :], cosine, sine)
        key_whole = key_whole.astype(jnp.bfloat16)[:, 0]
        value_ones = jnp.concatenate([value_whole, jnp.ones_like(value_whole)], 1)
        first_col = (my_model % sharers) * kv_local
        key_cols = lax.dynamic_slice_in_dim(key_whole, first_col, kv_local, 1)
        pairs = jnp.stack([key_cols, value_raw], 1).reshape(n_model, row_count, 2 * kv_local)
        queries = [queries[:, part] for part in halves]
        new_keys = [key_whole[part] for part in halves]
        new_values = [value_ones[part] for part in halves]

    pairs = lax.all_to_all(pairs, "mp", split_axis=0, concat_axis=0, tiled=True)
    arrived, new_keys, pairs = lax.optimization_barrier((arrived, list(new_keys), pairs))
    cache_rows = (
        pairs.reshape(kv_heads, sharers, row_count, 2, kv_local)
        .transpose(2, 0, 3, 1, 4)
        .reshape(1, row_count, kv_heads * 2 * HD)
    )
    prefix = order_blocks(arrived, where, prefix_count.reshape(1))
    mixed = attend(upper_half.reshape(1), queries, prefix, new_keys, new_values)
    width = w_out.shape[1] // COLUMN_CHUNKS
    shares = [
        jnp.dot(
            mixed,
            w_out[:, chunk * width : (chunk + 1) * width],
            preferred_element_type=jnp.float32,
        ).astype(jnp.bfloat16)
        for chunk in range(COLUMN_CHUNKS)
    ]

    order = [m for m in range(0, n_model, 2)] + [m for m in range(n_model - 1, 0, -2)]
    half = n_model // 2
    spot = jnp.where(my_model % 2 == 0, my_model // 2, n_model - 1 - my_model // 2)
    places = []
    for offset in range(n_model):
        index = (spot + offset) % n_model
        owner = jnp.where(index < half, 2 * index, 2 * (n_model - 1 - index) + 1)
        places.append((owner + n_model - upper_half * half) % n_model)
    scatters = [
        RingScatter(
            share.reshape(n_model, row_count, -1), places, order, 1 if chunk % 2 == 0 else -1
        )
        for chunk, share in enumerate(shares)
    ]
    sent, sums = [], []
    steps = n_model // 2
    for step in range(steps):
        for scatter in scatters:
            sent = scatter.step(sent, sums)
            if step == steps - 1:
                sums.append(scatter.finish())
    return (jnp.concatenate(sums, 1)[None], cache_rows)


def solution(mesh):
    placed = (
        P(("groups", "pool"), "mp", None),
        P(),
        P(None, "mp"),
        P("mp"),
        P(None, "mp"),
        P(None, "mp"),
        P("mp"),
        P("mp"),
        P("mp", None),
        P(("groups", "mp", "pool"), None, None, None),
        P("groups", None),
        P("groups", None),
        P("groups"),
    )
    return jax.shard_map(
        functools.partial(on_device, mesh.shape["mp"], mesh.shape["pool"]),
        mesh=mesh,
        in_specs=placed,
        out_specs=(P(("groups", "pool"), "mp", None), P(("groups", "pool"), "mp", None)),
        check_vma=False,
    )
```

```python
import functools
import math

import jax
import jax.numpy as jnp
from jax import lax
from jax.experimental import pallas as pl
from jax.experimental.pallas import tpu as pltpu
from jax.sharding import PartitionSpec as P

QH = 64
HD = 128
ROPE_BASE = 1000000.0
EPSILON = 1e-06
SCORE_SCALE = HD ** (-0.5) * math.log2(math.e)
VMEM_LIMIT = 56 * 1024 * 1024
ATTEND_VMEM = 28 * 1024 * 1024
COLUMN_CHUNKS = 2
STREAMS = 4
LINE_MODELS = 8


def angle_tables(positions):
    frequency = jnp.power(
        jnp.float32(ROPE_BASE), -2.0 * jnp.arange(HD // 2, dtype=jnp.float32) / HD
    )
    angles = positions.astype(jnp.float32)[:, None] * frequency[None, :]
    return jnp.cos(angles), jnp.sin(angles)


def rotate(vectors, cosine, sine):
    first_half = vectors[..., : HD // 2]
    second = vectors[..., HD // 2 :]
    cosine = cosine[:, None, :]
    sine = sine[:, None, :]
    return jnp.concatenate(
        [first_half * cosine - second * sine, second * cosine + first_half * sine], -1
    )


def normalize(states, gain_vec):
    values = states.astype(jnp.float32)
    inv_rms = lax.rsqrt(jnp.mean(values * values, axis=-1, keepdims=True) + EPSILON)
    return (values * inv_rms * gain_vec.astype(jnp.float32)).astype(jnp.bfloat16)


def listing(owned_mask, capacity):
    rank_order = jnp.cumsum(owned_mask.astype(jnp.int32), -1) - 1
    slot_index = jnp.arange(capacity, dtype=jnp.int32)
    return owned_mask[..., None, :] & (rank_order[..., None, :] == slot_index[:, None])


def swap(block, mask):
    return lax.ppermute(block, "mp", [(index, index ^ mask) for index in range(LINE_MODELS)])


def cross(block):
    pairs = []
    for index in range(LINE_MODELS):
        for core in range(2):
            if 2 <= index < 6:
                pairs.append((index * 2 + core, (index ^ 6) * 2 + core))
            else:
                pairs.append((index * 2 + core, index * 2 + 1 - core))
    return lax.ppermute(block, ("mp", "pool"), pairs)


def gather_and_exchange(own, outgoing, middle):
    arrived = {0: outgoing[0]}

    def after(block, *events):
        return lax.optimization_barrier((block, events))[0]

    def exchange(apart, *events):
        block = after(outgoing[apart], *events) if events else outgoing[apart]
        arrived[apart] = swap(block, apart)

    beside = swap(own, 2)
    over = cross(own)
    own_y = swap(own, 1)
    over_beside = cross(beside)
    over_passed = swap(over, 2)
    beside_y = swap(after(beside, own_y), 1)
    far_first = jnp.where(middle, over, over_passed)
    far_first_y = swap(after(far_first, beside_y), 1)
    over_beside_passed = swap(after(over_beside, outgoing[4]), 2)
    exchange(4, over_beside)
    exchange(6, over_beside)
    far_second = jnp.where(middle, over_beside, over_beside_passed)
    far_second_y = swap(after(far_second, far_first_y), 1)
    exchange(5, far_first_y, far_second)
    exchange(2, far_first_y, far_second)
    exchange(7, arrived[4], far_first_y)
    exchange(3, far_second_y)
    exchange(1, far_second_y)
    near = [after(own, far_second, arrived[4], arrived[6]), beside, own_y, beside_y]
    far = [far_first, far_second, far_first_y, far_second_y]
    return near, far, [arrived[apart] for apart in range(LINE_MODELS)]


def project_kernel(starts_ref, *refs):
    n_blocks = starts_ref.shape[0]
    blocks, refs = refs[:n_blocks], refs[n_blocks:]
    q_weights, (k_weight_ref, v_weight_ref), refs = refs[:STREAMS], refs[STREAMS:][:2], refs[STREAMS + 2 :]
    q_bias_ref, k_bias_ref, v_bias_ref, cos_ref, sin_ref = refs[:5]
    query_ref, key_ref, value_ref, pair_ref, tokens_ref, total_ref, sems = refs[5:]
    step = pl.program_id(0)
    depth = k_weight_ref.shape[0]
    q_width = q_weights[0].shape[1]
    rows = blocks[0].shape[0]

    @pl.when(step == 0)
    def _():
        copies = [
            pltpu.make_async_copy(
                block,
                tokens_ref.at[pl.ds(pl.multiple_of(starts_ref[index], rows), rows), :],
                sems.at[index],
            )
            for index, block in enumerate(blocks)
        ]
        for copy in copies:
            copy.start()
        total_ref[...] = jnp.zeros_like(total_ref)
        for copy in copies:
            copy.wait()

    tokens = tokens_ref[:, pl.ds(pl.multiple_of(step * depth, depth), depth)]
    q_weight = jnp.concatenate([ref[...] for ref in q_weights], axis=0)
    total_ref[:, :q_width] += jnp.dot(tokens, q_weight, preferred_element_type=jnp.float32)
    both = jnp.concatenate([k_weight_ref[...], v_weight_ref[...]], axis=1)
    total_ref[:, q_width:] += jnp.dot(tokens, both, preferred_element_type=jnp.float32)

    @pl.when(step == pl.num_programs(0) - 1)
    def _():
        cosine, sine = cos_ref[...], sin_ref[...]

        def turned(vectors):
            return vectors * cosine + pltpu.roll(vectors, HD // 2, 1) * sine

        for head in range(q_width // HD):
            cols = slice(head * HD, (head + 1) * HD)
            query = total_ref[:, cols] + q_bias_ref[:, cols].astype(jnp.float32)
            query_ref[head] = turned(query).astype(jnp.bfloat16)
        key = total_ref[:, q_width : q_width + HD] + k_bias_ref[...].astype(jnp.float32)
        key = turned(key.astype(jnp.bfloat16).astype(jnp.float32)).astype(jnp.bfloat16)
        value = total_ref[:, q_width + HD :] + v_bias_ref[...].astype(jnp.float32)
        value = value.astype(jnp.bfloat16)
        key_ref[...] = key
        value_ref[:, :HD] = value
        value_ref[:, HD:] = jnp.ones_like(value)
        pair_ref[:, :HD] = key
        pair_ref[:, HD:] = value


def project(starts, blocks, weights, biases, tables):
    width = blocks[0].shape[1]
    rows = sum(block.shape[0] for block in blocks)
    depth = math.gcd(width, 1024)
    q_width = weights[0].shape[1]
    out_width = q_width + 2 * HD
    fixed = lambda array: pl.BlockSpec(array.shape, lambda step: (0,) * len(array.shape))
    in_specs = [pl.BlockSpec(memory_space=pltpu.SMEM)]
    in_specs += [pl.BlockSpec(memory_space=pl.ANY)] * len(blocks)
    in_specs += [
        pl.BlockSpec((depth // STREAMS, q_width), lambda step, part=part: (step * STREAMS + part, 0))
        for part in range(STREAMS)
    ]
    in_specs += [pl.BlockSpec((depth, HD), lambda step: (step, 0))] * 2
    in_specs += [fixed(array) for array in (*biases, *tables)]
    out_shape = (
        jax.ShapeDtypeStruct((q_width // HD, rows, HD), jnp.bfloat16),
        jax.ShapeDtypeStruct((rows, HD), jnp.bfloat16),
        jax.ShapeDtypeStruct((rows, 2 * HD), jnp.bfloat16),
        jax.ShapeDtypeStruct((rows, 2 * HD), jnp.bfloat16),
    )
    return pl.pallas_call(
        project_kernel,
        grid=(width // depth,),
        out_shape=out_shape,
        in_specs=in_specs,
        out_specs=tuple(fixed(shape) for shape in out_shape),
        scratch_shapes=[
            pltpu.VMEM((rows, width), jnp.bfloat16),
            pltpu.VMEM((rows, out_width), jnp.float32),
            pltpu.SemaphoreType.DMA((len(blocks),)),
        ],
        compiler_params=pltpu.CompilerParams(vmem_limit_bytes=VMEM_LIMIT),
        cost_estimate=pl.CostEstimate(
            flops=2 * rows * width * out_width,
            bytes_accessed=2 * width * (rows + out_width) + 4 * rows * out_width,
            transcendentals=0,
        ),
        name="project",
    )(starts, *blocks, *weights[:1] * STREAMS, *weights[1:], *biases, *tables)


class RingScatter:
    def __init__(self, shares, places, order, way):
        self.shares, self.places, self.order, self.way = shares, places, order, way
        self.n_model = len(order)
        self.distance = {way: self.n_model // 2, -way: self.n_model // 2 - 1}
        self.moving = {}

    def share_of(self, offset):
        place = self.places[offset % self.n_model]
        return lax.dynamic_index_in_dim(self.shares, place, 0, keepdims=False)

    def step(self, *before):
        ways = [way for way in (self.way, -self.way) if self.distance[way]]
        blocks = []
        for way in ways:
            block = self.share_of(way * self.distance[way])
            if way in self.moving:
                arrived = self.moving[way].astype(jnp.float32)
                block = (block.astype(jnp.float32) + arrived).astype(jnp.bfloat16)
            blocks.append(block)
            self.distance[way] -= 1
        blocks, _ = lax.optimization_barrier((blocks, (before, list(self.moving.values()))))
        for way, block in zip(ways, blocks):
            pairs = [
                (self.order[i], self.order[(i + way) % self.n_model]) for i in range(self.n_model)
            ]
            self.moving[way] = lax.ppermute(block, "mp", pairs)
        return blocks

    def finish(self):
        total = self.share_of(0).astype(jnp.float32)
        for way in (1, -1):
            total = total + self.moving[way].astype(jnp.float32)
        return total.astype(jnp.bfloat16)


def pick_kernel(slots_ref, pool_ref, out_ref):
    def place(rank, _):
        out_ref[rank] = pool_ref[slots_ref[rank]]
        return 0

    lax.fori_loop(0, slots_ref.shape[0], place, 0)


def pick_blocks(pool, slots):
    return pl.pallas_call(
        pick_kernel,
        out_shape=jax.ShapeDtypeStruct((*slots.shape, *pool.shape[1:]), pool.dtype),
        in_specs=[
            pl.BlockSpec(memory_space=pltpu.SMEM),
            pl.BlockSpec(memory_space=pltpu.VMEM),
        ],
        out_specs=pl.BlockSpec(memory_space=pltpu.VMEM),
        compiler_params=pltpu.CompilerParams(vmem_limit_bytes=ATTEND_VMEM),
        name="pick_blocks",
    )(slots, pool)


def pack_kernel(lists, slots_ref, heads_ref, *refs):
    sources, out_refs = refs[: len(lists)], refs[len(lists) :]

    def place(rank, _):
        for listed, source_ref in zip(lists, sources):
            slot = slots_ref[listed, rank]
            for dest, out_ref in enumerate(out_refs):
                first = pl.multiple_of(heads_ref[dest] * 2 * HD, 2 * HD)
                out_ref[listed, rank] = source_ref[slot, :, pl.ds(first, 2 * HD)]
        return 0

    lax.fori_loop(0, slots_ref.shape[1], place, 0)


def pack_blocks(sources, slots, heads):
    dests = heads.shape[0]
    block_len = sources[0].shape[1]
    shape = jax.ShapeDtypeStruct((*slots.shape, block_len, 2 * HD), jnp.bfloat16)
    return pl.pallas_call(
        functools.partial(pack_kernel, range(len(sources))),
        out_shape=[shape] * dests,
        in_specs=[pl.BlockSpec(memory_space=pltpu.SMEM)] * 2
        + [pl.BlockSpec(memory_space=pltpu.VMEM)] * len(sources),
        out_specs=[pl.BlockSpec(memory_space=pltpu.VMEM)] * dests,
        compiler_params=pltpu.CompilerParams(vmem_limit_bytes=ATTEND_VMEM),
        name="pack_blocks",
    )(slots, heads, *sources)


def order_kernel(length_ref, where_ref, *refs):
    *arrived_refs, key_ref, value_ref, held_ref, sems = refs
    block_len = held_ref.shape[1]
    copies = []
    begin = 0
    for index, source in enumerate(arrived_refs):
        end = begin + source.shape[0]
        copies.append(pltpu.make_async_copy(source, held_ref.at[begin:end], sems.at[index]))
        begin = end
    for copy in copies:
        copy.start()
    for copy in copies:
        copy.wait()
    length = length_ref[0]
    first = held_ref[where_ref[0]][:1, :HD].astype(jnp.float32)
    row = lax.broadcasted_iota(jnp.int32, (block_len, HD), 0)

    def place(block_id, _):
        block = held_ref[where_ref[block_id]].astype(jnp.float32)
        start = pl.multiple_of(block_id * block_len, block_len)
        seen = row + start < length
        rows = pl.ds(start, block_len)
        key_ref[rows, :] = jnp.where(seen, block[:, :HD], first).astype(jnp.bfloat16)
        value_ref[rows, :HD] = jnp.where(seen, block[:, HD:], 0.0).astype(jnp.bfloat16)
        value_ref[rows, HD:] = jnp.where(seen, 1.0, 0.0).astype(jnp.bfloat16)
        return 0

    lax.fori_loop(0, where_ref.shape[0], place, 0, unroll=8)


def order_blocks(arrived, where, length):
    count = sum(array.shape[-3] for array in arrived)
    block_len = arrived[0].shape[-2]
    tokens = where.shape[0] * block_len
    return pl.pallas_call(
        order_kernel,
        out_shape=(
            jax.ShapeDtypeStruct((tokens, HD), jnp.bfloat16),
            jax.ShapeDtypeStruct((tokens, 2 * HD), jnp.bfloat16),
        ),
        in_specs=[pl.BlockSpec(memory_space=pltpu.SMEM)] * 2
        + [pl.BlockSpec(memory_space=pl.ANY)] * len(arrived),
        out_specs=(
            pl.BlockSpec(memory_space=pltpu.VMEM),
            pl.BlockSpec(memory_space=pltpu.VMEM),
        ),
        scratch_shapes=[
            pltpu.VMEM((count, block_len, 2 * HD), jnp.bfloat16),
            pltpu.SemaphoreType.DMA((len(arrived),)),
        ],
        compiler_params=pltpu.CompilerParams(vmem_limit_bytes=ATTEND_VMEM),
        name="order_blocks",
    )(length, where, *arrived)


def dot_keys(queries, keys):
    return lax.dot_general(
        queries, keys, (((1,), (1,)), ((), ())), preferred_element_type=jnp.float32
    )


def attend_kernel(span, half_ref, *refs):
    query_refs, (key_ref, value_ref), new_key_refs, new_value_refs, out_ref = (
        refs[:2],
        refs[2:4],
        refs[4:6],
        refs[6:8],
        refs[8],
    )
    rows = out_ref.shape[0]
    half = rows // 2
    queries = jnp.concatenate([ref[0] for ref in query_refs], 0)
    spans = key_ref.shape[0] // span
    turn = half_ref[0] * half
    token = lax.rem(lax.broadcasted_iota(jnp.int32, (rows, half), 0) + turn, rows)
    column = lax.broadcasted_iota(jnp.int32, (rows, half), 1)
    parts = []
    for side, ref in enumerate(new_key_refs):
        causal = column + lax.rem(turn + side * half, rows) <= token
        parts.append(jnp.where(causal, dot_keys(queries, ref[...]), -jnp.inf))
    scores = jnp.concatenate(parts, 1)
    peak = jnp.max(scores, axis=1, keepdims=True)
    total = None
    values = jnp.concatenate([ref[...] for ref in new_value_refs], 0)
    for index in range(spans + 1):
        if index < spans:
            next_scores = dot_keys(queries, key_ref[index * span : (index + 1) * span, :])
            next_peak = jnp.maximum(peak, jnp.max(next_scores, axis=1, keepdims=True))
        weights = jnp.exp2((scores - peak) * SCORE_SCALE).astype(jnp.bfloat16)
        product = jnp.dot(weights, values, preferred_element_type=jnp.float32)
        total = product if total is None else total + product
        if index < spans:
            total = total * jnp.exp2((peak - next_peak) * SCORE_SCALE)
            scores, peak = next_scores, next_peak
            values = value_ref[index * span : (index + 1) * span, :]
    out_ref[...] = (total[:, :HD] / total[:, HD:]).astype(jnp.bfloat16)


def attend(half, queries, prefix, new_keys, new_values):
    heads = queries[0].shape[0]
    rows = 2 * new_keys[0].shape[0]
    span = math.gcd(prefix[0].shape[0], 2048)
    whole = lambda array: pl.BlockSpec(array.shape, lambda step: (0, 0))
    count = prefix[0].shape[0] + rows
    query_spec = pl.BlockSpec((1, rows // 2, HD), lambda step: (step, 0, 0))
    fixed = (*prefix, *new_keys, *new_values)
    return pl.pallas_call(
        functools.partial(attend_kernel, span),
        grid=(heads,),
        out_shape=jax.ShapeDtypeStruct((rows, heads * HD), jnp.bfloat16),
        in_specs=[pl.BlockSpec(memory_space=pltpu.SMEM), query_spec, query_spec]
        + [whole(array) for array in fixed],
        out_specs=pl.BlockSpec((rows, HD), lambda step: (0, step)),
        compiler_params=pltpu.CompilerParams(vmem_limit_bytes=ATTEND_VMEM),
        cost_estimate=pl.CostEstimate(
            flops=heads * rows * count * HD * 8,
            bytes_accessed=2 * (count * 3 * HD + 2 * heads * rows * HD),
            transcendentals=heads * rows * count,
        ),
        name="attend",
    )(half, *queries, *fixed)


def on_device(
    n_model,
    n_pool,
    states,
    norm_gain,
    w_query,
    q_bias,
    w_key,
    w_value,
    k_bias,
    v_bias,
    w_out,
    kv_pool,
    hit_holder,
    hit_slot,
    prefix_len,
):
    my_model = lax.axis_index("mp")
    my_pool = lax.axis_index("pool")
    row_count = states.shape[1]
    suffix = row_count * n_model
    q_width = w_query.shape[1]
    q_local = q_width // HD
    kv_local = w_key.shape[1]
    kv_heads = kv_local * n_model // HD
    group_size = QH // kv_heads
    blocks_total = hit_holder.shape[1]
    block_len = kv_pool.shape[2]
    holders = n_model * n_pool
    capacity = 2 * blocks_total // holders
    sharers = HD // kv_local

    lined = n_model == LINE_MODELS

    self_holder = my_model * n_pool + my_pool
    chosen = listing(hit_holder == self_holder, capacity)
    slot_ids = jnp.sum(jnp.where(chosen, hit_slot[:, None, :], 0), -1)
    models = jnp.arange(n_model, dtype=jnp.int32)
    my_holder = hit_holder[my_pool]
    prefix_count = prefix_len[my_pool]
    block_ids = jnp.arange(blocks_total, dtype=jnp.int32)
    earlier = (my_holder[:, None] == my_holder[None, :]) & (block_ids[None, :] < block_ids[:, None])
    rank = jnp.sum(earlier.astype(jnp.int32), -1)
    normed = normalize(states[0], norm_gain)
    if lined:
        mine, others = (
            lax.dynamic_index_in_dim(slot_ids, pool, 0, keepdims=False)
            for pool in (my_pool, 1 - my_pool)
        )
        pool_blocks = kv_pool[0]
        picked, normed = lax.optimization_barrier((pick_blocks(pool_blocks, others), normed))
        got = lax.ppermute(picked, "pool", [(0, 1), (1, 0)])
        slots = jnp.stack([mine, jnp.arange(capacity, dtype=jnp.int32)])
        outgoing = pack_blocks((pool_blocks, got), slots, (models ^ my_model) * q_local // group_size)
        my_z, my_y = my_model // 2, my_model % 2
        near, far, arrived = gather_and_exchange(normed, outgoing, (my_z == 1) | (my_z == 2))
        arrived = [block.reshape(-1, block_len, 2 * HD) for block in arrived]
        distance = (my_holder // n_pool) ^ my_model
        where = (distance * n_pool + (my_holder % n_pool ^ my_pool)) * capacity + rank
    else:
        outgoing = pack_blocks((kv_pool[0],) * 2, slot_ids, models * q_local // group_size)
        outgoing = jnp.stack(outgoing).reshape(holders, capacity * block_len, 2 * HD)
        arrived = lax.all_to_all(outgoing, ("mp", "pool"), split_axis=0, concat_axis=0, tiled=True)
        arrived = [arrived.reshape(holders * capacity, block_len, 2 * HD)]
        where = my_holder * capacity + rank

    upper_half = (my_model // (n_model // 2)).astype(jnp.int32) if lined else jnp.int32(0)
    half_rows = suffix // 2
    order = (jnp.arange(suffix, dtype=jnp.int32) + upper_half * half_rows) % suffix
    cosine, sine = angle_tables(prefix_count + order)
    cosine, sine = jnp.concatenate([cosine, cosine], 1), jnp.concatenate([-sine, sine], 1)
    halves = [slice(0, half_rows), slice(half_rows, suffix)]
    biases = [bias.reshape(1, -1) for bias in (q_bias, k_bias, v_bias)]
    weights = (w_query, w_key, w_value)
    if lined:
        results = []
        for blocks, inner in ((near, my_z % 2), (far, upper_half)):
            starts = jnp.stack(
                [
                    2 * (inner ^ other) + (my_y ^ side)
                    for side in range(2)
                    for other in range(2)
                ]
            )
            table = [part[halves[len(results)]] for part in (cosine, sine)]
            results.append(
                project(starts.astype(jnp.int32) * row_count, blocks, weights, biases, table)
            )
        queries, new_keys, new_values, pairs = zip(*results)
        pairs = jnp.where(
            upper_half == 0, jnp.concatenate(pairs, 0), jnp.concatenate(pairs[::-1], 0)
        ).reshape(n_model, row_count, 2 * HD)
    else:
        tokens = lax.all_gather(normed, "mp", axis=0, tiled=True)
        linear, key_raw, value_raw = (
            jnp.dot(tokens, weight, preferred_element_type=jnp.float32) + bias.astype(jnp.float32)
            for weight, bias in zip(weights, biases)
        )
        cosine, sine = cosine[:, : HD // 2], sine[:, HD // 2 :]
        queries = rotate(linear.reshape(suffix, q_local, HD), cosine, sine)
        queries = queries.astype(jnp.bfloat16).transpose(1, 0, 2)
        key_raw, value_raw = key_raw.astype(jnp.bfloat16), value_raw.astype(jnp.bfloat16)
        together = [
            [first + other for other in range(sharers)] for first in range(0, n_model, sharers)
        ]
        key_whole, value_whole = (
            lax.all_gather(part, "mp", axis=1, tiled=True, axis_index_groups=together)
            for part in (key_raw, value_raw)
        )
        key_whole = rotate(key_whole.astype(jnp.float32)[:, None, :], cosine, sine)
        key_whole = key_whole.astype(jnp.bfloat16)[:, 0]
        value_ones = jnp.concatenate([value_whole, jnp.ones_like(value_whole)], 1)
        first_col = (my_model % sharers) * kv_local
        key_cols = lax.dynamic_slice_in_dim(key_whole, first_col, kv_local, 1)
        pairs = jnp.stack([key_cols, value_raw], 1).reshape(n_model, row_count, 2 * kv_local)
        queries = [queries[:, part] for part in halves]
        new_keys = [key_whole[part] for part in halves]
        new_values = [value_ones[part] for part in halves]

    pairs = lax.all_to_all(pairs, "mp", split_axis=0, concat_axis=0, tiled=True)
    arrived, new_keys, pairs = lax.optimization_barrier((arrived, list(new_keys), pairs))
    cache_rows = (
        pairs.reshape(kv_heads, sharers, row_count, 2, kv_local)
        .transpose(2, 0, 3, 1, 4)
        .reshape(1, row_count, kv_heads * 2 * HD)
    )
    prefix = order_blocks(arrived, where, prefix_count.reshape(1))
    mixed = attend(upper_half.reshape(1), queries, prefix, new_keys, new_values)
    width = w_out.shape[1] // COLUMN_CHUNKS
    shares = [
        jnp.dot(
            mixed,
            w_out[:, chunk * width : (chunk + 1) * width],
            preferred_element_type=jnp.float32,
        ).astype(jnp.bfloat16)
        for chunk in range(COLUMN_CHUNKS)
    ]

    order = [m for m in range(0, n_model, 2)] + [m for m in range(n_model - 1, 0, -2)]
    half = n_model // 2
    spot = jnp.where(my_model % 2 == 0, my_model // 2, n_model - 1 - my_model // 2)
    places = []
    for offset in range(n_model):
        index = (spot + offset) % n_model
        owner = jnp.where(index < half, 2 * index, 2 * (n_model - 1 - index) + 1)
        places.append((owner + n_model - upper_half * half) % n_model)
    scatters = [
        RingScatter(
            share.reshape(n_model, row_count, -1), places, order, 1 if chunk % 2 == 0 else -1
        )
        for chunk, share in enumerate(shares)
    ]
    sent, sums = [], []
    steps = n_model // 2
    for step in range(steps):
        for scatter in scatters:
            sent = scatter.step(sent, sums)
            if step == steps - 1:
                sums.append(scatter.finish())
    return (jnp.concatenate(sums, 1)[None], cache_rows)


def solution(mesh):
    placed = (
        P(("groups", "pool"), "mp", None),
        P(),
        P(None, "mp"),
        P("mp"),
        P(None, "mp"),
        P(None, "mp"),
        P("mp"),
        P("mp"),
        P("mp", None),
        P(("groups", "mp", "pool"), None, None, None),
        P("groups", None),
        P("groups", None),
        P("groups"),
    )
    return jax.shard_map(
        functools.partial(on_device, mesh.shape["mp"], mesh.shape["pool"]),
        mesh=mesh,
        in_specs=placed,
        out_specs=(P(("groups", "pool"), "mp", None), P(("groups", "pool"), "mp", None)),
        check_vma=False,
    )
```
